32 devices in a mesh: fsdp: 8 (over z, core), ctx: 4 (over y, x).
Axes of the slice: x: 2, y: 2, z: 4, core: 2. Of those that a mesh axis runs over, the one named last changes fastest.
Arguments:
- tokens: bfloat16 [8192, 2048], P(('fsdp', 'ctx')), may hold values from -6 to 6
- positions: int32 [8192], P(('fsdp', 'ctx')), may hold values from 0 to 1023, as said below
- gain_attn: bfloat16 [2048], P('fsdp'), may hold values from 0.25 to 1.75
- gain_mlp: bfloat16 [2048], P('fsdp'), may hold values from 0.25 to 1.75
- w_query: bfloat16 [2048, 2048], P('fsdp'), may hold values from -0.25 to 0.25
- w_key: bfloat16 [2048, 256], P('fsdp'), may hold values from -0.25 to 0.25
- w_value: bfloat16 [2048, 256], P('fsdp'), may hold values from -0.125 to 0.125
- w_out: bfloat16 [2048, 2048], P('fsdp'), may hold values from -1 to 1
- w_gate: bfloat16 [2048, 5632], P('fsdp'), may hold values from -0.125 to 0.125
- w_up: bfloat16 [2048, 5632], P('fsdp'), may hold values from -0.125 to 0.125
- w_down: bfloat16 [5632, 2048], P('fsdp'), may hold values from -0.15625 to 0.15625
- cotangent: bfloat16 [8192, 2048], P(('fsdp', 'ctx')), may hold values from -6 to 6
Outputs:
- output: bfloat16 [8192, 2048], P(('fsdp', 'ctx'))
- grad_tokens: float32 [8192, 2048], P(('fsdp', 'ctx'))
- grad_gain_attn: float32 [2048], P('fsdp')
- grad_gain_mlp: float32 [2048], P('fsdp')
- grad_query: float32 [2048, 2048], P('fsdp')
- grad_key: float32 [2048, 256], P('fsdp')
- grad_value: float32 [2048, 256], P('fsdp')
- grad_out: float32 [2048, 2048], P('fsdp')
- grad_gate: float32 [2048, 5632], P('fsdp')
- grad_up: float32 [2048, 5632], P('fsdp')
- grad_down: float32 [5632, 2048], P('fsdp')
The draws below stay inside these ranges and needn't reach their ends.
Inputs may be any that keep to these rules, and one draw needn't show every extreme that they name: positions count from 0 at a document's first token and rise by one per token within it; the first token of every sequence of 1024 has position 0; one sequence, drawn from the seed, is a single document of all 1024 tokens.
All inputs are finite; a program needn't handle non-finite values.
Results may differ from the reference program's by a relative error of at most 0.024.
Values may be sent and summed in bfloat16 or wider, within the bound.
A program may use at most 384 MiB of HBM per device.

```python
import jax
import jax.numpy as jnp
from jax import lax

D = 2048
HEADS = 32
KV_HEADS = 4
HEAD_DIM = 64
FF = 5632
TOK_DEV = 256
QD = 2048
KVD = 256
LENGTH = 1024
TOKENS = 8192
N_FSDP = 8


def draw_positions(key, part):
    key = jax.random.fold_in(key, 11)
    seq_count = N_FSDP
    seq_length = LENGTH
    key_begin, key_finish, key_marks, key_pick = jax.random.split(key, 4)
    half_block = max(TOK_DEV // 2, 2)
    chosen = jax.random.randint(key_pick, (), 0, seq_count)
    whole_doc = jnp.arange(seq_count, dtype=jnp.int32)[:, None] == chosen
    doc_start = jax.random.randint(key_begin, (seq_count, 1), 1, half_block)
    doc_stop = seq_length - jax.random.randint(key_finish, (seq_count, 1), 1, half_block)
    doc_start = jnp.where(whole_doc, 0, doc_start)
    doc_stop = jnp.where(whole_doc, seq_length, doc_stop)
    place_index = jnp.arange(seq_length, dtype=jnp.int32)[None, :]
    break_marks = jax.random.randint(key_marks, (seq_count, seq_length), 0, 16) == 0
    outside = (place_index < doc_start) | (place_index >= doc_stop)
    begins = (place_index == 0) | (place_index == doc_start) | (place_index == doc_stop) | break_marks & outside
    marked = jnp.where(begins, place_index, 0)
    doc_first = lax.cummax(marked, axis=1)
    return (place_index - doc_first).reshape(seq_count * seq_length).astype(jnp.int32)


def block_scale(key, extent, cuts, least, high):
    gain, own = 1.0, jax.random.fold_in(key, 6)
    for position, shards_of in cuts:
        heights = jnp.exp(jax.random.uniform(jax.random.fold_in(own, position), (shards_of,), jnp.float32, least / len(cuts), high / len(cuts)))
        gain = gain * jnp.repeat(heights, extent[position] // shards_of).reshape([-1 if axis == position else 1 for axis in range(len(extent))])
    return gain


def scatter_about(key, dims, scale, bound, cuts=(), held_as=jnp.bfloat16):
    array = scale * jax.random.normal(key, dims, jnp.float32)
    if cuts:
        array = array * block_scale(key, dims, cuts, -0.22, 0.18)
    return jnp.clip(array, -bound, bound).astype(held_as)


def setup_inputs(seed: int = 0) -> dict:
    key_list = jax.random.split(jax.random.key(seed), 13)
    return {
        "tokens": scatter_about(key_list[0], (TOKENS, D), 1.0, 6.0, ((0, 32),)),
        "positions": draw_positions(jax.random.fold_in(key_list[12], 71), 0),
        "gain_attn": jnp.clip(1.0 + 0.15 * jax.random.normal(key_list[2], (D,), jnp.float32), 0.25, 1.75).astype(jnp.bfloat16),
        "gain_mlp": jnp.clip(1.0 + 0.15 * jax.random.normal(key_list[3], (D,), jnp.float32), 0.25, 1.75).astype(jnp.bfloat16),
        "w_query": scatter_about(key_list[4], (D, QD), (D // 4) ** -0.5, 0.25, ((0, 8),)),
        "w_key": scatter_about(key_list[5], (D, KVD), (D // 4) ** -0.5, 0.25, ((0, 8),)),
        "w_value": scatter_about(key_list[6], (D, KVD), D ** -0.5, 0.125, ((0, 8),)),
        "w_out": scatter_about(key_list[7], (QD, D), (max(QD // 64, 1)) ** -0.5, 1.0, ((0, 8),)),
        "w_gate": scatter_about(key_list[8], (D, FF), D ** -0.5, 0.125, ((0, 8),)),
        "w_up": scatter_about(key_list[9], (D, FF), D ** -0.5, 0.125, ((0, 8),)),
        "w_down": scatter_about(key_list[10], (FF, D), (FF // 4) ** -0.5, 0.15625, ((0, 8),)),
        "cotangent": scatter_about(key_list[11], (TOKENS, D), 1.0, 6.0, ((0, 32),)),
    }


@jax.custom_vjp
def low(v):
    return lax.optimization_barrier(v.astype(jnp.bfloat16)).astype(jnp.float32)

@jax.custom_vjp
def low_back(v):
    return v

def low_keep(v):
    return (low(v), None)

def low_pass(kept, grad):
    return (grad,)

def back_keep(v):
    return (v, None)

def back_low(kept, grad):
    return (low(grad),)
low.defvjp(low_keep, low_pass)
low_back.defvjp(back_keep, back_low)
eps_norm = 1e-05
theta_base = 10000.0
neg_large = -1e+30
highest = lax.Precision.HIGHEST

def rms_scale(values_in, gain_row):
    return values_in * lax.rsqrt(lax.optimization_barrier(jnp.mean(values_in * values_in, axis=-1, keepdims=True)) + eps_norm) * gain_row

def rope_tables(positions):
    half_width = HEAD_DIM // 2
    frequency = theta_base ** (-(jnp.arange(half_width, dtype=jnp.float32) * 2.0) / HEAD_DIM)
    angles = positions.astype(jnp.float32)[:, None] * frequency[None, :]
    return (jnp.cos(angles)[:, None, :], jnp.sin(angles)[:, None, :])

def rotate(field, cosine, sine_table):
    half_width = field.shape[-1] // 2
    first_half = field[..., :half_width]
    second_half = field[..., half_width:]
    return jnp.concatenate([first_half * cosine - second_half * sine_table, second_half * cosine + first_half * sine_table], axis=-1)

def sequence_attention(query_seq, key_seq, value_seq, position_seq):
    block_rows = min(512, LENGTH)
    blocks = LENGTH // block_rows
    group_size = HEADS // KV_HEADS
    grouped = query_seq.reshape(blocks, block_rows, KV_HEADS, group_size, HEAD_DIM)
    token_place = jnp.arange(LENGTH, dtype=jnp.int32)
    begins = (token_place - position_seq).reshape(blocks, block_rows)
    places = token_place.reshape(blocks, block_rows)

    def one_block(block_items):
        query_block, query_place, query_begin = block_items
        scores = jnp.einsum('qkgd,lkd->qkgl', query_block, key_seq, precision=highest) * HEAD_DIM ** (-0.5)
        scores = low_back(scores)
        allowed = (token_place[None, :] <= query_place[:, None]) & (token_place[None, :] >= query_begin[:, None])
        scores = jnp.where(allowed[:, None, None, :], scores, neg_large)
        top_score = lax.optimization_barrier(jnp.max(scores, axis=-1, keepdims=True))
        weights = jnp.exp(scores - top_score)
        probs = low(weights / lax.optimization_barrier(jnp.sum(weights, axis=-1, keepdims=True)))
        return jnp.einsum('qkgl,lkd->qkgd', probs, value_seq, precision=highest)
    result = lax.map(jax.checkpoint(one_block), (grouped, places, begins))
    return result.reshape(LENGTH, HEADS * HEAD_DIM)

def reference(tokens, positions, gain_attn, gain_mlp, w_query, w_key, w_value, w_out, w_gate, w_up, w_down, cotangent):
    cosine, sine_table = rope_tables(positions)
    seq_count = TOKENS // LENGTH

    def layer(inputs, gain_one, gain_two, query_weight, key_weight, value_weight, out_weight, gate_weight, up_weight, down_weight):
        normed_one = low(rms_scale(inputs, gain_one))
        pre_query = low_back(jnp.dot(normed_one, query_weight, precision=highest))
        pre_key = low_back(jnp.dot(normed_one, key_weight, precision=highest))
        values = low(low_back(jnp.dot(normed_one, value_weight, precision=highest)))
        queries = low(rotate(pre_query.reshape(TOKENS, HEADS, HEAD_DIM), cosine, sine_table))
        key_rows = low(rotate(pre_key.reshape(TOKENS, KV_HEADS, HEAD_DIM), cosine, sine_table))

        def per_sequence(seq_items):
            return sequence_attention(seq_items[0], seq_items[1], seq_items[2], seq_items[3])
        attended = lax.map(per_sequence, (queries.reshape(seq_count, LENGTH, HEADS, HEAD_DIM), key_rows.reshape(seq_count, LENGTH, KV_HEADS, HEAD_DIM), values.reshape(seq_count, LENGTH, KV_HEADS, HEAD_DIM), positions.reshape(seq_count, LENGTH)))
        attended = low(low_back(attended.reshape(TOKENS, HEADS * HEAD_DIM)))
        middle = inputs + low_back(jnp.dot(attended, out_weight, precision=highest))
        normed_two = low(rms_scale(middle, gain_two))
        gate_pre = low_back(jnp.dot(normed_two, gate_weight, precision=highest))
        up_pre = low_back(jnp.dot(normed_two, up_weight, precision=highest))
        hidden = low(jax.nn.silu(gate_pre) * up_pre)
        return middle + low_back(jnp.dot(hidden, down_weight, precision=highest))
    output, pullback = jax.vjp(layer, tokens.astype(jnp.float32), gain_attn.astype(jnp.float32), gain_mlp.astype(jnp.float32), w_query.astype(jnp.float32), w_key.astype(jnp.float32), w_value.astype(jnp.float32), w_out.astype(jnp.float32), w_gate.astype(jnp.float32), w_up.astype(jnp.float32), w_down.astype(jnp.float32))
    grads = pullback(cotangent.astype(jnp.float32))
    return (output.astype(jnp.bfloat16), grads[0], grads[1], grads[2], grads[3], grads[4], grads[5], grads[6], grads[7], grads[8], grads[9])
```

```python
import jax
import jax.numpy as jnp
from jax import lax
from jax.sharding import PartitionSpec as P

HEADS = 32
KV_HEADS = 4
HEAD_DIM = 64

eps_norm = 1e-05
theta_base = 10000.0
neg_large = -1e30
bf16 = jnp.bfloat16
f32 = jnp.float32


def dot(a, b):
    return jnp.dot(a, b, preferred_element_type=f32)


def dot_nt(a, b):
    return lax.dot_general(a, b, (((1,), (1,)), ((), ())), preferred_element_type=f32)


def dot_tn(a, b):
    return lax.dot_general(a, b, (((0,), (0,)), ((), ())), preferred_element_type=f32)


def rope_tables(positions):
    half_width = HEAD_DIM // 2
    frequency = theta_base ** (-(jnp.arange(half_width, dtype=f32) * 2.0) / HEAD_DIM)
    angles = positions.astype(f32)[:, None] * frequency[None, :]
    return (jnp.cos(angles)[:, None, :], jnp.sin(angles)[:, None, :])


def rotate(field, cosine, sine_table, direction):
    half_width = field.shape[-1] // 2
    first_half = field[..., :half_width]
    second_half = field[..., half_width:]
    return jnp.concatenate(
        [
            first_half * cosine - direction * second_half * sine_table,
            second_half * cosine + direction * first_half * sine_table,
        ],
        axis=-1,
    )


def gather(x, axis_name, axis=0):
    return lax.all_gather(x, axis_name, axis=axis, tiled=True)


def scatter(x, axis_name, axis=0):
    return lax.psum_scatter(x.astype(bf16), axis_name, scatter_dimension=axis, tiled=True)


def per_device(
    tokens,
    positions,
    gain_attn,
    gain_mlp,
    w_query,
    w_key,
    w_value,
    w_out,
    w_gate,
    w_up,
    w_down,
    cotangent,
):
    n_ctx = lax.axis_size("ctx")
    n_fsdp = lax.axis_size("fsdp")
    c = lax.axis_index("ctx")
    rows = tokens.shape[0]
    width = tokens.shape[1]
    seq = rows * n_ctx
    own_rows = w_query.shape[0]
    my_heads = HEADS // n_ctx
    q_width = my_heads * HEAD_DIM
    kv_heads = max(1, KV_HEADS // n_ctx)
    copies = max(1, n_ctx // KV_HEADS)
    kv_width = kv_heads * HEAD_DIM
    per_kv = my_heads // kv_heads
    col_width = width // n_ctx
    ff_width = w_gate.shape[1]
    unit = ff_width // (n_fsdp * n_ctx)
    scale = HEAD_DIM ** (-0.5)

    def columns(w, start, count):
        return lax.dynamic_slice_in_dim(w, start, count, axis=1)

    gain_one = gain_attn.astype(f32)[:, None]
    gain_two = gain_mlp.astype(f32)[:, None]

    qkv_own = jnp.concatenate(
        [
            columns(w_query, c * q_width, q_width),
            columns(w_key, (c // copies) * kv_width, kv_width),
            columns(w_value, (c // copies) * kv_width, kv_width),
        ],
        axis=1,
    )
    qkv_own = (gain_one * qkv_own).astype(bf16)
    out_own = columns(w_out, c * col_width, col_width)

    def units(w):
        parts = w.reshape(own_rows, n_fsdp, n_ctx, unit)
        return lax.dynamic_index_in_dim(parts, c, axis=2, keepdims=False).reshape(
            own_rows, n_fsdp * unit
        )

    gate_own = (gain_two * units(w_gate)).astype(bf16)
    up_own = (gain_two * units(w_up)).astype(bf16)
    down_own = lax.dynamic_slice_in_dim(w_down, c * unit, unit, axis=0)

    x_all = gather(tokens, "ctx")
    pos_all = gather(positions, "ctx")
    qkv_w = gather(qkv_own, "fsdp")
    out_w = gather(out_own, "fsdp")
    gate_w = gather(gate_own, "fsdp")
    up_w = gather(up_own, "fsdp")
    down_w = gather(down_own, "fsdp")
    cot_all = gather(cotangent, "ctx")

    x_f = x_all.astype(f32)
    r_one = lax.rsqrt(jnp.mean(x_f * x_f, axis=-1, keepdims=True) + eps_norm)
    pre = dot(x_all, qkv_w) * r_one
    cosine, sine = rope_tables(pos_all)
    index = jnp.arange(seq, dtype=jnp.int32)
    begin = index - pos_all
    allowed = (index[None, :] <= index[:, None]) & (index[None, :] >= begin[:, None])

    q = rotate(pre[:, :q_width].reshape(seq, my_heads, HEAD_DIM), cosine, sine, 1.0).astype(bf16)
    k = rotate(
        pre[:, q_width : q_width + kv_width].reshape(seq, kv_heads, HEAD_DIM), cosine, sine, 1.0
    ).astype(bf16)
    v = pre[:, q_width + kv_width :].astype(bf16).reshape(seq, kv_heads, HEAD_DIM)
    q = q.reshape(seq, kv_heads, per_kv, HEAD_DIM)

    scores = jnp.einsum("qkgd,lkd->kgql", q, k, preferred_element_type=f32) * scale
    scores = jnp.where(allowed[None, None], scores, neg_large)
    top = jnp.max(scores, axis=-1, keepdims=True)
    weights = jnp.where(allowed[None, None], jnp.exp(scores - top), 0.0)
    probs = weights / jnp.sum(weights, axis=-1, keepdims=True)
    probs_low = probs.astype(bf16)
    attended = jnp.einsum("kgql,lkd->qkgd", probs_low, v, preferred_element_type=f32)
    att_own = attended.astype(bf16).reshape(seq, q_width)
    att_all = gather(att_own, "ctx", axis=1)

    mid_own = columns(x_all, c * col_width, col_width).astype(f32) + dot(att_all, out_w)
    mid_all = gather(mid_own.astype(bf16), "ctx", axis=1)
    mid_f = mid_all.astype(f32)
    r_two = lax.rsqrt(jnp.mean(mid_f * mid_f, axis=-1, keepdims=True) + eps_norm)
    gate = dot(mid_all, gate_w) * r_two
    up = dot(mid_all, up_w) * r_two
    sig = jax.nn.sigmoid(gate)
    hidden = (gate * sig * up).astype(bf16)
    mlp = scatter(dot(hidden, down_w), "ctx").astype(f32)
    mid_rows = lax.dynamic_slice_in_dim(mid_all, c * rows, rows, axis=0).astype(f32)
    output = (mid_rows + mlp).astype(bf16)

    grad_hidden = dot_nt(cot_all, down_w)
    grad_down_raw = scatter(dot_tn(hidden, cot_all), "fsdp")
    d_gate = grad_hidden * up * sig * (1.0 + gate * (1.0 - sig))
    d_up = grad_hidden * gate * sig
    stat_two = jnp.sum(d_gate * gate + d_up * up, axis=-1, keepdims=True)
    d_gate = (d_gate * r_two).astype(bf16)
    d_up = (d_up * r_two).astype(bf16)
    grad_gate_raw = scatter(dot_tn(mid_all, d_gate), "fsdp")
    grad_up_raw = scatter(dot_tn(mid_all, d_up), "fsdp")
    back_two = dot_nt(d_gate, gate_w) + dot_nt(d_up, up_w)
    back_two = back_two - mid_f * (r_two * r_two * stat_two * (1.0 / width))
    back_own = scatter(back_two, "ctx", axis=1).astype(f32)
    gm_own = columns(cot_all, c * col_width, col_width).astype(f32) + back_own
    gm_low = gm_own.astype(bf16)

    grad_out_raw = scatter(dot_tn(att_all, gm_low), "fsdp")
    d_att = scatter(dot_nt(gm_low, out_w), "ctx", axis=1).reshape(seq, kv_heads, per_kv, HEAD_DIM)
    d_probs = jnp.einsum("qkgd,lkd->kgql", d_att, v, preferred_element_type=f32)
    delta = jnp.sum(probs * d_probs, axis=-1, keepdims=True)
    d_scores = (probs * (d_probs - delta)).astype(bf16)
    d_q = jnp.einsum("kgql,lkd->qkgd", d_scores, k, preferred_element_type=f32) * scale
    d_k = jnp.einsum("kgql,qkgd->lkd", d_scores, q, preferred_element_type=f32) * scale
    d_v = jnp.einsum("kgql,qkgd->lkd", probs_low, d_att, preferred_element_type=f32)
    d_pre = jnp.concatenate(
        [
            rotate(d_q.reshape(seq, my_heads, HEAD_DIM), cosine, sine, -1.0).reshape(seq, q_width),
            rotate(d_k, cosine, sine, -1.0).reshape(seq, kv_width),
            d_v.reshape(seq, kv_width),
        ],
        axis=1,
    )
    stat_one = jnp.sum(d_pre * pre, axis=-1, keepdims=True)
    d_pre = (d_pre * r_one).astype(bf16)
    grad_qkv_raw = scatter(dot_tn(x_all, d_pre), "fsdp")
    back_one = dot_nt(d_pre, qkv_w) - x_f * (r_one * r_one * stat_one * (1.0 / width))
    at = (jnp.arange(width, dtype=jnp.int32) // col_width == c)[None, :]
    back_one = back_one + jnp.where(at, jnp.tile(gm_own, (1, n_ctx)), 0.0)
    grad_tokens = scatter(back_one, "ctx").astype(f32)

    qkv_grad = gather(grad_qkv_raw[None], "ctx").astype(f32)

    def joined(part):
        return jnp.moveaxis(part, 0, 1).reshape(own_rows, -1)

    raw_query = joined(qkv_grad[:, :, :q_width])

    def kv(part):
        part = part.reshape(n_ctx // copies, copies, own_rows, kv_width).sum(axis=1)
        return joined(part)

    raw_key = kv(qkv_grad[:, :, q_width : q_width + kv_width])
    raw_value = kv(qkv_grad[:, :, q_width + kv_width :])
    grad_out = gather(grad_out_raw, "ctx", axis=1).astype(f32)

    def spread(part):
        full = gather(part[None], "ctx").reshape(n_ctx, own_rows, n_fsdp, unit)
        return full.transpose(1, 2, 0, 3).reshape(own_rows, ff_width).astype(f32)

    raw_gate = spread(grad_gate_raw)
    raw_up = spread(grad_up_raw)
    grad_down = gather(grad_down_raw, "ctx").astype(f32)

    def gain_term(raw, w):
        return jnp.sum(raw * w.astype(f32), axis=1)

    grad_gain_one = (
        gain_term(raw_query, w_query) + gain_term(raw_key, w_key) + gain_term(raw_value, w_value)
    )
    grad_gain_two = gain_term(raw_gate, w_gate) + gain_term(raw_up, w_up)
    return (
        output,
        grad_tokens,
        grad_gain_one,
        grad_gain_two,
        gain_one * raw_query,
        gain_one * raw_key,
        gain_one * raw_value,
        grad_out,
        gain_two * raw_gate,
        gain_two * raw_up,
        grad_down,
    )


def solution(mesh):
    both = P(("fsdp", "ctx"), None)
    first = P("fsdp", None)
    return jax.shard_map(
        per_device,
        mesh=mesh,
        in_specs=(both, P(("fsdp", "ctx")), P("fsdp"), P("fsdp")) + (first,) * 7 + (both,),
        out_specs=(both, both, P("fsdp"), P("fsdp")) + (first,) * 7,
        check_vma=False,
    )
```

```python
import jax
import jax.numpy as jnp
from jax import lax
from jax.experimental import pallas as pl
from jax.experimental.pallas import tpu as pltpu
from jax.sharding import PartitionSpec as P

HEADS = 32
KV_HEADS = 4
HEAD_DIM = 64

eps_norm = 1e-05
theta_base = 10000.0
neg_large = -1e30
bf16 = jnp.bfloat16
f32 = jnp.float32
MESH_IDS = pl.DeviceIdType.MESH


def dot(a, b):
    return jnp.dot(a, b, preferred_element_type=f32)


def dot_nt(a, b):
    return lax.dot_general(a, b, (((1,), (1,)), ((), ())), preferred_element_type=f32)


def dot_tn(a, b):
    return lax.dot_general(a, b, (((0,), (0,)), ((), ())), preferred_element_type=f32)


class Place:
    def __init__(self):
        self.f = lax.axis_index("fsdp")
        self.c = lax.axis_index("ctx")
        self.depth = lax.axis_size("fsdp") // 2
        self.z = self.f // 2
        self.core = self.f % 2
        self.other = 1 - self.core
        self.cx = self.c + 1 - 2 * (self.c % 2)
        self.cy = self.c + 2 - 4 * (self.c // 2)
        self.cd = 3 - self.c
        self.sibling = {"fsdp": self.f + 1 - 2 * self.core}
        self.up = {"fsdp": self.f + 2}
        self.down = {"fsdp": self.f - 2}
        self.x = {"ctx": self.cx}
        self.y = {"ctx": self.cy}

    def has_up(self):
        return self.z < self.depth - 1

    def has_down(self):
        return self.z > 0

    def barrier(self):
        sem = pltpu.get_barrier_semaphore()

        def greet(device):
            pl.semaphore_signal(sem, inc=1, device_id=device, device_id_type=MESH_IDS)

        greet(self.sibling)
        greet(self.x)
        greet(self.y)

        @pl.when(self.has_up())
        def _():
            greet(self.up)

        @pl.when(self.has_down())
        def _():
            greet(self.down)

        last = self.depth - 1
        pl.semaphore_wait(sem, 4 - self.z // last + (self.z + last - 1) // last)


def remote(src, dst, send_sem, recv_sem, device):
    return pltpu.make_async_remote_copy(
        src_ref=src,
        dst_ref=dst,
        send_sem=send_sem,
        recv_sem=recv_sem,
        device_id=device,
        device_id_type=MESH_IDS,
    )


class LineGather:
    SEMS = 21

    def __init__(self, place, own, full, sems):
        self.p, self.own, self.full, self.sems = place, own, full, sems
        self.rows = own.shape[0]
        self.n = place.depth

    def view(self, level, core):
        start = pl.multiple_of((2 * level + core) * self.rows, 16)
        return self.full.at[pl.ds(start, self.rows)]

    def to_up(self, hop):
        p = self.p
        level = p.z - (hop - 1)
        src = self.own if hop == 1 else self.view(level, p.core)
        return remote(
            src, self.view(level, p.core), self.sems.at[hop - 1], self.sems.at[6 + hop - 1], p.up
        )

    def to_down(self, hop):
        p = self.p
        level = p.z + (hop - 1)
        src = self.own if hop == 1 else self.view(level, p.core)
        return remote(
            src, self.view(level, p.core), self.sems.at[3 + hop - 1], self.sems.at[9 + hop - 1], p.down
        )

    def to_sibling(self, level, own=False):
        p = self.p
        src = self.own if own else self.view(level, p.core)
        return remote(
            src, self.view(level, p.core), self.sems.at[12 + level], self.sems.at[16 + level], p.sibling
        )

    def local(self):
        p = self.p
        return pltpu.make_async_copy(self.own, self.view(p.z, p.core), self.sems.at[20])

    def start(self):
        p = self.p

        @pl.when(p.has_up())
        def _():
            self.to_up(1).start()

        @pl.when(p.has_down())
        def _():
            self.to_down(1).start()

        self.to_sibling(p.z, True).start()
        self.local().start()

    def arrived(self, level, sem):
        view = self.view(level, self.p.core)
        remote(view, view, self.sems.at[0], sem, self.p.sibling).wait_recv()

    def hop(self, s):
        p = self.p

        @pl.when(p.z >= s)
        def _():
            self.arrived(p.z - s, self.sems.at[6 + s - 1])
            if s < self.n - 1:

                @pl.when(p.has_up())
                def _():
                    self.to_up(s + 1).start()

            self.to_sibling(p.z - s).start()

        @pl.when(p.z + s < self.n)
        def _():
            self.arrived(p.z + s, self.sems.at[9 + s - 1])
            if s < self.n - 1:

                @pl.when(p.has_down())
                def _():
                    self.to_down(s + 1).start()

            self.to_sibling(p.z + s).start()

    def finish(self):
        p = self.p
        self.local().wait()
        for level in range(self.n):
            view = self.view(level, p.other)
            remote(view, view, self.sems.at[0], self.sems.at[16 + level], p.sibling).wait_recv()

    def drain(self):
        p = self.p
        for s in range(1, self.n):

            @pl.when(p.has_up() & (p.z >= s - 1))
            def _():
                self.to_up(s).wait_send()

            @pl.when(p.has_down() & (p.z + s - 1 < self.n))
            def _():
                self.to_down(s).wait_send()

        for level in range(self.n):
            self.to_sibling(level).wait_send()


class PlaneGather:
    SEMS = 8

    def __init__(self, place, view, half, sems, own=None):
        self.p, self.view, self.half, self.sems = place, view, half, sems
        self.own = own

    def src(self):
        return self.view(self.p.c) if self.own is None else self.own

    def to_x(self):
        p = self.p
        return remote(self.src(), self.view(p.c), self.sems.at[0], self.sems.at[2], p.x)

    def to_y(self):
        p = self.p
        return remote(self.src(), self.view(p.c), self.sems.at[1], self.sems.at[3], p.y)

    def on_to_y(self):
        p, h = self.p, self.half(self.p.cx, 0)
        return remote(h, h, self.sems.at[4], self.sems.at[6], p.y)

    def on_to_x(self):
        p, h = self.p, self.half(self.p.cy, 1)
        return remote(h, h, self.sems.at[5], self.sems.at[7], p.x)

    def start(self):
        self.to_x().start()
        self.to_y().start()

    def got(self, ref, sem):
        remote(ref, ref, self.sems.at[0], sem, self.p.x).wait_recv()

    def middle(self):
        p = self.p
        self.got(self.view(p.cx), self.sems.at[2])
        self.on_to_y().start()
        self.got(self.view(p.cy), self.sems.at[3])
        self.on_to_x().start()

    def finish(self):
        p = self.p
        self.got(self.half(p.cd, 0), self.sems.at[6])
        self.got(self.half(p.cd, 1), self.sems.at[7])

    def drain(self):
        self.to_x().wait_send()
        self.to_y().wait_send()
        self.on_to_y().wait_send()
        self.on_to_x().wait_send()


def rows_at(index, count):
    return pl.ds(pl.multiple_of(index * count, count), count)


def any_spec(count):
    return [pl.BlockSpec(memory_space=pl.ANY)] * count


def call(kernel, ins, outs, scratch, collective_id, flops, name):
    return pl.pallas_call(
        kernel,
        out_shape=[jax.ShapeDtypeStruct(s, d) for s, d in outs],
        in_specs=any_spec(len(ins)),
        out_specs=any_spec(len(outs)),
        scratch_shapes=scratch,
        compiler_params=pltpu.CompilerParams(
            collective_id=collective_id, has_side_effects=True, vmem_limit_bytes=60 * 2**20
        ),
        cost_estimate=pl.CostEstimate(flops=flops, bytes_accessed=2**26, transcendentals=2**22),
        name=name,
    )(*ins)


def forward_kernel(
    tok, tab, gains, wqkv_o, wout_o, wgate_o, wup_o, cot,
    x_out, xn_out, qt_out, kt_out, vt_out, lse_out, o_out, m_out,
    wqkv_out, wout_out, wgate, wup, cot_all, tab_out,
    X, XN, QT, KT, VT, K, LSE, O, M, WQ, WO, TAB, G8, GROW, BIAS, OT,
    line_sems, plane_sems, copy_sems,
):
    p = Place()
    n_ctx = 4
    rows = tok.shape[0]
    half = rows // 2
    qw = QT.shape[0]
    heads = qw // HEAD_DIM
    cw = O.shape[1] // n_ctx
    scale = HEAD_DIM ** (-0.5)

    p.barrier()

    gain_line = LineGather(p, gains, G8, line_sems.at[0])
    qkv_line = LineGather(p, wqkv_o, WQ, line_sems.at[1])
    out_line = LineGather(p, wout_o, WO, line_sems.at[2])
    gate_line = LineGather(p, wgate_o, wgate, line_sems.at[3])
    up_line = LineGather(p, wup_o, wup, line_sems.at[4])

    def row_block(ref):
        return (
            lambda c: ref.at[rows_at(c, rows)],
            lambda c, h: ref.at[pl.ds(pl.multiple_of(c * rows + h * half, half), half)],
        )

    tok_plane = PlaneGather(p, *row_block(X), plane_sems.at[0], own=tok)
    cot_plane = PlaneGather(p, *row_block(cot_all), plane_sems.at[1], own=cot)
    tab_rows = tab.shape[0]
    tab_plane = PlaneGather(
        p,
        lambda c: TAB.at[c],
        lambda c, h: TAB.at[c, pl.ds(h * (tab_rows // 2), tab_rows // 2)],
        plane_sems.at[2],
        own=tab,
    )

    def col_block(ref, b):
        def view(c):
            return ref.at[pl.ds(b * rows, rows), rows_at(c, cw)]

        def halves(c, h):
            return ref.at[pl.ds(b * rows + h * half, half), rows_at(c, cw)]

        return view, halves

    o_plane = [PlaneGather(p, *col_block(O, b), plane_sems.at[3 + b]) for b in range(n_ctx)]
    m_plane = [PlaneGather(p, *col_block(M, b), plane_sems.at[7 + b]) for b in range(n_ctx)]

    gain_line.start()
    qkv_line.start()
    tab_plane.start()
    tok_plane.start()
    out_line.start()
    own_tok = pltpu.make_async_copy(tok, X.at[rows_at(p.c, rows)], copy_sems.at[0])
    own_tab = pltpu.make_async_copy(tab, TAB.at[p.c], copy_sems.at[1])
    own_cot = pltpu.make_async_copy(cot, cot_all.at[rows_at(p.c, rows)], copy_sems.at[2])
    own_tok.start()
    own_tab.start()
    own_cot.start()

    gain_line.hop(1)
    tab_plane.middle()
    gain_line.hop(2)
    qkv_line.hop(1)
    gain_line.hop(3)
    gain_line.finish()
    for f in range(2 * p.depth):
        GROW[:, f * gains.shape[1] : (f + 1) * gains.shape[1]] = G8[16 * f : 16 * f + 8, :].astype(f32)

    def norm(c):
        at = rows_at(c, rows)
        x = X[at, :].astype(f32)
        r = lax.rsqrt(jnp.mean(x * x, axis=-1, keepdims=True) + eps_norm)
        XN[at, :] = (x * r * GROW[0:1, :]).astype(bf16)

    own_tok.wait()
    norm(p.c)
    out_line.hop(1)
    qkv_line.hop(2)
    tok_plane.middle()
    out_line.hop(2)
    gate_line.start()
    norm(p.cx)
    norm(p.cy)
    qkv_line.hop(3)
    tok_plane.finish()
    cot_plane.start()
    out_line.hop(3)
    up_line.start()
    norm(p.cd)
    x_copy = pltpu.make_async_copy(X, x_out, copy_sems.at[3])
    xn_copy = pltpu.make_async_copy(XN, xn_out, copy_sems.at[4])
    x_copy.start()
    xn_copy.start()
    own_tab.wait()
    tab_plane.finish()
    qkv_line.finish()

    @pl.loop(0, n_ctx)
    def _(b):
        at = rows_at(b, rows)
        pre = dot(XN[at, :], WQ[...]).T
        cosine = TAB[b, 0:32, :]
        sine = TAB[b, 32:64, :]
        for h in range(heads + 1):
            u = pre[64 * h : 64 * h + 32]
            w = pre[64 * h + 32 : 64 * h + 64]
            first = u * cosine - w * sine
            second = w * cosine + u * sine
            if h < heads:
                QT[64 * h : 64 * h + 32, at] = first.astype(bf16)
                QT[64 * h + 32 : 64 * h + 64, at] = second.astype(bf16)
            else:
                KT[0:32, at] = first.astype(bf16)
                KT[32:64, at] = second.astype(bf16)
                K[at, :] = jnp.concatenate([first, second], axis=0).T.astype(bf16)
        VT[:, at] = pre[qw + 64 :].astype(bf16)

    wq_copy = pltpu.make_async_copy(WQ, wqkv_out, copy_sems.at[5])
    wq_copy.start()
    gate_line.hop(1)

    def attend(b):
        n = (b + 1) * rows
        key = lax.broadcasted_iota(jnp.int32, (n, rows), 0)
        query = lax.broadcasted_iota(jnp.int32, (n, rows), 1) + b * rows
        begin = TAB[b, 64:65, :].astype(jnp.int32)
        BIAS[0:n, :] = jnp.where((key <= query) & (key >= begin), 0.0, neg_large)
        cols = slice(b * rows, (b + 1) * rows)

        @pl.loop(0, heads)
        def _(h):
            head = rows_at(h, HEAD_DIM)
            s = dot(K[0:n, :], QT[head, cols]) * scale + BIAS[0:n, :]
            top = jnp.max(s, axis=0, keepdims=True)
            e = jnp.exp(s - top)
            total = jnp.sum(e, axis=0, keepdims=True)
            probs = (e * (1.0 / total)).astype(bf16)
            OT[head, :] = dot(VT[:, 0:n], probs)
            LSE[rows_at(h, 8), cols] = jnp.broadcast_to(top + jnp.log(total), (8, rows))

        O[pl.ds(b * rows, rows), rows_at(p.c, cw)] = OT[...].T.astype(bf16)
        o_plane[b].start()

    def middle(b):
        at = pl.ds(b * rows, rows)
        mine = rows_at(p.c, cw)
        mid = X[at, mine].astype(f32) + dot(O[at, :], WO[...])
        M[at, mine] = mid.astype(bf16)
        m_plane[b].start()

    attend(0)
    attend(1)
    o_plane[0].middle()
    attend(2)
    o_plane[1].middle()
    attend(3)
    o_plane[2].middle()
    cot_plane.middle()
    out_line.finish()
    o_plane[0].finish()
    middle(0)
    o_plane[3].middle()
    up_line.hop(1)
    o_plane[1].finish()
    middle(1)
    m_plane[0].middle()
    o_plane[2].finish()
    middle(2)
    m_plane[1].middle()
    gate_line.hop(2)
    o_plane[3].finish()
    middle(3)
    m_plane[2].middle()
    up_line.hop(2)
    m_plane[3].middle()
    copies = [x_copy, xn_copy, wq_copy]
    for i, (src, dst) in enumerate(
        ((QT, qt_out), (KT, kt_out), (VT, vt_out), (LSE, lse_out), (O, o_out), (WO, wout_out), (TAB, tab_out))
    ):
        copy = pltpu.make_async_copy(src, dst, copy_sems.at[6 + i])
        copy.start()
        copies.append(copy)
    for b in range(n_ctx):
        m_plane[b].finish()
    m_copy = pltpu.make_async_copy(M, m_out, copy_sems.at[13])
    m_copy.start()
    copies.append(m_copy)
    gate_line.hop(3)
    up_line.hop(3)
    cot_plane.finish()
    gate_line.finish()
    up_line.finish()
    own_cot.wait()
    for copy in copies:
        copy.wait()
    for line in (gain_line, qkv_line, out_line, gate_line, up_line):
        line.drain()
    for plane in [tok_plane, cot_plane, tab_plane] + o_plane + m_plane:
        plane.drain()


def forward_stage(tok, tab, gains, wqkv_o, wout_o, wgate_o, wup_o, cot):
    n_fsdp, n_ctx = lax.axis_size("fsdp"), lax.axis_size("ctx")
    rows, width = tok.shape
    seq = rows * n_ctx
    whole = n_fsdp * wqkv_o.shape[0]
    nq, nw, nu = wqkv_o.shape[1], wout_o.shape[1], wgate_o.shape[1]
    qw = HEADS // n_ctx * HEAD_DIM
    heads = qw // HEAD_DIM
    tab_shape = (n_ctx,) + tab.shape
    outs = [
        ((seq, width), bf16), ((seq, width), bf16), ((qw, seq), bf16), ((64, seq), bf16), ((64, seq), bf16),
        ((8 * heads, seq), f32), ((seq, width), bf16), ((seq, width), bf16), ((whole, nq), bf16),
        ((whole, nw), bf16), ((whole, nu), bf16), ((whole, nu), bf16), ((seq, width), bf16), (tab_shape, f32),
    ]
    scratch = [
        pltpu.VMEM((seq, width), bf16),
        pltpu.VMEM((seq, width), bf16),
        pltpu.VMEM((qw, seq), bf16),
        pltpu.VMEM((64, seq), bf16),
        pltpu.VMEM((64, seq), bf16),
        pltpu.VMEM((seq, 64), bf16),
        pltpu.VMEM((8 * heads, seq), f32),
        pltpu.VMEM((seq, width), bf16),
        pltpu.VMEM((seq, width), bf16),
        pltpu.VMEM((whole, nq), bf16),
        pltpu.VMEM((whole, nw), bf16),
        pltpu.VMEM(tab_shape, f32),
        pltpu.VMEM((16 * n_fsdp, gains.shape[1]), bf16),
        pltpu.VMEM((8, width), f32),
        pltpu.VMEM((seq, rows), f32),
        pltpu.VMEM((qw, rows), f32),
        pltpu.SemaphoreType.DMA((5, LineGather.SEMS)),
        pltpu.SemaphoreType.DMA((11, PlaneGather.SEMS)),
        pltpu.SemaphoreType.DMA((14,)),
    ]
    ins = (tok, tab, gains, wqkv_o, wout_o, wgate_o, wup_o, cot)
    flops = 2 * seq * width * (nq + nw) + 8 * heads * seq * seq * HEAD_DIM
    return call(forward_kernel, ins, outs, scratch, 1, flops, "forward_stage")


middle_stage = None

backward_stage = None

def rotate(field, cosine, sine_table, direction):
    half_width = field.shape[-1] // 2
    first_half = field[..., :half_width]
    second_half = field[..., half_width:]
    return jnp.concatenate(
        [
            first_half * cosine - direction * second_half * sine_table,
            second_half * cosine + direction * first_half * sine_table,
        ],
        axis=-1,
    )


def gather(x, axis_name, axis=0):
    return lax.all_gather(x, axis_name, axis=axis, tiled=True)


def scatter(x, axis_name, axis=0):
    return lax.psum_scatter(x.astype(bf16), axis_name, scatter_dimension=axis, tiled=True)


def columns(w, start, count):
    return lax.dynamic_slice_in_dim(w, start, count, axis=1)


def visible(begin):
    seq = begin.shape[0]
    index = jnp.arange(seq, dtype=jnp.int32)
    return (index[None, :] <= index[:, None]) & (index[None, :] >= begin[:, None])


def forward_plain(tok, tab, gains, wqkv_o, wout_o, wgate_o, wup_o, cot):
    n_ctx = lax.axis_size("ctx")
    c = lax.axis_index("ctx")
    x = gather(tok, "ctx")
    tabs = gather(tab[None], "ctx")
    wqkv = gather(wqkv_o, "fsdp")
    wout = gather(wout_o, "fsdp")
    wgate = gather(wgate_o, "fsdp")
    wup = gather(wup_o, "fsdp")
    cot_all = gather(cot, "ctx")
    gain = gather(gains[0:1], "fsdp", axis=1).astype(f32)
    xf = x.astype(f32)
    r = lax.rsqrt(jnp.mean(xf * xf, axis=-1, keepdims=True) + eps_norm)
    xn = (xf * r * gain).astype(bf16)
    seq, width = x.shape
    heads = HEADS // n_ctx
    qw = heads * HEAD_DIM
    pre = dot(xn, wqkv)
    cosine = tabs[:, 0:32].transpose(0, 2, 1).reshape(seq, 1, 32)
    sine = tabs[:, 32:64].transpose(0, 2, 1).reshape(seq, 1, 32)
    begin = tabs[:, 64].reshape(seq).astype(jnp.int32)
    kvw = (wqkv.shape[1] - qw) // 2
    kv = kvw // HEAD_DIM
    q = rotate(pre[:, :qw].reshape(seq, heads, HEAD_DIM), cosine, sine, 1.0).astype(bf16)
    k = rotate(pre[:, qw : qw + kvw].reshape(seq, kv, HEAD_DIM), cosine, sine, 1.0).astype(bf16)
    v = pre[:, qw + kvw :].astype(bf16).reshape(seq, kv, HEAD_DIM)
    qg = q.reshape(seq, kv, heads // kv, HEAD_DIM)
    scores = jnp.einsum("qkgd,lkd->kgql", qg, k, preferred_element_type=f32) * HEAD_DIM ** (-0.5)
    scores = jnp.where(visible(begin)[None, None], scores, neg_large)
    top = jnp.max(scores, axis=-1, keepdims=True)
    weights = jnp.exp(scores - top)
    total = jnp.sum(weights, axis=-1, keepdims=True)
    probs_low = (weights / total).astype(bf16)
    att = jnp.einsum("kgql,lkd->qkgd", probs_low, v, preferred_element_type=f32)
    o = gather(att.astype(bf16).reshape(seq, qw), "ctx", axis=1)
    lse = (top + jnp.log(total)).reshape(heads, 1, seq)
    lse = jnp.broadcast_to(lse, (heads, 8, seq)).reshape(8 * heads, seq)
    cw = width // n_ctx
    mid = columns(x, c * cw, cw).astype(f32) + dot(o, wout)
    m = gather(mid.astype(bf16), "ctx", axis=1)
    qt = q.reshape(seq, qw).T
    kt = k.reshape(seq, kvw).T
    vt = v.reshape(seq, kvw).T
    return x, xn, qt, kt, vt, lse, o, m, wqkv, wout, wgate, wup, cot_all, tabs


def middle_plain(m, cot_all, wgate, wup, wdown_o):
    n_ctx = lax.axis_size("ctx")
    c = lax.axis_index("ctx")
    seq, width = m.shape
    rows = seq // n_ctx
    cw = width // n_ctx
    wdown = gather(wdown_o, "fsdp")
    mf = m.astype(f32)
    r = lax.rsqrt(jnp.mean(mf * mf, axis=-1, keepdims=True) + eps_norm)
    gate = dot(m, wgate) * r
    up = dot(m, wup) * r
    sig = jax.nn.sigmoid(gate)
    hidden = (gate * sig * up).astype(bf16)
    mlp = scatter(dot(hidden, wdown), "ctx").astype(f32)
    mid_rows = lax.dynamic_slice_in_dim(m, c * rows, rows, axis=0).astype(f32)
    output = (mid_rows + mlp).astype(bf16)
    grad_hidden = dot_nt(cot_all, wdown)
    down_raw = scatter(dot_tn(hidden, cot_all), "fsdp")
    d_gate = grad_hidden * up * sig * (1.0 + gate * (1.0 - sig))
    d_up = grad_hidden * gate * sig
    stat = jnp.sum(d_gate * gate + d_up * up, axis=-1, keepdims=True)
    d_gate = (d_gate * r).astype(bf16)
    d_up = (d_up * r).astype(bf16)
    gate_raw = dot_tn(m, d_gate).astype(bf16)
    up_raw = dot_tn(m, d_up).astype(bf16)
    back = dot_nt(d_gate, wgate) + dot_nt(d_up, wup) - mf * (r * r * stat * (1.0 / width))
    back_own = scatter(back, "ctx", axis=1).astype(f32)
    gm = (columns(cot_all, c * cw, cw).astype(f32) + back_own).astype(bf16)
    return output, down_raw, gate_raw, up_raw, gm


def backward_plain(x, xn, gain, qt, kt, vt, lse, o, gm, wqkv, wout, tabs, gate_raw, up_raw):
    n_ctx = lax.axis_size("ctx")
    c = lax.axis_index("ctx")
    seq, width = x.shape
    heads = HEADS // n_ctx
    qw = heads * HEAD_DIM
    kvw = kt.shape[0]
    kv = kvw // HEAD_DIM
    cw = width // n_ctx
    scale = HEAD_DIM ** (-0.5)
    cosine = tabs[:, 0:32].transpose(0, 2, 1).reshape(seq, 1, 32)
    sine = tabs[:, 32:64].transpose(0, 2, 1).reshape(seq, 1, 32)
    begin = tabs[:, 64].reshape(seq).astype(jnp.int32)
    gate_grad = scatter(gate_raw, "fsdp")
    up_grad = scatter(up_raw, "fsdp")
    out_grad = scatter(dot_tn(o, gm), "fsdp")
    d_att = scatter(dot_nt(gm, wout), "ctx", axis=1).reshape(seq, kv, heads // kv, HEAD_DIM)
    q = qt.T.reshape(seq, kv, heads // kv, HEAD_DIM)
    k = kt.T.reshape(seq, kv, HEAD_DIM)
    v = vt.T.reshape(seq, kv, HEAD_DIM)
    scores = jnp.einsum("qkgd,lkd->kgql", q, k, preferred_element_type=f32) * scale
    scores = jnp.where(visible(begin)[None, None], scores, neg_large)
    lse = lse.reshape(kv, heads // kv, 8, seq)[:, :, 0, :, None]
    probs = jnp.exp(scores - lse)
    d_probs = jnp.einsum("qkgd,lkd->kgql", d_att, v, preferred_element_type=f32)
    delta = jnp.sum(probs * d_probs, axis=-1, keepdims=True)
    d_scores = (probs * (d_probs - delta)).astype(bf16)
    d_q = jnp.einsum("kgql,lkd->qkgd", d_scores, k, preferred_element_type=f32) * scale
    d_k = jnp.einsum("kgql,qkgd->lkd", d_scores, q, preferred_element_type=f32) * scale
    d_v = jnp.einsum("kgql,qkgd->lkd", probs.astype(bf16), d_att, preferred_element_type=f32)
    stat = (
        jnp.sum(d_q * q, axis=(1, 2, 3)) + jnp.sum(d_k * k, axis=(1, 2)) + jnp.sum(d_v * v, axis=(1, 2))
    )[:, None]
    d_q = rotate(d_q.reshape(seq, heads, HEAD_DIM), cosine, sine, -1.0).reshape(seq, qw)
    d_k = rotate(d_k, cosine, sine, -1.0).reshape(seq, kvw)
    d_pre = jnp.concatenate([d_q, d_k, d_v.reshape(seq, kvw)], axis=1).astype(bf16)
    qkv_grad = scatter(dot_tn(xn, d_pre), "fsdp")
    xf = x.astype(f32)
    r = lax.rsqrt(jnp.mean(xf * xf, axis=-1, keepdims=True) + eps_norm)
    back = dot_nt(d_pre, wqkv) * (gain * r) - xf * (r * r * stat * (1.0 / width))
    at = (jnp.arange(width, dtype=jnp.int32) // cw == c)[None, :]
    back = back + jnp.where(at, jnp.tile(gm.astype(f32), (1, n_ctx)), 0.0)
    grad_tokens = scatter(back, "ctx").astype(f32)
    qkv_all = gather(qkv_grad[None], "ctx")
    out_all = gather(out_grad, "ctx", axis=1)
    gate_all = gather(gate_grad[None], "ctx")
    up_all = gather(up_grad[None], "ctx")
    return grad_tokens, qkv_all, out_all, gate_all, up_all


def per_device(
    tokens,
    positions,
    gain_attn,
    gain_mlp,
    w_query,
    w_key,
    w_value,
    w_out,
    w_gate,
    w_up,
    w_down,
    cotangent,
):
    n_ctx = lax.axis_size("ctx")
    n_fsdp = lax.axis_size("fsdp")
    kernels = n_ctx == 4 and n_fsdp == 8
    c = lax.axis_index("ctx")
    rows, width = tokens.shape
    own_rows = w_query.shape[0]
    qw = HEADS // n_ctx * HEAD_DIM
    copies = max(1, n_ctx // KV_HEADS)
    kvw = max(1, KV_HEADS // n_ctx) * HEAD_DIM
    cw = width // n_ctx
    ff_width = w_gate.shape[1]
    unit = ff_width // (n_fsdp * n_ctx)
    gain_one = gain_attn.astype(f32)[:, None]
    gain_two = gain_mlp.astype(f32)[:, None]

    wqkv_o = jnp.concatenate(
        [
            columns(w_query, c * qw, qw),
            columns(w_key, (c // copies) * kvw, kvw),
            columns(w_value, (c // copies) * kvw, kvw),
        ],
        axis=1,
    )
    wout_o = columns(w_out, c * cw, cw)

    def units(w):
        parts = w.reshape(own_rows, n_fsdp, n_ctx, unit)
        mine = lax.dynamic_index_in_dim(parts, c, axis=2, keepdims=False)
        return (gain_two * mine.reshape(own_rows, n_fsdp * unit)).astype(bf16)

    wgate_o, wup_o = units(w_gate), units(w_up)
    wdown_o = lax.dynamic_slice_in_dim(w_down, c * unit, unit, axis=0)
    gains = jnp.broadcast_to(gain_attn[None, :], (16, own_rows))
    frequency = theta_base ** (-(jnp.arange(HEAD_DIM // 2, dtype=f32) * 2.0) / HEAD_DIM)
    angles = frequency[:, None] * positions.astype(f32)[None, :]
    begin = c * rows + jnp.arange(rows, dtype=jnp.int32) - positions
    tab = jnp.concatenate(
        [jnp.cos(angles), jnp.sin(angles), jnp.broadcast_to(begin.astype(f32)[None, :], (16, rows))],
        axis=0,
    )

    forward = forward_stage if kernels else forward_plain
    x, xn, qt, kt, vt, lse, o, m, wqkv, wout, wgate, wup, cot_all, tabs = forward(
        tokens, tab, gains, wqkv_o, wout_o, wgate_o, wup_o, cotangent
    )
    middle = middle_plain
    output, down_raw, gate_raw, up_raw, gm = middle(m, cot_all, wgate, wup, wdown_o)
    gain_row = gather(gain_attn, "fsdp").astype(f32)[None, :]
    backward = backward_plain
    grad_tokens, qkv_all, out_all, gate_all, up_all = backward(
        x, xn, gain_row, qt, kt, vt, lse, o, gm, wqkv, wout, tabs, gate_raw, up_raw
    )

    qkv_all = qkv_all.astype(f32)

    def joined(part):
        return jnp.moveaxis(part, 0, 1).reshape(own_rows, -1)

    def kv_part(part):
        return joined(part.reshape(n_ctx // copies, copies, own_rows, kvw).sum(axis=1))

    grad_query = joined(qkv_all[:, :, :qw])
    grad_key = kv_part(qkv_all[:, :, qw : qw + kvw])
    grad_value = kv_part(qkv_all[:, :, qw + kvw :])
    grad_out = out_all.astype(f32)

    def spread(full):
        full = full.reshape(n_ctx, own_rows, n_fsdp, unit)
        return full.transpose(1, 2, 0, 3).reshape(own_rows, ff_width).astype(f32)

    raw_gate, raw_up = spread(gate_all), spread(up_all)
    grad_down = gather(down_raw, "ctx").astype(f32) if down_raw.shape[0] == unit else down_raw.astype(f32)

    def gain_term(grad, w):
        return jnp.sum(grad * w.astype(f32), axis=1)

    grad_gain_one = (
        gain_term(grad_query, w_query) + gain_term(grad_key, w_key) + gain_term(grad_value, w_value)
    ) / gain_one[:, 0]
    grad_gain_two = gain_term(raw_gate, w_gate) + gain_term(raw_up, w_up)
    return (
        output,
        grad_tokens,
        grad_gain_one,
        grad_gain_two,
        grad_query,
        grad_key,
        grad_value,
        grad_out,
        gain_two * raw_gate,
        gain_two * raw_up,
        grad_down,
    )


def solution(mesh):
    both = P(("fsdp", "ctx"), None)
    first = P("fsdp", None)
    return jax.shard_map(
        per_device,
        mesh=mesh,
        in_specs=(both, P(("fsdp", "ctx")), P("fsdp"), P("fsdp")) + (first,) * 7 + (both,),
        out_specs=(both, both, P("fsdp"), P("fsdp")) + (first,) * 7,
        check_vma=False,
    )
```

```python
import jax
import jax.numpy as jnp
from jax import lax
from jax.experimental import pallas as pl
from jax.experimental.pallas import tpu as pltpu
from jax.sharding import PartitionSpec as P

HEADS = 32
KV_HEADS = 4
HEAD_DIM = 64

eps_norm = 1e-05
theta_base = 10000.0
neg_large = -1e30
bf16 = jnp.bfloat16
f32 = jnp.float32
MESH_IDS = pl.DeviceIdType.MESH


def dot(a, b):
    return jnp.dot(a, b, preferred_element_type=f32)


def dot_nt(a, b):
    return lax.dot_general(a, b, (((1,), (1,)), ((), ())), preferred_element_type=f32)


def dot_tn(a, b):
    return lax.dot_general(a, b, (((0,), (0,)), ((), ())), preferred_element_type=f32)


class Place:
    def __init__(self):
        self.f = lax.axis_index("fsdp")
        self.c = lax.axis_index("ctx")
        self.depth = lax.axis_size("fsdp") // 2
        self.z = self.f // 2
        self.core = self.f % 2
        self.other = 1 - self.core
        self.cx = self.c + 1 - 2 * (self.c % 2)
        self.cy = self.c + 2 - 4 * (self.c // 2)
        self.cd = 3 - self.c
        self.sibling = {"fsdp": self.f + 1 - 2 * self.core}
        self.up = {"fsdp": self.f + 2}
        self.down = {"fsdp": self.f - 2}
        self.x = {"ctx": self.cx}
        self.y = {"ctx": self.cy}

    def has_up(self):
        return self.z < self.depth - 1

    def has_down(self):
        return self.z > 0

    def barrier(self):
        sem = pltpu.get_barrier_semaphore()

        def greet(device):
            pl.semaphore_signal(sem, inc=1, device_id=device, device_id_type=MESH_IDS)

        greet(self.sibling)
        greet(self.x)
        greet(self.y)

        @pl.when(self.has_up())
        def _():
            greet(self.up)

        @pl.when(self.has_down())
        def _():
            greet(self.down)

        last = self.depth - 1
        pl.semaphore_wait(sem, 4 - self.z // last + (self.z + last - 1) // last)


def remote(src, dst, send_sem, recv_sem, device):
    return pltpu.make_async_remote_copy(
        src_ref=src,
        dst_ref=dst,
        send_sem=send_sem,
        recv_sem=recv_sem,
        device_id=device,
        device_id_type=MESH_IDS,
    )


class LineGather:
    SEMS = 21

    def __init__(self, place, own, full, sems):
        self.p, self.own, self.full, self.sems = place, own, full, sems
        self.rows = own.shape[0]
        self.n = place.depth

    def view(self, level, core):
        start = pl.multiple_of((2 * level + core) * self.rows, 16)
        return self.full.at[pl.ds(start, self.rows)]

    def to_up(self, hop):
        p = self.p
        level = p.z - (hop - 1)
        src = self.own if hop == 1 else self.view(level, p.core)
        return remote(
            src, self.view(level, p.core), self.sems.at[hop - 1], self.sems.at[6 + hop - 1], p.up
        )

    def to_down(self, hop):
        p = self.p
        level = p.z + (hop - 1)
        src = self.own if hop == 1 else self.view(level, p.core)
        return remote(
            src, self.view(level, p.core), self.sems.at[3 + hop - 1], self.sems.at[9 + hop - 1], p.down
        )

    def to_sibling(self, level, own=False):
        p = self.p
        src = self.own if own else self.view(level, p.core)
        return remote(
            src, self.view(level, p.core), self.sems.at[12 + level], self.sems.at[16 + level], p.sibling
        )

    def local(self):
        p = self.p
        return pltpu.make_async_copy(self.own, self.view(p.z, p.core), self.sems.at[20])

    def start(self):
        p = self.p

        @pl.when(p.has_up())
        def _():
            self.to_up(1).start()

        @pl.when(p.has_down())
        def _():
            self.to_down(1).start()

        self.to_sibling(p.z, True).start()
        self.local().start()

    def arrived(self, level, sem):
        view = self.view(level, self.p.core)
        remote(view, view, self.sems.at[0], sem, self.p.sibling).wait_recv()

    def hop(self, s):
        p = self.p

        @pl.when(p.z >= s)
        def _():
            self.arrived(p.z - s, self.sems.at[6 + s - 1])
            if s < self.n - 1:

                @pl.when(p.has_up())
                def _():
                    self.to_up(s + 1).start()

            self.to_sibling(p.z - s).start()

        @pl.when(p.z + s < self.n)
        def _():
            self.arrived(p.z + s, self.sems.at[9 + s - 1])
            if s < self.n - 1:

                @pl.when(p.has_down())
                def _():
                    self.to_down(s + 1).start()

            self.to_sibling(p.z + s).start()

    def finish(self):
        p = self.p
        self.local().wait()
        for level in range(self.n):
            view = self.view(level, p.other)
            remote(view, view, self.sems.at[0], self.sems.at[16 + level], p.sibling).wait_recv()

    def drain(self):
        p = self.p
        for s in range(1, self.n):

            @pl.when(p.has_up() & (p.z >= s - 1))
            def _():
                self.to_up(s).wait_send()

            @pl.when(p.has_down() & (p.z + s - 1 < self.n))
            def _():
                self.to_down(s).wait_send()

        for level in range(self.n):
            self.to_sibling(level).wait_send()


class PlaneGather:
    SEMS = 8

    def __init__(self, place, view, half, sems, own=None):
        self.p, self.view, self.half, self.sems = place, view, half, sems
        self.own = own

    def src(self):
        return self.view(self.p.c) if self.own is None else self.own

    def to_x(self):
        p = self.p
        return remote(self.src(), self.view(p.c), self.sems.at[0], self.sems.at[2], p.x)

    def to_y(self):
        p = self.p
        return remote(self.src(), self.view(p.c), self.sems.at[1], self.sems.at[3], p.y)

    def on_to_y(self):
        p, h = self.p, self.half(self.p.cx, 0)
        return remote(h, h, self.sems.at[4], self.sems.at[6], p.y)

    def on_to_x(self):
        p, h = self.p, self.half(self.p.cy, 1)
        return remote(h, h, self.sems.at[5], self.sems.at[7], p.x)

    def start(self):
        self.to_x().start()
        self.to_y().start()

    def got(self, ref, sem):
        remote(ref, ref, self.sems.at[0], sem, self.p.x).wait_recv()

    def middle(self):
        p = self.p
        self.got(self.view(p.cx), self.sems.at[2])
        self.on_to_y().start()
        self.got(self.view(p.cy), self.sems.at[3])
        self.on_to_x().start()

    def finish(self):
        p = self.p
        self.got(self.half(p.cd, 0), self.sems.at[6])
        self.got(self.half(p.cd, 1), self.sems.at[7])

    def drain(self):
        self.to_x().wait_send()
        self.to_y().wait_send()
        self.on_to_y().wait_send()
        self.on_to_x().wait_send()


def rows_at(index, count):
    return pl.ds(pl.multiple_of(index * count, count), count)


def any_spec(count):
    return [pl.BlockSpec(memory_space=pl.ANY)] * count


def call(kernel, ins, outs, scratch, collective_id, flops, name):
    return pl.pallas_call(
        kernel,
        out_shape=[jax.ShapeDtypeStruct(s, d) for s, d in outs],
        in_specs=any_spec(len(ins)),
        out_specs=any_spec(len(outs)),
        scratch_shapes=scratch,
        compiler_params=pltpu.CompilerParams(
            collective_id=collective_id, has_side_effects=True, vmem_limit_bytes=60 * 2**20
        ),
        cost_estimate=pl.CostEstimate(flops=flops, bytes_accessed=2**26, transcendentals=2**22),
        name=name,
    )(*ins)


class PlaneScatter:
    SEMS = 8

    def __init__(self, place, part, half, first, second, sems):
        self.p, self.part, self.half = place, part, half
        self.first, self.second, self.sems = first, second, sems

    def ref(self):
        return self.part(self.p.c)

    def far_to_y(self):
        p = self.p
        return remote(self.half(p.cd, 0), self.first.at[0], self.sems.at[0], self.sems.at[2], p.y)

    def far_to_x(self):
        p = self.p
        return remote(self.half(p.cd, 1), self.first.at[1], self.sems.at[1], self.sems.at[3], p.x)

    def to_x(self):
        p = self.p
        return remote(self.part(p.cx), self.second.at[0], self.sems.at[4], self.sems.at[6], p.x)

    def to_y(self):
        p = self.p
        return remote(self.part(p.cy), self.second.at[1], self.sems.at[5], self.sems.at[7], p.y)

    def start(self):
        self.far_to_y().start()
        self.far_to_x().start()

    def got(self, ref, sem):
        remote(ref, ref, self.sems.at[0], sem, self.p.x).wait_recv()

    def add(self, ref, other):
        ref[...] = (ref[...].astype(f32) + other[...].astype(f32)).astype(bf16)

    def middle(self):
        p = self.p
        self.got(self.first.at[0], self.sems.at[2])
        self.add(self.half(p.cx, 0), self.first.at[0])
        self.to_x().start()
        self.got(self.first.at[1], self.sems.at[3])
        self.add(self.half(p.cy, 1), self.first.at[1])
        self.to_y().start()

    def finish(self):
        self.got(self.second.at[0], self.sems.at[6])
        self.got(self.second.at[1], self.sems.at[7])
        own = self.part(self.p.c)[...].astype(f32)
        return own + self.second[0].astype(f32) + self.second[1].astype(f32)

    def drain(self):
        self.far_to_y().wait_send()
        self.far_to_x().wait_send()
        self.to_x().wait_send()
        self.to_y().wait_send()


def forward_kernel(
    tok, tab, gains, wqkv_o, wout_o, wgate_o, wup_o, cot,
    x_out, xn_out, qt_out, kt_out, vt_out, lse_out, o_out, m_out,
    wqkv_out, wout_out, wgate, wup, cot_all, tab_out,
    X, XN, QT, KT, VT, K, LSE, O, M, WQ, WO, TAB, G8, GROW, BIAS, OT,
    line_sems, plane_sems, copy_sems,
):
    p = Place()
    n_ctx = 4
    rows = tok.shape[0]
    half = rows // 2
    qw = QT.shape[0]
    heads = qw // HEAD_DIM
    cw = O.shape[1] // n_ctx
    scale = HEAD_DIM ** (-0.5)

    p.barrier()

    gain_line = LineGather(p, gains, G8, line_sems.at[0])
    qkv_line = LineGather(p, wqkv_o, WQ, line_sems.at[1])
    out_line = LineGather(p, wout_o, WO, line_sems.at[2])
    gate_line = LineGather(p, wgate_o, wgate, line_sems.at[3])
    up_line = LineGather(p, wup_o, wup, line_sems.at[4])

    def row_block(ref):
        return (
            lambda c: ref.at[rows_at(c, rows)],
            lambda c, h: ref.at[pl.ds(pl.multiple_of(c * rows + h * half, half), half)],
        )

    tok_plane = PlaneGather(p, *row_block(X), plane_sems.at[0], own=tok)
    cot_plane = PlaneGather(p, *row_block(cot_all), plane_sems.at[1], own=cot)
    tab_rows = tab.shape[0]
    tab_plane = PlaneGather(
        p,
        lambda c: TAB.at[c],
        lambda c, h: TAB.at[c, pl.ds(h * (tab_rows // 2), tab_rows // 2)],
        plane_sems.at[2],
        own=tab,
    )

    def col_block(ref, b):
        def view(c):
            return ref.at[pl.ds(b * rows, rows), rows_at(c, cw)]

        def halves(c, h):
            return ref.at[pl.ds(b * rows + h * half, half), rows_at(c, cw)]

        return view, halves

    o_plane = [PlaneGather(p, *col_block(O, b), plane_sems.at[3 + b]) for b in range(n_ctx)]
    m_plane = [PlaneGather(p, *col_block(M, b), plane_sems.at[7 + b]) for b in range(n_ctx)]

    gain_line.start()
    qkv_line.start()
    tab_plane.start()
    tok_plane.start()
    out_line.start()
    own_tok = pltpu.make_async_copy(tok, X.at[rows_at(p.c, rows)], copy_sems.at[0])
    own_tab = pltpu.make_async_copy(tab, TAB.at[p.c], copy_sems.at[1])
    own_cot = pltpu.make_async_copy(cot, cot_all.at[rows_at(p.c, rows)], copy_sems.at[2])
    own_tok.start()
    own_tab.start()
    own_cot.start()

    gain_line.hop(1)
    tab_plane.middle()
    gain_line.hop(2)
    qkv_line.hop(1)
    gain_line.hop(3)
    gain_line.finish()
    for f in range(2 * p.depth):
        GROW[:, f * gains.shape[1] : (f + 1) * gains.shape[1]] = G8[16 * f : 16 * f + 8, :].astype(f32)

    def norm(c):
        at = rows_at(c, rows)
        x = X[at, :].astype(f32)
        r = lax.rsqrt(jnp.mean(x * x, axis=-1, keepdims=True) + eps_norm)
        XN[at, :] = (x * r * GROW[0:1, :]).astype(bf16)

    own_tok.wait()
    norm(p.c)
    out_line.hop(1)
    qkv_line.hop(2)
    tok_plane.middle()
    out_line.hop(2)
    gate_line.start()
    norm(p.cx)
    norm(p.cy)
    qkv_line.hop(3)
    tok_plane.finish()
    cot_plane.start()
    out_line.hop(3)
    up_line.start()
    norm(p.cd)
    x_copy = pltpu.make_async_copy(X, x_out, copy_sems.at[3])
    xn_copy = pltpu.make_async_copy(XN, xn_out, copy_sems.at[4])
    x_copy.start()
    xn_copy.start()
    own_tab.wait()
    tab_plane.finish()
    qkv_line.finish()

    @pl.loop(0, n_ctx)
    def _(b):
        at = rows_at(b, rows)
        pre = dot(XN[at, :], WQ[...]).T
        cosine = TAB[b, 0:32, :]
        sine = TAB[b, 32:64, :]
        for h in range(heads + 1):
            u = pre[64 * h : 64 * h + 32]
            w = pre[64 * h + 32 : 64 * h + 64]
            first = u * cosine - w * sine
            second = w * cosine + u * sine
            if h < heads:
                QT[64 * h : 64 * h + 32, at] = first.astype(bf16)
                QT[64 * h + 32 : 64 * h + 64, at] = second.astype(bf16)
            else:
                KT[0:32, at] = first.astype(bf16)
                KT[32:64, at] = second.astype(bf16)
                K[at, :] = jnp.concatenate([first, second], axis=0).T.astype(bf16)
        VT[:, at] = pre[qw + 64 :].astype(bf16)

    wq_copy = pltpu.make_async_copy(WQ, wqkv_out, copy_sems.at[5])
    wq_copy.start()
    gate_line.hop(1)

    def attend(b):
        n = (b + 1) * rows
        key = lax.broadcasted_iota(jnp.int32, (n, rows), 0)
        query = lax.broadcasted_iota(jnp.int32, (n, rows), 1) + b * rows
        begin = TAB[b, 64:65, :].astype(jnp.int32)
        BIAS[0:n, :] = jnp.where((key <= query) & (key >= begin), 0.0, neg_large)
        cols = slice(b * rows, (b + 1) * rows)

        @pl.loop(0, heads)
        def _(h):
            head = rows_at(h, HEAD_DIM)
            s = dot(K[0:n, :], QT[head, cols]) * scale + BIAS[0:n, :]
            top = jnp.max(s, axis=0, keepdims=True)
            e = jnp.exp(s - top)
            total = jnp.sum(e, axis=0, keepdims=True)
            probs = (e * (1.0 / total)).astype(bf16)
            OT[head, :] = dot(VT[:, 0:n], probs)
            LSE[rows_at(h, 8), cols] = jnp.broadcast_to(top + jnp.log(total), (8, rows))

        O[pl.ds(b * rows, rows), rows_at(p.c, cw)] = OT[...].T.astype(bf16)
        o_plane[b].start()

    def middle(b):
        at = pl.ds(b * rows, rows)
        mine = rows_at(p.c, cw)
        mid = X[at, mine].astype(f32) + dot(O[at, :], WO[...])
        M[at, mine] = mid.astype(bf16)
        m_plane[b].start()

    attend(0)
    attend(1)
    o_plane[0].middle()
    attend(2)
    o_plane[1].middle()
    attend(3)
    o_plane[2].middle()
    cot_plane.middle()
    out_line.finish()
    o_plane[0].finish()
    middle(0)
    o_plane[3].middle()
    up_line.hop(1)
    o_plane[1].finish()
    middle(1)
    m_plane[0].middle()
    o_plane[2].finish()
    middle(2)
    m_plane[1].middle()
    gate_line.hop(2)
    o_plane[3].finish()
    middle(3)
    m_plane[2].middle()
    up_line.hop(2)
    m_plane[3].middle()
    copies = [x_copy, xn_copy, wq_copy]
    for i, (src, dst) in enumerate(
        ((QT, qt_out), (KT, kt_out), (VT, vt_out), (LSE, lse_out), (O, o_out), (WO, wout_out), (TAB, tab_out))
    ):
        copy = pltpu.make_async_copy(src, dst, copy_sems.at[6 + i])
        copy.start()
        copies.append(copy)
    for b in range(n_ctx):
        m_plane[b].finish()
    m_copy = pltpu.make_async_copy(M, m_out, copy_sems.at[13])
    m_copy.start()
    copies.append(m_copy)
    gate_line.hop(3)
    up_line.hop(3)
    cot_plane.finish()
    gate_line.finish()
    up_line.finish()
    own_cot.wait()
    for copy in copies:
        copy.wait()
    for line in (gain_line, qkv_line, out_line, gate_line, up_line):
        line.drain()
    for plane in [tok_plane, cot_plane, tab_plane] + o_plane + m_plane:
        plane.drain()


def forward_stage(tok, tab, gains, wqkv_o, wout_o, wgate_o, wup_o, cot):
    n_fsdp, n_ctx = lax.axis_size("fsdp"), lax.axis_size("ctx")
    rows, width = tok.shape
    seq = rows * n_ctx
    whole = n_fsdp * wqkv_o.shape[0]
    nq, nw, nu = wqkv_o.shape[1], wout_o.shape[1], wgate_o.shape[1]
    qw = HEADS // n_ctx * HEAD_DIM
    heads = qw // HEAD_DIM
    tab_shape = (n_ctx,) + tab.shape
    outs = [
        ((seq, width), bf16), ((seq, width), bf16), ((qw, seq), bf16), ((64, seq), bf16), ((64, seq), bf16),
        ((8 * heads, seq), f32), ((seq, width), bf16), ((seq, width), bf16), ((whole, nq), bf16),
        ((whole, nw), bf16), ((whole, nu), bf16), ((whole, nu), bf16), ((seq, width), bf16), (tab_shape, f32),
    ]
    scratch = [
        pltpu.VMEM((seq, width), bf16),
        pltpu.VMEM((seq, width), bf16),
        pltpu.VMEM((qw, seq), bf16),
        pltpu.VMEM((64, seq), bf16),
        pltpu.VMEM((64, seq), bf16),
        pltpu.VMEM((seq, 64), bf16),
        pltpu.VMEM((8 * heads, seq), f32),
        pltpu.VMEM((seq, width), bf16),
        pltpu.VMEM((seq, width), bf16),
        pltpu.VMEM((whole, nq), bf16),
        pltpu.VMEM((whole, nw), bf16),
        pltpu.VMEM(tab_shape, f32),
        pltpu.VMEM((16 * n_fsdp, gains.shape[1]), bf16),
        pltpu.VMEM((8, width), f32),
        pltpu.VMEM((seq, rows), f32),
        pltpu.VMEM((qw, rows), f32),
        pltpu.SemaphoreType.DMA((5, LineGather.SEMS)),
        pltpu.SemaphoreType.DMA((11, PlaneGather.SEMS)),
        pltpu.SemaphoreType.DMA((14,)),
    ]
    ins = (tok, tab, gains, wqkv_o, wout_o, wgate_o, wup_o, cot)
    flops = 2 * seq * width * (nq + nw) + 8 * heads * seq * seq * HEAD_DIM
    return call(forward_kernel, ins, outs, scratch, 1, flops, "forward_stage")


def tiles_of(total, most):
    sizes, at = [], 0
    while at < total:
        sizes.append((at, min(most, total - at)))
        at += most
    return sizes


def middle_kernel(
    m_in, cot_in, wgate_in, wup_in, wdown_o,
    y_out, down_part, gate_part, up_part, gm_out,
    M, COT, WG, WU, WD, GATE, UP, HID, R2, PD, PH, D1, D2, H1, H2, GM, Y, STAGE_D, STAGE,
    line_sems, plane_sems, copy_sems, stage_sems,
):
    p = Place()
    n_ctx = 4
    seq, width = M.shape
    rows = seq // n_ctx
    half = rows // 2
    cw = width // n_ctx
    units = GATE.shape[1]
    loads = []
    for i, (src, dst) in enumerate(((m_in, M), (wgate_in, WG), (wup_in, WU), (cot_in, COT))):
        loads.append(pltpu.make_async_copy(src, dst, copy_sems.at[i]))
        loads[-1].start()

    p.barrier()
    down_line = LineGather(p, wdown_o, WD, line_sems.at[0])
    down_line.start()

    loads[0].wait()
    loads[1].wait()
    loads[2].wait()

    @pl.loop(0, n_ctx)
    def _(b):
        at = rows_at(b, rows)
        mf = M[at, :].astype(f32)
        r = lax.rsqrt(jnp.mean(mf * mf, axis=-1, keepdims=True) + eps_norm)
        gate = dot(M[at, :], WG[...]) * r
        up = dot(M[at, :], WU[...]) * r
        R2[at, :] = jnp.broadcast_to(r, (rows, 128))
        GATE[at, :] = gate.astype(bf16)
        UP[at, :] = up.astype(bf16)
        HID[at, :] = (gate * (1.0 / (1.0 + jnp.exp(-gate))) * up).astype(bf16)

    down_line.hop(1)
    loads[3].wait()
    stage_copies = {}
    for i, (at, size) in enumerate(tiles_of(units, STAGE_D.shape[1])):
        slot = i % 2
        if i >= 2:
            stage_copies[i - 2].wait()
        STAGE_D[slot, 0:size, :] = dot_tn(HID[:, at : at + size], COT[...]).astype(bf16)
        copy = pltpu.make_async_copy(
            STAGE_D.at[slot, pl.ds(0, size)], down_part.at[pl.ds(at, size)], stage_sems.at[slot]
        )
        copy.start()
        stage_copies[i] = copy
    n_down = len(stage_copies)
    down_line.hop(2)
    stage_copies[n_down - 2].wait()
    stage_copies[n_down - 1].wait()
    down_line.hop(3)
    down_line.finish()

    y_plane = PlaneScatter(
        p,
        lambda c: PD.at[rows_at(c, rows)],
        lambda c, h: PD.at[pl.ds(pl.multiple_of(c * rows + h * half, half), half)],
        D1,
        D2,
        plane_sems.at[0],
    )

    def col_scatter(b):
        return PlaneScatter(
            p,
            lambda c: PH.at[pl.ds(b * rows, rows), rows_at(c, cw)],
            lambda c, h: PH.at[pl.ds(b * rows + h * half, half), rows_at(c, cw)],
            H1.at[b],
            H2.at[b],
            plane_sems.at[1 + b],
        )

    h_plane = [col_scatter(b) for b in range(n_ctx)]

    def partial_out(c):
        at = rows_at(c, rows)
        PD[at, :] = dot(HID[at, :], WD[...]).astype(bf16)

    partial_out(p.cd)
    y_plane.start()
    partial_out(p.cx)
    partial_out(p.cy)
    y_plane.middle()
    partial_out(p.c)

    def back(b):
        at = pl.ds(b * rows, rows)
        r = R2[at, 0:1]
        grad_hidden = dot_nt(COT[at, :], WD[...])
        gate = GATE[at, :].astype(f32)
        up = UP[at, :].astype(f32)
        sig = 1.0 / (1.0 + jnp.exp(-gate))
        d_up = grad_hidden * gate * sig
        d_gate = grad_hidden * up * sig * (1.0 + gate * (1.0 - sig))
        stat = jnp.sum(d_gate * gate + d_up * up, axis=-1, keepdims=True)
        GATE[at, :] = (d_gate * r).astype(bf16)
        UP[at, :] = (d_up * r).astype(bf16)
        coef = r * r * stat * (1.0 / width)
        for j in range(0, width, cw):
            e = dot_nt(GATE[at, :], WG[j : j + cw, :]) + dot_nt(UP[at, :], WU[j : j + cw, :])
            PH[at, j : j + cw] = (e - M[at, j : j + cw].astype(f32) * coef).astype(bf16)
        h_plane[b].start()

    back(0)
    back(1)
    h_plane[0].middle()
    back(2)
    h_plane[1].middle()
    back(3)
    h_plane[2].middle()

    stage_copies = {}
    jobs = []
    for src, dst in ((GATE, gate_part), (UP, up_part)):
        for at, size in tiles_of(width, STAGE.shape[1]):
            jobs.append((src, dst, at, size))

    def weight_tile(i):
        src, dst, at, size = jobs[i]
        slot = i % 2
        if i >= 2:
            stage_copies[i - 2].wait()
        STAGE[slot] = dot_tn(M[:, at : at + size], src[...]).astype(bf16)
        copy = pltpu.make_async_copy(STAGE.at[slot], dst.at[pl.ds(at, size)], stage_sems.at[2 + slot])
        copy.start()
        stage_copies[i] = copy

    def finish_block(b):
        at = pl.ds(b * rows, rows)
        GM[at, :] = (COT[at, rows_at(p.c, cw)].astype(f32) + h_plane[b].finish()).astype(bf16)

    weight_tile(0)
    weight_tile(1)
    h_plane[3].middle()
    weight_tile(2)
    finish_block(0)
    weight_tile(3)
    finish_block(1)
    weight_tile(4)
    weight_tile(5)
    finish_block(2)
    weight_tile(6)
    weight_tile(7)
    Y[...] = (M[rows_at(p.c, rows), :].astype(f32) + y_plane.finish()).astype(bf16)
    y_copy = pltpu.make_async_copy(Y, y_out, copy_sems.at[4])
    y_copy.start()
    finish_block(3)
    gm_copy = pltpu.make_async_copy(GM, gm_out, copy_sems.at[5])
    gm_copy.start()
    stage_copies[6].wait()
    stage_copies[7].wait()
    y_copy.wait()
    gm_copy.wait()
    down_line.drain()
    y_plane.drain()
    for b in range(n_ctx):
        h_plane[b].drain()


def middle_stage(m, cot_all, wgate, wup, wdown_o):
    n_fsdp, n_ctx = lax.axis_size("fsdp"), lax.axis_size("ctx")
    seq, width = m.shape
    rows = seq // n_ctx
    cw = width // n_ctx
    units = wgate.shape[1]
    outs = [
        ((rows, width), bf16), ((units, width), bf16), ((width, units), bf16), ((width, units), bf16),
        ((seq, cw), bf16),
    ]
    scratch = [
        pltpu.VMEM((seq, width), bf16),
        pltpu.VMEM((seq, width), bf16),
        pltpu.VMEM((width, units), bf16),
        pltpu.VMEM((width, units), bf16),
        pltpu.VMEM((units, width), bf16),
        pltpu.VMEM((seq, units), bf16),
        pltpu.VMEM((seq, units), bf16),
        pltpu.VMEM((seq, units), bf16),
        pltpu.VMEM((seq, 128), f32),
        pltpu.VMEM((seq, width), bf16),
        pltpu.VMEM((seq, width), bf16),
        pltpu.VMEM((2, rows // 2, width), bf16),
        pltpu.VMEM((2, rows, width), bf16),
        pltpu.VMEM((n_ctx, 2, rows // 2, cw), bf16),
        pltpu.VMEM((n_ctx, 2, rows, cw), bf16),
        pltpu.VMEM((seq, cw), bf16),
        pltpu.VMEM((rows, width), bf16),
        pltpu.VMEM((2, 256, width), bf16),
        pltpu.VMEM((2, 512, units), bf16),
        pltpu.SemaphoreType.DMA((1, LineGather.SEMS)),
        pltpu.SemaphoreType.DMA((5, PlaneScatter.SEMS)),
        pltpu.SemaphoreType.DMA((6,)),
        pltpu.SemaphoreType.DMA((4,)),
    ]
    flops = 18 * seq * width * units
    return call(middle_kernel, (m, cot_all, wgate, wup, wdown_o), outs, scratch, 2, flops, "middle_stage")


def rotate(field, cosine, sine_table, direction):
    half_width = field.shape[-1] // 2
    first_half = field[..., :half_width]
    second_half = field[..., half_width:]
    return jnp.concatenate(
        [
            first_half * cosine - direction * second_half * sine_table,
            second_half * cosine + direction * first_half * sine_table,
        ],
        axis=-1,
    )


def gather(x, axis_name, axis=0):
    return lax.all_gather(x, axis_name, axis=axis, tiled=True)


def scatter(x, axis_name, axis=0):
    return lax.psum_scatter(x.astype(bf16), axis_name, scatter_dimension=axis, tiled=True)


def columns(w, start, count):
    return lax.dynamic_slice_in_dim(w, start, count, axis=1)


def visible(begin):
    seq = begin.shape[0]
    index = jnp.arange(seq, dtype=jnp.int32)
    return (index[None, :] <= index[:, None]) & (index[None, :] >= begin[:, None])


def forward_plain(tok, tab, gains, wqkv_o, wout_o, wgate_o, wup_o, cot):
    n_ctx = lax.axis_size("ctx")
    c = lax.axis_index("ctx")
    x = gather(tok, "ctx")
    tabs = gather(tab[None], "ctx")
    wqkv = gather(wqkv_o, "fsdp")
    wout = gather(wout_o, "fsdp")
    wgate = gather(wgate_o, "fsdp")
    wup = gather(wup_o, "fsdp")
    cot_all = gather(cot, "ctx")
    gain = gather(gains[0:1], "fsdp", axis=1).astype(f32)
    xf = x.astype(f32)
    r = lax.rsqrt(jnp.mean(xf * xf, axis=-1, keepdims=True) + eps_norm)
    xn = (xf * r * gain).astype(bf16)
    seq, width = x.shape
    heads = HEADS // n_ctx
    qw = heads * HEAD_DIM
    pre = dot(xn, wqkv)
    cosine = tabs[:, 0:32].transpose(0, 2, 1).reshape(seq, 1, 32)
    sine = tabs[:, 32:64].transpose(0, 2, 1).reshape(seq, 1, 32)
    begin = tabs[:, 64].reshape(seq).astype(jnp.int32)
    kvw = (wqkv.shape[1] - qw) // 2
    kv = kvw // HEAD_DIM
    q = rotate(pre[:, :qw].reshape(seq, heads, HEAD_DIM), cosine, sine, 1.0).astype(bf16)
    k = rotate(pre[:, qw : qw + kvw].reshape(seq, kv, HEAD_DIM), cosine, sine, 1.0).astype(bf16)
    v = pre[:, qw + kvw :].astype(bf16).reshape(seq, kv, HEAD_DIM)
    qg = q.reshape(seq, kv, heads // kv, HEAD_DIM)
    scores = jnp.einsum("qkgd,lkd->kgql", qg, k, preferred_element_type=f32) * HEAD_DIM ** (-0.5)
    scores = jnp.where(visible(begin)[None, None], scores, neg_large)
    top = jnp.max(scores, axis=-1, keepdims=True)
    weights = jnp.exp(scores - top)
    total = jnp.sum(weights, axis=-1, keepdims=True)
    probs_low = (weights / total).astype(bf16)
    att = jnp.einsum("kgql,lkd->qkgd", probs_low, v, preferred_element_type=f32)
    o = gather(att.astype(bf16).reshape(seq, qw), "ctx", axis=1)
    lse = (top + jnp.log(total)).reshape(heads, 1, seq)
    lse = jnp.broadcast_to(lse, (heads, 8, seq)).reshape(8 * heads, seq)
    cw = width // n_ctx
    mid = columns(x, c * cw, cw).astype(f32) + dot(o, wout)
    m = gather(mid.astype(bf16), "ctx", axis=1)
    qt = q.reshape(seq, qw).T
    kt = k.reshape(seq, kvw).T
    vt = v.reshape(seq, kvw).T
    return x, xn, qt, kt, vt, lse, o, m, wqkv, wout, wgate, wup, cot_all, tabs


def middle_plain(m, cot_all, wgate, wup, wdown_o):
    n_ctx = lax.axis_size("ctx")
    c = lax.axis_index("ctx")
    seq, width = m.shape
    rows = seq // n_ctx
    cw = width // n_ctx
    wdown = gather(wdown_o, "fsdp")
    mf = m.astype(f32)
    r = lax.rsqrt(jnp.mean(mf * mf, axis=-1, keepdims=True) + eps_norm)
    gate = dot(m, wgate) * r
    up = dot(m, wup) * r
    sig = jax.nn.sigmoid(gate)
    hidden = (gate * sig * up).astype(bf16)
    mlp = scatter(dot(hidden, wdown), "ctx").astype(f32)
    mid_rows = lax.dynamic_slice_in_dim(m, c * rows, rows, axis=0).astype(f32)
    output = (mid_rows + mlp).astype(bf16)
    grad_hidden = dot_nt(cot_all, wdown)
    down_raw = dot_tn(hidden, cot_all).astype(bf16)
    d_gate = grad_hidden * up * sig * (1.0 + gate * (1.0 - sig))
    d_up = grad_hidden * gate * sig
    stat = jnp.sum(d_gate * gate + d_up * up, axis=-1, keepdims=True)
    d_gate = (d_gate * r).astype(bf16)
    d_up = (d_up * r).astype(bf16)
    gate_raw = dot_tn(m, d_gate).astype(bf16)
    up_raw = dot_tn(m, d_up).astype(bf16)
    back = dot_nt(d_gate, wgate) + dot_nt(d_up, wup) - mf * (r * r * stat * (1.0 / width))
    back_own = scatter(back, "ctx", axis=1).astype(f32)
    gm = (columns(cot_all, c * cw, cw).astype(f32) + back_own).astype(bf16)
    return output, down_raw, gate_raw, up_raw, gm


def backward_plain(x, xn, gain, qt, kt, vt, lse, o, gm, wqkv, wout, tabs, gate_raw, up_raw, down_raw):
    n_ctx = lax.axis_size("ctx")
    c = lax.axis_index("ctx")
    seq, width = x.shape
    heads = HEADS // n_ctx
    qw = heads * HEAD_DIM
    kvw = kt.shape[0]
    kv = kvw // HEAD_DIM
    cw = width // n_ctx
    scale = HEAD_DIM ** (-0.5)
    cosine = tabs[:, 0:32].transpose(0, 2, 1).reshape(seq, 1, 32)
    sine = tabs[:, 32:64].transpose(0, 2, 1).reshape(seq, 1, 32)
    begin = tabs[:, 64].reshape(seq).astype(jnp.int32)
    gate_grad = scatter(gate_raw, "fsdp")
    up_grad = scatter(up_raw, "fsdp")
    down_grad = scatter(down_raw, "fsdp")
    out_grad = scatter(dot_tn(o, gm), "fsdp")
    d_att = scatter(dot_nt(gm, wout), "ctx", axis=1).reshape(seq, kv, heads // kv, HEAD_DIM)
    q = qt.T.reshape(seq, kv, heads // kv, HEAD_DIM)
    k = kt.T.reshape(seq, kv, HEAD_DIM)
    v = vt.T.reshape(seq, kv, HEAD_DIM)
    scores = jnp.einsum("qkgd,lkd->kgql", q, k, preferred_element_type=f32) * scale
    scores = jnp.where(visible(begin)[None, None], scores, neg_large)
    lse = lse.reshape(kv, heads // kv, 8, seq)[:, :, 0, :, None]
    probs = jnp.exp(scores - lse)
    d_probs = jnp.einsum("qkgd,lkd->kgql", d_att, v, preferred_element_type=f32)
    delta = jnp.sum(probs * d_probs, axis=-1, keepdims=True)
    d_scores = (probs * (d_probs - delta)).astype(bf16)
    d_q = jnp.einsum("kgql,lkd->qkgd", d_scores, k, preferred_element_type=f32) * scale
    d_k = jnp.einsum("kgql,qkgd->lkd", d_scores, q, preferred_element_type=f32) * scale
    d_v = jnp.einsum("kgql,qkgd->lkd", probs.astype(bf16), d_att, preferred_element_type=f32)
    stat = (
        jnp.sum(d_q * q, axis=(1, 2, 3)) + jnp.sum(d_k * k, axis=(1, 2)) + jnp.sum(d_v * v, axis=(1, 2))
    )[:, None]
    d_q = rotate(d_q.reshape(seq, heads, HEAD_DIM), cosine, sine, -1.0).reshape(seq, qw)
    d_k = rotate(d_k, cosine, sine, -1.0).reshape(seq, kvw)
    d_pre = jnp.concatenate([d_q, d_k, d_v.reshape(seq, kvw)], axis=1).astype(bf16)
    qkv_grad = scatter(dot_tn(xn, d_pre), "fsdp")
    xf = x.astype(f32)
    r = lax.rsqrt(jnp.mean(xf * xf, axis=-1, keepdims=True) + eps_norm)
    back = dot_nt(d_pre, wqkv) * (gain * r) - xf * (r * r * stat * (1.0 / width))
    at = (jnp.arange(width, dtype=jnp.int32) // cw == c)[None, :]
    back = back + jnp.where(at, jnp.tile(gm.astype(f32), (1, n_ctx)), 0.0)
    grad_tokens = scatter(back, "ctx").astype(f32)
    qkv_all = gather(qkv_grad[None], "ctx")
    out_all = gather(out_grad, "ctx", axis=1)
    gate_all = gather(gate_grad[None], "ctx")
    up_all = gather(up_grad[None], "ctx")
    down_all = gather(down_grad, "ctx")
    return grad_tokens, qkv_all, out_all, gate_all, up_all, down_all


def per_device(
    tokens,
    positions,
    gain_attn,
    gain_mlp,
    w_query,
    w_key,
    w_value,
    w_out,
    w_gate,
    w_up,
    w_down,
    cotangent,
):
    n_ctx = lax.axis_size("ctx")
    n_fsdp = lax.axis_size("fsdp")
    kernels = n_ctx == 4 and n_fsdp == 8
    c = lax.axis_index("ctx")
    rows, width = tokens.shape
    own_rows = w_query.shape[0]
    qw = HEADS // n_ctx * HEAD_DIM
    copies = max(1, n_ctx // KV_HEADS)
    kvw = max(1, KV_HEADS // n_ctx) * HEAD_DIM
    cw = width // n_ctx
    ff_width = w_gate.shape[1]
    unit = ff_width // (n_fsdp * n_ctx)
    gain_one = gain_attn.astype(f32)[:, None]
    gain_two = gain_mlp.astype(f32)[:, None]

    wqkv_o = jnp.concatenate(
        [
            columns(w_query, c * qw, qw),
            columns(w_key, (c // copies) * kvw, kvw),
            columns(w_value, (c // copies) * kvw, kvw),
        ],
        axis=1,
    )
    wout_o = columns(w_out, c * cw, cw)

    def units(w):
        parts = w.reshape(own_rows, n_fsdp, n_ctx, unit)
        mine = lax.dynamic_index_in_dim(parts, c, axis=2, keepdims=False)
        return (gain_two * mine.reshape(own_rows, n_fsdp * unit)).astype(bf16)

    wgate_o, wup_o = units(w_gate), units(w_up)
    wdown_o = lax.dynamic_slice_in_dim(w_down, c * unit, unit, axis=0)
    gains = jnp.broadcast_to(gain_attn[None, :], (16, own_rows))
    frequency = theta_base ** (-(jnp.arange(HEAD_DIM // 2, dtype=f32) * 2.0) / HEAD_DIM)
    angles = frequency[:, None] * positions.astype(f32)[None, :]
    begin = c * rows + jnp.arange(rows, dtype=jnp.int32) - positions
    tab = jnp.concatenate(
        [jnp.cos(angles), jnp.sin(angles), jnp.broadcast_to(begin.astype(f32)[None, :], (16, rows))],
        axis=0,
    )

    forward = forward_stage if kernels else forward_plain
    x, xn, qt, kt, vt, lse, o, m, wqkv, wout, wgate, wup, cot_all, tabs = forward(
        tokens, tab, gains, wqkv_o, wout_o, wgate_o, wup_o, cotangent
    )
    middle = middle_stage if kernels else middle_plain
    output, down_raw, gate_raw, up_raw, gm = middle(m, cot_all, wgate, wup, wdown_o)
    gain_row = gather(gain_attn, "fsdp").astype(f32)[None, :]
    backward = backward_plain
    grad_tokens, qkv_all, out_all, gate_all, up_all, down_all = backward(
        x, xn, gain_row, qt, kt, vt, lse, o, gm, wqkv, wout, tabs, gate_raw, up_raw, down_raw
    )

    qkv_all = qkv_all.astype(f32)

    def joined(part):
        return jnp.moveaxis(part, 0, 1).reshape(own_rows, -1)

    def kv_part(part):
        return joined(part.reshape(n_ctx // copies, copies, own_rows, kvw).sum(axis=1))

    grad_query = joined(qkv_all[:, :, :qw])
    grad_key = kv_part(qkv_all[:, :, qw : qw + kvw])
    grad_value = kv_part(qkv_all[:, :, qw + kvw :])
    grad_out = out_all.astype(f32)

    def spread(full):
        full = full.reshape(n_ctx, own_rows, n_fsdp, unit)
        return full.transpose(1, 2, 0, 3).reshape(own_rows, ff_width).astype(f32)

    raw_gate, raw_up = spread(gate_all), spread(up_all)
    grad_down = down_all.astype(f32)

    def gain_term(grad, w):
        return jnp.sum(grad * w.astype(f32), axis=1)

    grad_gain_one = (
        gain_term(grad_query, w_query) + gain_term(grad_key, w_key) + gain_term(grad_value, w_value)
    ) / gain_one[:, 0]
    grad_gain_two = gain_term(raw_gate, w_gate) + gain_term(raw_up, w_up)
    return (
        output,
        grad_tokens,
        grad_gain_one,
        grad_gain_two,
        grad_query,
        grad_key,
        grad_value,
        grad_out,
        gain_two * raw_gate,
        gain_two * raw_up,
        grad_down,
    )


def solution(mesh):
    both = P(("fsdp", "ctx"), None)
    first = P("fsdp", None)
    return jax.shard_map(
        per_device,
        mesh=mesh,
        in_specs=(both, P(("fsdp", "ctx")), P("fsdp"), P("fsdp")) + (first,) * 7 + (both,),
        out_specs=(both, both, P("fsdp"), P("fsdp")) + (first,) * 7,
        check_vma=False,
    )
```

```python
import jax
import jax.numpy as jnp
from jax import lax
from jax.experimental import pallas as pl
from jax.experimental.pallas import tpu as pltpu
from jax.sharding import PartitionSpec as P

HEADS = 32
KV_HEADS = 4
HEAD_DIM = 64

eps_norm = 1e-05
theta_base = 10000.0
neg_large = -1e30
bf16 = jnp.bfloat16
f32 = jnp.float32
MESH_IDS = pl.DeviceIdType.MESH


def dot(a, b):
    return jnp.dot(a, b, preferred_element_type=f32)


def dot_nt(a, b):
    return lax.dot_general(a, b, (((1,), (1,)), ((), ())), preferred_element_type=f32)


def dot_tn(a, b):
    return lax.dot_general(a, b, (((0,), (0,)), ((), ())), preferred_element_type=f32)


class Place:
    def __init__(self):
        self.f = lax.axis_index("fsdp")
        self.c = lax.axis_index("ctx")
        self.depth = lax.axis_size("fsdp") // 2
        self.z = self.f // 2
        self.core = self.f % 2
        self.other = 1 - self.core
        self.cx = self.c + 1 - 2 * (self.c % 2)
        self.cy = self.c + 2 - 4 * (self.c // 2)
        self.cd = 3 - self.c
        self.sibling = {"fsdp": self.f + 1 - 2 * self.core}
        self.up = {"fsdp": self.f + 2}
        self.down = {"fsdp": self.f - 2}
        self.x = {"ctx": self.cx}
        self.y = {"ctx": self.cy}

    def has_up(self):
        return self.z < self.depth - 1

    def has_down(self):
        return self.z > 0

    def barrier(self):
        sem = pltpu.get_barrier_semaphore()

        def greet(device):
            pl.semaphore_signal(sem, inc=1, device_id=device, device_id_type=MESH_IDS)

        greet(self.sibling)
        greet(self.x)
        greet(self.y)

        @pl.when(self.has_up())
        def _():
            greet(self.up)

        @pl.when(self.has_down())
        def _():
            greet(self.down)

        last = self.depth - 1
        pl.semaphore_wait(sem, 4 - self.z // last + (self.z + last - 1) // last)


def remote(src, dst, send_sem, recv_sem, device):
    return pltpu.make_async_remote_copy(
        src_ref=src,
        dst_ref=dst,
        send_sem=send_sem,
        recv_sem=recv_sem,
        device_id=device,
        device_id_type=MESH_IDS,
    )


class LineGather:
    SEMS = 21

    def __init__(self, place, own, full, sems):
        self.p, self.own, self.full, self.sems = place, own, full, sems
        self.rows = own.shape[0]
        self.n = place.depth

    def view(self, level, core):
        start = pl.multiple_of((2 * level + core) * self.rows, 16)
        return self.full.at[pl.ds(start, self.rows)]

    def to_up(self, hop):
        p = self.p
        level = p.z - (hop - 1)
        src = self.own if hop == 1 else self.view(level, p.core)
        return remote(
            src, self.view(level, p.core), self.sems.at[hop - 1], self.sems.at[6 + hop - 1], p.up
        )

    def to_down(self, hop):
        p = self.p
        level = p.z + (hop - 1)
        src = self.own if hop == 1 else self.view(level, p.core)
        return remote(
            src, self.view(level, p.core), self.sems.at[3 + hop - 1], self.sems.at[9 + hop - 1], p.down
        )

    def to_sibling(self, level, own=False):
        p = self.p
        src = self.own if own else self.view(level, p.core)
        return remote(
            src, self.view(level, p.core), self.sems.at[12 + level], self.sems.at[16 + level], p.sibling
        )

    def local(self):
        p = self.p
        return pltpu.make_async_copy(self.own, self.view(p.z, p.core), self.sems.at[20])

    def start(self):
        p = self.p

        @pl.when(p.has_up())
        def _():
            self.to_up(1).start()

        @pl.when(p.has_down())
        def _():
            self.to_down(1).start()

        self.to_sibling(p.z, True).start()
        self.local().start()

    def arrived(self, level, sem):
        view = self.view(level, self.p.core)
        remote(view, view, self.sems.at[0], sem, self.p.sibling).wait_recv()

    def hop(self, s):
        p = self.p

        @pl.when(p.z >= s)
        def _():
            self.arrived(p.z - s, self.sems.at[6 + s - 1])
            if s < self.n - 1:

                @pl.when(p.has_up())
                def _():
                    self.to_up(s + 1).start()

            self.to_sibling(p.z - s).start()

        @pl.when(p.z + s < self.n)
        def _():
            self.arrived(p.z + s, self.sems.at[9 + s - 1])
            if s < self.n - 1:

                @pl.when(p.has_down())
                def _():
                    self.to_down(s + 1).start()

            self.to_sibling(p.z + s).start()

    def finish(self):
        p = self.p
        self.local().wait()
        for level in range(self.n):
            view = self.view(level, p.other)
            remote(view, view, self.sems.at[0], self.sems.at[16 + level], p.sibling).wait_recv()

    def drain(self):
        p = self.p
        for s in range(1, self.n):

            @pl.when(p.has_up() & (p.z >= s - 1))
            def _():
                self.to_up(s).wait_send()

            @pl.when(p.has_down() & (p.z + s - 1 < self.n))
            def _():
                self.to_down(s).wait_send()

        for level in range(self.n):
            self.to_sibling(level).wait_send()


class PlaneGather:
    SEMS = 8

    def __init__(self, place, view, half, sems, own=None):
        self.p, self.view, self.half, self.sems = place, view, half, sems
        self.own = own

    def src(self):
        return self.view(self.p.c) if self.own is None else self.own

    def to_x(self):
        p = self.p
        return remote(self.src(), self.view(p.c), self.sems.at[0], self.sems.at[2], p.x)

    def to_y(self):
        p = self.p
        return remote(self.src(), self.view(p.c), self.sems.at[1], self.sems.at[3], p.y)

    def on_to_y(self):
        p, h = self.p, self.half(self.p.cx, 0)
        return remote(h, h, self.sems.at[4], self.sems.at[6], p.y)

    def on_to_x(self):
        p, h = self.p, self.half(self.p.cy, 1)
        return remote(h, h, self.sems.at[5], self.sems.at[7], p.x)

    def start(self):
        self.to_x().start()
        self.to_y().start()

    def got(self, ref, sem):
        remote(ref, ref, self.sems.at[0], sem, self.p.x).wait_recv()

    def middle(self):
        p = self.p
        self.got(self.view(p.cx), self.sems.at[2])
        self.on_to_y().start()
        self.got(self.view(p.cy), self.sems.at[3])
        self.on_to_x().start()

    def finish(self):
        p = self.p
        self.got(self.half(p.cd, 0), self.sems.at[6])
        self.got(self.half(p.cd, 1), self.sems.at[7])

    def drain(self):
        self.to_x().wait_send()
        self.to_y().wait_send()
        self.on_to_y().wait_send()
        self.on_to_x().wait_send()


def rows_at(index, count):
    return pl.ds(pl.multiple_of(index * count, count), count)


def any_spec(count):
    return [pl.BlockSpec(memory_space=pl.ANY)] * count


def call(kernel, ins, outs, scratch, collective_id, flops, name, vmem=60.0):
    return pl.pallas_call(
        kernel,
        out_shape=[jax.ShapeDtypeStruct(s, d) for s, d in outs],
        in_specs=any_spec(len(ins)),
        out_specs=any_spec(len(outs)),
        scratch_shapes=scratch,
        compiler_params=pltpu.CompilerParams(
            collective_id=collective_id, has_side_effects=True, vmem_limit_bytes=int(vmem * 2**20)
        ),
        cost_estimate=pl.CostEstimate(flops=flops, bytes_accessed=2**26, transcendentals=2**22),
        name=name,
    )(*ins)


class PlaneScatter:
    SEMS = 8

    def __init__(self, place, part, half, first, second, sems):
        self.p, self.part, self.half = place, part, half
        self.first, self.second, self.sems = first, second, sems

    def ref(self):
        return self.part(self.p.c)

    def far_to_y(self):
        p = self.p
        return remote(self.half(p.cd, 0), self.first.at[0], self.sems.at[0], self.sems.at[2], p.y)

    def far_to_x(self):
        p = self.p
        return remote(self.half(p.cd, 1), self.first.at[1], self.sems.at[1], self.sems.at[3], p.x)

    def to_x(self):
        p = self.p
        return remote(self.part(p.cx), self.second.at[0], self.sems.at[4], self.sems.at[6], p.x)

    def to_y(self):
        p = self.p
        return remote(self.part(p.cy), self.second.at[1], self.sems.at[5], self.sems.at[7], p.y)

    def start(self):
        self.far_to_y().start()
        self.far_to_x().start()

    def got(self, ref, sem):
        remote(ref, ref, self.sems.at[0], sem, self.p.x).wait_recv()

    def add(self, ref, other):
        ref[...] = (ref[...].astype(f32) + other[...].astype(f32)).astype(bf16)

    def middle(self):
        p = self.p
        self.got(self.first.at[0], self.sems.at[2])
        self.add(self.half(p.cx, 0), self.first.at[0])
        self.to_x().start()
        self.got(self.first.at[1], self.sems.at[3])
        self.add(self.half(p.cy, 1), self.first.at[1])
        self.to_y().start()

    def finish(self, at=slice(None), first=True):
        if first:
            self.got(self.second.at[0], self.sems.at[6])
            self.got(self.second.at[1], self.sems.at[7])
        own = self.part(self.p.c)[at].astype(f32)
        return own + self.second[0, at].astype(f32) + self.second[1, at].astype(f32)

    def drain(self):
        self.far_to_y().wait_send()
        self.far_to_x().wait_send()
        self.to_x().wait_send()
        self.to_y().wait_send()


class LineScatter:
    SEMS = 22

    def __init__(self, place, part, acc, slots, sems, stage=None):
        self.p, self.part, self.acc, self.slots, self.sems = place, part, acc, slots, sems
        self.stage = stage
        self.n = place.depth

    def to_sibling(self, level):
        p = self.p
        return remote(
            self.part(level, p.other), self.acc.at[level], self.sems.at[level], self.sems.at[4 + level], p.sibling
        )

    def start(self):
        for level in range(self.n):
            self.to_sibling(level).start()

    def load(self, level):
        return pltpu.make_async_copy(
            self.part(level, self.p.core), self.stage[level % 2], self.sems.at[20 + level % 2]
        )

    def got(self, ref, sem):
        remote(ref, ref, self.sems.at[0], sem, self.p.sibling).wait_recv()

    def add(self, ref, other):
        ref[...] = (ref[...].astype(f32) + other[...].astype(f32)).astype(bf16)

    def combine(self):
        if self.stage is not None:
            self.load(0).start()
            self.load(1).start()
        for level in range(self.n):
            self.got(self.acc.at[level], self.sems.at[4 + level])
            if self.stage is None:
                self.add(self.acc.at[level], self.part(level, self.p.core))
            else:
                self.load(level).wait()
                self.add(self.acc.at[level], self.stage[level % 2])
                if level + 2 < self.n:
                    self.load(level + 2).start()

    def slot(self, up, s):
        return self.slots.at[s - 1] if up else self.slots.at[(0, 3, 4)[s - 1]]

    def along(self, up, s):
        p = self.p
        level = p.z if up else self.n - 1 - p.z
        block = self.n - s + level
        block = block if up else self.n - 1 - block
        base = 8 if up else 14
        copy = remote(
            self.acc.at[block],
            self.slot(up, s),
            self.sems.at[base + s - 1],
            self.sems.at[base + 3 + s - 1],
            p.up if up else p.down,
        )
        return copy, (level <= s - 1) & (level < self.n - 1)

    def step(self, s):
        for up in (True, False):
            level = self.p.z if up else self.n - 1 - self.p.z
            if s > 1:
                block = self.n - s + level
                block = block if up else self.n - 1 - block
                base = 11 if up else 17

                @pl.when((level >= 1) & (s - 1 >= level))
                def _():
                    self.got(self.slot(up, s - 1), self.sems.at[base + s - 2])
                    self.add(self.acc.at[block], self.slot(up, s - 1))

            if s < self.n:
                copy, valid = self.along(up, s)

                @pl.when(valid)
                def _():
                    copy.start()

    def result(self):
        return self.acc.at[self.p.z]

    def drain(self):
        for level in range(self.n):
            self.to_sibling(level).wait_send()
        for up in (True, False):
            for s in range(1, self.n):
                copy, valid = self.along(up, s)

                @pl.when(valid)
                def _():
                    copy.wait_send()


def forward_kernel(
    tok, tab, gains, wqkv_o, wout_o, wgate_o, wup_o, cot,
    xn_out, r_out, grow_out, qt_out, kt_out, vt_out, lse_out, o_out, m_out,
    wqkv_out, wout_out, wgate, wup, cot_all, tab_out,
    X, XN, QT, KT, VT, K, LSE, O, M, WQ, WO, TAB, G8, GROW, BIAS, OT, R1,
    line_sems, plane_sems, copy_sems,
):
    p = Place()
    n_ctx = 4
    rows = tok.shape[0]
    half = rows // 2
    qw = QT.shape[0]
    heads = qw // HEAD_DIM
    cw = O.shape[1] // n_ctx
    scale = HEAD_DIM ** (-0.5)

    p.barrier()

    gain_line = LineGather(p, gains, G8, line_sems.at[0])
    qkv_line = LineGather(p, wqkv_o, WQ, line_sems.at[1])
    out_line = LineGather(p, wout_o, WO, line_sems.at[2])
    gate_line = LineGather(p, wgate_o, wgate, line_sems.at[3])
    up_line = LineGather(p, wup_o, wup, line_sems.at[4])

    def row_block(ref):
        return (
            lambda c: ref.at[rows_at(c, rows)],
            lambda c, h: ref.at[pl.ds(pl.multiple_of(c * rows + h * half, half), half)],
        )

    tok_plane = PlaneGather(p, *row_block(X), plane_sems.at[0], own=tok)
    cot_plane = PlaneGather(p, *row_block(cot_all), plane_sems.at[1], own=cot)
    tab_rows = tab.shape[0]
    tab_plane = PlaneGather(
        p,
        lambda c: TAB.at[c],
        lambda c, h: TAB.at[c, pl.ds(h * (tab_rows // 2), tab_rows // 2)],
        plane_sems.at[2],
        own=tab,
    )

    def col_block(ref, b):
        def view(c):
            return ref.at[pl.ds(b * rows, rows), rows_at(c, cw)]

        def halves(c, h):
            return ref.at[pl.ds(b * rows + h * half, half), rows_at(c, cw)]

        return view, halves

    o_plane = [PlaneGather(p, *col_block(O, b), plane_sems.at[3 + b]) for b in range(n_ctx)]
    m_plane = [PlaneGather(p, *col_block(M, b), plane_sems.at[7 + b]) for b in range(n_ctx)]

    gain_line.start()
    qkv_line.start()
    tab_plane.start()
    tok_plane.start()
    out_line.start()
    own_tok = pltpu.make_async_copy(tok, X.at[rows_at(p.c, rows)], copy_sems.at[0])
    own_tab = pltpu.make_async_copy(tab, TAB.at[p.c], copy_sems.at[1])
    own_cot = pltpu.make_async_copy(cot, cot_all.at[rows_at(p.c, rows)], copy_sems.at[2])
    own_tok.start()
    own_tab.start()
    own_cot.start()

    gain_line.hop(1)
    tab_plane.middle()
    gain_line.hop(2)
    qkv_line.hop(1)
    gain_line.hop(3)
    gain_line.finish()
    for f in range(2 * p.depth):
        GROW[:, f * gains.shape[1] : (f + 1) * gains.shape[1]] = G8[16 * f : 16 * f + 8, :].astype(f32)

    def norm(c):
        at = rows_at(c, rows)
        x = X[at, :].astype(f32)
        r = lax.rsqrt(jnp.mean(x * x, axis=-1, keepdims=True) + eps_norm)
        R1[at, :] = jnp.broadcast_to(r, (rows, 128))
        XN[at, :] = (x * r * GROW[0:1, :]).astype(bf16)

    own_tok.wait()
    norm(p.c)
    out_line.hop(1)
    qkv_line.hop(2)
    tok_plane.middle()
    out_line.hop(2)
    gate_line.start()
    norm(p.cx)
    norm(p.cy)
    qkv_line.hop(3)
    tok_plane.finish()
    cot_plane.start()
    out_line.hop(3)
    up_line.start()
    norm(p.cd)
    xn_copy = pltpu.make_async_copy(XN, xn_out, copy_sems.at[3])
    r_copy = pltpu.make_async_copy(R1, r_out, copy_sems.at[4])
    grow_copy = pltpu.make_async_copy(GROW, grow_out, copy_sems.at[14])
    xn_copy.start()
    r_copy.start()
    grow_copy.start()
    own_tab.wait()
    tab_plane.finish()
    qkv_line.finish()

    @pl.loop(0, n_ctx)
    def _(b):
        at = rows_at(b, rows)
        pre = dot(XN[at, :], WQ[...]).T
        cosine = TAB[b, 0:32, :]
        sine = TAB[b, 32:64, :]
        for h in range(heads + 1):
            u = pre[64 * h : 64 * h + 32]
            w = pre[64 * h + 32 : 64 * h + 64]
            first = u * cosine - w * sine
            second = w * cosine + u * sine
            if h < heads:
                QT[64 * h : 64 * h + 32, at] = first.astype(bf16)
                QT[64 * h + 32 : 64 * h + 64, at] = second.astype(bf16)
            else:
                KT[0:32, at] = first.astype(bf16)
                KT[32:64, at] = second.astype(bf16)
                K[at, :] = jnp.concatenate([first, second], axis=0).T.astype(bf16)
        VT[:, at] = pre[qw + 64 :].astype(bf16)

    wq_copy = pltpu.make_async_copy(WQ, wqkv_out, copy_sems.at[5])
    wq_copy.start()
    gate_line.hop(1)

    def attend(b):
        n = (b + 1) * rows
        key = lax.broadcasted_iota(jnp.int32, (n, rows), 0)
        query = lax.broadcasted_iota(jnp.int32, (n, rows), 1) + b * rows
        begin = TAB[b, 64:65, :].astype(jnp.int32)
        BIAS[0:n, :] = jnp.where((key <= query) & (key >= begin), 0.0, neg_large)
        cols = slice(b * rows, (b + 1) * rows)

        @pl.loop(0, heads)
        def _(h):
            head = rows_at(h, HEAD_DIM)
            s = dot(K[0:n, :], QT[head, cols]) * scale + BIAS[0:n, :]
            top = jnp.max(s, axis=0, keepdims=True)
            e = jnp.exp(s - top)
            total = jnp.sum(e, axis=0, keepdims=True)
            probs = (e * (1.0 / total)).astype(bf16)
            OT[head, :] = dot(VT[:, 0:n], probs)
            LSE[rows_at(h, 8), cols] = jnp.broadcast_to(top + jnp.log(total), (8, rows))

        O[pl.ds(b * rows, rows), rows_at(p.c, cw)] = OT[...].T.astype(bf16)
        o_plane[b].start()

    def middle(b):
        at = pl.ds(b * rows, rows)
        mine = rows_at(p.c, cw)
        mid = X[at, mine].astype(f32) + dot(O[at, :], WO[...])
        M[at, mine] = mid.astype(bf16)
        m_plane[b].start()

    attend(0)
    attend(1)
    o_plane[0].middle()
    attend(2)
    o_plane[1].middle()
    attend(3)
    o_plane[2].middle()
    cot_plane.middle()
    out_line.finish()
    o_plane[0].finish()
    middle(0)
    o_plane[3].middle()
    up_line.hop(1)
    o_plane[1].finish()
    middle(1)
    m_plane[0].middle()
    o_plane[2].finish()
    middle(2)
    m_plane[1].middle()
    gate_line.hop(2)
    o_plane[3].finish()
    middle(3)
    m_plane[2].middle()
    up_line.hop(2)
    m_plane[3].middle()
    copies = [xn_copy, r_copy, grow_copy, wq_copy]
    for i, (src, dst) in enumerate(
        ((QT, qt_out), (KT, kt_out), (VT, vt_out), (LSE, lse_out), (O, o_out), (WO, wout_out), (TAB, tab_out))
    ):
        copy = pltpu.make_async_copy(src, dst, copy_sems.at[6 + i])
        copy.start()
        copies.append(copy)
    for b in range(n_ctx):
        m_plane[b].finish()
    m_copy = pltpu.make_async_copy(M, m_out, copy_sems.at[13])
    m_copy.start()
    copies.append(m_copy)
    gate_line.hop(3)
    up_line.hop(3)
    cot_plane.finish()
    gate_line.finish()
    up_line.finish()
    own_cot.wait()
    for copy in copies:
        copy.wait()
    for line in (gain_line, qkv_line, out_line, gate_line, up_line):
        line.drain()
    for plane in [tok_plane, cot_plane, tab_plane] + o_plane + m_plane:
        plane.drain()


def forward_stage(tok, tab, gains, wqkv_o, wout_o, wgate_o, wup_o, cot):
    n_fsdp, n_ctx = lax.axis_size("fsdp"), lax.axis_size("ctx")
    rows, width = tok.shape
    seq = rows * n_ctx
    whole = n_fsdp * wqkv_o.shape[0]
    nq, nw, nu = wqkv_o.shape[1], wout_o.shape[1], wgate_o.shape[1]
    qw = HEADS // n_ctx * HEAD_DIM
    heads = qw // HEAD_DIM
    tab_shape = (n_ctx,) + tab.shape
    outs = [
        ((seq, width), bf16), ((seq, 128), f32), ((8, width), f32), ((qw, seq), bf16), ((64, seq), bf16),
        ((64, seq), bf16), ((8 * heads, seq), f32), ((seq, width), bf16), ((seq, width), bf16), ((whole, nq), bf16),
        ((whole, nw), bf16), ((whole, nu), bf16), ((whole, nu), bf16), ((seq, width), bf16), (tab_shape, f32),
    ]
    scratch = [
        pltpu.VMEM((seq, width), bf16),
        pltpu.VMEM((seq, width), bf16),
        pltpu.VMEM((qw, seq), bf16),
        pltpu.VMEM((64, seq), bf16),
        pltpu.VMEM((64, seq), bf16),
        pltpu.VMEM((seq, 64), bf16),
        pltpu.VMEM((8 * heads, seq), f32),
        pltpu.VMEM((seq, width), bf16),
        pltpu.VMEM((seq, width), bf16),
        pltpu.VMEM((whole, nq), bf16),
        pltpu.VMEM((whole, nw), bf16),
        pltpu.VMEM(tab_shape, f32),
        pltpu.VMEM((16 * n_fsdp, gains.shape[1]), bf16),
        pltpu.VMEM((8, width), f32),
        pltpu.VMEM((seq, rows), f32),
        pltpu.VMEM((qw, rows), f32),
        pltpu.VMEM((seq, 128), f32),
        pltpu.SemaphoreType.DMA((5, LineGather.SEMS)),
        pltpu.SemaphoreType.DMA((11, PlaneGather.SEMS)),
        pltpu.SemaphoreType.DMA((15,)),
    ]
    ins = (tok, tab, gains, wqkv_o, wout_o, wgate_o, wup_o, cot)
    flops = 2 * seq * width * (nq + nw) + 8 * heads * seq * seq * HEAD_DIM
    return call(forward_kernel, ins, outs, scratch, 1, flops, "forward_stage")


def tiles_of(total, most):
    sizes, at = [], 0
    while at < total:
        sizes.append((at, min(most, total - at)))
        at += most
    return sizes


def middle_kernel(
    m_in, cot_in, wgate_in, wup_in, wdown_o,
    y_out, down_part, gate_part, up_part, gm_out,
    M, COT, WG, WU, WD, GATE, UP, HID, R2, PD, PH, D1, D2, H1, H2, GM, Y, STAGE_D, STAGE,
    line_sems, plane_sems, copy_sems, stage_sems,
):
    p = Place()
    n_ctx = 4
    seq, width = M.shape
    rows = seq // n_ctx
    half = rows // 2
    cw = width // n_ctx
    units = GATE.shape[1]
    loads = []
    for i, (src, dst) in enumerate(((m_in, M), (wgate_in, WG), (wup_in, WU), (cot_in, COT))):
        loads.append(pltpu.make_async_copy(src, dst, copy_sems.at[i]))
        loads[-1].start()

    p.barrier()
    down_line = LineGather(p, wdown_o, WD, line_sems.at[0])
    down_line.start()

    loads[0].wait()
    loads[1].wait()
    loads[2].wait()

    @pl.loop(0, n_ctx)
    def _(b):
        at = rows_at(b, rows)
        mf = M[at, :].astype(f32)
        r = lax.rsqrt(jnp.mean(mf * mf, axis=-1, keepdims=True) + eps_norm)
        gate = dot(M[at, :], WG[...]) * r
        up = dot(M[at, :], WU[...]) * r
        R2[at, :] = jnp.broadcast_to(r, (rows, 128))
        GATE[at, :] = gate.astype(bf16)
        UP[at, :] = up.astype(bf16)
        HID[at, :] = (gate * (1.0 / (1.0 + jnp.exp(-gate))) * up).astype(bf16)

    down_line.hop(1)
    loads[3].wait()
    stage_copies = {}
    for i, (at, size) in enumerate(tiles_of(units, STAGE_D.shape[1])):
        slot = i % 2
        if i >= 2:
            stage_copies[i - 2].wait()
        STAGE_D[slot, 0:size, :] = dot_tn(HID[:, at : at + size], COT[...]).astype(bf16)
        copy = pltpu.make_async_copy(
            STAGE_D.at[slot, pl.ds(0, size)], down_part.at[pl.ds(at, size)], stage_sems.at[slot]
        )
        copy.start()
        stage_copies[i] = copy
    n_down = len(stage_copies)
    down_line.hop(2)
    stage_copies[n_down - 2].wait()
    stage_copies[n_down - 1].wait()
    down_line.hop(3)
    down_line.finish()

    y_plane = PlaneScatter(
        p,
        lambda c: PD.at[rows_at(c, rows)],
        lambda c, h: PD.at[pl.ds(pl.multiple_of(c * rows + h * half, half), half)],
        D1,
        D2,
        plane_sems.at[0],
    )

    def col_scatter(b):
        return PlaneScatter(
            p,
            lambda c: PH.at[pl.ds(b * rows, rows), rows_at(c, cw)],
            lambda c, h: PH.at[pl.ds(b * rows + h * half, half), rows_at(c, cw)],
            H1.at[b],
            H2.at[b],
            plane_sems.at[1 + b],
        )

    h_plane = [col_scatter(b) for b in range(n_ctx)]

    def partial_out(c):
        at = rows_at(c, rows)
        PD[at, :] = dot(HID[at, :], WD[...]).astype(bf16)

    partial_out(p.cd)
    y_plane.start()
    partial_out(p.cx)
    partial_out(p.cy)
    y_plane.middle()
    partial_out(p.c)

    def back(b):
        at = pl.ds(b * rows, rows)
        r = R2[at, 0:1]
        grad_hidden = dot_nt(COT[at, :], WD[...])
        gate = GATE[at, :].astype(f32)
        up = UP[at, :].astype(f32)
        sig = 1.0 / (1.0 + jnp.exp(-gate))
        d_up = grad_hidden * gate * sig
        d_gate = grad_hidden * up * sig * (1.0 + gate * (1.0 - sig))
        stat = jnp.sum(d_gate * gate + d_up * up, axis=-1, keepdims=True)
        GATE[at, :] = (d_gate * r).astype(bf16)
        UP[at, :] = (d_up * r).astype(bf16)
        coef = r * r * stat * (1.0 / width)
        for j in range(0, width, cw):
            e = dot_nt(GATE[at, :], WG[j : j + cw, :]) + dot_nt(UP[at, :], WU[j : j + cw, :])
            PH[at, j : j + cw] = (e - M[at, j : j + cw].astype(f32) * coef).astype(bf16)
        h_plane[b].start()

    back(0)
    back(1)
    h_plane[0].middle()
    back(2)
    h_plane[1].middle()
    back(3)
    h_plane[2].middle()

    stage_copies = {}
    jobs = []
    for src, dst in ((GATE, gate_part), (UP, up_part)):
        for at, size in tiles_of(width, STAGE.shape[1]):
            jobs.append((src, dst, at, size))

    def weight_tile(i):
        src, dst, at, size = jobs[i]
        slot = i % 2
        if i >= 2:
            stage_copies[i - 2].wait()
        STAGE[slot] = dot_tn(M[:, at : at + size], src[...]).astype(bf16)
        copy = pltpu.make_async_copy(STAGE.at[slot], dst.at[pl.ds(at, size)], stage_sems.at[2 + slot])
        copy.start()
        stage_copies[i] = copy

    def finish_block(b):
        at = pl.ds(b * rows, rows)
        GM[at, :] = (COT[at, rows_at(p.c, cw)].astype(f32) + h_plane[b].finish()).astype(bf16)

    weight_tile(0)
    weight_tile(1)
    h_plane[3].middle()
    weight_tile(2)
    finish_block(0)
    weight_tile(3)
    finish_block(1)
    weight_tile(4)
    weight_tile(5)
    finish_block(2)
    weight_tile(6)
    weight_tile(7)
    Y[...] = (M[rows_at(p.c, rows), :].astype(f32) + y_plane.finish()).astype(bf16)
    y_copy = pltpu.make_async_copy(Y, y_out, copy_sems.at[4])
    y_copy.start()
    finish_block(3)
    gm_copy = pltpu.make_async_copy(GM, gm_out, copy_sems.at[5])
    gm_copy.start()
    stage_copies[6].wait()
    stage_copies[7].wait()
    y_copy.wait()
    gm_copy.wait()
    down_line.drain()
    y_plane.drain()
    for b in range(n_ctx):
        h_plane[b].drain()


def middle_stage(m, cot_all, wgate, wup, wdown_o):
    n_fsdp, n_ctx = lax.axis_size("fsdp"), lax.axis_size("ctx")
    seq, width = m.shape
    rows = seq // n_ctx
    cw = width // n_ctx
    units = wgate.shape[1]
    outs = [
        ((rows, width), bf16), ((units, width), bf16), ((width, units), bf16), ((width, units), bf16),
        ((seq, cw), bf16),
    ]
    scratch = [
        pltpu.VMEM((seq, width), bf16),
        pltpu.VMEM((seq, width), bf16),
        pltpu.VMEM((width, units), bf16),
        pltpu.VMEM((width, units), bf16),
        pltpu.VMEM((units, width), bf16),
        pltpu.VMEM((seq, units), bf16),
        pltpu.VMEM((seq, units), bf16),
        pltpu.VMEM((seq, units), bf16),
        pltpu.VMEM((seq, 128), f32),
        pltpu.VMEM((seq, width), bf16),
        pltpu.VMEM((seq, width), bf16),
        pltpu.VMEM((2, rows // 2, width), bf16),
        pltpu.VMEM((2, rows, width), bf16),
        pltpu.VMEM((n_ctx, 2, rows // 2, cw), bf16),
        pltpu.VMEM((n_ctx, 2, rows, cw), bf16),
        pltpu.VMEM((seq, cw), bf16),
        pltpu.VMEM((rows, width), bf16),
        pltpu.VMEM((2, 256, width), bf16),
        pltpu.VMEM((2, 512, units), bf16),
        pltpu.SemaphoreType.DMA((1, LineGather.SEMS)),
        pltpu.SemaphoreType.DMA((5, PlaneScatter.SEMS)),
        pltpu.SemaphoreType.DMA((6,)),
        pltpu.SemaphoreType.DMA((4,)),
    ]
    flops = 18 * seq * width * units
    return call(middle_kernel, (m, cot_all, wgate, wup, wdown_o), outs, scratch, 2, flops, "middle_stage")


def backward_kernel(
    xn_in, r_in, grow_in, qt_in, kt_in, vt_in, lse_in, o_in, gm_in, wqkv_in, wout_in, tab_in,
    gate_part, up_part, down_part,
    tok_out, qkv_all, out_all, gate_all, up_all, down_all,
    XN, R1, GROW, QT, KT, VT, LSE, O, GM, WQ, WO, TAB,
    K, V, DK, DV, DOT, DQT, DPRE, STAT, BIAS, PT, G1, G2, T1, T2, TOK,
    DACC, DSLOT, GACC, GSLOT, UACC, USLOT, OACC, OSLOT, QACC, QSLOT,
    line_sems, plane_sems, scatter_sems, copy_sems,
):
    p = Place()
    n_ctx = 4
    seq, width = XN.shape
    rows = seq // n_ctx
    half = rows // 2
    cw = width // n_ctx
    qw = QT.shape[0]
    heads = qw // HEAD_DIM
    nq = WQ.shape[1]
    own_rows = QACC.shape[1]
    scale = HEAD_DIM ** (-0.5)
    loads = []
    for i, (src, dst) in enumerate(
        (
            (gm_in, GM), (wout_in, WO), (o_in, O), (kt_in, KT), (vt_in, VT), (qt_in, QT), (lse_in, LSE),
            (tab_in, TAB), (xn_in, XN), (wqkv_in, WQ), (r_in, R1), (grow_in, GROW),
        )
    ):
        loads.append(pltpu.make_async_copy(src, dst, copy_sems.at[i]))
        if dst is not XN:
            loads[-1].start()

    p.barrier()

    def block_rows(ref):
        count = ref.shape[0] // (2 * p.depth)
        return lambda level, core: ref.at[pl.ds(pl.multiple_of((2 * level + core) * count, 16), count)]

    unit, nu = DACC.shape[1], GACC.shape[2]
    rows_stage = [XN.at[pl.ds(i * unit, unit)] for i in range(2)]
    cols_stage = [XN.at[pl.ds(i * own_rows, own_rows), pl.ds(0, nu)] for i in range(2)]
    down_line = LineScatter(p, block_rows(down_part), DACC, DSLOT, line_sems.at[0], rows_stage)
    gate_line = LineScatter(p, block_rows(gate_part), GACC, GSLOT, line_sems.at[1], cols_stage)
    up_line = LineScatter(p, block_rows(up_part), UACC, USLOT, line_sems.at[2], cols_stage)
    out_line = LineScatter(p, block_rows(WO), OACC, OSLOT, line_sems.at[3])

    def qkv_block(level, core):
        f = 2 * level + core
        at = pl.ds(pl.multiple_of((f % p.depth) * own_rows, own_rows), own_rows)
        return O.at[at, pl.ds(pl.multiple_of((f // p.depth) * nq, 128), nq)]

    qkv_line = LineScatter(p, qkv_block, QACC, QSLOT, line_sems.at[4])
    down_line.start()
    gate_line.start()
    up_line.start()

    def col_scatter(b):
        return PlaneScatter(
            p,
            lambda c: PT.at[pl.ds(b * rows, rows), rows_at(c, cw)],
            lambda c, h: PT.at[pl.ds(b * rows + h * half, half), rows_at(c, cw)],
            G1.at[b],
            G2.at[b],
            scatter_sems.at[b],
        )

    g_plane = [col_scatter(b) for b in range(n_ctx)]
    t_plane = PlaneScatter(
        p,
        lambda c: PT.at[rows_at(c, rows)],
        lambda c, h: PT.at[pl.ds(pl.multiple_of(c * rows + h * half, half), half)],
        T1,
        T2,
        scatter_sems.at[n_ctx],
    )

    def whole(ref, line, index, first):
        count = line.acc.shape[1]

        def halves(c, h):
            return ref(c).at[pl.ds(h * first, count - first if h else first)]

        plane = PlaneGather(p, ref, halves, plane_sems.at[index], own=line.result())
        own = pltpu.make_async_copy(line.result(), ref(p.c), plane_sems.at[index, PlaneGather.SEMS])
        return plane, own

    down_plane, down_own = whole(lambda c: down_all.at[c], down_line, 0, 96)
    gate_plane, gate_own = whole(lambda c: gate_all.at[c], gate_line, 1, half)
    up_plane, up_own = whole(lambda c: up_all.at[c], up_line, 2, half)
    out_plane, out_own = whole(lambda c: out_all.at[c], out_line, 3, half)
    qkv_plane, qkv_own = whole(lambda c: qkv_all.at[c], qkv_line, 4, half)

    loads[0].wait()
    loads[1].wait()
    for b in range(n_ctx):
        at = pl.ds(b * rows, rows)
        for j in range(0, width, 512):
            PT[at, j : j + 512] = dot_nt(GM[at, :], WO[j : j + 512, :]).astype(bf16)
        g_plane[b].start()
    down_line.combine()
    down_line.step(1)
    g_plane[0].middle()
    loads[2].wait()

    @pl.loop(0, width // 512)
    def _(i):
        at = rows_at(i, 512)
        WO[at, :] = dot_tn(O[:, at], GM[...]).astype(bf16)

    out_line.start()
    g_plane[1].middle()
    gate_line.combine()
    loads[8].start()
    gate_line.step(1)
    g_plane[2].middle()
    for i in (3, 4, 5, 6, 7, 10):
        loads[i].wait()

    @pl.loop(0, n_ctx)
    def _(b):
        at = rows_at(b, rows)
        K[at, :] = KT[:, at].astype(f32).T.astype(bf16)
        V[at, :] = VT[:, at].astype(f32).T.astype(bf16)
        DK[at, :] = jnp.zeros((rows, HEAD_DIM), f32)
        DV[at, :] = jnp.zeros((rows, HEAD_DIM), f32)

    g_plane[3].middle()

    def attend_back(b):
        n = (b + 1) * rows
        cols = slice(b * rows, (b + 1) * rows)
        DOT[...] = g_plane[b].finish().T.astype(bf16)
        at = pl.ds(b * rows, rows)
        DQT[...] = O[at, rows_at(p.c, cw)].astype(f32).T
        key = lax.broadcasted_iota(jnp.int32, (n, rows), 0)
        query = lax.broadcasted_iota(jnp.int32, (n, rows), 1) + b * rows
        begin = TAB[b, 64:65, :].astype(jnp.int32)
        BIAS[0:n, :] = jnp.where((key <= query) & (key >= begin), 0.0, neg_large)
        STAT[...] = jnp.zeros((8, rows), f32)

        @pl.loop(0, heads)
        def _(h):
            head = rows_at(h, HEAD_DIM)
            q = QT[head, cols]
            d_out = DOT[head, :]
            delta = jnp.sum(d_out.astype(f32) * DQT[head, :], axis=0, keepdims=True)
            s = dot(K[0:n, :], q) * scale + BIAS[0:n, :]
            probs = jnp.exp(s - LSE[rows_at(h, 8), cols][0:1])
            d_probs = dot(V[0:n, :], d_out)
            d_s = (probs * (d_probs - delta)).astype(bf16)
            d_q = dot(KT[:, 0:n], d_s) * scale
            DK[0:n, :] += dot_nt(d_s, q) * scale
            DV[0:n, :] += dot_nt(probs.astype(bf16), d_out)
            STAT[...] += jnp.broadcast_to(jnp.sum(d_q * q.astype(f32), axis=0, keepdims=True), (8, rows))
            u, w = d_q[0:32], d_q[32:64]
            cosine, sine = TAB[b, 0:32, :], TAB[b, 32:64, :]
            DQT[head, :] = jnp.concatenate([u * cosine + w * sine, w * cosine - u * sine], axis=0)

        DPRE[at, 0:qw] = DQT[...].T.astype(bf16)
        R1[at, 0:8] = STAT[...].T

    attend_back(0)
    down_line.step(2)
    attend_back(1)
    gate_line.step(2)
    attend_back(2)
    down_line.step(3)
    attend_back(3)
    gate_line.step(3)
    loads[8].wait()
    loads[9].wait()
    loads[11].wait()

    @pl.loop(0, n_ctx)
    def _(b):
        at = rows_at(b, rows)
        d_k = DK[at, :].T
        d_v = DV[at, :].T
        stat = jnp.sum(d_k * KT[:, at].astype(f32) + d_v * VT[:, at].astype(f32), axis=0, keepdims=True)
        R1[at, 0:8] += jnp.broadcast_to(stat, (8, rows)).T
        u, w = d_k[0:32], d_k[32:64]
        cosine, sine = TAB[b, 0:32, :], TAB[b, 32:64, :]
        both = jnp.concatenate([u * cosine + w * sine, w * cosine - u * sine, d_v], axis=0)
        DPRE[at, qw:] = both.T.astype(bf16)

    def tokens(c):
        at = rows_at(c, rows)
        r = R1[at, 127:128]
        coef = r * R1[at, 0:1] * (1.0 / width)
        for j in range(0, width, 512):
            cols = slice(j, j + 512)
            gain = GROW[0:1, cols]
            e = dot_nt(DPRE[at, :], WQ[cols, :])
            PT[at, cols] = (e * (gain * r) - XN[at, cols].astype(f32) * ((1.0 / gain) * coef)).astype(bf16)
        mine = rows_at(p.c, cw)
        PT[at, mine] = (PT[at, mine].astype(f32) + GM[at, :].astype(f32)).astype(bf16)

    for b in range(n_ctx):
        g_plane[b].drain()
    tokens(p.cd)
    t_plane.start()
    tokens(p.cx)
    tokens(p.cy)
    t_plane.middle()
    tokens(p.c)

    @pl.loop(0, p.depth)
    def _(i):
        for j in range(2):
            at = rows_at(i + j * p.depth, own_rows)
            O[rows_at(i, own_rows), j * nq : (j + 1) * nq] = dot_tn(XN[:, at], DPRE[...]).astype(bf16)

    qkv_line.start()
    down_line.step(4)
    down_plane.start()
    down_own.start()
    up_line.combine()
    up_line.step(1)
    out_line.combine()
    out_line.step(1)
    gate_line.step(4)
    gate_plane.start()
    gate_own.start()
    tok_copies = []
    for i in range(n_ctx):
        if i >= 2:
            tok_copies[i - 2].wait()
        at = pl.ds(i * (rows // n_ctx), rows // n_ctx)
        TOK[i % 2] = t_plane.finish(at, i == 0)
        tok_copies.append(pltpu.make_async_copy(TOK.at[i % 2], tok_out.at[at], copy_sems.at[12 + i % 2]))
        tok_copies[-1].start()
    down_plane.middle()
    up_line.step(2)
    out_line.step(2)
    gate_plane.middle()
    qkv_line.combine()
    qkv_line.step(1)
    up_line.step(3)
    out_line.step(3)
    qkv_line.step(2)
    up_line.step(4)
    up_plane.start()
    up_own.start()
    out_line.step(4)
    out_plane.start()
    out_own.start()
    qkv_line.step(3)
    up_plane.middle()
    out_plane.middle()
    qkv_line.step(4)
    qkv_plane.start()
    qkv_own.start()
    qkv_plane.middle()
    for plane, own in (
        (down_plane, down_own), (gate_plane, gate_own), (up_plane, up_own), (out_plane, out_own), (qkv_plane, qkv_own),
    ):
        plane.finish()
        own.wait()
        plane.drain()
    tok_copies[2].wait()
    tok_copies[3].wait()
    t_plane.drain()
    for line in (down_line, gate_line, up_line, out_line, qkv_line):
        line.drain()


def backward_stage(xn, r, grow, qt, kt, vt, lse, o, gm, wqkv, wout, tabs, gate_part, up_part, down_part):
    n_fsdp, n_ctx = lax.axis_size("fsdp"), lax.axis_size("ctx")
    seq, width = xn.shape
    rows = seq // n_ctx
    half = rows // 2
    cw = width // n_ctx
    own = width // n_fsdp
    depth = n_fsdp // 2
    nq, nu = wqkv.shape[1], gate_part.shape[1]
    unit = down_part.shape[0] // n_fsdp
    qw = qt.shape[0]
    outs = [
        ((rows, width), f32), ((n_ctx, own, nq), bf16), ((n_ctx, own, cw), bf16), ((n_ctx, own, nu), bf16),
        ((n_ctx, own, nu), bf16), ((n_ctx, unit, width), bf16),
    ]
    ins = (xn, r, grow, qt, kt, vt, lse, o, gm, wqkv, wout, tabs, gate_part, up_part, down_part)
    scratch = [pltpu.VMEM(a.shape, a.dtype) for a in ins[:12]] + [
        pltpu.VMEM((seq, HEAD_DIM), bf16),
        pltpu.VMEM((seq, HEAD_DIM), bf16),
        pltpu.VMEM((seq, HEAD_DIM), f32),
        pltpu.VMEM((seq, HEAD_DIM), f32),
        pltpu.VMEM((qw, rows), bf16),
        pltpu.VMEM((qw, rows), f32),
        pltpu.VMEM((seq, nq), bf16),
        pltpu.VMEM((8, rows), f32),
        pltpu.VMEM((seq, rows), f32),
        pltpu.VMEM((seq, width), bf16),
        pltpu.VMEM((n_ctx, 2, half, cw), bf16),
        pltpu.VMEM((n_ctx, 2, rows, cw), bf16),
        pltpu.VMEM((2, half, width), bf16),
        pltpu.VMEM((2, rows, width), bf16),
        pltpu.VMEM((2, rows // n_ctx, width), f32),
        pltpu.VMEM((depth, unit, width), bf16),
        pltpu.VMEM((5, unit, width), bf16),
        pltpu.VMEM((depth, own, nu), bf16),
        pltpu.VMEM((5, own, nu), bf16),
        pltpu.VMEM((depth, own, nu), bf16),
        pltpu.VMEM((5, own, nu), bf16),
        pltpu.VMEM((depth, own, cw), bf16),
        pltpu.VMEM((5, own, cw), bf16),
        pltpu.VMEM((depth, own, nq), bf16),
        pltpu.VMEM((5, own, nq), bf16),
        pltpu.SemaphoreType.DMA((5, LineScatter.SEMS)),
        pltpu.SemaphoreType.DMA((5, PlaneGather.SEMS + 1)),
        pltpu.SemaphoreType.DMA((n_ctx + 1, PlaneScatter.SEMS)),
        pltpu.SemaphoreType.DMA((14,)),
    ]
    flops = 4 * seq * width * (nq + cw) + 20 * qw * seq * seq
    return call(backward_kernel, ins, outs, scratch, 3, flops, "backward_stage")


def rotate(field, cosine, sine_table, direction):
    half_width = field.shape[-1] // 2
    first_half = field[..., :half_width]
    second_half = field[..., half_width:]
    return jnp.concatenate(
        [
            first_half * cosine - direction * second_half * sine_table,
            second_half * cosine + direction * first_half * sine_table,
        ],
        axis=-1,
    )


def gather(x, axis_name, axis=0):
    return lax.all_gather(x, axis_name, axis=axis, tiled=True)


def scatter(x, axis_name, axis=0):
    return lax.psum_scatter(x.astype(bf16), axis_name, scatter_dimension=axis, tiled=True)


def columns(w, start, count):
    return lax.dynamic_slice_in_dim(w, start, count, axis=1)


def visible(begin):
    seq = begin.shape[0]
    index = jnp.arange(seq, dtype=jnp.int32)
    return (index[None, :] <= index[:, None]) & (index[None, :] >= begin[:, None])


def forward_plain(tok, tab, gains, wqkv_o, wout_o, wgate_o, wup_o, cot):
    n_ctx = lax.axis_size("ctx")
    c = lax.axis_index("ctx")
    x = gather(tok, "ctx")
    tabs = gather(tab[None], "ctx")
    wqkv = gather(wqkv_o, "fsdp")
    wout = gather(wout_o, "fsdp")
    wgate = gather(wgate_o, "fsdp")
    wup = gather(wup_o, "fsdp")
    cot_all = gather(cot, "ctx")
    gain = gather(gains[0:1], "fsdp", axis=1).astype(f32)
    xf = x.astype(f32)
    r = lax.rsqrt(jnp.mean(xf * xf, axis=-1, keepdims=True) + eps_norm)
    xn = (xf * r * gain).astype(bf16)
    seq, width = x.shape
    heads = HEADS // n_ctx
    qw = heads * HEAD_DIM
    pre = dot(xn, wqkv)
    cosine = tabs[:, 0:32].transpose(0, 2, 1).reshape(seq, 1, 32)
    sine = tabs[:, 32:64].transpose(0, 2, 1).reshape(seq, 1, 32)
    begin = tabs[:, 64].reshape(seq).astype(jnp.int32)
    kvw = (wqkv.shape[1] - qw) // 2
    kv = kvw // HEAD_DIM
    q = rotate(pre[:, :qw].reshape(seq, heads, HEAD_DIM), cosine, sine, 1.0).astype(bf16)
    k = rotate(pre[:, qw : qw + kvw].reshape(seq, kv, HEAD_DIM), cosine, sine, 1.0).astype(bf16)
    v = pre[:, qw + kvw :].astype(bf16).reshape(seq, kv, HEAD_DIM)
    qg = q.reshape(seq, kv, heads // kv, HEAD_DIM)
    scores = jnp.einsum("qkgd,lkd->kgql", qg, k, preferred_element_type=f32) * HEAD_DIM ** (-0.5)
    scores = jnp.where(visible(begin)[None, None], scores, neg_large)
    top = jnp.max(scores, axis=-1, keepdims=True)
    weights = jnp.exp(scores - top)
    total = jnp.sum(weights, axis=-1, keepdims=True)
    probs_low = (weights / total).astype(bf16)
    att = jnp.einsum("kgql,lkd->qkgd", probs_low, v, preferred_element_type=f32)
    o = gather(att.astype(bf16).reshape(seq, qw), "ctx", axis=1)
    lse = (top + jnp.log(total)).reshape(heads, 1, seq)
    lse = jnp.broadcast_to(lse, (heads, 8, seq)).reshape(8 * heads, seq)
    cw = width // n_ctx
    mid = columns(x, c * cw, cw).astype(f32) + dot(o, wout)
    m = gather(mid.astype(bf16), "ctx", axis=1)
    qt = q.reshape(seq, qw).T
    kt = k.reshape(seq, kvw).T
    vt = v.reshape(seq, kvw).T
    r = jnp.broadcast_to(r, (seq, 128))
    grow = jnp.broadcast_to(gain, (8, width))
    return xn, r, grow, qt, kt, vt, lse, o, m, wqkv, wout, wgate, wup, cot_all, tabs


def middle_plain(m, cot_all, wgate, wup, wdown_o):
    n_ctx = lax.axis_size("ctx")
    c = lax.axis_index("ctx")
    seq, width = m.shape
    rows = seq // n_ctx
    cw = width // n_ctx
    wdown = gather(wdown_o, "fsdp")
    mf = m.astype(f32)
    r = lax.rsqrt(jnp.mean(mf * mf, axis=-1, keepdims=True) + eps_norm)
    gate = dot(m, wgate) * r
    up = dot(m, wup) * r
    sig = jax.nn.sigmoid(gate)
    hidden = (gate * sig * up).astype(bf16)
    mlp = scatter(dot(hidden, wdown), "ctx").astype(f32)
    mid_rows = lax.dynamic_slice_in_dim(m, c * rows, rows, axis=0).astype(f32)
    output = (mid_rows + mlp).astype(bf16)
    grad_hidden = dot_nt(cot_all, wdown)
    down_raw = dot_tn(hidden, cot_all).astype(bf16)
    d_gate = grad_hidden * up * sig * (1.0 + gate * (1.0 - sig))
    d_up = grad_hidden * gate * sig
    stat = jnp.sum(d_gate * gate + d_up * up, axis=-1, keepdims=True)
    d_gate = (d_gate * r).astype(bf16)
    d_up = (d_up * r).astype(bf16)
    gate_raw = dot_tn(m, d_gate).astype(bf16)
    up_raw = dot_tn(m, d_up).astype(bf16)
    back = dot_nt(d_gate, wgate) + dot_nt(d_up, wup) - mf * (r * r * stat * (1.0 / width))
    back_own = scatter(back, "ctx", axis=1).astype(f32)
    gm = (columns(cot_all, c * cw, cw).astype(f32) + back_own).astype(bf16)
    return output, down_raw, gate_raw, up_raw, gm


def backward_plain(xn, r, grow, qt, kt, vt, lse, o, gm, wqkv, wout, tabs, gate_raw, up_raw, down_raw):
    n_ctx = lax.axis_size("ctx")
    c = lax.axis_index("ctx")
    seq, width = xn.shape
    r, gain = r[:, 0:1], grow[0:1]
    heads = HEADS // n_ctx
    qw = heads * HEAD_DIM
    kvw = kt.shape[0]
    kv = kvw // HEAD_DIM
    cw = width // n_ctx
    scale = HEAD_DIM ** (-0.5)
    cosine = tabs[:, 0:32].transpose(0, 2, 1).reshape(seq, 1, 32)
    sine = tabs[:, 32:64].transpose(0, 2, 1).reshape(seq, 1, 32)
    begin = tabs[:, 64].reshape(seq).astype(jnp.int32)
    gate_grad = scatter(gate_raw, "fsdp")
    up_grad = scatter(up_raw, "fsdp")
    down_grad = scatter(down_raw, "fsdp")
    out_grad = scatter(dot_tn(o, gm), "fsdp")
    d_att = scatter(dot_nt(gm, wout), "ctx", axis=1).reshape(seq, kv, heads // kv, HEAD_DIM)
    q = qt.T.reshape(seq, kv, heads // kv, HEAD_DIM)
    k = kt.T.reshape(seq, kv, HEAD_DIM)
    v = vt.T.reshape(seq, kv, HEAD_DIM)
    scores = jnp.einsum("qkgd,lkd->kgql", q, k, preferred_element_type=f32) * scale
    scores = jnp.where(visible(begin)[None, None], scores, neg_large)
    lse = lse.reshape(kv, heads // kv, 8, seq)[:, :, 0, :, None]
    probs = jnp.exp(scores - lse)
    d_probs = jnp.einsum("qkgd,lkd->kgql", d_att, v, preferred_element_type=f32)
    delta = jnp.sum(probs * d_probs, axis=-1, keepdims=True)
    d_scores = (probs * (d_probs - delta)).astype(bf16)
    d_q = jnp.einsum("kgql,lkd->qkgd", d_scores, k, preferred_element_type=f32) * scale
    d_k = jnp.einsum("kgql,qkgd->lkd", d_scores, q, preferred_element_type=f32) * scale
    d_v = jnp.einsum("kgql,qkgd->lkd", probs.astype(bf16), d_att, preferred_element_type=f32)
    stat = (
        jnp.sum(d_q * q, axis=(1, 2, 3)) + jnp.sum(d_k * k, axis=(1, 2)) + jnp.sum(d_v * v, axis=(1, 2))
    )[:, None]
    d_q = rotate(d_q.reshape(seq, heads, HEAD_DIM), cosine, sine, -1.0).reshape(seq, qw)
    d_k = rotate(d_k, cosine, sine, -1.0).reshape(seq, kvw)
    d_pre = jnp.concatenate([d_q, d_k, d_v.reshape(seq, kvw)], axis=1).astype(bf16)
    qkv_grad = scatter(dot_tn(xn, d_pre), "fsdp")
    back = dot_nt(d_pre, wqkv) * (gain * r)
    back = back - xn.astype(f32) * ((1.0 / gain) * (r * stat * (1.0 / width)))
    at = (jnp.arange(width, dtype=jnp.int32) // cw == c)[None, :]
    back = back + jnp.where(at, jnp.tile(gm.astype(f32), (1, n_ctx)), 0.0)
    grad_tokens = scatter(back, "ctx").astype(f32)
    qkv_all = gather(qkv_grad[None], "ctx")
    out_all = gather(out_grad[None], "ctx")
    gate_all = gather(gate_grad[None], "ctx")
    up_all = gather(up_grad[None], "ctx")
    down_all = gather(down_grad[None], "ctx")
    return grad_tokens, qkv_all, out_all, gate_all, up_all, down_all


def per_device(
    tokens,
    positions,
    gain_attn,
    gain_mlp,
    w_query,
    w_key,
    w_value,
    w_out,
    w_gate,
    w_up,
    w_down,
    cotangent,
):
    n_ctx = lax.axis_size("ctx")
    n_fsdp = lax.axis_size("fsdp")
    kernels = n_ctx == 4 and n_fsdp == 8
    c = lax.axis_index("ctx")
    rows, width = tokens.shape
    own_rows = w_query.shape[0]
    qw = HEADS // n_ctx * HEAD_DIM
    copies = max(1, n_ctx // KV_HEADS)
    kvw = max(1, KV_HEADS // n_ctx) * HEAD_DIM
    cw = width // n_ctx
    ff_width = w_gate.shape[1]
    unit = ff_width // (n_fsdp * n_ctx)
    gain_one = gain_attn.astype(f32)[:, None]
    gain_two = gain_mlp.astype(f32)[:, None]

    wqkv_o = jnp.concatenate(
        [
            columns(w_query, c * qw, qw),
            columns(w_key, (c // copies) * kvw, kvw),
            columns(w_value, (c // copies) * kvw, kvw),
        ],
        axis=1,
    )
    wout_o = columns(w_out, c * cw, cw)

    def units(w):
        parts = w.reshape(own_rows, n_fsdp, n_ctx, unit)
        mine = lax.dynamic_index_in_dim(parts, c, axis=2, keepdims=False)
        return (gain_two * mine.reshape(own_rows, n_fsdp * unit)).astype(bf16)

    wgate_o, wup_o = units(w_gate), units(w_up)
    wdown_o = lax.dynamic_slice_in_dim(w_down, c * unit, unit, axis=0)
    gains = jnp.broadcast_to(gain_attn[None, :], (16, own_rows))
    frequency = theta_base ** (-(jnp.arange(HEAD_DIM // 2, dtype=f32) * 2.0) / HEAD_DIM)
    angles = frequency[:, None] * positions.astype(f32)[None, :]
    begin = c * rows + jnp.arange(rows, dtype=jnp.int32) - positions
    tab = jnp.concatenate(
        [jnp.cos(angles), jnp.sin(angles), jnp.broadcast_to(begin.astype(f32)[None, :], (16, rows))],
        axis=0,
    )

    forward = forward_stage if kernels else forward_plain
    xn, r, grow, qt, kt, vt, lse, o, m, wqkv, wout, wgate, wup, cot_all, tabs = forward(
        tokens, tab, gains, wqkv_o, wout_o, wgate_o, wup_o, cotangent
    )
    middle = middle_stage if kernels else middle_plain
    output, down_raw, gate_raw, up_raw, gm = middle(m, cot_all, wgate, wup, wdown_o)
    backward = backward_stage if kernels else backward_plain
    grad_tokens, qkv_all, out_all, gate_all, up_all, down_all = backward(
        xn, r, grow, qt, kt, vt, lse, o, gm, wqkv, wout, tabs, gate_raw, up_raw, down_raw
    )

    qkv_all = qkv_all.astype(f32)

    def joined(part):
        return jnp.moveaxis(part, 0, 1).reshape(own_rows, -1)

    def kv_part(part):
        return joined(part.reshape(n_ctx // copies, copies, own_rows, kvw).sum(axis=1))

    grad_query = joined(qkv_all[:, :, :qw])
    grad_key = kv_part(qkv_all[:, :, qw : qw + kvw])
    grad_value = kv_part(qkv_all[:, :, qw + kvw :])
    grad_out = joined(out_all.astype(f32))

    def spread(full):
        full = full.reshape(n_ctx, own_rows, n_fsdp, unit)
        return full.transpose(1, 2, 0, 3).reshape(own_rows, ff_width).astype(f32)

    raw_gate, raw_up = spread(gate_all), spread(up_all)
    grad_down = down_all.astype(f32).reshape(-1, width)

    def gain_term(grad, w):
        return jnp.sum(grad * w.astype(f32), axis=1)

    grad_gain_one = (
        gain_term(grad_query, w_query) + gain_term(grad_key, w_key) + gain_term(grad_value, w_value)
    ) / gain_one[:, 0]
    grad_gain_two = gain_term(raw_gate, w_gate) + gain_term(raw_up, w_up)
    return (
        output,
        grad_tokens,
        grad_gain_one,
        grad_gain_two,
        grad_query,
        grad_key,
        grad_value,
        grad_out,
        gain_two * raw_gate,
        gain_two * raw_up,
        grad_down,
    )


def solution(mesh):
    both = P(("fsdp", "ctx"), None)
    first = P("fsdp", None)
    return jax.shard_map(
        per_device,
        mesh=mesh,
        in_specs=(both, P(("fsdp", "ctx")), P("fsdp"), P("fsdp")) + (first,) * 7 + (both,),
        out_specs=(both, both, P("fsdp"), P("fsdp")) + (first,) * 7,
        check_vma=False,
    )
```

```python
import functools

import jax
import jax.numpy as jnp
from jax import lax
from jax.experimental import pallas as pl
from jax.experimental.pallas import tpu as pltpu
from jax.sharding import PartitionSpec as P

HEADS = 32
KV_HEADS = 4
HEAD_DIM = 64

eps_norm = 1e-05
theta_base = 10000.0
neg_large = -1e30
bf16 = jnp.bfloat16
f32 = jnp.float32
MESH_IDS = pl.DeviceIdType.MESH


def dot(a, b):
    return jnp.dot(a, b, preferred_element_type=f32)


def dot_nt(a, b):
    return lax.dot_general(a, b, (((1,), (1,)), ((), ())), preferred_element_type=f32)


def dot_tn(a, b):
    return lax.dot_general(a, b, (((0,), (0,)), ((), ())), preferred_element_type=f32)


class Place:
    def __init__(self):
        self.f = lax.axis_index("fsdp")
        self.c = lax.axis_index("ctx")
        self.depth = lax.axis_size("fsdp") // 2
        self.z = self.f // 2
        self.core = self.f % 2
        self.other = 1 - self.core
        self.cx = self.c + 1 - 2 * (self.c % 2)
        self.cy = self.c + 2 - 4 * (self.c // 2)
        self.cd = 3 - self.c
        self.sibling = {"fsdp": self.f + 1 - 2 * self.core}
        self.up = {"fsdp": self.f + 2}
        self.down = {"fsdp": self.f - 2}
        self.x = {"ctx": self.cx}
        self.y = {"ctx": self.cy}

    def has_up(self):
        return self.z < self.depth - 1

    def has_down(self):
        return self.z > 0

    def barrier(self):
        sem = pltpu.get_barrier_semaphore()

        def greet(device):
            pl.semaphore_signal(sem, inc=1, device_id=device, device_id_type=MESH_IDS)

        greet(self.sibling)
        greet(self.x)
        greet(self.y)

        @pl.when(self.has_up())
        def _():
            greet(self.up)

        @pl.when(self.has_down())
        def _():
            greet(self.down)

        last = self.depth - 1
        pl.semaphore_wait(sem, 4 - self.z // last + (self.z + last - 1) // last)


def remote(src, dst, send_sem, recv_sem, device):
    return pltpu.make_async_remote_copy(
        src_ref=src,
        dst_ref=dst,
        send_sem=send_sem,
        recv_sem=recv_sem,
        device_id=device,
        device_id_type=MESH_IDS,
    )


class LineGather:
    SEMS = 21

    def __init__(self, place, own, full, sems):
        self.p, self.own, self.full, self.sems = place, own, full, sems
        self.n = place.depth
        self.rows = full.shape[0] // (2 * self.n)

    def view(self, level, core):
        start = pl.multiple_of((2 * level + core) * self.rows, 16)
        return self.full.at[pl.ds(start, self.rows)]

    def to_up(self, hop):
        p = self.p
        level = p.z - (hop - 1)
        src = self.own if hop == 1 and self.own is not None else self.view(level, p.core)
        return remote(
            src, self.view(level, p.core), self.sems.at[hop - 1], self.sems.at[6 + hop - 1], p.up
        )

    def to_down(self, hop):
        p = self.p
        level = p.z + (hop - 1)
        src = self.own if hop == 1 and self.own is not None else self.view(level, p.core)
        return remote(
            src, self.view(level, p.core), self.sems.at[3 + hop - 1], self.sems.at[9 + hop - 1], p.down
        )

    def to_sibling(self, level, own=False):
        p = self.p
        src = self.own if own and self.own is not None else self.view(level, p.core)
        return remote(
            src, self.view(level, p.core), self.sems.at[12 + level], self.sems.at[16 + level], p.sibling
        )

    def local(self):
        p = self.p
        return pltpu.make_async_copy(self.own, self.view(p.z, p.core), self.sems.at[20])

    def start(self):
        p = self.p

        @pl.when(p.has_up())
        def _():
            self.to_up(1).start()

        @pl.when(p.has_down())
        def _():
            self.to_down(1).start()

        self.to_sibling(p.z, True).start()
        if self.own is not None:
            self.local().start()

    def arrived(self, level, sem):
        view = self.view(level, self.p.core)
        remote(view, view, self.sems.at[0], sem, self.p.sibling).wait_recv()

    def hop(self, s):
        p = self.p

        @pl.when(p.z >= s)
        def _():
            self.arrived(p.z - s, self.sems.at[6 + s - 1])
            if s < self.n - 1:

                @pl.when(p.has_up())
                def _():
                    self.to_up(s + 1).start()

            self.to_sibling(p.z - s).start()

        @pl.when(p.z + s < self.n)
        def _():
            self.arrived(p.z + s, self.sems.at[9 + s - 1])
            if s < self.n - 1:

                @pl.when(p.has_down())
                def _():
                    self.to_down(s + 1).start()

            self.to_sibling(p.z + s).start()

    def finish(self):
        p = self.p
        if self.own is not None:
            self.local().wait()
        for level in range(self.n):
            view = self.view(level, p.other)
            remote(view, view, self.sems.at[0], self.sems.at[16 + level], p.sibling).wait_recv()

    def drain(self):
        p = self.p
        for s in range(1, self.n):

            @pl.when(p.has_up() & (p.z >= s - 1))
            def _():
                self.to_up(s).wait_send()

            @pl.when(p.has_down() & (p.z + s - 1 < self.n))
            def _():
                self.to_down(s).wait_send()

        for level in range(self.n):
            self.to_sibling(level).wait_send()


class PlaneGather:
    SEMS = 8

    def __init__(self, place, view, half, sems, own=None):
        self.p, self.view, self.half, self.sems = place, view, half, sems
        self.own = own

    def src(self):
        return self.view(self.p.c) if self.own is None else self.own

    def to_x(self):
        p = self.p
        return remote(self.src(), self.view(p.c), self.sems.at[0], self.sems.at[2], p.x)

    def to_y(self):
        p = self.p
        return remote(self.src(), self.view(p.c), self.sems.at[1], self.sems.at[3], p.y)

    def on_to_y(self):
        p, h = self.p, self.half(self.p.cx, 0)
        return remote(h, h, self.sems.at[4], self.sems.at[6], p.y)

    def on_to_x(self):
        p, h = self.p, self.half(self.p.cy, 1)
        return remote(h, h, self.sems.at[5], self.sems.at[7], p.x)

    def start(self):
        self.to_x().start()
        self.to_y().start()

    def got(self, ref, sem):
        remote(ref, ref, self.sems.at[0], sem, self.p.x).wait_recv()

    def middle(self):
        p = self.p
        self.got(self.view(p.cx), self.sems.at[2])
        self.on_to_y().start()
        self.got(self.view(p.cy), self.sems.at[3])
        self.on_to_x().start()

    def finish(self):
        p = self.p
        self.got(self.half(p.cd, 0), self.sems.at[6])
        self.got(self.half(p.cd, 1), self.sems.at[7])

    def drain(self):
        self.to_x().wait_send()
        self.to_y().wait_send()
        self.on_to_y().wait_send()
        self.on_to_x().wait_send()


def rows_at(index, count):
    return pl.ds(pl.multiple_of(index * count, count), count)


def any_spec(count):
    return [pl.BlockSpec(memory_space=pl.ANY)] * count


def call(kernel, ins, outs, scratch, collective_id, flops, name, vmem=60.0):
    return pl.pallas_call(
        kernel,
        out_shape=[jax.ShapeDtypeStruct(s, d) for s, d in outs],
        in_specs=any_spec(len(ins)),
        out_specs=any_spec(len(outs)),
        scratch_shapes=scratch,
        compiler_params=pltpu.CompilerParams(
            collective_id=collective_id, has_side_effects=True, vmem_limit_bytes=int(vmem * 2**20)
        ),
        cost_estimate=pl.CostEstimate(flops=flops, bytes_accessed=2**26, transcendentals=2**22),
        name=name,
    )(*ins)


class PlaneScatter:
    SEMS = 8

    def __init__(self, place, part, half, first, second, sems):
        self.p, self.part, self.half = place, part, half
        self.first, self.second, self.sems = first, second, sems

    def ref(self):
        return self.part(self.p.c)

    def far_to_y(self):
        p = self.p
        return remote(self.half(p.cd, 0), self.first.at[0], self.sems.at[0], self.sems.at[2], p.y)

    def far_to_x(self):
        p = self.p
        return remote(self.half(p.cd, 1), self.first.at[1], self.sems.at[1], self.sems.at[3], p.x)

    def to_x(self):
        p = self.p
        return remote(self.part(p.cx), self.second.at[0], self.sems.at[4], self.sems.at[6], p.x)

    def to_y(self):
        p = self.p
        return remote(self.part(p.cy), self.second.at[1], self.sems.at[5], self.sems.at[7], p.y)

    def start(self):
        self.far_to_y().start()
        self.far_to_x().start()

    def got(self, ref, sem):
        remote(ref, ref, self.sems.at[0], sem, self.p.x).wait_recv()

    def add(self, ref, other):
        ref[...] = (ref[...].astype(f32) + other[...].astype(f32)).astype(bf16)

    def middle(self):
        p = self.p
        self.got(self.first.at[0], self.sems.at[2])
        self.add(self.half(p.cx, 0), self.first.at[0])
        self.to_x().start()
        self.got(self.first.at[1], self.sems.at[3])
        self.add(self.half(p.cy, 1), self.first.at[1])
        self.to_y().start()

    def finish(self, at=slice(None), first=True):
        if first:
            self.got(self.second.at[0], self.sems.at[6])
            self.got(self.second.at[1], self.sems.at[7])
        own = self.part(self.p.c)[at].astype(f32)
        return own + self.second[0, at].astype(f32) + self.second[1, at].astype(f32)

    def drain(self):
        self.far_to_y().wait_send()
        self.far_to_x().wait_send()
        self.to_x().wait_send()
        self.to_y().wait_send()


class LineScatter:
    SEMS = 22

    def __init__(self, place, part, acc, slots, sems, stage=None):
        self.p, self.part, self.acc, self.slots, self.sems = place, part, acc, slots, sems
        self.stage = stage
        self.n = place.depth

    def to_sibling(self, level):
        p = self.p
        return remote(
            self.part(level, p.other), self.acc.at[level], self.sems.at[level], self.sems.at[4 + level], p.sibling
        )

    def start(self):
        for level in range(self.n):
            self.to_sibling(level).start()

    def load(self, level):
        return pltpu.make_async_copy(
            self.part(level, self.p.core), self.stage[level % 2], self.sems.at[20 + level % 2]
        )

    def got(self, ref, sem):
        remote(ref, ref, self.sems.at[0], sem, self.p.sibling).wait_recv()

    def add(self, ref, other):
        ref[...] = (ref[...].astype(f32) + other[...].astype(f32)).astype(bf16)

    def combine(self):
        if self.stage is not None:
            self.load(0).start()
            self.load(1).start()
        for level in range(self.n):
            self.got(self.acc.at[level], self.sems.at[4 + level])
            if self.stage is None:
                self.add(self.acc.at[level], self.part(level, self.p.core))
            else:
                self.load(level).wait()
                self.add(self.acc.at[level], self.stage[level % 2])
                if level + 2 < self.n:
                    self.load(level + 2).start()

    def slot(self, up, s):
        return self.slots.at[s - 1] if up else self.slots.at[(0, 3, 4)[s - 1]]

    def along(self, up, s):
        p = self.p
        level = p.z if up else self.n - 1 - p.z
        block = self.n - s + level
        block = block if up else self.n - 1 - block
        base = 8 if up else 14
        copy = remote(
            self.acc.at[block],
            self.slot(up, s),
            self.sems.at[base + s - 1],
            self.sems.at[base + 3 + s - 1],
            p.up if up else p.down,
        )
        return copy, (level <= s - 1) & (level < self.n - 1)

    def step(self, s):
        for up in (True, False):
            level = self.p.z if up else self.n - 1 - self.p.z
            if s > 1:
                block = self.n - s + level
                block = block if up else self.n - 1 - block
                base = 11 if up else 17

                @pl.when((level >= 1) & (s - 1 >= level))
                def _():
                    self.got(self.slot(up, s - 1), self.sems.at[base + s - 2])
                    self.add(self.acc.at[block], self.slot(up, s - 1))

            if s < self.n:
                copy, valid = self.along(up, s)

                @pl.when(valid)
                def _():
                    copy.start()

    def result(self):
        return self.acc.at[self.p.z]

    def drain(self):
        for level in range(self.n):
            self.to_sibling(level).wait_send()
        for up in (True, False):
            for s in range(1, self.n):
                copy, valid = self.along(up, s)

                @pl.when(valid)
                def _():
                    copy.wait_send()


def forward_kernel(
    tok, tab, gains, gcol, w_query, w_key, w_value, w_out, w_gate, w_up, cot,
    xn_out, r_out, grow_out, qt_out, kt_out, vt_out, lse_out, o_out, m_out,
    wqkv_out, wout_out, wgate, wup, cot_all, tab_out,
    X, XN, QT, KT, VT, K, LSE, O, M, WQ, WO, TAB, G8, GROW, BIAS, OT, R1,
    WK, WV, GF, UF, GO, UO, GCOL,
    line_sems, plane_sems, copy_sems,
):
    p = Place()
    n_ctx = 4
    rows = tok.shape[0]
    half = rows // 2
    qw = QT.shape[0]
    heads = qw // HEAD_DIM
    cw = O.shape[1] // n_ctx
    scale = HEAD_DIM ** (-0.5)

    mine = rows_at(p.f, WK.shape[0])
    loads = []
    for i, (src, dst) in enumerate(
        (
            (w_query.at[:, rows_at(p.c, qw)], WQ.at[mine, pl.ds(0, qw)]),
            (w_key, WK), (w_value, WV), (w_gate, GF), (w_up, UF), (gcol, GCOL),
        )
    ):
        loads.append(pltpu.make_async_copy(src, dst, copy_sems.at[15 + i]))
        loads[-1].start()

    p.barrier()

    gain_line = LineGather(p, gains, G8, line_sems.at[0])
    qkv_line = LineGather(p, None, WQ, line_sems.at[1])
    out_line = LineGather(p, w_out.at[:, rows_at(p.c, cw)], WO, line_sems.at[2])
    gate_line = LineGather(p, GO, wgate, line_sems.at[3])
    up_line = LineGather(p, UO, wup, line_sems.at[4])

    def row_block(ref):
        return (
            lambda c: ref.at[rows_at(c, rows)],
            lambda c, h: ref.at[pl.ds(pl.multiple_of(c * rows + h * half, half), half)],
        )

    tok_plane = PlaneGather(p, *row_block(X), plane_sems.at[0], own=tok)
    cot_plane = PlaneGather(p, *row_block(cot_all), plane_sems.at[1], own=cot)
    tab_rows = tab.shape[0]
    tab_plane = PlaneGather(
        p,
        lambda c: TAB.at[c],
        lambda c, h: TAB.at[c, pl.ds(h * (tab_rows // 2), tab_rows // 2)],
        plane_sems.at[2],
        own=tab,
    )

    def col_block(ref, b):
        def view(c):
            return ref.at[pl.ds(b * rows, rows), rows_at(c, cw)]

        def halves(c, h):
            return ref.at[pl.ds(b * rows + h * half, half), rows_at(c, cw)]

        return view, halves

    o_plane = [PlaneGather(p, *col_block(O, b), plane_sems.at[3 + b]) for b in range(n_ctx)]
    m_plane = [PlaneGather(p, *col_block(M, b), plane_sems.at[7 + b]) for b in range(n_ctx)]

    gain_line.start()
    tab_plane.start()
    tok_plane.start()
    out_line.start()
    for i in range(3):
        loads[i].wait()
    for c in range(n_ctx):

        @pl.when(p.c == c)
        def _():
            WQ[mine, qw : qw + HEAD_DIM] = WK[:, HEAD_DIM * c : HEAD_DIM * (c + 1)]
            WQ[mine, qw + HEAD_DIM :] = WV[:, HEAD_DIM * c : HEAD_DIM * (c + 1)]

    qkv_line.start()
    own_tok = pltpu.make_async_copy(tok, X.at[rows_at(p.c, rows)], copy_sems.at[0])
    own_tab = pltpu.make_async_copy(tab, TAB.at[p.c], copy_sems.at[1])
    own_cot = pltpu.make_async_copy(cot, cot_all.at[rows_at(p.c, rows)], copy_sems.at[2])
    own_tok.start()
    own_tab.start()
    own_cot.start()

    for i in range(3, 6):
        loads[i].wait()
    unit = GO.shape[1] // (2 * p.depth)
    for c in range(n_ctx):

        @pl.when(p.c == c)
        def _():
            for f in range(2 * p.depth):
                at = (f * n_ctx + c) * unit
                for src, dst in ((GF, GO), (UF, UO)):
                    part = src[:, at : at + unit].astype(f32) * GCOL[:, 0:1]
                    dst[:, f * unit : (f + 1) * unit] = part.astype(bf16)

    gain_line.hop(1)
    tab_plane.middle()
    gain_line.hop(2)
    qkv_line.hop(1)
    gain_line.hop(3)
    gain_line.finish()
    for f in range(2 * p.depth):
        GROW[:, f * gains.shape[1] : (f + 1) * gains.shape[1]] = G8[16 * f : 16 * f + 8, :].astype(f32)

    def norm(c):
        at = rows_at(c, rows)
        x = X[at, :].astype(f32)
        r = lax.rsqrt(jnp.mean(x * x, axis=-1, keepdims=True) + eps_norm)
        R1[at, :] = jnp.broadcast_to(r, (rows, 128))
        XN[at, :] = (x * r * GROW[0:1, :]).astype(bf16)

    own_tok.wait()
    norm(p.c)
    out_line.hop(1)
    qkv_line.hop(2)
    tok_plane.middle()
    out_line.hop(2)
    gate_line.start()
    norm(p.cx)
    norm(p.cy)
    qkv_line.hop(3)
    tok_plane.finish()
    cot_plane.start()
    out_line.hop(3)
    up_line.start()
    norm(p.cd)
    xn_copy = pltpu.make_async_copy(XN, xn_out, copy_sems.at[3])
    r_copy = pltpu.make_async_copy(R1, r_out, copy_sems.at[4])
    grow_copy = pltpu.make_async_copy(GROW, grow_out, copy_sems.at[14])
    xn_copy.start()
    r_copy.start()
    grow_copy.start()
    own_tab.wait()
    tab_plane.finish()
    qkv_line.finish()

    @pl.loop(0, n_ctx)
    def _(b):
        at = rows_at(b, rows)
        pre = dot(XN[at, :], WQ[...]).T
        cosine = TAB[b, 0:32, :]
        sine = TAB[b, 32:64, :]
        for h in range(heads + 1):
            u = pre[64 * h : 64 * h + 32]
            w = pre[64 * h + 32 : 64 * h + 64]
            first = u * cosine - w * sine
            second = w * cosine + u * sine
            if h < heads:
                QT[64 * h : 64 * h + 32, at] = first.astype(bf16)
                QT[64 * h + 32 : 64 * h + 64, at] = second.astype(bf16)
            else:
                KT[0:32, at] = first.astype(bf16)
                KT[32:64, at] = second.astype(bf16)
                K[at, :] = jnp.concatenate([first, second], axis=0).T.astype(bf16)
        VT[:, at] = pre[qw + 64 :].astype(bf16)

    wq_copy = pltpu.make_async_copy(WQ, wqkv_out, copy_sems.at[5])
    wq_copy.start()
    gate_line.hop(1)

    def attend(b):
        n = (b + 1) * rows
        key = lax.broadcasted_iota(jnp.int32, (n, rows), 0)
        query = lax.broadcasted_iota(jnp.int32, (n, rows), 1) + b * rows
        begin = TAB[b, 64:65, :].astype(jnp.int32)
        BIAS[0:n, :] = jnp.where((key <= query) & (key >= begin), 0.0, neg_large)
        cols = slice(b * rows, (b + 1) * rows)

        @pl.loop(0, heads)
        def _(h):
            head = rows_at(h, HEAD_DIM)
            s = dot(K[0:n, :], QT[head, cols]) * scale + BIAS[0:n, :]
            top = jnp.max(s, axis=0, keepdims=True)
            e = jnp.exp(s - top)
            total = jnp.sum(e, axis=0, keepdims=True)
            probs = (e * (1.0 / total)).astype(bf16)
            OT[head, :] = dot(VT[:, 0:n], probs)
            LSE[rows_at(h, 8), cols] = jnp.broadcast_to(top + jnp.log(total), (8, rows))

        O[pl.ds(b * rows, rows), rows_at(p.c, cw)] = OT[...].T.astype(bf16)
        o_plane[b].start()

    def middle(b):
        at = pl.ds(b * rows, rows)
        cols = rows_at(p.c, cw)
        mid = X[at, cols].astype(f32) + dot(O[at, :], WO[...])
        M[at, cols] = mid.astype(bf16)
        m_plane[b].start()

    attend(0)
    attend(1)
    o_plane[0].middle()
    attend(2)
    o_plane[1].middle()
    attend(3)
    o_plane[2].middle()
    cot_plane.middle()
    out_line.finish()
    o_plane[0].finish()
    middle(0)
    o_plane[3].middle()
    up_line.hop(1)
    o_plane[1].finish()
    middle(1)
    m_plane[0].middle()
    o_plane[2].finish()
    middle(2)
    m_plane[1].middle()
    gate_line.hop(2)
    o_plane[3].finish()
    middle(3)
    m_plane[2].middle()
    up_line.hop(2)
    m_plane[3].middle()
    copies = [xn_copy, r_copy, grow_copy, wq_copy]
    for i, (src, dst) in enumerate(
        ((QT, qt_out), (KT, kt_out), (VT, vt_out), (LSE, lse_out), (O, o_out), (WO, wout_out), (TAB, tab_out))
    ):
        copy = pltpu.make_async_copy(src, dst, copy_sems.at[6 + i])
        copy.start()
        copies.append(copy)
    for b in range(n_ctx):
        m_plane[b].finish()
    m_copy = pltpu.make_async_copy(M, m_out, copy_sems.at[13])
    m_copy.start()
    copies.append(m_copy)
    gate_line.hop(3)
    up_line.hop(3)
    cot_plane.finish()
    gate_line.finish()
    up_line.finish()
    own_cot.wait()
    for copy in copies:
        copy.wait()
    for line in (gain_line, qkv_line, out_line, gate_line, up_line):
        line.drain()
    for plane in [tok_plane, cot_plane, tab_plane] + o_plane + m_plane:
        plane.drain()


def forward_stage(tok, tab, gains, gcol, w_query, w_key, w_value, w_out, w_gate, w_up, cot):
    n_fsdp, n_ctx = lax.axis_size("fsdp"), lax.axis_size("ctx")
    rows, width = tok.shape
    seq = rows * n_ctx
    own = w_query.shape[0]
    whole = n_fsdp * own
    qw = HEADS // n_ctx * HEAD_DIM
    nq, nw, nu = qw + 2 * HEAD_DIM, width // n_ctx, w_gate.shape[1] // n_ctx
    heads = qw // HEAD_DIM
    tab_shape = (n_ctx,) + tab.shape
    outs = [
        ((seq, width), bf16), ((seq, 128), f32), ((8, width), f32), ((qw, seq), bf16), ((64, seq), bf16),
        ((64, seq), bf16), ((8 * heads, seq), f32), ((seq, width), bf16), ((seq, width), bf16), ((whole, nq), bf16),
        ((whole, nw), bf16), ((whole, nu), bf16), ((whole, nu), bf16), ((seq, width), bf16), (tab_shape, f32),
    ]
    scratch = [
        pltpu.VMEM((seq, width), bf16),
        pltpu.VMEM((seq, width), bf16),
        pltpu.VMEM((qw, seq), bf16),
        pltpu.VMEM((64, seq), bf16),
        pltpu.VMEM((64, seq), bf16),
        pltpu.VMEM((seq, 64), bf16),
        pltpu.VMEM((8 * heads, seq), f32),
        pltpu.VMEM((seq, width), bf16),
        pltpu.VMEM((seq, width), bf16),
        pltpu.VMEM((whole, nq), bf16),
        pltpu.VMEM((whole, nw), bf16),
        pltpu.VMEM(tab_shape, f32),
        pltpu.VMEM((16 * n_fsdp, gains.shape[1]), bf16),
        pltpu.VMEM((8, width), f32),
        pltpu.VMEM((seq, rows), f32),
        pltpu.VMEM((qw, rows), f32),
        pltpu.VMEM((seq, 128), f32),
        pltpu.VMEM(w_key.shape, bf16),
        pltpu.VMEM(w_value.shape, bf16),
        pltpu.VMEM(w_gate.shape, bf16),
        pltpu.VMEM(w_up.shape, bf16),
        pltpu.VMEM((own, nu), bf16),
        pltpu.VMEM((own, nu), bf16),
        pltpu.VMEM(gcol.shape, f32),
        pltpu.SemaphoreType.DMA((5, LineGather.SEMS)),
        pltpu.SemaphoreType.DMA((11, PlaneGather.SEMS)),
        pltpu.SemaphoreType.DMA((21,)),
    ]
    ins = (tok, tab, gains, gcol, w_query, w_key, w_value, w_out, w_gate, w_up, cot)
    flops = 2 * seq * width * (nq + nw) + 8 * heads * seq * seq * HEAD_DIM
    return call(forward_kernel, ins, outs, scratch, 1, flops, "forward_stage")


def tiles_of(total, most):
    sizes, at = [], 0
    while at < total:
        sizes.append((at, min(most, total - at)))
        at += most
    return sizes


def middle_kernel(
    m_in, cot_in, wgate_in, wup_in, w_down,
    y_out, down_part, gate_part, up_part, gm_out,
    M, COT, WG, WU, WD, GATE, UP, HID, R2, PD, PH, D1, D2, H1, H2, GM, Y, STAGE_D, STAGE,
    line_sems, plane_sems, copy_sems, stage_sems,
):
    p = Place()
    n_ctx = 4
    seq, width = M.shape
    rows = seq // n_ctx
    half = rows // 2
    cw = width // n_ctx
    units = GATE.shape[1]
    loads = []
    for i, (src, dst) in enumerate(((m_in, M), (wgate_in, WG), (wup_in, WU), (cot_in, COT))):
        loads.append(pltpu.make_async_copy(src, dst, copy_sems.at[i]))
        loads[-1].start()

    p.barrier()
    unit = w_down.shape[0] // n_ctx
    down_own = w_down.at[pl.ds(pl.multiple_of(p.c * unit, 16), unit)]
    down_line = LineGather(p, down_own, WD, line_sems.at[0])
    down_line.start()

    loads[0].wait()
    loads[1].wait()
    loads[2].wait()

    @pl.loop(0, n_ctx)
    def _(b):
        at = rows_at(b, rows)
        mf = M[at, :].astype(f32)
        r = lax.rsqrt(jnp.mean(mf * mf, axis=-1, keepdims=True) + eps_norm)
        gate = dot(M[at, :], WG[...]) * r
        up = dot(M[at, :], WU[...]) * r
        R2[at, :] = jnp.broadcast_to(r, (rows, 128))
        GATE[at, :] = gate.astype(bf16)
        UP[at, :] = up.astype(bf16)
        HID[at, :] = (gate * (1.0 / (1.0 + jnp.exp(-gate))) * up).astype(bf16)

    down_line.hop(1)
    loads[3].wait()
    stage_copies = {}
    for i, (at, size) in enumerate(tiles_of(units, STAGE_D.shape[1])):
        slot = i % 2
        if i >= 2:
            stage_copies[i - 2].wait()
        STAGE_D[slot, 0:size, :] = dot_tn(HID[:, at : at + size], COT[...]).astype(bf16)
        copy = pltpu.make_async_copy(
            STAGE_D.at[slot, pl.ds(0, size)], down_part.at[pl.ds(at, size)], stage_sems.at[slot]
        )
        copy.start()
        stage_copies[i] = copy
    n_down = len(stage_copies)
    down_line.hop(2)
    stage_copies[n_down - 2].wait()
    stage_copies[n_down - 1].wait()
    down_line.hop(3)
    down_line.finish()

    y_plane = PlaneScatter(
        p,
        lambda c: PD.at[rows_at(c, rows)],
        lambda c, h: PD.at[pl.ds(pl.multiple_of(c * rows + h * half, half), half)],
        D1,
        D2,
        plane_sems.at[0],
    )

    def col_scatter(b):
        return PlaneScatter(
            p,
            lambda c: PH.at[pl.ds(b * rows, rows), rows_at(c, cw)],
            lambda c, h: PH.at[pl.ds(b * rows + h * half, half), rows_at(c, cw)],
            H1.at[b],
            H2.at[b],
            plane_sems.at[1 + b],
        )

    h_plane = [col_scatter(b) for b in range(n_ctx)]

    def partial_out(c):
        at = rows_at(c, rows)
        PD[at, :] = dot(HID[at, :], WD[...]).astype(bf16)

    partial_out(p.cd)
    y_plane.start()
    partial_out(p.cx)
    partial_out(p.cy)
    y_plane.middle()
    partial_out(p.c)

    def back(b):
        at = pl.ds(b * rows, rows)
        r = R2[at, 0:1]
        grad_hidden = dot_nt(COT[at, :], WD[...])
        gate = GATE[at, :].astype(f32)
        up = UP[at, :].astype(f32)
        sig = 1.0 / (1.0 + jnp.exp(-gate))
        d_up = grad_hidden * gate * sig
        d_gate = grad_hidden * up * sig * (1.0 + gate * (1.0 - sig))
        stat = jnp.sum(d_gate * gate + d_up * up, axis=-1, keepdims=True)
        GATE[at, :] = (d_gate * r).astype(bf16)
        UP[at, :] = (d_up * r).astype(bf16)
        coef = r * r * stat * (1.0 / width)
        for j in range(0, width, cw):
            e = dot_nt(GATE[at, :], WG[j : j + cw, :]) + dot_nt(UP[at, :], WU[j : j + cw, :])
            PH[at, j : j + cw] = (e - M[at, j : j + cw].astype(f32) * coef).astype(bf16)
        h_plane[b].start()

    back(0)
    back(1)
    h_plane[0].middle()
    back(2)
    h_plane[1].middle()
    back(3)
    h_plane[2].middle()

    stage_copies = {}
    jobs = []
    for src, dst in ((GATE, gate_part), (UP, up_part)):
        for at, size in tiles_of(width, STAGE.shape[1]):
            jobs.append((src, dst, at, size))

    def weight_tile(i):
        src, dst, at, size = jobs[i]
        slot = i % 2
        if i >= 2:
            stage_copies[i - 2].wait()
        STAGE[slot] = dot_tn(M[:, at : at + size], src[...]).astype(bf16)
        copy = pltpu.make_async_copy(STAGE.at[slot], dst.at[pl.ds(at, size)], stage_sems.at[2 + slot])
        copy.start()
        stage_copies[i] = copy

    def finish_block(b):
        at = pl.ds(b * rows, rows)
        GM[at, :] = (COT[at, rows_at(p.c, cw)].astype(f32) + h_plane[b].finish()).astype(bf16)

    weight_tile(0)
    weight_tile(1)
    h_plane[3].middle()
    weight_tile(2)
    finish_block(0)
    weight_tile(3)
    finish_block(1)
    weight_tile(4)
    weight_tile(5)
    finish_block(2)
    weight_tile(6)
    weight_tile(7)
    Y[...] = (M[rows_at(p.c, rows), :].astype(f32) + y_plane.finish()).astype(bf16)
    y_copy = pltpu.make_async_copy(Y, y_out, copy_sems.at[4])
    y_copy.start()
    finish_block(3)
    gm_copy = pltpu.make_async_copy(GM, gm_out, copy_sems.at[5])
    gm_copy.start()
    stage_copies[6].wait()
    stage_copies[7].wait()
    y_copy.wait()
    gm_copy.wait()
    down_line.drain()
    y_plane.drain()
    for b in range(n_ctx):
        h_plane[b].drain()


def middle_stage(m, cot_all, wgate, wup, w_down):
    n_fsdp, n_ctx = lax.axis_size("fsdp"), lax.axis_size("ctx")
    seq, width = m.shape
    rows = seq // n_ctx
    cw = width // n_ctx
    units = wgate.shape[1]
    outs = [
        ((rows, width), bf16), ((units, width), bf16), ((width, units), bf16), ((width, units), bf16),
        ((seq, cw), bf16),
    ]
    scratch = [
        pltpu.VMEM((seq, width), bf16),
        pltpu.VMEM((seq, width), bf16),
        pltpu.VMEM((width, units), bf16),
        pltpu.VMEM((width, units), bf16),
        pltpu.VMEM((units, width), bf16),
        pltpu.VMEM((seq, units), bf16),
        pltpu.VMEM((seq, units), bf16),
        pltpu.VMEM((seq, units), bf16),
        pltpu.VMEM((seq, 128), f32),
        pltpu.VMEM((seq, width), bf16),
        pltpu.VMEM((seq, width), bf16),
        pltpu.VMEM((2, rows // 2, width), bf16),
        pltpu.VMEM((2, rows, width), bf16),
        pltpu.VMEM((n_ctx, 2, rows // 2, cw), bf16),
        pltpu.VMEM((n_ctx, 2, rows, cw), bf16),
        pltpu.VMEM((seq, cw), bf16),
        pltpu.VMEM((rows, width), bf16),
        pltpu.VMEM((2, 256, width), bf16),
        pltpu.VMEM((2, 512, units), bf16),
        pltpu.SemaphoreType.DMA((1, LineGather.SEMS)),
        pltpu.SemaphoreType.DMA((5, PlaneScatter.SEMS)),
        pltpu.SemaphoreType.DMA((6,)),
        pltpu.SemaphoreType.DMA((4,)),
    ]
    flops = 18 * seq * width * units
    return call(middle_kernel, (m, cot_all, wgate, wup, w_down), outs, scratch, 2, flops, "middle_stage")


def backward_kernel(
    xn_in, r_in, grow_in, qt_in, kt_in, vt_in, lse_in, o_in, gm_in, wqkv_in, wout_in, tab_in,
    gate_part, up_part, down_part,
    tok_out, qkv_all, out_all, gate_all, up_all, down_all,
    XN, R1, GROW, QT, KT, VT, LSE, O, GM, WQ, WO, TAB,
    K, V, DK, DV, DOT, DQT, DPRE, STAT, BIAS, PT, G1, G2, T1, T2, TOK,
    DACC, DSLOT, GACC, GSLOT, UACC, USLOT, OACC, OSLOT, QACC, QSLOT,
    line_sems, plane_sems, scatter_sems, copy_sems,
):
    p = Place()
    n_ctx = 4
    seq, width = XN.shape
    rows = seq // n_ctx
    half = rows // 2
    cw = width // n_ctx
    qw = QT.shape[0]
    heads = qw // HEAD_DIM
    nq = WQ.shape[1]
    own_rows = QACC.shape[1]
    scale = HEAD_DIM ** (-0.5)
    loads = []
    for i, (src, dst) in enumerate(
        (
            (gm_in, GM), (wout_in, WO), (o_in, O), (kt_in, KT), (vt_in, VT), (qt_in, QT), (lse_in, LSE),
            (tab_in, TAB), (xn_in, XN), (wqkv_in, WQ), (r_in, R1), (grow_in, GROW),
        )
    ):
        loads.append(pltpu.make_async_copy(src, dst, copy_sems.at[i]))
        if dst is not XN:
            loads[-1].start()

    p.barrier()

    def block_rows(ref):
        count = ref.shape[0] // (2 * p.depth)
        return lambda level, core: ref.at[pl.ds(pl.multiple_of((2 * level + core) * count, 16), count)]

    unit, nu = DACC.shape[1], GACC.shape[2]
    rows_stage = [XN.at[pl.ds(i * unit, unit)] for i in range(2)]
    cols_stage = [XN.at[pl.ds(i * own_rows, own_rows), pl.ds(0, nu)] for i in range(2)]
    down_line = LineScatter(p, block_rows(down_part), DACC, DSLOT, line_sems.at[0], rows_stage)
    gate_line = LineScatter(p, block_rows(gate_part), GACC, GSLOT, line_sems.at[1], cols_stage)
    up_line = LineScatter(p, block_rows(up_part), UACC, USLOT, line_sems.at[2], cols_stage)
    out_line = LineScatter(p, block_rows(WO), OACC, OSLOT, line_sems.at[3])

    def qkv_block(level, core):
        f = 2 * level + core
        at = pl.ds(pl.multiple_of((f % p.depth) * own_rows, own_rows), own_rows)
        return O.at[at, pl.ds(pl.multiple_of((f // p.depth) * nq, 128), nq)]

    qkv_line = LineScatter(p, qkv_block, QACC, QSLOT, line_sems.at[4])
    down_line.start()
    gate_line.start()
    up_line.start()

    def col_scatter(b):
        return PlaneScatter(
            p,
            lambda c: PT.at[pl.ds(b * rows, rows), rows_at(c, cw)],
            lambda c, h: PT.at[pl.ds(b * rows + h * half, half), rows_at(c, cw)],
            G1.at[b],
            G2.at[b],
            scatter_sems.at[b],
        )

    g_plane = [col_scatter(b) for b in range(n_ctx)]
    t_plane = PlaneScatter(
        p,
        lambda c: PT.at[rows_at(c, rows)],
        lambda c, h: PT.at[pl.ds(pl.multiple_of(c * rows + h * half, half), half)],
        T1,
        T2,
        scatter_sems.at[n_ctx],
    )

    def whole(ref, line, index, first):
        count = line.acc.shape[1]

        def halves(c, h):
            return ref(c).at[pl.ds(h * first, count - first if h else first)]

        plane = PlaneGather(p, ref, halves, plane_sems.at[index], own=line.result())
        own = pltpu.make_async_copy(line.result(), ref(p.c), plane_sems.at[index, PlaneGather.SEMS])
        return plane, own

    down_plane, down_own = whole(lambda c: down_all.at[c], down_line, 0, 96)
    gate_plane, gate_own = whole(lambda c: gate_all.at[c], gate_line, 1, half)
    up_plane, up_own = whole(lambda c: up_all.at[c], up_line, 2, half)
    out_plane, out_own = whole(lambda c: out_all.at[c], out_line, 3, half)
    qkv_plane, qkv_own = whole(lambda c: qkv_all.at[c], qkv_line, 4, half)

    loads[0].wait()
    loads[1].wait()
    for b in range(n_ctx):
        at = pl.ds(b * rows, rows)
        for j in range(0, width, 512):
            PT[at, j : j + 512] = dot_nt(GM[at, :], WO[j : j + 512, :]).astype(bf16)
        g_plane[b].start()
    down_line.combine()
    down_line.step(1)
    g_plane[0].middle()
    loads[2].wait()

    @pl.loop(0, width // 512)
    def _(i):
        at = rows_at(i, 512)
        WO[at, :] = dot_tn(O[:, at], GM[...]).astype(bf16)

    out_line.start()
    g_plane[1].middle()
    gate_line.combine()
    loads[8].start()
    gate_line.step(1)
    g_plane[2].middle()
    for i in (3, 4, 5, 6, 7, 10):
        loads[i].wait()

    @pl.loop(0, n_ctx)
    def _(b):
        at = rows_at(b, rows)
        K[at, :] = KT[:, at].astype(f32).T.astype(bf16)
        V[at, :] = VT[:, at].astype(f32).T.astype(bf16)
        DK[at, :] = jnp.zeros((rows, HEAD_DIM), f32)
        DV[at, :] = jnp.zeros((rows, HEAD_DIM), f32)

    g_plane[3].middle()

    def attend_back(b):
        n = (b + 1) * rows
        cols = slice(b * rows, (b + 1) * rows)
        DOT[...] = g_plane[b].finish().T.astype(bf16)
        at = pl.ds(b * rows, rows)
        DQT[...] = O[at, rows_at(p.c, cw)].astype(f32).T
        key = lax.broadcasted_iota(jnp.int32, (n, rows), 0)
        query = lax.broadcasted_iota(jnp.int32, (n, rows), 1) + b * rows
        begin = TAB[b, 64:65, :].astype(jnp.int32)
        BIAS[0:n, :] = jnp.where((key <= query) & (key >= begin), 0.0, neg_large)
        STAT[...] = jnp.zeros((8, rows), f32)

        @pl.loop(0, heads)
        def _(h):
            head = rows_at(h, HEAD_DIM)
            q = QT[head, cols]
            d_out = DOT[head, :]
            delta = jnp.sum(d_out.astype(f32) * DQT[head, :], axis=0, keepdims=True)
            s = dot(K[0:n, :], q) * scale + BIAS[0:n, :]
            probs = jnp.exp(s - LSE[rows_at(h, 8), cols][0:1])
            d_probs = dot(V[0:n, :], d_out)
            d_s = (probs * (d_probs - delta)).astype(bf16)
            d_q = dot(KT[:, 0:n], d_s) * scale
            DK[0:n, :] += dot_nt(d_s, q) * scale
            DV[0:n, :] += dot_nt(probs.astype(bf16), d_out)
            STAT[...] += jnp.broadcast_to(jnp.sum(d_q * q.astype(f32), axis=0, keepdims=True), (8, rows))
            u, w = d_q[0:32], d_q[32:64]
            cosine, sine = TAB[b, 0:32, :], TAB[b, 32:64, :]
            DQT[head, :] = jnp.concatenate([u * cosine + w * sine, w * cosine - u * sine], axis=0)

        DPRE[at, 0:qw] = DQT[...].T.astype(bf16)
        R1[at, 0:8] = STAT[...].T

    attend_back(0)
    down_line.step(2)
    attend_back(1)
    gate_line.step(2)
    attend_back(2)
    down_line.step(3)
    attend_back(3)
    gate_line.step(3)
    loads[8].wait()
    loads[9].wait()
    loads[11].wait()

    @pl.loop(0, n_ctx)
    def _(b):
        at = rows_at(b, rows)
        d_k = DK[at, :].T
        d_v = DV[at, :].T
        stat = jnp.sum(d_k * KT[:, at].astype(f32) + d_v * VT[:, at].astype(f32), axis=0, keepdims=True)
        R1[at, 0:8] += jnp.broadcast_to(stat, (8, rows)).T
        u, w = d_k[0:32], d_k[32:64]
        cosine, sine = TAB[b, 0:32, :], TAB[b, 32:64, :]
        both = jnp.concatenate([u * cosine + w * sine, w * cosine - u * sine, d_v], axis=0)
        DPRE[at, qw:] = both.T.astype(bf16)

    def tokens(c):
        at = rows_at(c, rows)
        r = R1[at, 127:128]
        coef = r * R1[at, 0:1] * (1.0 / width)
        for j in range(0, width, 512):
            cols = slice(j, j + 512)
            gain = GROW[0:1, cols]
            e = dot_nt(DPRE[at, :], WQ[cols, :])
            PT[at, cols] = (e * (gain * r) - XN[at, cols].astype(f32) * ((1.0 / gain) * coef)).astype(bf16)
        mine = rows_at(p.c, cw)
        PT[at, mine] = (PT[at, mine].astype(f32) + GM[at, :].astype(f32)).astype(bf16)

    for b in range(n_ctx):
        g_plane[b].drain()
    tokens(p.cd)
    t_plane.start()
    tokens(p.cx)
    tokens(p.cy)
    t_plane.middle()
    tokens(p.c)

    @pl.loop(0, p.depth)
    def _(i):
        for j in range(2):
            at = rows_at(i + j * p.depth, own_rows)
            O[rows_at(i, own_rows), j * nq : (j + 1) * nq] = dot_tn(XN[:, at], DPRE[...]).astype(bf16)

    qkv_line.start()
    down_line.step(4)
    down_plane.start()
    down_own.start()
    up_line.combine()
    up_line.step(1)
    out_line.combine()
    out_line.step(1)
    gate_line.step(4)
    gate_plane.start()
    gate_own.start()
    tok_copies = []
    for i in range(n_ctx):
        if i >= 2:
            tok_copies[i - 2].wait()
        at = pl.ds(i * (rows // n_ctx), rows // n_ctx)
        TOK[i % 2] = t_plane.finish(at, i == 0)
        tok_copies.append(pltpu.make_async_copy(TOK.at[i % 2], tok_out.at[at], copy_sems.at[12 + i % 2]))
        tok_copies[-1].start()
    down_plane.middle()
    up_line.step(2)
    out_line.step(2)
    gate_plane.middle()
    qkv_line.combine()
    qkv_line.step(1)
    up_line.step(3)
    out_line.step(3)
    qkv_line.step(2)
    up_line.step(4)
    up_plane.start()
    up_own.start()
    out_line.step(4)
    out_plane.start()
    out_own.start()
    qkv_line.step(3)
    up_plane.middle()
    out_plane.middle()
    qkv_line.step(4)
    qkv_plane.start()
    qkv_own.start()
    qkv_plane.middle()
    for plane, own in (
        (down_plane, down_own), (gate_plane, gate_own), (up_plane, up_own), (out_plane, out_own), (qkv_plane, qkv_own),
    ):
        plane.finish()
        own.wait()
        plane.drain()
    tok_copies[2].wait()
    tok_copies[3].wait()
    t_plane.drain()
    for line in (down_line, gate_line, up_line, out_line, qkv_line):
        line.drain()


def backward_stage(xn, r, grow, qt, kt, vt, lse, o, gm, wqkv, wout, tabs, gate_part, up_part, down_part):
    n_fsdp, n_ctx = lax.axis_size("fsdp"), lax.axis_size("ctx")
    seq, width = xn.shape
    rows = seq // n_ctx
    half = rows // 2
    cw = width // n_ctx
    own = width // n_fsdp
    depth = n_fsdp // 2
    nq, nu = wqkv.shape[1], gate_part.shape[1]
    unit = down_part.shape[0] // n_fsdp
    qw = qt.shape[0]
    outs = [
        ((rows, width), f32), ((n_ctx, own, nq), bf16), ((n_ctx, own, cw), bf16), ((n_ctx, own, nu), bf16),
        ((n_ctx, own, nu), bf16), ((n_ctx, unit, width), bf16),
    ]
    ins = (xn, r, grow, qt, kt, vt, lse, o, gm, wqkv, wout, tabs, gate_part, up_part, down_part)
    scratch = [pltpu.VMEM(a.shape, a.dtype) for a in ins[:12]] + [
        pltpu.VMEM((seq, HEAD_DIM), bf16),
        pltpu.VMEM((seq, HEAD_DIM), bf16),
        pltpu.VMEM((seq, HEAD_DIM), f32),
        pltpu.VMEM((seq, HEAD_DIM), f32),
        pltpu.VMEM((qw, rows), bf16),
        pltpu.VMEM((qw, rows), f32),
        pltpu.VMEM((seq, nq), bf16),
        pltpu.VMEM((8, rows), f32),
        pltpu.VMEM((seq, rows), f32),
        pltpu.VMEM((seq, width), bf16),
        pltpu.VMEM((n_ctx, 2, half, cw), bf16),
        pltpu.VMEM((n_ctx, 2, rows, cw), bf16),
        pltpu.VMEM((2, half, width), bf16),
        pltpu.VMEM((2, rows, width), bf16),
        pltpu.VMEM((2, rows // n_ctx, width), f32),
        pltpu.VMEM((depth, unit, width), bf16),
        pltpu.VMEM((5, unit, width), bf16),
        pltpu.VMEM((depth, own, nu), bf16),
        pltpu.VMEM((5, own, nu), bf16),
        pltpu.VMEM((depth, own, nu), bf16),
        pltpu.VMEM((5, own, nu), bf16),
        pltpu.VMEM((depth, own, cw), bf16),
        pltpu.VMEM((5, own, cw), bf16),
        pltpu.VMEM((depth, own, nq), bf16),
        pltpu.VMEM((5, own, nq), bf16),
        pltpu.SemaphoreType.DMA((5, LineScatter.SEMS)),
        pltpu.SemaphoreType.DMA((5, PlaneGather.SEMS + 1)),
        pltpu.SemaphoreType.DMA((n_ctx + 1, PlaneScatter.SEMS)),
        pltpu.SemaphoreType.DMA((14,)),
    ]
    flops = 4 * seq * width * (nq + cw) + 20 * qw * seq * seq
    return call(backward_kernel, ins, outs, scratch, 3, flops, "backward_stage")


def finish_kernel(
    unit, qkv, out, gate, up, down, tok, y, w_query, w_key, w_value, w_gate, w_up, g1, g2,
    o_query, o_key, o_value, o_out, o_gate, o_up, o_down, o_tok, o_y, o_g1, o_g2,
):
    n_ctx = qkv.shape[0]
    qw = o_query.shape[1] // n_ctx
    cw = out.shape[2]
    for c in range(n_ctx):
        o_query[:, c * qw : (c + 1) * qw] = qkv[c, :, 0:qw].astype(f32)
        o_key[:, c * HEAD_DIM : (c + 1) * HEAD_DIM] = qkv[c, :, qw : qw + HEAD_DIM].astype(f32)
        o_value[:, c * HEAD_DIM : (c + 1) * HEAD_DIM] = qkv[c, :, qw + HEAD_DIM :].astype(f32)
        o_out[:, c * cw : (c + 1) * cw] = out[c].astype(f32)

    def total(ref, w):
        return jnp.sum(ref[...] * w[...].astype(f32), axis=-1, keepdims=True)

    first = total(o_query, w_query) + total(o_key, w_key) + total(o_value, w_value)
    o_g1[...] = jnp.broadcast_to(first / g1[:, 0:1], o_g1.shape)
    gain = g2[:, 0:1]
    for src, dst in ((gate, o_gate), (up, o_up)):
        for f in range(src.shape[2] // unit):
            for c in range(n_ctx):
                at = (f * n_ctx + c) * unit
                dst[:, at : at + unit] = src[c, :, f * unit : (f + 1) * unit].astype(f32) * gain
    second = total(o_gate, w_gate) + total(o_up, w_up)
    o_g2[...] = jnp.broadcast_to(second / gain, o_g2.shape)
    o_down[...] = down[...].astype(f32)
    o_tok[...] = tok[...]
    o_y[...] = y[...]


def finish_stage(qkv, out, gate, up, down, tok, y, w_query, w_key, w_value, w_gate, w_up, g1, g2):
    steps = 4
    n_fsdp = lax.axis_size("fsdp")
    own = w_query.shape[0]
    down = down.reshape(-1, down.shape[-1])
    unit = gate.shape[2] // n_fsdp

    def spec(shape):
        if len(shape) == 3:
            return pl.BlockSpec((shape[0], shape[1] // steps, shape[2]), lambda i: (0, i, 0))
        return pl.BlockSpec((shape[0] // steps, shape[1]), lambda i: (i, 0))

    ins = (qkv, out, gate, up, down, tok, y, w_query, w_key, w_value, w_gate, w_up, g1, g2)
    outs = [
        (w_query.shape, f32), (w_key.shape, f32), (w_value.shape, f32), ((own, out.shape[0] * out.shape[2]), f32),
        (w_gate.shape, f32), (w_up.shape, f32), (down.shape, f32), (tok.shape, f32), (y.shape, bf16),
        ((own, 128), f32), ((own, 128), f32),
    ]
    return pl.pallas_call(
        functools.partial(finish_kernel, unit),
        grid=(steps,),
        out_shape=[jax.ShapeDtypeStruct(s, d) for s, d in outs],
        in_specs=[spec(a.shape) for a in ins],
        out_specs=[spec(s) for s, d in outs],
        compiler_params=pltpu.CompilerParams(vmem_limit_bytes=56 * 2**20),
        name="finish_stage",
    )(*ins)


def rotate(field, cosine, sine_table, direction):
    half_width = field.shape[-1] // 2
    first_half = field[..., :half_width]
    second_half = field[..., half_width:]
    return jnp.concatenate(
        [
            first_half * cosine - direction * second_half * sine_table,
            second_half * cosine + direction * first_half * sine_table,
        ],
        axis=-1,
    )


def gather(x, axis_name, axis=0):
    return lax.all_gather(x, axis_name, axis=axis, tiled=True)


def scatter(x, axis_name, axis=0):
    return lax.psum_scatter(x.astype(bf16), axis_name, scatter_dimension=axis, tiled=True)


def columns(w, start, count):
    return lax.dynamic_slice_in_dim(w, start, count, axis=1)


def visible(begin):
    seq = begin.shape[0]
    index = jnp.arange(seq, dtype=jnp.int32)
    return (index[None, :] <= index[:, None]) & (index[None, :] >= begin[:, None])


def forward_plain(tok, tab, gains, gcol, w_query, w_key, w_value, w_out, w_gate, w_up, cot):
    n_ctx, n_fsdp = lax.axis_size("ctx"), lax.axis_size("fsdp")
    c = lax.axis_index("ctx")
    own_rows = w_query.shape[0]
    qw = HEADS // n_ctx * HEAD_DIM
    copies = max(1, n_ctx // KV_HEADS)
    kvw = max(1, KV_HEADS // n_ctx) * HEAD_DIM
    unit = w_gate.shape[1] // (n_fsdp * n_ctx)
    cw = tok.shape[1] // n_ctx
    wqkv_o = jnp.concatenate(
        [
            columns(w_query, c * qw, qw),
            columns(w_key, (c // copies) * kvw, kvw),
            columns(w_value, (c // copies) * kvw, kvw),
        ],
        axis=1,
    )
    wout_o = columns(w_out, c * cw, cw)

    def units(w):
        parts = w.reshape(own_rows, n_fsdp, n_ctx, unit)
        mine = lax.dynamic_index_in_dim(parts, c, axis=2, keepdims=False)
        return (gcol[:, 0:1] * mine.reshape(own_rows, n_fsdp * unit)).astype(bf16)

    wgate_o, wup_o = units(w_gate), units(w_up)
    x = gather(tok, "ctx")
    tabs = gather(tab[None], "ctx")
    wqkv = gather(wqkv_o, "fsdp")
    wout = gather(wout_o, "fsdp")
    wgate = gather(wgate_o, "fsdp")
    wup = gather(wup_o, "fsdp")
    cot_all = gather(cot, "ctx")
    gain = gather(gains[0:1], "fsdp", axis=1).astype(f32)
    xf = x.astype(f32)
    r = lax.rsqrt(jnp.mean(xf * xf, axis=-1, keepdims=True) + eps_norm)
    xn = (xf * r * gain).astype(bf16)
    seq, width = x.shape
    heads = HEADS // n_ctx
    qw = heads * HEAD_DIM
    pre = dot(xn, wqkv)
    cosine = tabs[:, 0:32].transpose(0, 2, 1).reshape(seq, 1, 32)
    sine = tabs[:, 32:64].transpose(0, 2, 1).reshape(seq, 1, 32)
    begin = tabs[:, 64].reshape(seq).astype(jnp.int32)
    kvw = (wqkv.shape[1] - qw) // 2
    kv = kvw // HEAD_DIM
    q = rotate(pre[:, :qw].reshape(seq, heads, HEAD_DIM), cosine, sine, 1.0).astype(bf16)
    k = rotate(pre[:, qw : qw + kvw].reshape(seq, kv, HEAD_DIM), cosine, sine, 1.0).astype(bf16)
    v = pre[:, qw + kvw :].astype(bf16).reshape(seq, kv, HEAD_DIM)
    qg = q.reshape(seq, kv, heads // kv, HEAD_DIM)
    scores = jnp.einsum("qkgd,lkd->kgql", qg, k, preferred_element_type=f32) * HEAD_DIM ** (-0.5)
    scores = jnp.where(visible(begin)[None, None], scores, neg_large)
    top = jnp.max(scores, axis=-1, keepdims=True)
    weights = jnp.exp(scores - top)
    total = jnp.sum(weights, axis=-1, keepdims=True)
    probs_low = (weights / total).astype(bf16)
    att = jnp.einsum("kgql,lkd->qkgd", probs_low, v, preferred_element_type=f32)
    o = gather(att.astype(bf16).reshape(seq, qw), "ctx", axis=1)
    lse = (top + jnp.log(total)).reshape(heads, 1, seq)
    lse = jnp.broadcast_to(lse, (heads, 8, seq)).reshape(8 * heads, seq)
    cw = width // n_ctx
    mid = columns(x, c * cw, cw).astype(f32) + dot(o, wout)
    m = gather(mid.astype(bf16), "ctx", axis=1)
    qt = q.reshape(seq, qw).T
    kt = k.reshape(seq, kvw).T
    vt = v.reshape(seq, kvw).T
    r = jnp.broadcast_to(r, (seq, 128))
    grow = jnp.broadcast_to(gain, (8, width))
    return xn, r, grow, qt, kt, vt, lse, o, m, wqkv, wout, wgate, wup, cot_all, tabs


def middle_plain(m, cot_all, wgate, wup, w_down):
    n_ctx = lax.axis_size("ctx")
    c = lax.axis_index("ctx")
    unit = w_down.shape[0] // n_ctx
    wdown_o = lax.dynamic_slice_in_dim(w_down, c * unit, unit, axis=0)
    seq, width = m.shape
    rows = seq // n_ctx
    cw = width // n_ctx
    wdown = gather(wdown_o, "fsdp")
    mf = m.astype(f32)
    r = lax.rsqrt(jnp.mean(mf * mf, axis=-1, keepdims=True) + eps_norm)
    gate = dot(m, wgate) * r
    up = dot(m, wup) * r
    sig = jax.nn.sigmoid(gate)
    hidden = (gate * sig * up).astype(bf16)
    mlp = scatter(dot(hidden, wdown), "ctx").astype(f32)
    mid_rows = lax.dynamic_slice_in_dim(m, c * rows, rows, axis=0).astype(f32)
    output = (mid_rows + mlp).astype(bf16)
    grad_hidden = dot_nt(cot_all, wdown)
    down_raw = dot_tn(hidden, cot_all).astype(bf16)
    d_gate = grad_hidden * up * sig * (1.0 + gate * (1.0 - sig))
    d_up = grad_hidden * gate * sig
    stat = jnp.sum(d_gate * gate + d_up * up, axis=-1, keepdims=True)
    d_gate = (d_gate * r).astype(bf16)
    d_up = (d_up * r).astype(bf16)
    gate_raw = dot_tn(m, d_gate).astype(bf16)
    up_raw = dot_tn(m, d_up).astype(bf16)
    back = dot_nt(d_gate, wgate) + dot_nt(d_up, wup) - mf * (r * r * stat * (1.0 / width))
    back_own = scatter(back, "ctx", axis=1).astype(f32)
    gm = (columns(cot_all, c * cw, cw).astype(f32) + back_own).astype(bf16)
    return output, down_raw, gate_raw, up_raw, gm


def backward_plain(xn, r, grow, qt, kt, vt, lse, o, gm, wqkv, wout, tabs, gate_raw, up_raw, down_raw):
    n_ctx = lax.axis_size("ctx")
    c = lax.axis_index("ctx")
    seq, width = xn.shape
    r, gain = r[:, 0:1], grow[0:1]
    heads = HEADS // n_ctx
    qw = heads * HEAD_DIM
    kvw = kt.shape[0]
    kv = kvw // HEAD_DIM
    cw = width // n_ctx
    scale = HEAD_DIM ** (-0.5)
    cosine = tabs[:, 0:32].transpose(0, 2, 1).reshape(seq, 1, 32)
    sine = tabs[:, 32:64].transpose(0, 2, 1).reshape(seq, 1, 32)
    begin = tabs[:, 64].reshape(seq).astype(jnp.int32)
    gate_grad = scatter(gate_raw, "fsdp")
    up_grad = scatter(up_raw, "fsdp")
    down_grad = scatter(down_raw, "fsdp")
    out_grad = scatter(dot_tn(o, gm), "fsdp")
    d_att = scatter(dot_nt(gm, wout), "ctx", axis=1).reshape(seq, kv, heads // kv, HEAD_DIM)
    q = qt.T.reshape(seq, kv, heads // kv, HEAD_DIM)
    k = kt.T.reshape(seq, kv, HEAD_DIM)
    v = vt.T.reshape(seq, kv, HEAD_DIM)
    scores = jnp.einsum("qkgd,lkd->kgql", q, k, preferred_element_type=f32) * scale
    scores = jnp.where(visible(begin)[None, None], scores, neg_large)
    lse = lse.reshape(kv, heads // kv, 8, seq)[:, :, 0, :, None]
    probs = jnp.exp(scores - lse)
    d_probs = jnp.einsum("qkgd,lkd->kgql", d_att, v, preferred_element_type=f32)
    delta = jnp.sum(probs * d_probs, axis=-1, keepdims=True)
    d_scores = (probs * (d_probs - delta)).astype(bf16)
    d_q = jnp.einsum("kgql,lkd->qkgd", d_scores, k, preferred_element_type=f32) * scale
    d_k = jnp.einsum("kgql,qkgd->lkd", d_scores, q, preferred_element_type=f32) * scale
    d_v = jnp.einsum("kgql,qkgd->lkd", probs.astype(bf16), d_att, preferred_element_type=f32)
    stat = (
        jnp.sum(d_q * q, axis=(1, 2, 3)) + jnp.sum(d_k * k, axis=(1, 2)) + jnp.sum(d_v * v, axis=(1, 2))
    )[:, None]
    d_q = rotate(d_q.reshape(seq, heads, HEAD_DIM), cosine, sine, -1.0).reshape(seq, qw)
    d_k = rotate(d_k, cosine, sine, -1.0).reshape(seq, kvw)
    d_pre = jnp.concatenate([d_q, d_k, d_v.reshape(seq, kvw)], axis=1).astype(bf16)
    qkv_grad = scatter(dot_tn(xn, d_pre), "fsdp")
    back = dot_nt(d_pre, wqkv) * (gain * r)
    back = back - xn.astype(f32) * ((1.0 / gain) * (r * stat * (1.0 / width)))
    at = (jnp.arange(width, dtype=jnp.int32) // cw == c)[None, :]
    back = back + jnp.where(at, jnp.tile(gm.astype(f32), (1, n_ctx)), 0.0)
    grad_tokens = scatter(back, "ctx").astype(f32)
    qkv_all = gather(qkv_grad[None], "ctx")
    out_all = gather(out_grad[None], "ctx")
    gate_all = gather(gate_grad[None], "ctx")
    up_all = gather(up_grad[None], "ctx")
    down_all = gather(down_grad[None], "ctx")
    return grad_tokens, qkv_all, out_all, gate_all, up_all, down_all


def finish_plain(qkv_all, out_all, gate_all, up_all, down_all, tok, y, w_query, w_key, w_value, w_gate, w_up, g1, g2):
    n_ctx, n_fsdp = lax.axis_size("ctx"), lax.axis_size("fsdp")
    own_rows = w_query.shape[0]
    qw = HEADS // n_ctx * HEAD_DIM
    copies = max(1, n_ctx // KV_HEADS)
    kvw = max(1, KV_HEADS // n_ctx) * HEAD_DIM
    ff_width = w_gate.shape[1]
    unit = ff_width // (n_fsdp * n_ctx)
    qkv_all = qkv_all.astype(f32)

    def joined(part):
        return jnp.moveaxis(part, 0, 1).reshape(own_rows, -1)

    def kv_part(part):
        return joined(part.reshape(n_ctx // copies, copies, own_rows, kvw).sum(axis=1))

    grad_query = joined(qkv_all[:, :, :qw])
    grad_key = kv_part(qkv_all[:, :, qw : qw + kvw])
    grad_value = kv_part(qkv_all[:, :, qw + kvw :])
    grad_out = joined(out_all.astype(f32))

    def spread(full):
        full = full.reshape(n_ctx, own_rows, n_fsdp, unit)
        return full.transpose(1, 2, 0, 3).reshape(own_rows, ff_width).astype(f32)

    raw_gate, raw_up = spread(gate_all), spread(up_all)
    grad_down = down_all.astype(f32).reshape(-1, down_all.shape[-1])

    def gain_term(grad, w):
        return jnp.sum(grad * w.astype(f32), axis=1, keepdims=True)

    first = gain_term(grad_query, w_query) + gain_term(grad_key, w_key) + gain_term(grad_value, w_value)
    second = gain_term(raw_gate, w_gate) + gain_term(raw_up, w_up)
    g1, g2 = g1[:, 0:1], g2[:, 0:1]
    return (
        grad_query, grad_key, grad_value, grad_out, g2 * raw_gate, g2 * raw_up, grad_down, tok, y, first / g1, second,
    )


def per_device(
    tokens,
    positions,
    gain_attn,
    gain_mlp,
    w_query,
    w_key,
    w_value,
    w_out,
    w_gate,
    w_up,
    w_down,
    cotangent,
):
    kernels = lax.axis_size("ctx") == 4 and lax.axis_size("fsdp") == 8
    c = lax.axis_index("ctx")
    rows = tokens.shape[0]
    own_rows = w_query.shape[0]
    gains = jnp.broadcast_to(gain_attn[None, :], (16, own_rows))
    gain_one = jnp.broadcast_to(gain_attn.astype(f32)[:, None], (own_rows, 128))
    gain_two = jnp.broadcast_to(gain_mlp.astype(f32)[:, None], (own_rows, 128))
    frequency = theta_base ** (-(jnp.arange(HEAD_DIM // 2, dtype=f32) * 2.0) / HEAD_DIM)
    angles = frequency[:, None] * positions.astype(f32)[None, :]
    begin = c * rows + jnp.arange(rows, dtype=jnp.int32) - positions
    tab = jnp.concatenate(
        [jnp.cos(angles), jnp.sin(angles), jnp.broadcast_to(begin.astype(f32)[None, :], (16, rows))],
        axis=0,
    )

    forward = forward_stage if kernels else forward_plain
    xn, r, grow, qt, kt, vt, lse, o, m, wqkv, wout, wgate, wup, cot_all, tabs = forward(
        tokens, tab, gains, gain_two, w_query, w_key, w_value, w_out, w_gate, w_up, cotangent
    )
    middle = middle_stage if kernels else middle_plain
    y, down_raw, gate_raw, up_raw, gm = middle(m, cot_all, wgate, wup, w_down)
    backward = backward_stage if kernels else backward_plain
    tok, qkv_all, out_all, gate_all, up_all, down_all = backward(
        xn, r, grow, qt, kt, vt, lse, o, gm, wqkv, wout, tabs, gate_raw, up_raw, down_raw
    )
    finish = finish_stage if kernels else finish_plain
    g_query, g_key, g_value, g_out, g_gate, g_up, g_down, tok, y, g_one, g_two = finish(
        qkv_all, out_all, gate_all, up_all, down_all, tok, y,
        w_query, w_key, w_value, w_gate, w_up, gain_one, gain_two,
    )
    return (y, tok, g_one[:, 0], g_two[:, 0], g_query, g_key, g_value, g_out, g_gate, g_up, g_down)


def solution(mesh):
    both = P(("fsdp", "ctx"), None)
    first = P("fsdp", None)
    return jax.shard_map(
        per_device,
        mesh=mesh,
        in_specs=(both, P(("fsdp", "ctx")), P("fsdp"), P("fsdp")) + (first,) * 7 + (both,),
        out_specs=(both, both, P("fsdp"), P("fsdp")) + (first,) * 7,
        check_vma=False,
    )
```

```python
import functools

import jax
import jax.numpy as jnp
from jax import lax
from jax.experimental import pallas as pl
from jax.experimental.pallas import tpu as pltpu
from jax.sharding import PartitionSpec as P

HEADS = 32
KV_HEADS = 4
HEAD_DIM = 64

eps_norm = 1e-05
theta_base = 10000.0
neg_large = -1e30
bf16 = jnp.bfloat16
f32 = jnp.float32
MESH_IDS = pl.DeviceIdType.MESH


def dot(a, b):
    return jnp.dot(a, b, preferred_element_type=f32)


def dot_nt(a, b):
    return lax.dot_general(a, b, (((1,), (1,)), ((), ())), preferred_element_type=f32)


def dot_tn(a, b):
    return lax.dot_general(a, b, (((0,), (0,)), ((), ())), preferred_element_type=f32)


class Place:
    def __init__(self):
        self.f = lax.axis_index("fsdp")
        self.c = lax.axis_index("ctx")
        self.depth = lax.axis_size("fsdp") // 2
        self.z = self.f // 2
        self.core = self.f % 2
        self.other = 1 - self.core
        self.cx = self.c + 1 - 2 * (self.c % 2)
        self.cy = self.c + 2 - 4 * (self.c // 2)
        self.cd = 3 - self.c
        self.sibling = {"fsdp": self.f + 1 - 2 * self.core}
        self.up = {"fsdp": self.f + 2}
        self.down = {"fsdp": self.f - 2}
        self.x = {"ctx": self.cx}
        self.y = {"ctx": self.cy}

    def has_up(self):
        return self.z < self.depth - 1

    def has_down(self):
        return self.z > 0

    def barrier(self):
        sem = pltpu.get_barrier_semaphore()

        def greet(device):
            pl.semaphore_signal(sem, inc=1, device_id=device, device_id_type=MESH_IDS)

        greet(self.sibling)
        greet(self.x)
        greet(self.y)

        @pl.when(self.has_up())
        def _():
            greet(self.up)

        @pl.when(self.has_down())
        def _():
            greet(self.down)

        last = self.depth - 1
        pl.semaphore_wait(sem, 4 - self.z // last + (self.z + last - 1) // last)


def remote(src, dst, send_sem, recv_sem, device):
    return pltpu.make_async_remote_copy(
        src_ref=src,
        dst_ref=dst,
        send_sem=send_sem,
        recv_sem=recv_sem,
        device_id=device,
        device_id_type=MESH_IDS,
    )


class LineGather:
    SEMS = 21

    def __init__(self, place, own, full, sems):
        self.p, self.own, self.full, self.sems = place, own, full, sems
        self.n = place.depth
        self.rows = full.shape[0] // (2 * self.n)

    def view(self, level, core):
        start = pl.multiple_of((2 * level + core) * self.rows, 16)
        return self.full.at[pl.ds(start, self.rows)]

    def to_up(self, hop):
        p = self.p
        level = p.z - (hop - 1)
        src = self.own if hop == 1 and self.own is not None else self.view(level, p.core)
        return remote(
            src, self.view(level, p.core), self.sems.at[hop - 1], self.sems.at[6 + hop - 1], p.up
        )

    def to_down(self, hop):
        p = self.p
        level = p.z + (hop - 1)
        src = self.own if hop == 1 and self.own is not None else self.view(level, p.core)
        return remote(
            src, self.view(level, p.core), self.sems.at[3 + hop - 1], self.sems.at[9 + hop - 1], p.down
        )

    def to_sibling(self, level, own=False):
        p = self.p
        src = self.own if own and self.own is not None else self.view(level, p.core)
        return remote(
            src, self.view(level, p.core), self.sems.at[12 + level], self.sems.at[16 + level], p.sibling
        )

    def local(self):
        p = self.p
        return pltpu.make_async_copy(self.own, self.view(p.z, p.core), self.sems.at[20])

    def start(self):
        p = self.p

        @pl.when(p.has_up())
        def _():
            self.to_up(1).start()

        @pl.when(p.has_down())
        def _():
            self.to_down(1).start()

        self.to_sibling(p.z, True).start()
        if self.own is not None:
            self.local().start()

    def arrived(self, level, sem):
        view = self.view(level, self.p.core)
        remote(view, view, self.sems.at[0], sem, self.p.sibling).wait_recv()

    def hop(self, s):
        p = self.p

        @pl.when(p.z >= s)
        def _():
            self.arrived(p.z - s, self.sems.at[6 + s - 1])
            if s < self.n - 1:

                @pl.when(p.has_up())
                def _():
                    self.to_up(s + 1).start()

            self.to_sibling(p.z - s).start()

        @pl.when(p.z + s < self.n)
        def _():
            self.arrived(p.z + s, self.sems.at[9 + s - 1])
            if s < self.n - 1:

                @pl.when(p.has_down())
                def _():
                    self.to_down(s + 1).start()

            self.to_sibling(p.z + s).start()

    def finish(self):
        p = self.p
        if self.own is not None:
            self.local().wait()
        for level in range(self.n):
            view = self.view(level, p.other)
            remote(view, view, self.sems.at[0], self.sems.at[16 + level], p.sibling).wait_recv()

    def drain(self):
        p = self.p
        for s in range(1, self.n):

            @pl.when(p.has_up() & (p.z >= s - 1))
            def _():
                self.to_up(s).wait_send()

            @pl.when(p.has_down() & (p.z + s - 1 < self.n))
            def _():
                self.to_down(s).wait_send()

        for level in range(self.n):
            self.to_sibling(level).wait_send()


class PlaneGather:
    SEMS = 8

    def __init__(self, place, view, half, sems, own=None):
        self.p, self.view, self.half, self.sems = place, view, half, sems
        self.own = own

    def src(self):
        return self.view(self.p.c) if self.own is None else self.own

    def to_x(self):
        p = self.p
        return remote(self.src(), self.view(p.c), self.sems.at[0], self.sems.at[2], p.x)

    def to_y(self):
        p = self.p
        return remote(self.src(), self.view(p.c), self.sems.at[1], self.sems.at[3], p.y)

    def on_to_y(self):
        p, h = self.p, self.half(self.p.cx, 0)
        return remote(h, h, self.sems.at[4], self.sems.at[6], p.y)

    def on_to_x(self):
        p, h = self.p, self.half(self.p.cy, 1)
        return remote(h, h, self.sems.at[5], self.sems.at[7], p.x)

    def start(self):
        self.to_x().start()
        self.to_y().start()

    def got(self, ref, sem):
        remote(ref, ref, self.sems.at[0], sem, self.p.x).wait_recv()

    def middle(self):
        p = self.p
        self.got(self.view(p.cx), self.sems.at[2])
        self.on_to_y().start()
        self.got(self.view(p.cy), self.sems.at[3])
        self.on_to_x().start()

    def finish(self):
        p = self.p
        self.got(self.half(p.cd, 0), self.sems.at[6])
        self.got(self.half(p.cd, 1), self.sems.at[7])

    def drain(self):
        self.to_x().wait_send()
        self.to_y().wait_send()
        self.on_to_y().wait_send()
        self.on_to_x().wait_send()


def rows_at(index, count):
    return pl.ds(pl.multiple_of(index * count, count), count)


def any_spec(count):
    return [pl.BlockSpec(memory_space=pl.ANY)] * count


def call(kernel, ins, outs, scratch, collective_id, flops, name, vmem=60.0):
    return pl.pallas_call(
        kernel,
        out_shape=[jax.ShapeDtypeStruct(s, d) for s, d in outs],
        in_specs=any_spec(len(ins)),
        out_specs=any_spec(len(outs)),
        scratch_shapes=scratch,
        compiler_params=pltpu.CompilerParams(
            collective_id=collective_id, has_side_effects=True, vmem_limit_bytes=int(vmem * 2**20)
        ),
        cost_estimate=pl.CostEstimate(flops=flops, bytes_accessed=2**26, transcendentals=2**22),
        name=name,
    )(*ins)


def tiles_of(total, most):
    sizes, at = [], 0
    while at < total:
        sizes.append((at, min(most, total - at)))
        at += most
    return sizes


def add_to(ref, other):
    for start, size in tiles_of(ref.shape[0], 96):
        at = pl.ds(start, size)
        ref[at, :] = (ref[at, :].astype(f32) + other[at, :].astype(f32)).astype(bf16)


class PlaneScatter:
    SEMS = 8

    def __init__(self, place, part, half, first, second, sems):
        self.p, self.part, self.half = place, part, half
        self.first, self.second, self.sems = first, second, sems

    def ref(self):
        return self.part(self.p.c)

    def far_to_y(self):
        p = self.p
        return remote(self.half(p.cd, 0), self.first.at[0], self.sems.at[0], self.sems.at[2], p.y)

    def far_to_x(self):
        p = self.p
        return remote(self.half(p.cd, 1), self.first.at[1], self.sems.at[1], self.sems.at[3], p.x)

    def to_x(self):
        p = self.p
        return remote(self.part(p.cx), self.second.at[0], self.sems.at[4], self.sems.at[6], p.x)

    def to_y(self):
        p = self.p
        return remote(self.part(p.cy), self.second.at[1], self.sems.at[5], self.sems.at[7], p.y)

    def start(self):
        self.far_to_y().start()
        self.far_to_x().start()

    def got(self, ref, sem):
        remote(ref, ref, self.sems.at[0], sem, self.p.x).wait_recv()

    def add(self, ref, other):
        add_to(ref, other)

    def middle(self):
        p = self.p
        self.got(self.first.at[0], self.sems.at[2])
        self.add(self.half(p.cx, 0), self.first.at[0])
        self.to_x().start()
        self.got(self.first.at[1], self.sems.at[3])
        self.add(self.half(p.cy, 1), self.first.at[1])
        self.to_y().start()

    def finish(self, at=slice(None), first=True):
        if first:
            self.got(self.second.at[0], self.sems.at[6])
            self.got(self.second.at[1], self.sems.at[7])
        own = self.part(self.p.c)[at].astype(f32)
        return own + self.second[0, at].astype(f32) + self.second[1, at].astype(f32)

    def drain(self):
        self.far_to_y().wait_send()
        self.far_to_x().wait_send()
        self.to_x().wait_send()
        self.to_y().wait_send()


class LineScatter:
    SEMS = 22

    def __init__(self, place, part, acc, slots, sems, stage=None):
        self.p, self.part, self.acc, self.slots, self.sems = place, part, acc, slots, sems
        self.stage = stage
        self.n = place.depth

    def to_sibling(self, level):
        p = self.p
        return remote(
            self.part(level, p.other), self.acc.at[level], self.sems.at[level], self.sems.at[4 + level], p.sibling
        )

    def start(self):
        for level in range(self.n):
            self.to_sibling(level).start()

    def load(self, level):
        return pltpu.make_async_copy(
            self.part(level, self.p.core), self.stage[level % 2], self.sems.at[20 + level % 2]
        )

    def got(self, ref, sem):
        remote(ref, ref, self.sems.at[0], sem, self.p.sibling).wait_recv()

    def add(self, ref, other):
        add_to(ref, other)

    def combine(self):
        if self.stage is not None:
            self.load(0).start()
            self.load(1).start()
        for level in range(self.n):
            self.got(self.acc.at[level], self.sems.at[4 + level])
            if self.stage is None:
                self.add(self.acc.at[level], self.part(level, self.p.core))
            else:
                self.load(level).wait()
                self.add(self.acc.at[level], self.stage[level % 2])
                if level + 2 < self.n:
                    self.load(level + 2).start()

    def slot(self, up, s):
        return self.slots.at[s - 1] if up else self.slots.at[(0, 3, 4)[s - 1]]

    def along(self, up, s):
        p = self.p
        level = p.z if up else self.n - 1 - p.z
        block = self.n - s + level
        block = block if up else self.n - 1 - block
        base = 8 if up else 14
        copy = remote(
            self.acc.at[block],
            self.slot(up, s),
            self.sems.at[base + s - 1],
            self.sems.at[base + 3 + s - 1],
            p.up if up else p.down,
        )
        return copy, (level <= s - 1) & (level < self.n - 1)

    def step(self, s):
        for up in (True, False):
            level = self.p.z if up else self.n - 1 - self.p.z
            if s > 1:
                block = self.n - s + level
                block = block if up else self.n - 1 - block
                base = 11 if up else 17

                @pl.when((level >= 1) & (s - 1 >= level))
                def _():
                    self.got(self.slot(up, s - 1), self.sems.at[base + s - 2])
                    self.add(self.acc.at[block], self.slot(up, s - 1))

            if s < self.n:
                copy, valid = self.along(up, s)

                @pl.when(valid)
                def _():
                    copy.start()

    def result(self):
        return self.acc.at[self.p.z]

    def drain(self):
        for level in range(self.n):
            self.to_sibling(level).wait_send()
        for up in (True, False):
            for s in range(1, self.n):
                copy, valid = self.along(up, s)

                @pl.when(valid)
                def _():
                    copy.wait_send()


def forward_kernel(
    tok, tab, gains, gcol, w_query, w_key, w_value, w_out, w_gate, w_up, cot,
    xn_out, r_out, grow_out, qt_out, kt_out, vt_out, lse_out, o_out, m_out,
    wqkv_out, wout_out, wgate, wup, cot_all, tab_out,
    X, XN, QT, KT, VT, K, LSE, O, M, WQ, WO, TAB, G8, GROW, BIAS, OT, R1,
    WK, WV, GF, UF, GO, UO, GCOL,
    line_sems, plane_sems, copy_sems,
):
    p = Place()
    n_ctx = 4
    rows = tok.shape[0]
    half = rows // 2
    qw = QT.shape[0]
    heads = qw // HEAD_DIM
    cw = O.shape[1] // n_ctx
    scale = HEAD_DIM ** (-0.5)

    mine = rows_at(p.f, WK.shape[0])
    loads = []
    for i, (src, dst) in enumerate(
        (
            (w_query.at[:, rows_at(p.c, qw)], WQ.at[mine, pl.ds(0, qw)]),
            (w_key, WK), (w_value, WV), (w_gate, GF), (w_up, UF), (gcol, GCOL),
        )
    ):
        loads.append(pltpu.make_async_copy(src, dst, copy_sems.at[15 + i]))
        loads[-1].start()

    p.barrier()

    gain_line = LineGather(p, gains, G8, line_sems.at[0])
    qkv_line = LineGather(p, None, WQ, line_sems.at[1])
    out_line = LineGather(p, w_out.at[:, rows_at(p.c, cw)], WO, line_sems.at[2])
    gate_line = LineGather(p, GO, wgate, line_sems.at[3])
    up_line = LineGather(p, UO, wup, line_sems.at[4])

    def row_block(ref):
        return (
            lambda c: ref.at[rows_at(c, rows)],
            lambda c, h: ref.at[pl.ds(pl.multiple_of(c * rows + h * half, half), half)],
        )

    tok_plane = PlaneGather(p, *row_block(X), plane_sems.at[0], own=tok)
    cot_plane = PlaneGather(p, *row_block(cot_all), plane_sems.at[1], own=cot)
    tab_rows = tab.shape[0]
    tab_plane = PlaneGather(
        p,
        lambda c: TAB.at[c],
        lambda c, h: TAB.at[c, pl.ds(h * (tab_rows // 2), tab_rows // 2)],
        plane_sems.at[2],
        own=tab,
    )

    def col_block(ref, b):
        def view(c):
            return ref.at[pl.ds(b * rows, rows), rows_at(c, cw)]

        def halves(c, h):
            return ref.at[pl.ds(b * rows + h * half, half), rows_at(c, cw)]

        return view, halves

    o_plane = [PlaneGather(p, *col_block(O, b), plane_sems.at[3 + b]) for b in range(n_ctx)]
    m_plane = [PlaneGather(p, *col_block(M, b), plane_sems.at[7 + b]) for b in range(n_ctx)]

    gain_line.start()
    tab_plane.start()
    tok_plane.start()
    out_line.start()
    for i in range(3):
        loads[i].wait()
    for c in range(n_ctx):

        @pl.when(p.c == c)
        def _():
            WQ[mine, qw : qw + HEAD_DIM] = WK[:, HEAD_DIM * c : HEAD_DIM * (c + 1)]
            WQ[mine, qw + HEAD_DIM :] = WV[:, HEAD_DIM * c : HEAD_DIM * (c + 1)]

    qkv_line.start()
    own_tok = pltpu.make_async_copy(tok, X.at[rows_at(p.c, rows)], copy_sems.at[0])
    own_tab = pltpu.make_async_copy(tab, TAB.at[p.c], copy_sems.at[1])
    own_cot = pltpu.make_async_copy(cot, cot_all.at[rows_at(p.c, rows)], copy_sems.at[2])
    own_tok.start()
    own_tab.start()
    own_cot.start()

    for i in range(3, 6):
        loads[i].wait()
    unit = GO.shape[1] // (2 * p.depth)
    for c in range(n_ctx):

        @pl.when(p.c == c)
        def _():
            for f in range(2 * p.depth):
                at = (f * n_ctx + c) * unit
                for src, dst in ((GF, GO), (UF, UO)):
                    part = src[:, at : at + unit].astype(f32) * GCOL[:, 0:1]
                    dst[:, f * unit : (f + 1) * unit] = part.astype(bf16)

    gain_line.hop(1)
    tab_plane.middle()
    gain_line.hop(2)
    qkv_line.hop(1)
    gain_line.hop(3)
    gain_line.finish()
    for f in range(2 * p.depth):
        GROW[:, f * gains.shape[1] : (f + 1) * gains.shape[1]] = G8[16 * f : 16 * f + 8, :].astype(f32)

    def norm(c):
        at = rows_at(c, rows)
        x = X[at, :].astype(f32)
        r = lax.rsqrt(jnp.mean(x * x, axis=-1, keepdims=True) + eps_norm)
        R1[at, :] = jnp.broadcast_to(r, (rows, 128))
        XN[at, :] = (x * r * GROW[0:1, :]).astype(bf16)

    own_tok.wait()
    norm(p.c)
    out_line.hop(1)
    qkv_line.hop(2)
    tok_plane.middle()
    out_line.hop(2)
    gate_line.start()
    norm(p.cx)
    norm(p.cy)
    qkv_line.hop(3)
    tok_plane.finish()
    cot_plane.start()
    out_line.hop(3)
    up_line.start()
    norm(p.cd)
    xn_copy = pltpu.make_async_copy(XN, xn_out, copy_sems.at[3])
    r_copy = pltpu.make_async_copy(R1, r_out, copy_sems.at[4])
    grow_copy = pltpu.make_async_copy(GROW, grow_out, copy_sems.at[14])
    xn_copy.start()
    r_copy.start()
    grow_copy.start()
    own_tab.wait()
    tab_plane.finish()
    qkv_line.finish()

    @pl.loop(0, n_ctx)
    def _(b):
        at = rows_at(b, rows)
        pre = dot(XN[at, :], WQ[...]).T
        cosine = TAB[b, 0:32, :]
        sine = TAB[b, 32:64, :]
        for h in range(heads + 1):
            u = pre[64 * h : 64 * h + 32]
            w = pre[64 * h + 32 : 64 * h + 64]
            first = u * cosine - w * sine
            second = w * cosine + u * sine
            if h < heads:
                QT[64 * h : 64 * h + 32, at] = first.astype(bf16)
                QT[64 * h + 32 : 64 * h + 64, at] = second.astype(bf16)
            else:
                KT[0:32, at] = first.astype(bf16)
                KT[32:64, at] = second.astype(bf16)
                K[at, :] = jnp.concatenate([first, second], axis=0).T.astype(bf16)
        VT[:, at] = pre[qw + 64 :].astype(bf16)

    wq_copy = pltpu.make_async_copy(WQ, wqkv_out, copy_sems.at[5])
    wq_copy.start()
    gate_line.hop(1)

    def attend(b):
        n = (b + 1) * rows
        key = lax.broadcasted_iota(jnp.int32, (n, rows), 0)
        query = lax.broadcasted_iota(jnp.int32, (n, rows), 1) + b * rows
        begin = TAB[b, 64:65, :].astype(jnp.int32)
        BIAS[0:n, :] = jnp.where((key <= query) & (key >= begin), 0.0, neg_large)
        cols = slice(b * rows, (b + 1) * rows)

        @pl.loop(0, heads)
        def _(h):
            head = rows_at(h, HEAD_DIM)
            s = dot(K[0:n, :], QT[head, cols]) * scale + BIAS[0:n, :]
            top = jnp.max(s, axis=0, keepdims=True)
            e = jnp.exp(s - top)
            total = jnp.sum(e, axis=0, keepdims=True)
            probs = (e * (1.0 / total)).astype(bf16)
            OT[head, :] = dot(VT[:, 0:n], probs)
            LSE[rows_at(h, 8), cols] = jnp.broadcast_to(top + jnp.log(total), (8, rows))

        O[pl.ds(b * rows, rows), rows_at(p.c, cw)] = OT[...].T.astype(bf16)
        o_plane[b].start()

    def middle(b):
        at = pl.ds(b * rows, rows)
        cols = rows_at(p.c, cw)
        mid = X[at, cols].astype(f32) + dot(O[at, :], WO[...])
        M[at, cols] = mid.astype(bf16)
        m_plane[b].start()

    attend(0)
    attend(1)
    o_plane[0].middle()
    attend(2)
    o_plane[1].middle()
    attend(3)
    o_plane[2].middle()
    cot_plane.middle()
    out_line.finish()
    o_plane[0].finish()
    middle(0)
    o_plane[3].middle()
    up_line.hop(1)
    o_plane[1].finish()
    middle(1)
    m_plane[0].middle()
    o_plane[2].finish()
    middle(2)
    m_plane[1].middle()
    gate_line.hop(2)
    o_plane[3].finish()
    middle(3)
    m_plane[2].middle()
    up_line.hop(2)
    m_plane[3].middle()
    copies = [xn_copy, r_copy, grow_copy, wq_copy]
    for i, (src, dst) in enumerate(
        ((QT, qt_out), (KT, kt_out), (VT, vt_out), (LSE, lse_out), (O, o_out), (WO, wout_out), (TAB, tab_out))
    ):
        copy = pltpu.make_async_copy(src, dst, copy_sems.at[6 + i])
        copy.start()
        copies.append(copy)
    for b in range(n_ctx):
        m_plane[b].finish()
    m_copy = pltpu.make_async_copy(M, m_out, copy_sems.at[13])
    m_copy.start()
    copies.append(m_copy)
    gate_line.hop(3)
    up_line.hop(3)
    cot_plane.finish()
    gate_line.finish()
    up_line.finish()
    own_cot.wait()
    for copy in copies:
        copy.wait()
    for line in (gain_line, qkv_line, out_line, gate_line, up_line):
        line.drain()
    for plane in [tok_plane, cot_plane, tab_plane] + o_plane + m_plane:
        plane.drain()


def forward_stage(tok, tab, gains, gcol, w_query, w_key, w_value, w_out, w_gate, w_up, cot):
    n_fsdp, n_ctx = lax.axis_size("fsdp"), lax.axis_size("ctx")
    rows, width = tok.shape
    seq = rows * n_ctx
    own = w_query.shape[0]
    whole = n_fsdp * own
    qw = HEADS // n_ctx * HEAD_DIM
    nq, nw, nu = qw + 2 * HEAD_DIM, width // n_ctx, w_gate.shape[1] // n_ctx
    heads = qw // HEAD_DIM
    tab_shape = (n_ctx,) + tab.shape
    outs = [
        ((seq, width), bf16), ((seq, 128), f32), ((8, width), f32), ((qw, seq), bf16), ((64, seq), bf16),
        ((64, seq), bf16), ((8 * heads, seq), f32), ((seq, width), bf16), ((seq, width), bf16), ((whole, nq), bf16),
        ((whole, nw), bf16), ((whole, nu), bf16), ((whole, nu), bf16), ((seq, width), bf16), (tab_shape, f32),
    ]
    scratch = [
        pltpu.VMEM((seq, width), bf16),
        pltpu.VMEM((seq, width), bf16),
        pltpu.VMEM((qw, seq), bf16),
        pltpu.VMEM((64, seq), bf16),
        pltpu.VMEM((64, seq), bf16),
        pltpu.VMEM((seq, 64), bf16),
        pltpu.VMEM((8 * heads, seq), f32),
        pltpu.VMEM((seq, width), bf16),
        pltpu.VMEM((seq, width), bf16),
        pltpu.VMEM((whole, nq), bf16),
        pltpu.VMEM((whole, nw), bf16),
        pltpu.VMEM(tab_shape, f32),
        pltpu.VMEM((16 * n_fsdp, gains.shape[1]), bf16),
        pltpu.VMEM((8, width), f32),
        pltpu.VMEM((seq, rows), f32),
        pltpu.VMEM((qw, rows), f32),
        pltpu.VMEM((seq, 128), f32),
        pltpu.VMEM(w_key.shape, bf16),
        pltpu.VMEM(w_value.shape, bf16),
        pltpu.VMEM(w_gate.shape, bf16),
        pltpu.VMEM(w_up.shape, bf16),
        pltpu.VMEM((own, nu), bf16),
        pltpu.VMEM((own, nu), bf16),
        pltpu.VMEM(gcol.shape, f32),
        pltpu.SemaphoreType.DMA((5, LineGather.SEMS)),
        pltpu.SemaphoreType.DMA((11, PlaneGather.SEMS)),
        pltpu.SemaphoreType.DMA((21,)),
    ]
    ins = (tok, tab, gains, gcol, w_query, w_key, w_value, w_out, w_gate, w_up, cot)
    flops = 2 * seq * width * (nq + nw) + 8 * heads * seq * seq * HEAD_DIM
    return call(forward_kernel, ins, outs, scratch, 1, flops, "forward_stage")


def middle_kernel(
    m_in, cot_in, wgate_in, wup_in, w_down,
    y_out, down_part, down_sum, gate_part, up_part, gm_out,
    M, COT, WG, WU, WD, GATE, UP, HID, R2, PD, PH, D1, D2, H1, H2, DACC, DSLOT,
    line_sems, sum_sems, plane_sems, copy_sems, stage_sems,
):
    p = Place()
    n_ctx = 4
    seq, width = M.shape
    rows = seq // n_ctx
    half = rows // 2
    cw = width // n_ctx
    units = GATE.shape[1]
    loads = []
    for i, (src, dst) in enumerate(((m_in, M), (wgate_in, WG), (wup_in, WU), (cot_in, COT))):
        loads.append(pltpu.make_async_copy(src, dst, copy_sems.at[i]))
        loads[-1].start()

    p.barrier()
    unit = w_down.shape[0] // n_ctx
    down_own = w_down.at[pl.ds(pl.multiple_of(p.c * unit, 16), unit)]
    down_line = LineGather(p, down_own, WD, line_sems.at[0])
    down_line.start()

    loads[0].wait()
    loads[1].wait()
    loads[2].wait()

    @pl.loop(0, n_ctx)
    def _(b):
        at = rows_at(b, rows)
        mf = M[at, :].astype(f32)
        r = lax.rsqrt(jnp.mean(mf * mf, axis=-1, keepdims=True) + eps_norm)
        R2[at, :] = jnp.broadcast_to(r, (rows, 128))
        for start, size in tiles_of(units, 512):
            cols = slice(start, start + size)
            gate = dot(M[at, :], WG[:, cols]) * r
            up = dot(M[at, :], WU[:, cols]) * r
            GATE[at, cols] = gate.astype(bf16)
            UP[at, cols] = up.astype(bf16)
            HID[at, cols] = (gate * (1.0 / (1.0 + jnp.exp(-gate))) * up).astype(bf16)

    down_line.hop(1)
    loads[3].wait()
    stage_copies = {}
    for i, (at, size) in enumerate(tiles_of(units, rows)):
        slot = pl.ds(i % 2 * rows, size)
        if i >= 2:
            stage_copies[i - 2].wait()
        for j in range(0, width, cw):
            PH[slot, j : j + cw] = dot_tn(HID[:, at : at + size], COT[:, j : j + cw]).astype(bf16)
        copy = pltpu.make_async_copy(PH.at[slot], down_part.at[pl.ds(at, size)], stage_sems.at[i % 2])
        copy.start()
        stage_copies[i] = copy
    n_down = len(stage_copies)
    stage_copies[n_down - 2].wait()
    stage_copies[n_down - 1].wait()

    def down_block(level, core):
        return down_part.at[pl.ds(pl.multiple_of((2 * level + core) * unit, 16), unit)]

    down_stage = [PD.at[pl.ds(i * rows, unit)] for i in range(2)]
    sum_line = LineScatter(p, down_block, DACC, DSLOT, sum_sems.at[0], down_stage)
    sum_line.start()
    down_line.hop(2)
    sum_line.combine()
    sum_line.step(1)
    down_line.hop(3)
    down_line.finish()

    y_plane = PlaneScatter(
        p,
        lambda c: PD.at[rows_at(c, rows)],
        lambda c, h: PD.at[pl.ds(pl.multiple_of(c * rows + h * half, half), half)],
        D1,
        D2,
        plane_sems.at[0],
    )

    def col_scatter(b):
        return PlaneScatter(
            p,
            lambda c: PH.at[pl.ds(b * rows, rows), rows_at(c, cw)],
            lambda c, h: PH.at[pl.ds(b * rows + h * half, half), rows_at(c, cw)],
            H1.at[b],
            H2.at[b],
            plane_sems.at[1 + b],
        )

    h_plane = [col_scatter(b) for b in range(n_ctx)]

    def partial_out(c):
        at = rows_at(c, rows)
        for j in range(0, width, cw):
            PD[at, j : j + cw] = dot(HID[at, :], WD[:, j : j + cw]).astype(bf16)

    partial_out(p.cd)
    y_plane.start()
    partial_out(p.cx)
    partial_out(p.cy)
    y_plane.middle()
    partial_out(p.c)
    sum_line.step(2)

    def back(b):
        at = pl.ds(b * rows, rows)
        r = R2[at, 0:1]
        stat = jnp.zeros((rows, 1), f32)
        for start, size in tiles_of(units, 512):
            cols = slice(start, start + size)
            grad_hidden = dot_nt(COT[at, :], WD[cols, :])
            gate = GATE[at, cols].astype(f32)
            up = UP[at, cols].astype(f32)
            sig = 1.0 / (1.0 + jnp.exp(-gate))
            d_up = grad_hidden * gate * sig
            d_gate = grad_hidden * up * sig * (1.0 + gate * (1.0 - sig))
            stat += jnp.sum(d_gate * gate + d_up * up, axis=-1, keepdims=True)
            GATE[at, cols] = (d_gate * r).astype(bf16)
            UP[at, cols] = (d_up * r).astype(bf16)
        coef = r * r * stat * (1.0 / width)
        for j in range(0, width, cw):
            e = dot_nt(GATE[at, :], WG[j : j + cw, :]) + dot_nt(UP[at, :], WU[j : j + cw, :])
            PH[at, j : j + cw] = (e - M[at, j : j + cw].astype(f32) * coef).astype(bf16)
        h_plane[b].start()

    back(0)
    back(1)
    h_plane[0].middle()
    sum_line.step(3)
    back(2)
    h_plane[1].middle()
    back(3)
    h_plane[2].middle()

    stage_copies = {}
    jobs = []
    for src, dst in ((GATE, gate_part), (UP, up_part)):
        for at, size in tiles_of(width, 512):
            jobs.append((src, dst, at, size))

    def weight_tile(i):
        src, dst, at, size = jobs[i]
        slot = pl.ds(i % 2 * size, size)
        if i >= 2:
            stage_copies[i - 2].wait()
        for start, part in tiles_of(units, 512):
            cols = slice(start, start + part)
            HID[slot, cols] = dot_tn(M[:, at : at + size], src[:, cols]).astype(bf16)
        copy = pltpu.make_async_copy(HID.at[slot], dst.at[pl.ds(at, size)], stage_sems.at[2 + i % 2])
        copy.start()
        stage_copies[i] = copy

    def finish_block(b):
        at = pl.ds(b * rows, rows)
        mine = rows_at(p.c, cw)
        COT[at, mine] = (COT[at, mine].astype(f32) + h_plane[b].finish()).astype(bf16)

    weight_tile(0)
    weight_tile(1)
    h_plane[3].middle()
    sum_line.step(4)
    sum_copy = pltpu.make_async_copy(sum_line.result(), down_sum, copy_sems.at[6])
    sum_copy.start()
    weight_tile(2)
    finish_block(0)
    weight_tile(3)
    finish_block(1)
    weight_tile(4)
    weight_tile(5)
    finish_block(2)
    weight_tile(6)
    weight_tile(7)
    piece = rows // n_ctx
    for i in range(n_ctx):
        own = pl.ds(pl.multiple_of(p.c * rows + i * piece, piece), piece)
        mlp = y_plane.finish(pl.ds(i * piece, piece), i == 0)
        PD[own, :] = (M[own, :].astype(f32) + mlp).astype(bf16)
    y_copy = pltpu.make_async_copy(PD.at[rows_at(p.c, rows)], y_out, copy_sems.at[4])
    y_copy.start()
    finish_block(3)
    gm_copy = pltpu.make_async_copy(COT.at[:, rows_at(p.c, cw)], gm_out, copy_sems.at[5])
    gm_copy.start()
    stage_copies[6].wait()
    stage_copies[7].wait()
    y_copy.wait()
    gm_copy.wait()
    sum_copy.wait()
    sum_line.drain()
    down_line.drain()
    y_plane.drain()
    for b in range(n_ctx):
        h_plane[b].drain()


def middle_stage(m, cot_all, wgate, wup, w_down):
    n_fsdp, n_ctx = lax.axis_size("fsdp"), lax.axis_size("ctx")
    seq, width = m.shape
    rows = seq // n_ctx
    cw = width // n_ctx
    units = wgate.shape[1]
    unit = units // n_fsdp
    outs = [
        ((rows, width), bf16), ((units, width), bf16), ((unit, width), bf16), ((width, units), bf16),
        ((width, units), bf16), ((seq, cw), bf16),
    ]
    scratch = [
        pltpu.VMEM((seq, width), bf16),
        pltpu.VMEM((seq, width), bf16),
        pltpu.VMEM((width, units), bf16),
        pltpu.VMEM((width, units), bf16),
        pltpu.VMEM((units, width), bf16),
        pltpu.VMEM((seq, units), bf16),
        pltpu.VMEM((seq, units), bf16),
        pltpu.VMEM((seq, units), bf16),
        pltpu.VMEM((seq, 128), f32),
        pltpu.VMEM((seq, width), bf16),
        pltpu.VMEM((seq, width), bf16),
        pltpu.VMEM((2, rows // 2, width), bf16),
        pltpu.VMEM((2, rows, width), bf16),
        pltpu.VMEM((n_ctx, 2, rows // 2, cw), bf16),
        pltpu.VMEM((n_ctx, 2, rows, cw), bf16),
        pltpu.VMEM((n_fsdp // 2, unit, width), bf16),
        pltpu.VMEM((5, unit, width), bf16),
        pltpu.SemaphoreType.DMA((1, LineGather.SEMS)),
        pltpu.SemaphoreType.DMA((1, LineScatter.SEMS)),
        pltpu.SemaphoreType.DMA((5, PlaneScatter.SEMS)),
        pltpu.SemaphoreType.DMA((7,)),
        pltpu.SemaphoreType.DMA((4,)),
    ]
    flops = 18 * seq * width * units
    return call(middle_kernel, (m, cot_all, wgate, wup, w_down), outs, scratch, 2, flops, "middle_stage")


def backward_kernel(
    xn_in, r_in, grow_in, qt_in, kt_in, vt_in, lse_in, o_in, gm_in, wqkv_in, wout_in, tab_in,
    gate_part, up_part, down_sum,
    tok_out, qkv_all, out_all, gate_all, up_all, down_all,
    XN, R1, GROW, QT, KT, VT, LSE, O, GM, WQ, WO, TAB,
    K, V, DK, DV, DOT, DQT, DPRE, STAT, BIAS, PT, G1, G2, T1, T2, TOK,
    GACC, GSLOT, UACC, USLOT, OACC, OSLOT, QACC, QSLOT,
    line_sems, plane_sems, scatter_sems, copy_sems,
):
    p = Place()
    n_ctx = 4
    seq, width = XN.shape
    rows = seq // n_ctx
    half = rows // 2
    cw = width // n_ctx
    qw = QT.shape[0]
    heads = qw // HEAD_DIM
    nq = WQ.shape[1]
    own_rows = QACC.shape[1]
    scale = HEAD_DIM ** (-0.5)
    loads = []
    for i, (src, dst) in enumerate(
        (
            (gm_in, GM), (wout_in, WO), (o_in, O), (kt_in, KT), (vt_in, VT), (qt_in, QT), (lse_in, LSE),
            (tab_in, TAB), (xn_in, XN), (wqkv_in, WQ), (r_in, R1), (grow_in, GROW),
        )
    ):
        loads.append(pltpu.make_async_copy(src, dst, copy_sems.at[i]))
        if dst is not XN:
            loads[-1].start()

    p.barrier()

    def block_rows(ref):
        count = ref.shape[0] // (2 * p.depth)
        return lambda level, core: ref.at[pl.ds(pl.multiple_of((2 * level + core) * count, 16), count)]

    nu = GACC.shape[2]
    cols_stage = [XN.at[pl.ds(i * own_rows, own_rows), pl.ds(0, nu)] for i in range(2)]
    gate_line = LineScatter(p, block_rows(gate_part), GACC, GSLOT, line_sems.at[1], cols_stage)
    up_line = LineScatter(p, block_rows(up_part), UACC, USLOT, line_sems.at[2], cols_stage)
    out_line = LineScatter(p, block_rows(WO), OACC, OSLOT, line_sems.at[3])

    def qkv_block(level, core):
        f = 2 * level + core
        at = pl.ds(pl.multiple_of((f % p.depth) * own_rows, own_rows), own_rows)
        return O.at[at, pl.ds(pl.multiple_of((f // p.depth) * nq, 128), nq)]

    qkv_line = LineScatter(p, qkv_block, QACC, QSLOT, line_sems.at[4])
    gate_line.start()
    up_line.start()

    def col_scatter(b):
        return PlaneScatter(
            p,
            lambda c: PT.at[pl.ds(b * rows, rows), rows_at(c, cw)],
            lambda c, h: PT.at[pl.ds(b * rows + h * half, half), rows_at(c, cw)],
            G1.at[b],
            G2.at[b],
            scatter_sems.at[b],
        )

    g_plane = [col_scatter(b) for b in range(n_ctx)]
    t_plane = PlaneScatter(
        p,
        lambda c: PT.at[rows_at(c, rows)],
        lambda c, h: PT.at[pl.ds(pl.multiple_of(c * rows + h * half, half), half)],
        T1,
        T2,
        scatter_sems.at[n_ctx],
    )

    def whole(ref, own, index, first):
        count = own.shape[0]

        def halves(c, h):
            return ref(c).at[pl.ds(h * first, count - first if h else first)]

        plane = PlaneGather(p, ref, halves, plane_sems.at[index], own=own)
        return plane, pltpu.make_async_copy(own, ref(p.c), plane_sems.at[index, PlaneGather.SEMS])

    unit = down_sum.shape[0]
    down_plane, down_own = whole(lambda c: down_all.at[c], down_sum, 0, unit // 32 * 16 + unit // 16 % 2 * 16)
    gate_plane, gate_own = whole(lambda c: gate_all.at[c], gate_line.result(), 1, own_rows // 2)
    up_plane, up_own = whole(lambda c: up_all.at[c], up_line.result(), 2, own_rows // 2)
    out_plane, out_own = whole(lambda c: out_all.at[c], out_line.result(), 3, own_rows // 2)
    qkv_plane, qkv_own = whole(lambda c: qkv_all.at[c], qkv_line.result(), 4, own_rows // 2)

    loads[0].wait()
    loads[1].wait()
    for b in range(n_ctx):
        at = pl.ds(b * rows, rows)
        for j in range(0, width, 512):
            PT[at, j : j + 512] = dot_nt(GM[at, :], WO[j : j + 512, :]).astype(bf16)
        g_plane[b].start()
    gate_line.combine()
    gate_line.step(1)
    g_plane[0].middle()
    loads[2].wait()

    @pl.loop(0, width // 512)
    def _(i):
        at = rows_at(i, 512)
        WO[at, :] = dot_tn(O[:, at], GM[...]).astype(bf16)

    out_line.start()
    g_plane[1].middle()
    up_line.combine()
    loads[8].start()
    up_line.step(1)
    g_plane[2].middle()
    for i in (3, 4, 5, 6, 7, 10):
        loads[i].wait()

    @pl.loop(0, n_ctx)
    def _(b):
        at = rows_at(b, rows)
        K[at, :] = KT[:, at].astype(f32).T.astype(bf16)
        V[at, :] = VT[:, at].astype(f32).T.astype(bf16)
        DK[at, :] = jnp.zeros((rows, HEAD_DIM), f32)
        DV[at, :] = jnp.zeros((rows, HEAD_DIM), f32)

    g_plane[3].middle()

    def attend_back(b):
        n = (b + 1) * rows
        cols = slice(b * rows, (b + 1) * rows)
        DOT[...] = g_plane[b].finish().T.astype(bf16)
        at = pl.ds(b * rows, rows)
        DQT[...] = O[at, rows_at(p.c, cw)].astype(f32).T
        key = lax.broadcasted_iota(jnp.int32, (n, rows), 0)
        query = lax.broadcasted_iota(jnp.int32, (n, rows), 1) + b * rows
        begin = TAB[b, 64:65, :].astype(jnp.int32)
        BIAS[0:n, :] = jnp.where((key <= query) & (key >= begin), 0.0, neg_large)
        STAT[...] = jnp.zeros((8, rows), f32)

        @pl.loop(0, heads)
        def _(h):
            head = rows_at(h, HEAD_DIM)
            q = QT[head, cols]
            d_out = DOT[head, :]
            delta = jnp.sum(d_out.astype(f32) * DQT[head, :], axis=0, keepdims=True)
            s = dot(K[0:n, :], q) * scale + BIAS[0:n, :]
            probs = jnp.exp(s - LSE[rows_at(h, 8), cols][0:1])
            d_probs = dot(V[0:n, :], d_out)
            d_s = (probs * (d_probs - delta)).astype(bf16)
            d_q = dot(KT[:, 0:n], d_s) * scale
            DK[0:n, :] += dot_nt(d_s, q) * scale
            DV[0:n, :] += dot_nt(probs.astype(bf16), d_out)
            STAT[...] += jnp.broadcast_to(jnp.sum(d_q * q.astype(f32), axis=0, keepdims=True), (8, rows))
            u, w = d_q[0:32], d_q[32:64]
            cosine, sine = TAB[b, 0:32, :], TAB[b, 32:64, :]
            DQT[head, :] = jnp.concatenate([u * cosine + w * sine, w * cosine - u * sine], axis=0)

        DPRE[at, 0:qw] = DQT[...].T.astype(bf16)
        R1[at, 0:8] = STAT[...].T

    attend_back(0)
    gate_line.step(2)
    attend_back(1)
    attend_back(2)
    down_plane.start()
    down_own.start()
    up_line.step(2)
    attend_back(3)
    loads[8].wait()
    loads[9].wait()
    loads[11].wait()

    @pl.loop(0, n_ctx)
    def _(b):
        at = rows_at(b, rows)
        d_k = DK[at, :].T
        d_v = DV[at, :].T
        stat = jnp.sum(d_k * KT[:, at].astype(f32) + d_v * VT[:, at].astype(f32), axis=0, keepdims=True)
        R1[at, 0:8] += jnp.broadcast_to(stat, (8, rows)).T
        u, w = d_k[0:32], d_k[32:64]
        cosine, sine = TAB[b, 0:32, :], TAB[b, 32:64, :]
        both = jnp.concatenate([u * cosine + w * sine, w * cosine - u * sine, d_v], axis=0)
        DPRE[at, qw:] = both.T.astype(bf16)

    def tokens(c):
        at = rows_at(c, rows)
        r = R1[at, 127:128]
        coef = r * R1[at, 0:1] * (1.0 / width)
        for j in range(0, width, 512):
            cols = slice(j, j + 512)
            gain = GROW[0:1, cols]
            e = dot_nt(DPRE[at, :], WQ[cols, :])
            PT[at, cols] = (e * (gain * r) - XN[at, cols].astype(f32) * ((1.0 / gain) * coef)).astype(bf16)
        mine = rows_at(p.c, cw)
        PT[at, mine] = (PT[at, mine].astype(f32) + GM[at, :].astype(f32)).astype(bf16)

    for b in range(n_ctx):
        g_plane[b].drain()
    tokens(p.cd)
    t_plane.start()
    tokens(p.cx)
    tokens(p.cy)
    t_plane.middle()
    tokens(p.c)

    @pl.loop(0, p.depth)
    def _(i):
        for j in range(2):
            at = rows_at(i + j * p.depth, own_rows)
            O[rows_at(i, own_rows), j * nq : (j + 1) * nq] = dot_tn(XN[:, at], DPRE[...]).astype(bf16)

    qkv_line.start()
    gate_line.step(3)
    down_plane.middle()
    out_line.combine()
    out_line.step(1)
    up_line.step(3)
    qkv_line.combine()
    qkv_line.step(1)
    gate_line.step(4)
    gate_plane.start()
    gate_own.start()
    out_line.step(2)
    tok_copies = []
    for i in range(n_ctx):
        if i >= 2:
            tok_copies[i - 2].wait()
        at = pl.ds(i * (rows // n_ctx), rows // n_ctx)
        TOK[i % 2] = t_plane.finish(at, i == 0)
        tok_copies.append(pltpu.make_async_copy(TOK.at[i % 2], tok_out.at[at], copy_sems.at[12 + i % 2]))
        tok_copies[-1].start()
    qkv_line.step(2)
    up_line.step(4)
    up_plane.start()
    up_own.start()
    gate_plane.middle()
    out_line.step(3)
    qkv_line.step(3)
    out_line.step(4)
    out_plane.start()
    out_own.start()
    up_plane.middle()
    qkv_line.step(4)
    qkv_plane.start()
    qkv_own.start()
    out_plane.middle()
    qkv_plane.middle()
    for plane, own in (
        (down_plane, down_own), (gate_plane, gate_own), (up_plane, up_own), (out_plane, out_own), (qkv_plane, qkv_own),
    ):
        plane.finish()
        own.wait()
        plane.drain()
    tok_copies[2].wait()
    tok_copies[3].wait()
    t_plane.drain()
    for line in (gate_line, up_line, out_line, qkv_line):
        line.drain()


def backward_stage(xn, r, grow, qt, kt, vt, lse, o, gm, wqkv, wout, tabs, gate_part, up_part, down_sum):
    n_fsdp, n_ctx = lax.axis_size("fsdp"), lax.axis_size("ctx")
    seq, width = xn.shape
    rows = seq // n_ctx
    half = rows // 2
    cw = width // n_ctx
    own = width // n_fsdp
    depth = n_fsdp // 2
    nq, nu = wqkv.shape[1], gate_part.shape[1]
    unit = down_sum.shape[0]
    qw = qt.shape[0]
    outs = [
        ((rows, width), f32), ((n_ctx, own, nq), bf16), ((n_ctx, own, cw), bf16), ((n_ctx, own, nu), bf16),
        ((n_ctx, own, nu), bf16), ((n_ctx, unit, width), bf16),
    ]
    ins = (xn, r, grow, qt, kt, vt, lse, o, gm, wqkv, wout, tabs, gate_part, up_part, down_sum)
    scratch = [pltpu.VMEM(a.shape, a.dtype) for a in ins[:12]] + [
        pltpu.VMEM((seq, HEAD_DIM), bf16),
        pltpu.VMEM((seq, HEAD_DIM), bf16),
        pltpu.VMEM((seq, HEAD_DIM), f32),
        pltpu.VMEM((seq, HEAD_DIM), f32),
        pltpu.VMEM((qw, rows), bf16),
        pltpu.VMEM((qw, rows), f32),
        pltpu.VMEM((seq, nq), bf16),
        pltpu.VMEM((8, rows), f32),
        pltpu.VMEM((seq, rows), f32),
        pltpu.VMEM((seq, width), bf16),
        pltpu.VMEM((n_ctx, 2, half, cw), bf16),
        pltpu.VMEM((n_ctx, 2, rows, cw), bf16),
        pltpu.VMEM((2, half, width), bf16),
        pltpu.VMEM((2, rows, width), bf16),
        pltpu.VMEM((2, rows // n_ctx, width), f32),
        pltpu.VMEM((depth, own, nu), bf16),
        pltpu.VMEM((5, own, nu), bf16),
        pltpu.VMEM((depth, own, nu), bf16),
        pltpu.VMEM((5, own, nu), bf16),
        pltpu.VMEM((depth, own, cw), bf16),
        pltpu.VMEM((5, own, cw), bf16),
        pltpu.VMEM((depth, own, nq), bf16),
        pltpu.VMEM((5, own, nq), bf16),
        pltpu.SemaphoreType.DMA((5, LineScatter.SEMS)),
        pltpu.SemaphoreType.DMA((5, PlaneGather.SEMS + 1)),
        pltpu.SemaphoreType.DMA((n_ctx + 1, PlaneScatter.SEMS)),
        pltpu.SemaphoreType.DMA((14,)),
    ]
    flops = 4 * seq * width * (nq + cw) + 20 * qw * seq * seq
    return call(backward_kernel, ins, outs, scratch, 3, flops, "backward_stage")


def finish_kernel(
    unit, qkv, out, gate, up, down, tok, y, w_query, w_key, w_value, w_gate, w_up, g1, g2,
    o_query, o_key, o_value, o_out, o_gate, o_up, o_down, o_tok, o_y, o_g1, o_g2,
):
    n_ctx = qkv.shape[0]
    qw = o_query.shape[1] // n_ctx
    cw = out.shape[2]
    for c in range(n_ctx):
        o_query[:, c * qw : (c + 1) * qw] = qkv[c, :, 0:qw].astype(f32)
        o_key[:, c * HEAD_DIM : (c + 1) * HEAD_DIM] = qkv[c, :, qw : qw + HEAD_DIM].astype(f32)
        o_value[:, c * HEAD_DIM : (c + 1) * HEAD_DIM] = qkv[c, :, qw + HEAD_DIM :].astype(f32)
        o_out[:, c * cw : (c + 1) * cw] = out[c].astype(f32)

    def total(ref, w):
        return jnp.sum(ref[...] * w[...].astype(f32), axis=-1, keepdims=True)

    first = total(o_query, w_query) + total(o_key, w_key) + total(o_value, w_value)
    o_g1[...] = jnp.broadcast_to(first / g1[:, 0:1], o_g1.shape)
    gain = g2[:, 0:1]
    for src, dst in ((gate, o_gate), (up, o_up)):
        for f in range(src.shape[2] // unit):
            for c in range(n_ctx):
                at = (f * n_ctx + c) * unit
                dst[:, at : at + unit] = src[c, :, f * unit : (f + 1) * unit].astype(f32) * gain
    second = total(o_gate, w_gate) + total(o_up, w_up)
    o_g2[...] = jnp.broadcast_to(second / gain, o_g2.shape)
    o_down[...] = down[...].astype(f32)
    o_tok[...] = tok[...]
    o_y[...] = y[...]


def finish_stage(qkv, out, gate, up, down, tok, y, w_query, w_key, w_value, w_gate, w_up, g1, g2):
    steps = 4
    n_fsdp = lax.axis_size("fsdp")
    own = w_query.shape[0]
    down = down.reshape(-1, down.shape[-1])
    unit = gate.shape[2] // n_fsdp

    def spec(shape):
        if len(shape) == 3:
            return pl.BlockSpec((shape[0], shape[1] // steps, shape[2]), lambda i: (0, i, 0))
        return pl.BlockSpec((shape[0] // steps, shape[1]), lambda i: (i, 0))

    ins = (qkv, out, gate, up, down, tok, y, w_query, w_key, w_value, w_gate, w_up, g1, g2)
    outs = [
        (w_query.shape, f32), (w_key.shape, f32), (w_value.shape, f32), ((own, out.shape[0] * out.shape[2]), f32),
        (w_gate.shape, f32), (w_up.shape, f32), (down.shape, f32), (tok.shape, f32), (y.shape, bf16),
        ((own, 128), f32), ((own, 128), f32),
    ]
    return pl.pallas_call(
        functools.partial(finish_kernel, unit),
        grid=(steps,),
        out_shape=[jax.ShapeDtypeStruct(s, d) for s, d in outs],
        in_specs=[spec(a.shape) for a in ins],
        out_specs=[spec(s) for s, d in outs],
        compiler_params=pltpu.CompilerParams(vmem_limit_bytes=56 * 2**20),
        name="finish_stage",
    )(*ins)


def rotate(field, cosine, sine_table, direction):
    half_width = field.shape[-1] // 2
    first_half = field[..., :half_width]
    second_half = field[..., half_width:]
    return jnp.concatenate(
        [
            first_half * cosine - direction * second_half * sine_table,
            second_half * cosine + direction * first_half * sine_table,
        ],
        axis=-1,
    )


def gather(x, axis_name, axis=0):
    return lax.all_gather(x, axis_name, axis=axis, tiled=True)


def scatter(x, axis_name, axis=0):
    return lax.psum_scatter(x.astype(bf16), axis_name, scatter_dimension=axis, tiled=True)


def columns(w, start, count):
    return lax.dynamic_slice_in_dim(w, start, count, axis=1)


def visible(begin):
    seq = begin.shape[0]
    index = jnp.arange(seq, dtype=jnp.int32)
    return (index[None, :] <= index[:, None]) & (index[None, :] >= begin[:, None])


def forward_plain(tok, tab, gains, gcol, w_query, w_key, w_value, w_out, w_gate, w_up, cot):
    n_ctx, n_fsdp = lax.axis_size("ctx"), lax.axis_size("fsdp")
    c = lax.axis_index("ctx")
    own_rows = w_query.shape[0]
    qw = HEADS // n_ctx * HEAD_DIM
    copies = max(1, n_ctx // KV_HEADS)
    kvw = max(1, KV_HEADS // n_ctx) * HEAD_DIM
    unit = w_gate.shape[1] // (n_fsdp * n_ctx)
    cw = tok.shape[1] // n_ctx
    wqkv_o = jnp.concatenate(
        [
            columns(w_query, c * qw, qw),
            columns(w_key, (c // copies) * kvw, kvw),
            columns(w_value, (c // copies) * kvw, kvw),
        ],
        axis=1,
    )
    wout_o = columns(w_out, c * cw, cw)

    def units(w):
        parts = w.reshape(own_rows, n_fsdp, n_ctx, unit)
        mine = lax.dynamic_index_in_dim(parts, c, axis=2, keepdims=False)
        return (gcol[:, 0:1] * mine.reshape(own_rows, n_fsdp * unit)).astype(bf16)

    wgate_o, wup_o = units(w_gate), units(w_up)
    x = gather(tok, "ctx")
    tabs = gather(tab[None], "ctx")
    wqkv = gather(wqkv_o, "fsdp")
    wout = gather(wout_o, "fsdp")
    wgate = gather(wgate_o, "fsdp")
    wup = gather(wup_o, "fsdp")
    cot_all = gather(cot, "ctx")
    gain = gather(gains[0:1], "fsdp", axis=1).astype(f32)
    xf = x.astype(f32)
    r = lax.rsqrt(jnp.mean(xf * xf, axis=-1, keepdims=True) + eps_norm)
    xn = (xf * r * gain).astype(bf16)
    seq, width = x.shape
    heads = HEADS // n_ctx
    qw = heads * HEAD_DIM
    pre = dot(xn, wqkv)
    cosine = tabs[:, 0:32].transpose(0, 2, 1).reshape(seq, 1, 32)
    sine = tabs[:, 32:64].transpose(0, 2, 1).reshape(seq, 1, 32)
    begin = tabs[:, 64].reshape(seq).astype(jnp.int32)
    kvw = (wqkv.shape[1] - qw) // 2
    kv = kvw // HEAD_DIM
    q = rotate(pre[:, :qw].reshape(seq, heads, HEAD_DIM), cosine, sine, 1.0).astype(bf16)
    k = rotate(pre[:, qw : qw + kvw].reshape(seq, kv, HEAD_DIM), cosine, sine, 1.0).astype(bf16)
    v = pre[:, qw + kvw :].astype(bf16).reshape(seq, kv, HEAD_DIM)
    qg = q.reshape(seq, kv, heads // kv, HEAD_DIM)
    scores = jnp.einsum("qkgd,lkd->kgql", qg, k, preferred_element_type=f32) * HEAD_DIM ** (-0.5)
    scores = jnp.where(visible(begin)[None, None], scores, neg_large)
    top = jnp.max(scores, axis=-1, keepdims=True)
    weights = jnp.exp(scores - top)
    total = jnp.sum(weights, axis=-1, keepdims=True)
    probs_low = (weights / total).astype(bf16)
    att = jnp.einsum("kgql,lkd->qkgd", probs_low, v, preferred_element_type=f32)
    o = gather(att.astype(bf16).reshape(seq, qw), "ctx", axis=1)
    lse = (top + jnp.log(total)).reshape(heads, 1, seq)
    lse = jnp.broadcast_to(lse, (heads, 8, seq)).reshape(8 * heads, seq)
    cw = width // n_ctx
    mid = columns(x, c * cw, cw).astype(f32) + dot(o, wout)
    m = gather(mid.astype(bf16), "ctx", axis=1)
    qt = q.reshape(seq, qw).T
    kt = k.reshape(seq, kvw).T
    vt = v.reshape(seq, kvw).T
    r = jnp.broadcast_to(r, (seq, 128))
    grow = jnp.broadcast_to(gain, (8, width))
    return xn, r, grow, qt, kt, vt, lse, o, m, wqkv, wout, wgate, wup, cot_all, tabs


def middle_plain(m, cot_all, wgate, wup, w_down):
    n_ctx = lax.axis_size("ctx")
    c = lax.axis_index("ctx")
    unit = w_down.shape[0] // n_ctx
    wdown_o = lax.dynamic_slice_in_dim(w_down, c * unit, unit, axis=0)
    seq, width = m.shape
    rows = seq // n_ctx
    cw = width // n_ctx
    wdown = gather(wdown_o, "fsdp")
    mf = m.astype(f32)
    r = lax.rsqrt(jnp.mean(mf * mf, axis=-1, keepdims=True) + eps_norm)
    gate = dot(m, wgate) * r
    up = dot(m, wup) * r
    sig = jax.nn.sigmoid(gate)
    hidden = (gate * sig * up).astype(bf16)
    mlp = scatter(dot(hidden, wdown), "ctx").astype(f32)
    mid_rows = lax.dynamic_slice_in_dim(m, c * rows, rows, axis=0).astype(f32)
    output = (mid_rows + mlp).astype(bf16)
    grad_hidden = dot_nt(cot_all, wdown)
    down_sum = scatter(dot_tn(hidden, cot_all), "fsdp")
    d_gate = grad_hidden * up * sig * (1.0 + gate * (1.0 - sig))
    d_up = grad_hidden * gate * sig
    stat = jnp.sum(d_gate * gate + d_up * up, axis=-1, keepdims=True)
    d_gate = (d_gate * r).astype(bf16)
    d_up = (d_up * r).astype(bf16)
    gate_raw = dot_tn(m, d_gate).astype(bf16)
    up_raw = dot_tn(m, d_up).astype(bf16)
    back = dot_nt(d_gate, wgate) + dot_nt(d_up, wup) - mf * (r * r * stat * (1.0 / width))
    back_own = scatter(back, "ctx", axis=1).astype(f32)
    gm = (columns(cot_all, c * cw, cw).astype(f32) + back_own).astype(bf16)
    return output, None, down_sum, gate_raw, up_raw, gm


def backward_plain(xn, r, grow, qt, kt, vt, lse, o, gm, wqkv, wout, tabs, gate_raw, up_raw, down_sum):
    n_ctx = lax.axis_size("ctx")
    c = lax.axis_index("ctx")
    seq, width = xn.shape
    r, gain = r[:, 0:1], grow[0:1]
    heads = HEADS // n_ctx
    qw = heads * HEAD_DIM
    kvw = kt.shape[0]
    kv = kvw // HEAD_DIM
    cw = width // n_ctx
    scale = HEAD_DIM ** (-0.5)
    cosine = tabs[:, 0:32].transpose(0, 2, 1).reshape(seq, 1, 32)
    sine = tabs[:, 32:64].transpose(0, 2, 1).reshape(seq, 1, 32)
    begin = tabs[:, 64].reshape(seq).astype(jnp.int32)
    gate_grad = scatter(gate_raw, "fsdp")
    up_grad = scatter(up_raw, "fsdp")
    out_grad = scatter(dot_tn(o, gm), "fsdp")
    d_att = scatter(dot_nt(gm, wout), "ctx", axis=1).reshape(seq, kv, heads // kv, HEAD_DIM)
    q = qt.T.reshape(seq, kv, heads // kv, HEAD_DIM)
    k = kt.T.reshape(seq, kv, HEAD_DIM)
    v = vt.T.reshape(seq, kv, HEAD_DIM)
    scores = jnp.einsum("qkgd,lkd->kgql", q, k, preferred_element_type=f32) * scale
    scores = jnp.where(visible(begin)[None, None], scores, neg_large)
    lse = lse.reshape(kv, heads // kv, 8, seq)[:, :, 0, :, None]
    probs = jnp.exp(scores - lse)
    d_probs = jnp.einsum("qkgd,lkd->kgql", d_att, v, preferred_element_type=f32)
    delta = jnp.sum(probs * d_probs, axis=-1, keepdims=True)
    d_scores = (probs * (d_probs - delta)).astype(bf16)
    d_q = jnp.einsum("kgql,lkd->qkgd", d_scores, k, preferred_element_type=f32) * scale
    d_k = jnp.einsum("kgql,qkgd->lkd", d_scores, q, preferred_element_type=f32) * scale
    d_v = jnp.einsum("kgql,qkgd->lkd", probs.astype(bf16), d_att, preferred_element_type=f32)
    stat = (
        jnp.sum(d_q * q, axis=(1, 2, 3)) + jnp.sum(d_k * k, axis=(1, 2)) + jnp.sum(d_v * v, axis=(1, 2))
    )[:, None]
    d_q = rotate(d_q.reshape(seq, heads, HEAD_DIM), cosine, sine, -1.0).reshape(seq, qw)
    d_k = rotate(d_k, cosine, sine, -1.0).reshape(seq, kvw)
    d_pre = jnp.concatenate([d_q, d_k, d_v.reshape(seq, kvw)], axis=1).astype(bf16)
    qkv_grad = scatter(dot_tn(xn, d_pre), "fsdp")
    back = dot_nt(d_pre, wqkv) * (gain * r)
    back = back - xn.astype(f32) * ((1.0 / gain) * (r * stat * (1.0 / width)))
    at = (jnp.arange(width, dtype=jnp.int32) // cw == c)[None, :]
    back = back + jnp.where(at, jnp.tile(gm.astype(f32), (1, n_ctx)), 0.0)
    grad_tokens = scatter(back, "ctx").astype(f32)
    qkv_all = gather(qkv_grad[None], "ctx")
    out_all = gather(out_grad[None], "ctx")
    gate_all = gather(gate_grad[None], "ctx")
    up_all = gather(up_grad[None], "ctx")
    down_all = gather(down_sum[None], "ctx")
    return grad_tokens, qkv_all, out_all, gate_all, up_all, down_all


def finish_plain(qkv_all, out_all, gate_all, up_all, down_all, tok, y, w_query, w_key, w_value, w_gate, w_up, g1, g2):
    n_ctx, n_fsdp = lax.axis_size("ctx"), lax.axis_size("fsdp")
    own_rows = w_query.shape[0]
    qw = HEADS // n_ctx * HEAD_DIM
    copies = max(1, n_ctx // KV_HEADS)
    kvw = max(1, KV_HEADS // n_ctx) * HEAD_DIM
    ff_width = w_gate.shape[1]
    unit = ff_width // (n_fsdp * n_ctx)
    qkv_all = qkv_all.astype(f32)

    def joined(part):
        return jnp.moveaxis(part, 0, 1).reshape(own_rows, -1)

    def kv_part(part):
        return joined(part.reshape(n_ctx // copies, copies, own_rows, kvw).sum(axis=1))

    grad_query = joined(qkv_all[:, :, :qw])
    grad_key = kv_part(qkv_all[:, :, qw : qw + kvw])
    grad_value = kv_part(qkv_all[:, :, qw + kvw :])
    grad_out = joined(out_all.astype(f32))

    def spread(full):
        full = full.reshape(n_ctx, own_rows, n_fsdp, unit)
        return full.transpose(1, 2, 0, 3).reshape(own_rows, ff_width).astype(f32)

    raw_gate, raw_up = spread(gate_all), spread(up_all)
    grad_down = down_all.astype(f32).reshape(-1, down_all.shape[-1])

    def gain_term(grad, w):
        return jnp.sum(grad * w.astype(f32), axis=1, keepdims=True)

    first = gain_term(grad_query, w_query) + gain_term(grad_key, w_key) + gain_term(grad_value, w_value)
    second = gain_term(raw_gate, w_gate) + gain_term(raw_up, w_up)
    g1, g2 = g1[:, 0:1], g2[:, 0:1]
    return (
        grad_query, grad_key, grad_value, grad_out, g2 * raw_gate, g2 * raw_up, grad_down, tok, y, first / g1, second,
    )


def per_device(
    tokens,
    positions,
    gain_attn,
    gain_mlp,
    w_query,
    w_key,
    w_value,
    w_out,
    w_gate,
    w_up,
    w_down,
    cotangent,
):
    kernels = lax.axis_size("ctx") == 4 and lax.axis_size("fsdp") == 8
    c = lax.axis_index("ctx")
    rows = tokens.shape[0]
    own_rows = w_query.shape[0]
    gains = jnp.broadcast_to(gain_attn[None, :], (16, own_rows))
    gain_one = jnp.broadcast_to(gain_attn.astype(f32)[:, None], (own_rows, 128))
    gain_two = jnp.broadcast_to(gain_mlp.astype(f32)[:, None], (own_rows, 128))
    frequency = theta_base ** (-(jnp.arange(HEAD_DIM // 2, dtype=f32) * 2.0) / HEAD_DIM)
    angles = frequency[:, None] * positions.astype(f32)[None, :]
    begin = c * rows + jnp.arange(rows, dtype=jnp.int32) - positions
    tab = jnp.concatenate(
        [jnp.cos(angles), jnp.sin(angles), jnp.broadcast_to(begin.astype(f32)[None, :], (16, rows))],
        axis=0,
    )

    forward = forward_stage if kernels else forward_plain
    xn, r, grow, qt, kt, vt, lse, o, m, wqkv, wout, wgate, wup, cot_all, tabs = forward(
        tokens, tab, gains, gain_two, w_query, w_key, w_value, w_out, w_gate, w_up, cotangent
    )
    middle = middle_stage if kernels else middle_plain
    y, _, down_sum, gate_raw, up_raw, gm = middle(m, cot_all, wgate, wup, w_down)
    backward = backward_stage if kernels else backward_plain
    tok, qkv_all, out_all, gate_all, up_all, down_all = backward(
        xn, r, grow, qt, kt, vt, lse, o, gm, wqkv, wout, tabs, gate_raw, up_raw, down_sum
    )
    finish = finish_stage if kernels else finish_plain
    g_query, g_key, g_value, g_out, g_gate, g_up, g_down, tok, y, g_one, g_two = finish(
        qkv_all, out_all, gate_all, up_all, down_all, tok, y,
        w_query, w_key, w_value, w_gate, w_up, gain_one, gain_two,
    )
    return (y, tok, g_one[:, 0], g_two[:, 0], g_query, g_key, g_value, g_out, g_gate, g_up, g_down)


def solution(mesh):
    both = P(("fsdp", "ctx"), None)
    first = P("fsdp", None)
    return jax.shard_map(
        per_device,
        mesh=mesh,
        in_specs=(both, P(("fsdp", "ctx")), P("fsdp"), P("fsdp")) + (first,) * 7 + (both,),
        out_specs=(both, both, P("fsdp"), P("fsdp")) + (first,) * 7,
        check_vma=False,
    )
```

```python
import functools

import jax
import jax.numpy as jnp
from jax import lax
from jax.experimental import pallas as pl
from jax.experimental.pallas import tpu as pltpu
from jax.sharding import PartitionSpec as P

HEADS = 32
KV_HEADS = 4
HEAD_DIM = 64

eps_norm = 1e-05
theta_base = 10000.0
neg_large = -1e30
bf16 = jnp.bfloat16
f32 = jnp.float32
MESH_IDS = pl.DeviceIdType.MESH


def dot(a, b):
    return jnp.dot(a, b, preferred_element_type=f32)


def dot_nt(a, b):
    return lax.dot_general(a, b, (((1,), (1,)), ((), ())), preferred_element_type=f32)


def dot_tn(a, b):
    return lax.dot_general(a, b, (((0,), (0,)), ((), ())), preferred_element_type=f32)


class Place:
    def __init__(self):
        self.f = lax.axis_index("fsdp")
        self.c = lax.axis_index("ctx")
        self.depth = lax.axis_size("fsdp") // 2
        self.z = self.f // 2
        self.core = self.f % 2
        self.other = 1 - self.core
        self.cx = self.c + 1 - 2 * (self.c % 2)
        self.cy = self.c + 2 - 4 * (self.c // 2)
        self.cd = 3 - self.c
        self.sibling = {"fsdp": self.f + 1 - 2 * self.core}
        self.up = {"fsdp": self.f + 2}
        self.down = {"fsdp": self.f - 2}
        self.x = {"ctx": self.cx}
        self.y = {"ctx": self.cy}

    def has_up(self):
        return self.z < self.depth - 1

    def has_down(self):
        return self.z > 0

    def barrier(self):
        sem = pltpu.get_barrier_semaphore()

        def greet(device):
            pl.semaphore_signal(sem, inc=1, device_id=device, device_id_type=MESH_IDS)

        greet(self.sibling)
        greet(self.x)
        greet(self.y)

        @pl.when(self.has_up())
        def _():
            greet(self.up)

        @pl.when(self.has_down())
        def _():
            greet(self.down)

        last = self.depth - 1
        pl.semaphore_wait(sem, 4 - self.z // last + (self.z + last - 1) // last)


def remote(src, dst, send_sem, recv_sem, device):
    return pltpu.make_async_remote_copy(
        src_ref=src,
        dst_ref=dst,
        send_sem=send_sem,
        recv_sem=recv_sem,
        device_id=device,
        device_id_type=MESH_IDS,
    )


class LineGather:
    SEMS = 21

    def __init__(self, place, own, full, sems):
        self.p, self.own, self.full, self.sems = place, own, full, sems
        self.n = place.depth
        self.rows = full.shape[0] // (2 * self.n)

    def view(self, level, core):
        start = pl.multiple_of((2 * level + core) * self.rows, 16)
        return self.full.at[pl.ds(start, self.rows)]

    def to_up(self, hop):
        p = self.p
        level = p.z - (hop - 1)
        src = self.own if hop == 1 and self.own is not None else self.view(level, p.core)
        return remote(
            src, self.view(level, p.core), self.sems.at[hop - 1], self.sems.at[6 + hop - 1], p.up
        )

    def to_down(self, hop):
        p = self.p
        level = p.z + (hop - 1)
        src = self.own if hop == 1 and self.own is not None else self.view(level, p.core)
        return remote(
            src, self.view(level, p.core), self.sems.at[3 + hop - 1], self.sems.at[9 + hop - 1], p.down
        )

    def to_sibling(self, level, own=False):
        p = self.p
        src = self.own if own and self.own is not None else self.view(level, p.core)
        return remote(
            src, self.view(level, p.core), self.sems.at[12 + level], self.sems.at[16 + level], p.sibling
        )

    def local(self):
        p = self.p
        return pltpu.make_async_copy(self.own, self.view(p.z, p.core), self.sems.at[20])

    def start(self):
        p = self.p

        @pl.when(p.has_up())
        def _():
            self.to_up(1).start()

        @pl.when(p.has_down())
        def _():
            self.to_down(1).start()

        self.to_sibling(p.z, True).start()
        if self.own is not None:
            self.local().start()

    def arrived(self, level, sem):
        view = self.view(level, self.p.core)
        remote(view, view, self.sems.at[0], sem, self.p.sibling).wait_recv()

    def hop(self, s):
        p = self.p

        @pl.when(p.z >= s)
        def _():
            self.arrived(p.z - s, self.sems.at[6 + s - 1])
            if s < self.n - 1:

                @pl.when(p.has_up())
                def _():
                    self.to_up(s + 1).start()

            self.to_sibling(p.z - s).start()

        @pl.when(p.z + s < self.n)
        def _():
            self.arrived(p.z + s, self.sems.at[9 + s - 1])
            if s < self.n - 1:

                @pl.when(p.has_down())
                def _():
                    self.to_down(s + 1).start()

            self.to_sibling(p.z + s).start()

    def finish(self):
        p = self.p
        if self.own is not None:
            self.local().wait()
        for level in range(self.n):
            view = self.view(level, p.other)
            remote(view, view, self.sems.at[0], self.sems.at[16 + level], p.sibling).wait_recv()

    def drain(self):
        p = self.p
        for s in range(1, self.n):

            @pl.when(p.has_up() & (p.z >= s - 1))
            def _():
                self.to_up(s).wait_send()

            @pl.when(p.has_down() & (p.z + s - 1 < self.n))
            def _():
                self.to_down(s).wait_send()

        for level in range(self.n):
            self.to_sibling(level).wait_send()


class PlaneGather:
    SEMS = 8

    def __init__(self, place, view, half, sems, own=None):
        self.p, self.view, self.half, self.sems = place, view, half, sems
        self.own = own

    def src(self):
        return self.view(self.p.c) if self.own is None else self.own

    def to_x(self):
        p = self.p
        return remote(self.src(), self.view(p.c), self.sems.at[0], self.sems.at[2], p.x)

    def to_y(self):
        p = self.p
        return remote(self.src(), self.view(p.c), self.sems.at[1], self.sems.at[3], p.y)

    def on_to_y(self):
        p, h = self.p, self.half(self.p.cx, 0)
        return remote(h, h, self.sems.at[4], self.sems.at[6], p.y)

    def on_to_x(self):
        p, h = self.p, self.half(self.p.cy, 1)
        return remote(h, h, self.sems.at[5], self.sems.at[7], p.x)

    def start(self):
        self.to_x().start()
        self.to_y().start()

    def got(self, ref, sem):
        remote(ref, ref, self.sems.at[0], sem, self.p.x).wait_recv()

    def middle(self):
        p = self.p
        self.got(self.view(p.cx), self.sems.at[2])
        self.on_to_y().start()
        self.got(self.view(p.cy), self.sems.at[3])
        self.on_to_x().start()

    def finish(self):
        p = self.p
        self.got(self.half(p.cd, 0), self.sems.at[6])
        self.got(self.half(p.cd, 1), self.sems.at[7])

    def drain(self):
        self.to_x().wait_send()
        self.to_y().wait_send()
        self.on_to_y().wait_send()
        self.on_to_x().wait_send()


def rows_at(index, count):
    return pl.ds(pl.multiple_of(index * count, count), count)


def any_spec(count):
    return [pl.BlockSpec(memory_space=pl.ANY)] * count


def call(kernel, ins, outs, scratch, collective_id, flops, name, vmem=60.0):
    return pl.pallas_call(
        kernel,
        out_shape=[jax.ShapeDtypeStruct(s, d) for s, d in outs],
        in_specs=any_spec(len(ins)),
        out_specs=any_spec(len(outs)),
        scratch_shapes=scratch,
        compiler_params=pltpu.CompilerParams(
            collective_id=collective_id, has_side_effects=True, vmem_limit_bytes=int(vmem * 2**20)
        ),
        cost_estimate=pl.CostEstimate(flops=flops, bytes_accessed=2**26, transcendentals=2**22),
        name=name,
    )(*ins)


def tiles_of(total, most):
    sizes, at = [], 0
    while at < total:
        sizes.append((at, min(most, total - at)))
        at += most
    return sizes


def add_to(ref, other):
    for start, size in tiles_of(ref.shape[0], 96):
        at = pl.ds(start, size)
        ref[at, :] = (ref[at, :].astype(f32) + other[at, :].astype(f32)).astype(bf16)


class PlaneScatter:
    SEMS = 8

    def __init__(self, place, part, half, first, second, sems):
        self.p, self.part, self.half = place, part, half
        self.first, self.second, self.sems = first, second, sems

    def ref(self):
        return self.part(self.p.c)

    def far_to_y(self):
        p = self.p
        return remote(self.half(p.cd, 0), self.first.at[0], self.sems.at[0], self.sems.at[2], p.y)

    def far_to_x(self):
        p = self.p
        return remote(self.half(p.cd, 1), self.first.at[1], self.sems.at[1], self.sems.at[3], p.x)

    def to_x(self):
        p = self.p
        return remote(self.part(p.cx), self.second.at[0], self.sems.at[4], self.sems.at[6], p.x)

    def to_y(self):
        p = self.p
        return remote(self.part(p.cy), self.second.at[1], self.sems.at[5], self.sems.at[7], p.y)

    def start(self):
        self.far_to_y().start()
        self.far_to_x().start()

    def got(self, ref, sem):
        remote(ref, ref, self.sems.at[0], sem, self.p.x).wait_recv()

    def add(self, ref, other):
        add_to(ref, other)

    def middle(self):
        p = self.p
        self.got(self.first.at[0], self.sems.at[2])
        self.add(self.half(p.cx, 0), self.first.at[0])
        self.to_x().start()
        self.got(self.first.at[1], self.sems.at[3])
        self.add(self.half(p.cy, 1), self.first.at[1])
        self.to_y().start()

    def finish(self, at=slice(None), first=True):
        if first:
            self.got(self.second.at[0], self.sems.at[6])
            self.got(self.second.at[1], self.sems.at[7])
        own = self.part(self.p.c)[at].astype(f32)
        return own + self.second[0, at].astype(f32) + self.second[1, at].astype(f32)

    def drain(self):
        self.far_to_y().wait_send()
        self.far_to_x().wait_send()
        self.to_x().wait_send()
        self.to_y().wait_send()


class LineScatter:
    SEMS = 22

    def __init__(self, place, part, acc, slots, sems, stage=None):
        self.p, self.part, self.acc, self.slots, self.sems = place, part, acc, slots, sems
        self.stage = stage
        self.n = place.depth

    def to_sibling(self, level):
        p = self.p
        return remote(
            self.part(level, p.other), self.acc.at[level], self.sems.at[level], self.sems.at[4 + level], p.sibling
        )

    def start(self):
        for level in range(self.n):
            self.to_sibling(level).start()

    def load(self, level):
        return pltpu.make_async_copy(
            self.part(level, self.p.core), self.stage[level % 2], self.sems.at[20 + level % 2]
        )

    def got(self, ref, sem):
        remote(ref, ref, self.sems.at[0], sem, self.p.sibling).wait_recv()

    def add(self, ref, other):
        add_to(ref, other)

    def combine(self):
        if self.stage is not None:
            self.load(0).start()
            self.load(1).start()
        for level in range(self.n):
            self.got(self.acc.at[level], self.sems.at[4 + level])
            if self.stage is None:
                self.add(self.acc.at[level], self.part(level, self.p.core))
            else:
                self.load(level).wait()
                self.add(self.acc.at[level], self.stage[level % 2])
                if level + 2 < self.n:
                    self.load(level + 2).start()

    def slot(self, up, s):
        return self.slots.at[s - 1] if up else self.slots.at[(0, 3, 4)[s - 1]]

    def along(self, up, s):
        p = self.p
        level = p.z if up else self.n - 1 - p.z
        block = self.n - s + level
        block = block if up else self.n - 1 - block
        base = 8 if up else 14
        copy = remote(
            self.acc.at[block],
            self.slot(up, s),
            self.sems.at[base + s - 1],
            self.sems.at[base + 3 + s - 1],
            p.up if up else p.down,
        )
        return copy, (level <= s - 1) & (level < self.n - 1)

    def step(self, s):
        for up in (True, False):
            level = self.p.z if up else self.n - 1 - self.p.z
            if s > 1:
                block = self.n - s + level
                block = block if up else self.n - 1 - block
                base = 11 if up else 17

                @pl.when((level >= 1) & (s - 1 >= level))
                def _():
                    self.got(self.slot(up, s - 1), self.sems.at[base + s - 2])
                    self.add(self.acc.at[block], self.slot(up, s - 1))

            if s < self.n:
                copy, valid = self.along(up, s)

                @pl.when(valid)
                def _():
                    copy.start()

    def result(self):
        return self.acc.at[self.p.z]

    def drain(self):
        for level in range(self.n):
            self.to_sibling(level).wait_send()
        for up in (True, False):
            for s in range(1, self.n):
                copy, valid = self.along(up, s)

                @pl.when(valid)
                def _():
                    copy.wait_send()


def forward_kernel(
    tok, tab, gains, gcol, w_query, w_key, w_value, w_out, w_gate, w_up,
    xn_out, r_out, grow_out, qt_out, kt_out, vt_out, lse_out, o_out, m_out,
    wqkv_out, wout_out, wgate, wup, tab_out,
    X, XN, QT, KT, VT, K, LSE, O, M, WQ, WO, TAB, G8, GROW, BIAS, OT, R1,
    WK, WV, GF, UF, GO, UO, GCOL,
    line_sems, plane_sems, copy_sems,
):
    p = Place()
    n_ctx = 4
    rows = tok.shape[0]
    half = rows // 2
    qw = QT.shape[0]
    heads = qw // HEAD_DIM
    cw = O.shape[1] // n_ctx
    scale = HEAD_DIM ** (-0.5)

    mine = rows_at(p.f, WK.shape[0])
    loads = []
    for i, (src, dst) in enumerate(
        (
            (w_query.at[:, rows_at(p.c, qw)], WQ.at[mine, pl.ds(0, qw)]),
            (w_key, WK), (w_value, WV), (w_gate, GF), (w_up, UF), (gcol, GCOL),
        )
    ):
        loads.append(pltpu.make_async_copy(src, dst, copy_sems.at[15 + i]))
        loads[-1].start()

    p.barrier()

    gain_line = LineGather(p, gains, G8, line_sems.at[0])
    qkv_line = LineGather(p, None, WQ, line_sems.at[1])
    out_line = LineGather(p, w_out.at[:, rows_at(p.c, cw)], WO, line_sems.at[2])
    gate_line = LineGather(p, GO, wgate, line_sems.at[3])
    up_line = LineGather(p, UO, wup, line_sems.at[4])

    def row_block(ref):
        return (
            lambda c: ref.at[rows_at(c, rows)],
            lambda c, h: ref.at[pl.ds(pl.multiple_of(c * rows + h * half, half), half)],
        )

    tok_plane = PlaneGather(p, *row_block(X), plane_sems.at[0], own=tok)
    tab_rows = tab.shape[0]
    tab_plane = PlaneGather(
        p,
        lambda c: TAB.at[c],
        lambda c, h: TAB.at[c, pl.ds(h * (tab_rows // 2), tab_rows // 2)],
        plane_sems.at[2],
        own=tab,
    )

    def col_block(ref, b):
        def view(c):
            return ref.at[pl.ds(b * rows, rows), rows_at(c, cw)]

        def halves(c, h):
            return ref.at[pl.ds(b * rows + h * half, half), rows_at(c, cw)]

        return view, halves

    o_plane = [PlaneGather(p, *col_block(O, b), plane_sems.at[3 + b]) for b in range(n_ctx)]
    m_plane = [PlaneGather(p, *col_block(M, b), plane_sems.at[7 + b]) for b in range(n_ctx)]

    gain_line.start()
    tab_plane.start()
    tok_plane.start()
    out_line.start()
    for i in range(3):
        loads[i].wait()
    for c in range(n_ctx):

        @pl.when(p.c == c)
        def _():
            WQ[mine, qw : qw + HEAD_DIM] = WK[:, HEAD_DIM * c : HEAD_DIM * (c + 1)]
            WQ[mine, qw + HEAD_DIM :] = WV[:, HEAD_DIM * c : HEAD_DIM * (c + 1)]

    qkv_line.start()
    own_tok = pltpu.make_async_copy(tok, X.at[rows_at(p.c, rows)], copy_sems.at[0])
    own_tab = pltpu.make_async_copy(tab, TAB.at[p.c], copy_sems.at[1])
    own_tok.start()
    own_tab.start()

    for i in range(3, 6):
        loads[i].wait()
    unit = GO.shape[1] // (2 * p.depth)
    for c in range(n_ctx):

        @pl.when(p.c == c)
        def _():
            for f in range(2 * p.depth):
                at = (f * n_ctx + c) * unit
                for src, dst in ((GF, GO), (UF, UO)):
                    part = src[:, at : at + unit].astype(f32) * GCOL[:, 0:1]
                    dst[:, f * unit : (f + 1) * unit] = part.astype(bf16)

    gain_line.hop(1)
    tab_plane.middle()
    gain_line.hop(2)
    qkv_line.hop(1)
    gain_line.hop(3)
    gain_line.finish()
    for f in range(2 * p.depth):
        GROW[:, f * gains.shape[1] : (f + 1) * gains.shape[1]] = G8[16 * f : 16 * f + 8, :].astype(f32)

    def norm(c):
        at = rows_at(c, rows)
        x = X[at, :].astype(f32)
        r = lax.rsqrt(jnp.mean(x * x, axis=-1, keepdims=True) + eps_norm)
        R1[at, :] = jnp.broadcast_to(r, (rows, 128))
        XN[at, :] = (x * r * GROW[0:1, :]).astype(bf16)

    own_tok.wait()
    norm(p.c)
    out_line.hop(1)
    qkv_line.hop(2)
    tok_plane.middle()
    out_line.hop(2)
    gate_line.start()
    norm(p.cx)
    norm(p.cy)
    qkv_line.hop(3)
    tok_plane.finish()
    out_line.hop(3)
    up_line.start()
    norm(p.cd)
    xn_copy = pltpu.make_async_copy(XN, xn_out, copy_sems.at[3])
    r_copy = pltpu.make_async_copy(R1, r_out, copy_sems.at[4])
    grow_copy = pltpu.make_async_copy(GROW, grow_out, copy_sems.at[14])
    xn_copy.start()
    r_copy.start()
    grow_copy.start()
    own_tab.wait()
    tab_plane.finish()
    qkv_line.finish()

    @pl.loop(0, n_ctx)
    def _(b):
        at = rows_at(b, rows)
        pre = dot(XN[at, :], WQ[...]).T
        cosine = TAB[b, 0:32, :]
        sine = TAB[b, 32:64, :]
        for h in range(heads + 1):
            u = pre[64 * h : 64 * h + 32]
            w = pre[64 * h + 32 : 64 * h + 64]
            first = u * cosine - w * sine
            second = w * cosine + u * sine
            if h < heads:
                QT[64 * h : 64 * h + 32, at] = first.astype(bf16)
                QT[64 * h + 32 : 64 * h + 64, at] = second.astype(bf16)
            else:
                KT[0:32, at] = first.astype(bf16)
                KT[32:64, at] = second.astype(bf16)
                K[at, :] = jnp.concatenate([first, second], axis=0).T.astype(bf16)
        VT[:, at] = pre[qw + 64 :].astype(bf16)

    wq_copy = pltpu.make_async_copy(WQ, wqkv_out, copy_sems.at[5])
    wq_copy.start()

    def attend(b):
        n = (b + 1) * rows
        key = lax.broadcasted_iota(jnp.int32, (n, rows), 0)
        query = lax.broadcasted_iota(jnp.int32, (n, rows), 1) + b * rows
        begin = TAB[b, 64:65, :].astype(jnp.int32)
        BIAS[0:n, :] = jnp.where((key <= query) & (key >= begin), 0.0, neg_large)
        cols = slice(b * rows, (b + 1) * rows)

        @pl.loop(0, heads)
        def _(h):
            head = rows_at(h, HEAD_DIM)
            s = dot(K[0:n, :], QT[head, cols]) * scale + BIAS[0:n, :]
            top = jnp.max(s, axis=0, keepdims=True)
            e = jnp.exp(s - top)
            total = jnp.sum(e, axis=0, keepdims=True)
            probs = (e * (1.0 / total)).astype(bf16)
            OT[head, :] = dot(VT[:, 0:n], probs)
            LSE[rows_at(h, 8), cols] = jnp.broadcast_to(top + jnp.log(total), (8, rows))

        O[pl.ds(b * rows, rows), rows_at(p.c, cw)] = OT[...].T.astype(bf16)
        o_plane[b].start()

    def middle(b):
        at = pl.ds(b * rows, rows)
        cols = rows_at(p.c, cw)
        mid = X[at, cols].astype(f32) + dot(O[at, :], WO[...])
        M[at, cols] = mid.astype(bf16)
        m_plane[b].start()

    attend(0)
    attend(1)
    o_plane[0].middle()
    attend(2)
    gate_line.hop(1)
    o_plane[1].middle()
    attend(3)
    o_plane[2].middle()
    out_line.finish()
    o_plane[0].finish()
    middle(0)
    o_plane[1].finish()
    middle(1)
    o_plane[3].middle()
    up_line.hop(1)
    m_plane[0].middle()
    o_plane[2].finish()
    middle(2)
    m_plane[1].middle()
    o_plane[3].finish()
    middle(3)
    m_plane[2].middle()
    gate_line.hop(2)
    m_plane[3].middle()
    up_line.hop(2)
    copies = [xn_copy, r_copy, grow_copy, wq_copy]
    for i, (src, dst) in enumerate(
        ((QT, qt_out), (KT, kt_out), (VT, vt_out), (LSE, lse_out), (O, o_out), (WO, wout_out), (TAB, tab_out))
    ):
        copy = pltpu.make_async_copy(src, dst, copy_sems.at[6 + i])
        copy.start()
        copies.append(copy)
    for b in range(n_ctx):
        m_plane[b].finish()
    m_copy = pltpu.make_async_copy(M, m_out, copy_sems.at[13])
    m_copy.start()
    copies.append(m_copy)
    gate_line.hop(3)
    up_line.hop(3)
    gate_line.finish()
    up_line.finish()
    for copy in copies:
        copy.wait()
    for line in (gain_line, qkv_line, out_line, gate_line, up_line):
        line.drain()
    for plane in [tok_plane, tab_plane] + o_plane + m_plane:
        plane.drain()


def forward_stage(tok, tab, gains, gcol, w_query, w_key, w_value, w_out, w_gate, w_up):
    n_fsdp, n_ctx = lax.axis_size("fsdp"), lax.axis_size("ctx")
    rows, width = tok.shape
    seq = rows * n_ctx
    own = w_query.shape[0]
    whole = n_fsdp * own
    qw = HEADS // n_ctx * HEAD_DIM
    nq, nw, nu = qw + 2 * HEAD_DIM, width // n_ctx, w_gate.shape[1] // n_ctx
    heads = qw // HEAD_DIM
    tab_shape = (n_ctx,) + tab.shape
    outs = [
        ((seq, width), bf16), ((seq, 128), f32), ((8, width), f32), ((qw, seq), bf16), ((64, seq), bf16),
        ((64, seq), bf16), ((8 * heads, seq), f32), ((seq, width), bf16), ((seq, width), bf16), ((whole, nq), bf16),
        ((whole, nw), bf16), ((whole, nu), bf16), ((whole, nu), bf16), (tab_shape, f32),
    ]
    scratch = [
        pltpu.VMEM((seq, width), bf16),
        pltpu.VMEM((seq, width), bf16),
        pltpu.VMEM((qw, seq), bf16),
        pltpu.VMEM((64, seq), bf16),
        pltpu.VMEM((64, seq), bf16),
        pltpu.VMEM((seq, 64), bf16),
        pltpu.VMEM((8 * heads, seq), f32),
        pltpu.VMEM((seq, width), bf16),
        pltpu.VMEM((seq, width), bf16),
        pltpu.VMEM((whole, nq), bf16),
        pltpu.VMEM((whole, nw), bf16),
        pltpu.VMEM(tab_shape, f32),
        pltpu.VMEM((16 * n_fsdp, gains.shape[1]), bf16),
        pltpu.VMEM((8, width), f32),
        pltpu.VMEM((seq, rows), f32),
        pltpu.VMEM((qw, rows), f32),
        pltpu.VMEM((seq, 128), f32),
        pltpu.VMEM(w_key.shape, bf16),
        pltpu.VMEM(w_value.shape, bf16),
        pltpu.VMEM(w_gate.shape, bf16),
        pltpu.VMEM(w_up.shape, bf16),
        pltpu.VMEM((own, nu), bf16),
        pltpu.VMEM((own, nu), bf16),
        pltpu.VMEM(gcol.shape, f32),
        pltpu.SemaphoreType.DMA((5, LineGather.SEMS)),
        pltpu.SemaphoreType.DMA((11, PlaneGather.SEMS)),
        pltpu.SemaphoreType.DMA((21,)),
    ]
    ins = (tok, tab, gains, gcol, w_query, w_key, w_value, w_out, w_gate, w_up)
    flops = 2 * seq * width * (nq + nw) + 8 * heads * seq * seq * HEAD_DIM
    return call(forward_kernel, ins, outs, scratch, 1, flops, "forward_stage")


def middle_kernel(
    m_in, cot, wgate_in, wup_in, w_down,
    y_out, down_part, down_sum, gate_part, up_part, gm_out,
    M, COT, WG, WU, WD, GATE, UP, HID, R2, PD, PH, D1, D2, H1, H2, DACC, DSLOT,
    line_sems, sum_sems, plane_sems, copy_sems, stage_sems,
):
    p = Place()
    n_ctx = 4
    seq, width = M.shape
    rows = seq // n_ctx
    half = rows // 2
    cw = width // n_ctx
    units = GATE.shape[1]
    loads = []
    for i, (src, dst) in enumerate(((m_in, M), (wgate_in, WG), (wup_in, WU), (cot, COT.at[rows_at(p.c, rows)]))):
        loads.append(pltpu.make_async_copy(src, dst, copy_sems.at[i]))
        loads[-1].start()

    p.barrier()
    unit = w_down.shape[0] // n_ctx
    down_own = w_down.at[pl.ds(pl.multiple_of(p.c * unit, 16), unit)]
    down_line = LineGather(p, down_own, WD, line_sems.at[0])
    down_line.start()
    cot_plane = PlaneGather(
        p,
        lambda c: COT.at[rows_at(c, rows)],
        lambda c, h: COT.at[pl.ds(pl.multiple_of(c * rows + h * half, half), half)],
        plane_sems.at[5],
        own=cot,
    )
    cot_plane.start()

    loads[0].wait()
    loads[1].wait()
    loads[2].wait()

    def activate(b):
        at = rows_at(b, rows)
        mf = M[at, :].astype(f32)
        r = lax.rsqrt(jnp.mean(mf * mf, axis=-1, keepdims=True) + eps_norm)
        R2[at, :] = jnp.broadcast_to(r, (rows, 128))
        for start, size in tiles_of(units, 512):
            cols = slice(start, start + size)
            gate = dot(M[at, :], WG[:, cols]) * r
            up = dot(M[at, :], WU[:, cols]) * r
            GATE[at, cols] = gate.astype(bf16)
            UP[at, cols] = up.astype(bf16)
            HID[at, cols] = (gate * (1.0 / (1.0 + jnp.exp(-gate))) * up).astype(bf16)

    pl.loop(0, 2)(activate)
    down_line.hop(1)
    pl.loop(2, 4)(activate)
    cot_plane.middle()
    down_line.hop(2)
    loads[3].wait()
    cot_plane.finish()
    stage_copies = {}
    for i, (at, size) in enumerate(tiles_of(units, rows)):
        slot = pl.ds(i % 2 * rows, size)
        if i >= 2:
            stage_copies[i - 2].wait()
        for j in range(0, width, cw):
            PH[slot, j : j + cw] = dot_tn(HID[:, at : at + size], COT[:, j : j + cw]).astype(bf16)
        copy = pltpu.make_async_copy(PH.at[slot], down_part.at[pl.ds(at, size)], stage_sems.at[i % 2])
        copy.start()
        stage_copies[i] = copy
    n_down = len(stage_copies)
    stage_copies[n_down - 2].wait()
    stage_copies[n_down - 1].wait()

    def down_block(level, core):
        return down_part.at[pl.ds(pl.multiple_of((2 * level + core) * unit, 16), unit)]

    down_stage = [PH.at[pl.ds(i * rows, unit)] for i in range(2)]
    sum_line = LineScatter(p, down_block, DACC, DSLOT, sum_sems.at[0], down_stage)
    sum_line.start()
    down_line.hop(3)
    down_line.finish()

    y_plane = PlaneScatter(
        p,
        lambda c: PD.at[rows_at(c, rows)],
        lambda c, h: PD.at[pl.ds(pl.multiple_of(c * rows + h * half, half), half)],
        D1,
        D2,
        plane_sems.at[0],
    )

    def col_scatter(b):
        return PlaneScatter(
            p,
            lambda c: PH.at[pl.ds(b * rows, rows), rows_at(c, cw)],
            lambda c, h: PH.at[pl.ds(b * rows + h * half, half), rows_at(c, cw)],
            H1.at[b],
            H2.at[b],
            plane_sems.at[1 + b],
        )

    h_plane = [col_scatter(b) for b in range(n_ctx)]

    def partial_out(c):
        at = rows_at(c, rows)
        for j in range(0, width, cw):
            PD[at, j : j + cw] = dot(HID[at, :], WD[:, j : j + cw]).astype(bf16)

    partial_out(p.cd)
    y_plane.start()
    partial_out(p.cx)
    partial_out(p.cy)
    sum_line.combine()
    sum_line.step(1)
    partial_out(p.c)

    def back(b):
        at = pl.ds(b * rows, rows)
        r = R2[at, 0:1]
        stat = jnp.zeros((rows, 1), f32)
        for start, size in tiles_of(units, 512):
            cols = slice(start, start + size)
            grad_hidden = dot_nt(COT[at, :], WD[cols, :])
            gate = GATE[at, cols].astype(f32)
            up = UP[at, cols].astype(f32)
            sig = 1.0 / (1.0 + jnp.exp(-gate))
            d_up = grad_hidden * gate * sig
            d_gate = grad_hidden * up * sig * (1.0 + gate * (1.0 - sig))
            stat += jnp.sum(d_gate * gate + d_up * up, axis=-1, keepdims=True)
            GATE[at, cols] = (d_gate * r).astype(bf16)
            UP[at, cols] = (d_up * r).astype(bf16)
        coef = r * r * stat * (1.0 / width)
        for j in range(0, width, cw):
            e = dot_nt(GATE[at, :], WG[j : j + cw, :]) + dot_nt(UP[at, :], WU[j : j + cw, :])
            PH[at, j : j + cw] = (e - M[at, j : j + cw].astype(f32) * coef).astype(bf16)
        h_plane[b].start()

    back(0)
    y_plane.middle()
    back(1)
    h_plane[0].middle()
    sum_line.step(2)
    back(2)
    h_plane[1].middle()
    back(3)
    h_plane[2].middle()

    stage_copies = {}
    jobs = []
    for src, dst in ((GATE, gate_part), (UP, up_part)):
        for at, size in tiles_of(width, 512):
            jobs.append((src, dst, at, size))

    def weight_tile(i):
        src, dst, at, size = jobs[i]
        slot = pl.ds(i % 2 * size, size)
        if i >= 2:
            stage_copies[i - 2].wait()
        for start, part in tiles_of(units, 512):
            cols = slice(start, start + part)
            HID[slot, cols] = dot_tn(M[:, at : at + size], src[:, cols]).astype(bf16)
        copy = pltpu.make_async_copy(HID.at[slot], dst.at[pl.ds(at, size)], stage_sems.at[2 + i % 2])
        copy.start()
        stage_copies[i] = copy

    def finish_block(b):
        at = pl.ds(b * rows, rows)
        mine = rows_at(p.c, cw)
        COT[at, mine] = (COT[at, mine].astype(f32) + h_plane[b].finish()).astype(bf16)

    weight_tile(0)
    cot_plane.drain()
    sum_line.step(3)
    h_plane[3].middle()
    weight_tile(1)
    weight_tile(2)
    finish_block(0)
    weight_tile(3)
    weight_tile(4)
    finish_block(1)
    weight_tile(5)
    weight_tile(6)
    finish_block(2)
    weight_tile(7)
    sum_line.step(4)
    sum_copy = pltpu.make_async_copy(sum_line.result(), down_sum, copy_sems.at[6])
    sum_copy.start()
    piece = rows // n_ctx
    for i in range(n_ctx):
        own = pl.ds(pl.multiple_of(p.c * rows + i * piece, piece), piece)
        mlp = y_plane.finish(pl.ds(i * piece, piece), i == 0)
        PD[own, :] = (M[own, :].astype(f32) + mlp).astype(bf16)
    y_copy = pltpu.make_async_copy(PD.at[rows_at(p.c, rows)], y_out, copy_sems.at[4])
    y_copy.start()
    finish_block(3)
    gm_copy = pltpu.make_async_copy(COT.at[:, rows_at(p.c, cw)], gm_out, copy_sems.at[5])
    gm_copy.start()
    stage_copies[6].wait()
    stage_copies[7].wait()
    y_copy.wait()
    gm_copy.wait()
    sum_copy.wait()
    sum_line.drain()
    down_line.drain()
    y_plane.drain()
    for b in range(n_ctx):
        h_plane[b].drain()


def middle_stage(m, cot, wgate, wup, w_down):
    n_fsdp, n_ctx = lax.axis_size("fsdp"), lax.axis_size("ctx")
    seq, width = m.shape
    rows = seq // n_ctx
    cw = width // n_ctx
    units = wgate.shape[1]
    unit = units // n_fsdp
    outs = [
        ((rows, width), bf16), ((units, width), bf16), ((unit, width), bf16), ((width, units), bf16),
        ((width, units), bf16), ((seq, cw), bf16),
    ]
    scratch = [
        pltpu.VMEM((seq, width), bf16),
        pltpu.VMEM((seq, width), bf16),
        pltpu.VMEM((width, units), bf16),
        pltpu.VMEM((width, units), bf16),
        pltpu.VMEM((units, width), bf16),
        pltpu.VMEM((seq, units), bf16),
        pltpu.VMEM((seq, units), bf16),
        pltpu.VMEM((seq, units), bf16),
        pltpu.VMEM((seq, 128), f32),
        pltpu.VMEM((seq, width), bf16),
        pltpu.VMEM((seq, width), bf16),
        pltpu.VMEM((2, rows // 2, width), bf16),
        pltpu.VMEM((2, rows, width), bf16),
        pltpu.VMEM((n_ctx, 2, rows // 2, cw), bf16),
        pltpu.VMEM((n_ctx, 2, rows, cw), bf16),
        pltpu.VMEM((n_fsdp // 2, unit, width), bf16),
        pltpu.VMEM((5, unit, width), bf16),
        pltpu.SemaphoreType.DMA((1, LineGather.SEMS)),
        pltpu.SemaphoreType.DMA((1, LineScatter.SEMS)),
        pltpu.SemaphoreType.DMA((6, PlaneScatter.SEMS)),
        pltpu.SemaphoreType.DMA((7,)),
        pltpu.SemaphoreType.DMA((4,)),
    ]
    flops = 18 * seq * width * units
    return call(middle_kernel, (m, cot, wgate, wup, w_down), outs, scratch, 2, flops, "middle_stage")


def backward_kernel(
    xn_in, r_in, grow_in, qt_in, kt_in, vt_in, lse_in, o_in, gm_in, wqkv_in, wout_in, tab_in,
    gate_part, up_part, down_sum,
    tok_out, qkv_all, out_all, gate_all, up_all, down_all,
    XN, R1, GROW, QT, KT, VT, LSE, O, GM, WQ, WO, TAB,
    K, V, DK, DV, DOT, DQT, DPRE, STAT, BIAS, PT, G1, G2, T1, T2, TOK,
    GACC, GSLOT, UACC, USLOT, OACC, OSLOT, QACC, QSLOT,
    line_sems, plane_sems, scatter_sems, copy_sems,
):
    p = Place()
    n_ctx = 4
    seq, width = XN.shape
    rows = seq // n_ctx
    half = rows // 2
    cw = width // n_ctx
    qw = QT.shape[0]
    heads = qw // HEAD_DIM
    nq = WQ.shape[1]
    own_rows = QACC.shape[1]
    scale = HEAD_DIM ** (-0.5)
    loads = []
    for i, (src, dst) in enumerate(
        (
            (gm_in, GM), (wout_in, WO), (o_in, O), (kt_in, KT), (vt_in, VT), (qt_in, QT), (lse_in, LSE),
            (tab_in, TAB), (xn_in, XN), (wqkv_in, WQ), (r_in, R1), (grow_in, GROW),
        )
    ):
        loads.append(pltpu.make_async_copy(src, dst, copy_sems.at[i]))
    loads[0].start()
    loads[1].start()

    p.barrier()

    def block_rows(ref):
        count = ref.shape[0] // (2 * p.depth)
        return lambda level, core: ref.at[pl.ds(pl.multiple_of((2 * level + core) * count, 16), count)]

    nu = GACC.shape[2]
    cols_stage = [XN.at[pl.ds(i * own_rows, own_rows), pl.ds(0, nu)] for i in range(2)]
    gate_line = LineScatter(p, block_rows(gate_part), GACC, GSLOT, line_sems.at[1], cols_stage)
    up_line = LineScatter(p, block_rows(up_part), UACC, USLOT, line_sems.at[2], cols_stage)
    out_line = LineScatter(p, block_rows(WO), OACC, OSLOT, line_sems.at[3])

    def qkv_block(level, core):
        f = 2 * level + core
        at = pl.ds(pl.multiple_of((f % p.depth) * own_rows, own_rows), own_rows)
        return O.at[at, pl.ds(pl.multiple_of((f // p.depth) * nq, 128), nq)]

    qkv_line = LineScatter(p, qkv_block, QACC, QSLOT, line_sems.at[4])
    gate_line.start()
    up_line.start()
    for i in (2, 3, 4, 5, 6, 7, 9, 10, 11):
        loads[i].start()

    def col_scatter(b):
        return PlaneScatter(
            p,
            lambda c: PT.at[pl.ds(b * rows, rows), rows_at(c, cw)],
            lambda c, h: PT.at[pl.ds(b * rows + h * half, half), rows_at(c, cw)],
            G1.at[b],
            G2.at[b],
            scatter_sems.at[b],
        )

    g_plane = [col_scatter(b) for b in range(n_ctx)]
    t_plane = PlaneScatter(
        p,
        lambda c: PT.at[rows_at(c, rows)],
        lambda c, h: PT.at[pl.ds(pl.multiple_of(c * rows + h * half, half), half)],
        T1,
        T2,
        scatter_sems.at[n_ctx],
    )

    def whole(ref, own, index, first):
        count = own.shape[0]

        def halves(c, h):
            return ref(c).at[pl.ds(h * first, count - first if h else first)]

        plane = PlaneGather(p, ref, halves, plane_sems.at[index], own=own)
        return plane, pltpu.make_async_copy(own, ref(p.c), plane_sems.at[index, PlaneGather.SEMS])

    unit = down_sum.shape[0]
    down_plane, down_own = whole(lambda c: down_all.at[c], down_sum, 0, unit // 32 * 16 + unit // 16 % 2 * 16)
    gate_plane, gate_own = whole(lambda c: gate_all.at[c], gate_line.result(), 1, own_rows // 2)
    up_plane, up_own = whole(lambda c: up_all.at[c], up_line.result(), 2, own_rows // 2)
    out_plane, out_own = whole(lambda c: out_all.at[c], out_line.result(), 3, own_rows // 2)
    qkv_plane, qkv_own = whole(lambda c: qkv_all.at[c], qkv_line.result(), 4, own_rows // 2)

    loads[0].wait()
    loads[1].wait()
    for b in range(n_ctx):
        at = pl.ds(b * rows, rows)
        for j in range(0, width, 512):
            PT[at, j : j + 512] = dot_nt(GM[at, :], WO[j : j + 512, :]).astype(bf16)
        g_plane[b].start()
    gate_line.combine()
    gate_line.step(1)
    g_plane[0].middle()
    loads[2].wait()

    @pl.loop(0, width // 512)
    def _(i):
        at = rows_at(i, 512)
        WO[at, :] = dot_tn(O[:, at], GM[...]).astype(bf16)

    out_line.start()
    g_plane[1].middle()
    up_line.combine()
    loads[8].start()
    up_line.step(1)
    g_plane[2].middle()
    for i in (3, 4, 5, 6, 7, 10):
        loads[i].wait()

    @pl.loop(0, n_ctx)
    def _(b):
        at = rows_at(b, rows)
        K[at, :] = KT[:, at].astype(f32).T.astype(bf16)
        V[at, :] = VT[:, at].astype(f32).T.astype(bf16)
        DK[at, :] = jnp.zeros((rows, HEAD_DIM), f32)
        DV[at, :] = jnp.zeros((rows, HEAD_DIM), f32)

    g_plane[3].middle()

    def attend_back(b):
        n = (b + 1) * rows
        cols = slice(b * rows, (b + 1) * rows)
        DOT[...] = g_plane[b].finish().T.astype(bf16)
        at = pl.ds(b * rows, rows)
        DQT[...] = O[at, rows_at(p.c, cw)].astype(f32).T
        key = lax.broadcasted_iota(jnp.int32, (n, rows), 0)
        query = lax.broadcasted_iota(jnp.int32, (n, rows), 1) + b * rows
        begin = TAB[b, 64:65, :].astype(jnp.int32)
        BIAS[0:n, :] = jnp.where((key <= query) & (key >= begin), 0.0, neg_large)
        STAT[...] = jnp.zeros((8, rows), f32)

        @pl.loop(0, heads)
        def _(h):
            head = rows_at(h, HEAD_DIM)
            q = QT[head, cols]
            d_out = DOT[head, :]
            delta = jnp.sum(d_out.astype(f32) * DQT[head, :], axis=0, keepdims=True)
            s = dot(K[0:n, :], q) * scale + BIAS[0:n, :]
            probs = jnp.exp(s - LSE[rows_at(h, 8), cols][0:1])
            d_probs = dot(V[0:n, :], d_out)
            d_s = (probs * (d_probs - delta)).astype(bf16)
            d_q = dot(KT[:, 0:n], d_s) * scale
            DK[0:n, :] += dot_nt(d_s, q) * scale
            DV[0:n, :] += dot_nt(probs.astype(bf16), d_out)
            STAT[...] += jnp.broadcast_to(jnp.sum(d_q * q.astype(f32), axis=0, keepdims=True), (8, rows))
            u, w = d_q[0:32], d_q[32:64]
            cosine, sine = TAB[b, 0:32, :], TAB[b, 32:64, :]
            DQT[head, :] = jnp.concatenate([u * cosine + w * sine, w * cosine - u * sine], axis=0)

        DPRE[at, 0:qw] = DQT[...].T.astype(bf16)
        R1[at, 0:8] = STAT[...].T

    attend_back(0)
    gate_line.step(2)
    attend_back(1)
    attend_back(2)
    down_plane.start()
    down_own.start()
    up_line.step(2)
    attend_back(3)
    loads[8].wait()
    loads[9].wait()
    loads[11].wait()

    @pl.loop(0, n_ctx)
    def _(b):
        at = rows_at(b, rows)
        d_k = DK[at, :].T
        d_v = DV[at, :].T
        stat = jnp.sum(d_k * KT[:, at].astype(f32) + d_v * VT[:, at].astype(f32), axis=0, keepdims=True)
        R1[at, 0:8] += jnp.broadcast_to(stat, (8, rows)).T
        u, w = d_k[0:32], d_k[32:64]
        cosine, sine = TAB[b, 0:32, :], TAB[b, 32:64, :]
        both = jnp.concatenate([u * cosine + w * sine, w * cosine - u * sine, d_v], axis=0)
        DPRE[at, qw:] = both.T.astype(bf16)

    def tokens(c):
        at = rows_at(c, rows)
        r = R1[at, 127:128]
        coef = r * R1[at, 0:1] * (1.0 / width)
        for j in range(0, width, 512):
            cols = slice(j, j + 512)
            gain = GROW[0:1, cols]
            e = dot_nt(DPRE[at, :], WQ[cols, :])
            PT[at, cols] = (e * (gain * r) - XN[at, cols].astype(f32) * ((1.0 / gain) * coef)).astype(bf16)
        mine = rows_at(p.c, cw)
        PT[at, mine] = (PT[at, mine].astype(f32) + GM[at, :].astype(f32)).astype(bf16)

    for b in range(n_ctx):
        g_plane[b].drain()
    tokens(p.cd)
    t_plane.start()
    tokens(p.cx)
    tokens(p.cy)
    t_plane.middle()
    tokens(p.c)

    @pl.loop(0, p.depth)
    def _(i):
        for j in range(2):
            at = rows_at(i + j * p.depth, own_rows)
            O[rows_at(i, own_rows), j * nq : (j + 1) * nq] = dot_tn(XN[:, at], DPRE[...]).astype(bf16)

    qkv_line.start()
    gate_line.step(3)
    down_plane.middle()
    out_line.combine()
    out_line.step(1)
    up_line.step(3)
    qkv_line.combine()
    qkv_line.step(1)
    gate_line.step(4)
    gate_plane.start()
    gate_own.start()
    out_line.step(2)
    tok_copies = []
    for i in range(n_ctx):
        if i >= 2:
            tok_copies[i - 2].wait()
        at = pl.ds(i * (rows // n_ctx), rows // n_ctx)
        TOK[i % 2] = t_plane.finish(at, i == 0)
        tok_copies.append(pltpu.make_async_copy(TOK.at[i % 2], tok_out.at[at], copy_sems.at[12 + i % 2]))
        tok_copies[-1].start()
    qkv_line.step(2)
    up_line.step(4)
    up_plane.start()
    up_own.start()
    gate_plane.middle()
    out_line.step(3)
    qkv_line.step(3)
    out_line.step(4)
    out_plane.start()
    out_own.start()
    up_plane.middle()
    qkv_line.step(4)
    qkv_plane.start()
    qkv_own.start()
    out_plane.middle()
    qkv_plane.middle()
    for plane, own in (
        (down_plane, down_own), (gate_plane, gate_own), (up_plane, up_own), (out_plane, out_own), (qkv_plane, qkv_own),
    ):
        plane.finish()
        own.wait()
        plane.drain()
    tok_copies[2].wait()
    tok_copies[3].wait()
    t_plane.drain()
    for line in (gate_line, up_line, out_line, qkv_line):
        line.drain()


def backward_stage(xn, r, grow, qt, kt, vt, lse, o, gm, wqkv, wout, tabs, gate_part, up_part, down_sum):
    n_fsdp, n_ctx = lax.axis_size("fsdp"), lax.axis_size("ctx")
    seq, width = xn.shape
    rows = seq // n_ctx
    half = rows // 2
    cw = width // n_ctx
    own = width // n_fsdp
    depth = n_fsdp // 2
    nq, nu = wqkv.shape[1], gate_part.shape[1]
    unit = down_sum.shape[0]
    qw = qt.shape[0]
    outs = [
        ((rows, width), f32), ((n_ctx, own, nq), bf16), ((n_ctx, own, cw), bf16), ((n_ctx, own, nu), bf16),
        ((n_ctx, own, nu), bf16), ((n_ctx, unit, width), bf16),
    ]
    ins = (xn, r, grow, qt, kt, vt, lse, o, gm, wqkv, wout, tabs, gate_part, up_part, down_sum)
    scratch = [pltpu.VMEM(a.shape, a.dtype) for a in ins[:12]] + [
        pltpu.VMEM((seq, HEAD_DIM), bf16),
        pltpu.VMEM((seq, HEAD_DIM), bf16),
        pltpu.VMEM((seq, HEAD_DIM), f32),
        pltpu.VMEM((seq, HEAD_DIM), f32),
        pltpu.VMEM((qw, rows), bf16),
        pltpu.VMEM((qw, rows), f32),
        pltpu.VMEM((seq, nq), bf16),
        pltpu.VMEM((8, rows), f32),
        pltpu.VMEM((seq, rows), f32),
        pltpu.VMEM((seq, width), bf16),
        pltpu.VMEM((n_ctx, 2, half, cw), bf16),
        pltpu.VMEM((n_ctx, 2, rows, cw), bf16),
        pltpu.VMEM((2, half, width), bf16),
        pltpu.VMEM((2, rows, width), bf16),
        pltpu.VMEM((2, rows // n_ctx, width), f32),
        pltpu.VMEM((depth, own, nu), bf16),
        pltpu.VMEM((5, own, nu), bf16),
        pltpu.VMEM((depth, own, nu), bf16),
        pltpu.VMEM((5, own, nu), bf16),
        pltpu.VMEM((depth, own, cw), bf16),
        pltpu.VMEM((5, own, cw), bf16),
        pltpu.VMEM((depth, own, nq), bf16),
        pltpu.VMEM((5, own, nq), bf16),
        pltpu.SemaphoreType.DMA((5, LineScatter.SEMS)),
        pltpu.SemaphoreType.DMA((5, PlaneGather.SEMS + 1)),
        pltpu.SemaphoreType.DMA((n_ctx + 1, PlaneScatter.SEMS)),
        pltpu.SemaphoreType.DMA((14,)),
    ]
    flops = 4 * seq * width * (nq + cw) + 20 * qw * seq * seq
    return call(backward_kernel, ins, outs, scratch, 3, flops, "backward_stage")


def finish_kernel(
    unit, qkv, out, gate, up, down, tok, y, w_query, w_key, w_value, w_gate, w_up, g1, g2,
    o_query, o_key, o_value, o_out, o_gate, o_up, o_down, o_tok, o_y, o_g1, o_g2,
):
    n_ctx = qkv.shape[0]
    qw = o_query.shape[1] // n_ctx
    cw = out.shape[2]
    for c in range(n_ctx):
        o_query[:, c * qw : (c + 1) * qw] = qkv[c, :, 0:qw].astype(f32)
        o_key[:, c * HEAD_DIM : (c + 1) * HEAD_DIM] = qkv[c, :, qw : qw + HEAD_DIM].astype(f32)
        o_value[:, c * HEAD_DIM : (c + 1) * HEAD_DIM] = qkv[c, :, qw + HEAD_DIM :].astype(f32)
        o_out[:, c * cw : (c + 1) * cw] = out[c].astype(f32)

    def total(ref, w):
        return jnp.sum(ref[...] * w[...].astype(f32), axis=-1, keepdims=True)

    first = total(o_query, w_query) + total(o_key, w_key) + total(o_value, w_value)
    o_g1[...] = jnp.broadcast_to(first / g1[:, 0:1], o_g1.shape)
    gain = g2[:, 0:1]
    for src, dst in ((gate, o_gate), (up, o_up)):
        for f in range(src.shape[2] // unit):
            for c in range(n_ctx):
                at = (f * n_ctx + c) * unit
                dst[:, at : at + unit] = src[c, :, f * unit : (f + 1) * unit].astype(f32) * gain
    second = total(o_gate, w_gate) + total(o_up, w_up)
    o_g2[...] = jnp.broadcast_to(second / gain, o_g2.shape)
    o_down[...] = down[...].astype(f32)
    o_tok[...] = tok[...]
    o_y[...] = y[...]


def finish_stage(qkv, out, gate, up, down, tok, y, w_query, w_key, w_value, w_gate, w_up, g1, g2):
    steps = 4
    n_fsdp = lax.axis_size("fsdp")
    own = w_query.shape[0]
    down = down.reshape(-1, down.shape[-1])
    unit = gate.shape[2] // n_fsdp

    def spec(shape):
        if len(shape) == 3:
            return pl.BlockSpec((shape[0], shape[1] // steps, shape[2]), lambda i: (0, i, 0))
        return pl.BlockSpec((shape[0] // steps, shape[1]), lambda i: (i, 0))

    ins = (qkv, out, gate, up, down, tok, y, w_query, w_key, w_value, w_gate, w_up, g1, g2)
    outs = [
        (w_query.shape, f32), (w_key.shape, f32), (w_value.shape, f32), ((own, out.shape[0] * out.shape[2]), f32),
        (w_gate.shape, f32), (w_up.shape, f32), (down.shape, f32), (tok.shape, f32), (y.shape, bf16),
        ((own, 128), f32), ((own, 128), f32),
    ]
    return pl.pallas_call(
        functools.partial(finish_kernel, unit),
        grid=(steps,),
        out_shape=[jax.ShapeDtypeStruct(s, d) for s, d in outs],
        in_specs=[spec(a.shape) for a in ins],
        out_specs=[spec(s) for s, d in outs],
        compiler_params=pltpu.CompilerParams(vmem_limit_bytes=56 * 2**20),
        name="finish_stage",
    )(*ins)


def rotate(field, cosine, sine_table, direction):
    half_width = field.shape[-1] // 2
    first_half = field[..., :half_width]
    second_half = field[..., half_width:]
    return jnp.concatenate(
        [
            first_half * cosine - direction * second_half * sine_table,
            second_half * cosine + direction * first_half * sine_table,
        ],
        axis=-1,
    )


def gather(x, axis_name, axis=0):
    return lax.all_gather(x, axis_name, axis=axis, tiled=True)


def scatter(x, axis_name, axis=0):
    return lax.psum_scatter(x.astype(bf16), axis_name, scatter_dimension=axis, tiled=True)


def columns(w, start, count):
    return lax.dynamic_slice_in_dim(w, start, count, axis=1)


def visible(begin):
    seq = begin.shape[0]
    index = jnp.arange(seq, dtype=jnp.int32)
    return (index[None, :] <= index[:, None]) & (index[None, :] >= begin[:, None])


def forward_plain(tok, tab, gains, gcol, w_query, w_key, w_value, w_out, w_gate, w_up):
    n_ctx, n_fsdp = lax.axis_size("ctx"), lax.axis_size("fsdp")
    c = lax.axis_index("ctx")
    own_rows = w_query.shape[0]
    qw = HEADS // n_ctx * HEAD_DIM
    copies = max(1, n_ctx // KV_HEADS)
    kvw = max(1, KV_HEADS // n_ctx) * HEAD_DIM
    unit = w_gate.shape[1] // (n_fsdp * n_ctx)
    cw = tok.shape[1] // n_ctx
    wqkv_o = jnp.concatenate(
        [
            columns(w_query, c * qw, qw),
            columns(w_key, (c // copies) * kvw, kvw),
            columns(w_value, (c // copies) * kvw, kvw),
        ],
        axis=1,
    )
    wout_o = columns(w_out, c * cw, cw)

    def units(w):
        parts = w.reshape(own_rows, n_fsdp, n_ctx, unit)
        mine = lax.dynamic_index_in_dim(parts, c, axis=2, keepdims=False)
        return (gcol[:, 0:1] * mine.reshape(own_rows, n_fsdp * unit)).astype(bf16)

    wgate_o, wup_o = units(w_gate), units(w_up)
    x = gather(tok, "ctx")
    tabs = gather(tab[None], "ctx")
    wqkv = gather(wqkv_o, "fsdp")
    wout = gather(wout_o, "fsdp")
    wgate = gather(wgate_o, "fsdp")
    wup = gather(wup_o, "fsdp")
    gain = gather(gains[0:1], "fsdp", axis=1).astype(f32)
    xf = x.astype(f32)
    r = lax.rsqrt(jnp.mean(xf * xf, axis=-1, keepdims=True) + eps_norm)
    xn = (xf * r * gain).astype(bf16)
    seq, width = x.shape
    heads = HEADS // n_ctx
    qw = heads * HEAD_DIM
    pre = dot(xn, wqkv)
    cosine = tabs[:, 0:32].transpose(0, 2, 1).reshape(seq, 1, 32)
    sine = tabs[:, 32:64].transpose(0, 2, 1).reshape(seq, 1, 32)
    begin = tabs[:, 64].reshape(seq).astype(jnp.int32)
    kvw = (wqkv.shape[1] - qw) // 2
    kv = kvw // HEAD_DIM
    q = rotate(pre[:, :qw].reshape(seq, heads, HEAD_DIM), cosine, sine, 1.0).astype(bf16)
    k = rotate(pre[:, qw : qw + kvw].reshape(seq, kv, HEAD_DIM), cosine, sine, 1.0).astype(bf16)
    v = pre[:, qw + kvw :].astype(bf16).reshape(seq, kv, HEAD_DIM)
    qg = q.reshape(seq, kv, heads // kv, HEAD_DIM)
    scores = jnp.einsum("qkgd,lkd->kgql", qg, k, preferred_element_type=f32) * HEAD_DIM ** (-0.5)
    scores = jnp.where(visible(begin)[None, None], scores, neg_large)
    top = jnp.max(scores, axis=-1, keepdims=True)
    weights = jnp.exp(scores - top)
    total = jnp.sum(weights, axis=-1, keepdims=True)
    probs_low = (weights / total).astype(bf16)
    att = jnp.einsum("kgql,lkd->qkgd", probs_low, v, preferred_element_type=f32)
    o = gather(att.astype(bf16).reshape(seq, qw), "ctx", axis=1)
    lse = (top + jnp.log(total)).reshape(heads, 1, seq)
    lse = jnp.broadcast_to(lse, (heads, 8, seq)).reshape(8 * heads, seq)
    cw = width // n_ctx
    mid = columns(x, c * cw, cw).astype(f32) + dot(o, wout)
    m = gather(mid.astype(bf16), "ctx", axis=1)
    qt = q.reshape(seq, qw).T
    kt = k.reshape(seq, kvw).T
    vt = v.reshape(seq, kvw).T
    r = jnp.broadcast_to(r, (seq, 128))
    grow = jnp.broadcast_to(gain, (8, width))
    return xn, r, grow, qt, kt, vt, lse, o, m, wqkv, wout, wgate, wup, tabs


def middle_plain(m, cot, wgate, wup, w_down):
    n_ctx = lax.axis_size("ctx")
    c = lax.axis_index("ctx")
    unit = w_down.shape[0] // n_ctx
    wdown_o = lax.dynamic_slice_in_dim(w_down, c * unit, unit, axis=0)
    seq, width = m.shape
    rows = seq // n_ctx
    cw = width // n_ctx
    wdown = gather(wdown_o, "fsdp")
    cot_all = gather(cot, "ctx")
    mf = m.astype(f32)
    r = lax.rsqrt(jnp.mean(mf * mf, axis=-1, keepdims=True) + eps_norm)
    gate = dot(m, wgate) * r
    up = dot(m, wup) * r
    sig = jax.nn.sigmoid(gate)
    hidden = (gate * sig * up).astype(bf16)
    mlp = scatter(dot(hidden, wdown), "ctx").astype(f32)
    mid_rows = lax.dynamic_slice_in_dim(m, c * rows, rows, axis=0).astype(f32)
    output = (mid_rows + mlp).astype(bf16)
    grad_hidden = dot_nt(cot_all, wdown)
    down_sum = scatter(dot_tn(hidden, cot_all), "fsdp")
    d_gate = grad_hidden * up * sig * (1.0 + gate * (1.0 - sig))
    d_up = grad_hidden * gate * sig
    stat = jnp.sum(d_gate * gate + d_up * up, axis=-1, keepdims=True)
    d_gate = (d_gate * r).astype(bf16)
    d_up = (d_up * r).astype(bf16)
    gate_raw = dot_tn(m, d_gate).astype(bf16)
    up_raw = dot_tn(m, d_up).astype(bf16)
    back = dot_nt(d_gate, wgate) + dot_nt(d_up, wup) - mf * (r * r * stat * (1.0 / width))
    back_own = scatter(back, "ctx", axis=1).astype(f32)
    gm = (columns(cot_all, c * cw, cw).astype(f32) + back_own).astype(bf16)
    return output, None, down_sum, gate_raw, up_raw, gm


def backward_plain(xn, r, grow, qt, kt, vt, lse, o, gm, wqkv, wout, tabs, gate_raw, up_raw, down_sum):
    n_ctx = lax.axis_size("ctx")
    c = lax.axis_index("ctx")
    seq, width = xn.shape
    r, gain = r[:, 0:1], grow[0:1]
    heads = HEADS // n_ctx
    qw = heads * HEAD_DIM
    kvw = kt.shape[0]
    kv = kvw // HEAD_DIM
    cw = width // n_ctx
    scale = HEAD_DIM ** (-0.5)
    cosine = tabs[:, 0:32].transpose(0, 2, 1).reshape(seq, 1, 32)
    sine = tabs[:, 32:64].transpose(0, 2, 1).reshape(seq, 1, 32)
    begin = tabs[:, 64].reshape(seq).astype(jnp.int32)
    gate_grad = scatter(gate_raw, "fsdp")
    up_grad = scatter(up_raw, "fsdp")
    out_grad = scatter(dot_tn(o, gm), "fsdp")
    d_att = scatter(dot_nt(gm, wout), "ctx", axis=1).reshape(seq, kv, heads // kv, HEAD_DIM)
    q = qt.T.reshape(seq, kv, heads // kv, HEAD_DIM)
    k = kt.T.reshape(seq, kv, HEAD_DIM)
    v = vt.T.reshape(seq, kv, HEAD_DIM)
    scores = jnp.einsum("qkgd,lkd->kgql", q, k, preferred_element_type=f32) * scale
    scores = jnp.where(visible(begin)[None, None], scores, neg_large)
    lse = lse.reshape(kv, heads // kv, 8, seq)[:, :, 0, :, None]
    probs = jnp.exp(scores - lse)
    d_probs = jnp.einsum("qkgd,lkd->kgql", d_att, v, preferred_element_type=f32)
    delta = jnp.sum(probs * d_probs, axis=-1, keepdims=True)
    d_scores = (probs * (d_probs - delta)).astype(bf16)
    d_q = jnp.einsum("kgql,lkd->qkgd", d_scores, k, preferred_element_type=f32) * scale
    d_k = jnp.einsum("kgql,qkgd->lkd", d_scores, q, preferred_element_type=f32) * scale
    d_v = jnp.einsum("kgql,qkgd->lkd", probs.astype(bf16), d_att, preferred_element_type=f32)
    stat = (
        jnp.sum(d_q * q, axis=(1, 2, 3)) + jnp.sum(d_k * k, axis=(1, 2)) + jnp.sum(d_v * v, axis=(1, 2))
    )[:, None]
    d_q = rotate(d_q.reshape(seq, heads, HEAD_DIM), cosine, sine, -1.0).reshape(seq, qw)
    d_k = rotate(d_k, cosine, sine, -1.0).reshape(seq, kvw)
    d_pre = jnp.concatenate([d_q, d_k, d_v.reshape(seq, kvw)], axis=1).astype(bf16)
    qkv_grad = scatter(dot_tn(xn, d_pre), "fsdp")
    back = dot_nt(d_pre, wqkv) * (gain * r)
    back = back - xn.astype(f32) * ((1.0 / gain) * (r * stat * (1.0 / width)))
    at = (jnp.arange(width, dtype=jnp.int32) // cw == c)[None, :]
    back = back + jnp.where(at, jnp.tile(gm.astype(f32), (1, n_ctx)), 0.0)
    grad_tokens = scatter(back, "ctx").astype(f32)
    qkv_all = gather(qkv_grad[None], "ctx")
    out_all = gather(out_grad[None], "ctx")
    gate_all = gather(gate_grad[None], "ctx")
    up_all = gather(up_grad[None], "ctx")
    down_all = gather(down_sum[None], "ctx")
    return grad_tokens, qkv_all, out_all, gate_all, up_all, down_all


def finish_plain(qkv_all, out_all, gate_all, up_all, down_all, tok, y, w_query, w_key, w_value, w_gate, w_up, g1, g2):
    n_ctx, n_fsdp = lax.axis_size("ctx"), lax.axis_size("fsdp")
    own_rows = w_query.shape[0]
    qw = HEADS // n_ctx * HEAD_DIM
    copies = max(1, n_ctx // KV_HEADS)
    kvw = max(1, KV_HEADS // n_ctx) * HEAD_DIM
    ff_width = w_gate.shape[1]
    unit = ff_width // (n_fsdp * n_ctx)
    qkv_all = qkv_all.astype(f32)

    def joined(part):
        return jnp.moveaxis(part, 0, 1).reshape(own_rows, -1)

    def kv_part(part):
        return joined(part.reshape(n_ctx // copies, copies, own_rows, kvw).sum(axis=1))

    grad_query = joined(qkv_all[:, :, :qw])
    grad_key = kv_part(qkv_all[:, :, qw : qw + kvw])
    grad_value = kv_part(qkv_all[:, :, qw + kvw :])
    grad_out = joined(out_all.astype(f32))

    def spread(full):
        full = full.reshape(n_ctx, own_rows, n_fsdp, unit)
        return full.transpose(1, 2, 0, 3).reshape(own_rows, ff_width).astype(f32)

    raw_gate, raw_up = spread(gate_all), spread(up_all)
    grad_down = down_all.astype(f32).reshape(-1, down_all.shape[-1])

    def gain_term(grad, w):
        return jnp.sum(grad * w.astype(f32), axis=1, keepdims=True)

    first = gain_term(grad_query, w_query) + gain_term(grad_key, w_key) + gain_term(grad_value, w_value)
    second = gain_term(raw_gate, w_gate) + gain_term(raw_up, w_up)
    g1, g2 = g1[:, 0:1], g2[:, 0:1]
    return (
        grad_query, grad_key, grad_value, grad_out, g2 * raw_gate, g2 * raw_up, grad_down, tok, y, first / g1, second,
    )


def per_device(
    tokens,
    positions,
    gain_attn,
    gain_mlp,
    w_query,
    w_key,
    w_value,
    w_out,
    w_gate,
    w_up,
    w_down,
    cotangent,
):
    kernels = lax.axis_size("ctx") == 4 and lax.axis_size("fsdp") == 8
    c = lax.axis_index("ctx")
    rows = tokens.shape[0]
    own_rows = w_query.shape[0]
    gains = jnp.broadcast_to(gain_attn[None, :], (16, own_rows))
    gain_one = jnp.broadcast_to(gain_attn.astype(f32)[:, None], (own_rows, 128))
    gain_two = jnp.broadcast_to(gain_mlp.astype(f32)[:, None], (own_rows, 128))
    frequency = theta_base ** (-(jnp.arange(HEAD_DIM // 2, dtype=f32) * 2.0) / HEAD_DIM)
    angles = frequency[:, None] * positions.astype(f32)[None, :]
    begin = c * rows + jnp.arange(rows, dtype=jnp.int32) - positions
    tab = jnp.concatenate(
        [jnp.cos(angles), jnp.sin(angles), jnp.broadcast_to(begin.astype(f32)[None, :], (16, rows))],
        axis=0,
    )

    forward = forward_stage if kernels else forward_plain
    xn, r, grow, qt, kt, vt, lse, o, m, wqkv, wout, wgate, wup, tabs = forward(
        tokens, tab, gains, gain_two, w_query, w_key, w_value, w_out, w_gate, w_up
    )
    middle = middle_stage if kernels else middle_plain
    y, _, down_sum, gate_raw, up_raw, gm = middle(m, cotangent, wgate, wup, w_down)
    backward = backward_stage if kernels else backward_plain
    tok, qkv_all, out_all, gate_all, up_all, down_all = backward(
        xn, r, grow, qt, kt, vt, lse, o, gm, wqkv, wout, tabs, gate_raw, up_raw, down_sum
    )
    finish = finish_stage if kernels else finish_plain
    g_query, g_key, g_value, g_out, g_gate, g_up, g_down, tok, y, g_one, g_two = finish(
        qkv_all, out_all, gate_all, up_all, down_all, tok, y,
        w_query, w_key, w_value, w_gate, w_up, gain_one, gain_two,
    )
    return (y, tok, g_one[:, 0], g_two[:, 0], g_query, g_key, g_value, g_out, g_gate, g_up, g_down)


def solution(mesh):
    both = P(("fsdp", "ctx"), None)
    first = P("fsdp", None)
    return jax.shard_map(
        per_device,
        mesh=mesh,
        in_specs=(both, P(("fsdp", "ctx")), P("fsdp"), P("fsdp")) + (first,) * 7 + (both,),
        out_specs=(both, both, P("fsdp"), P("fsdp")) + (first,) * 7,
        check_vma=False,
    )
```

```python
import functools

import jax
import jax.numpy as jnp
from jax import lax
from jax.experimental import pallas as pl
from jax.experimental.pallas import tpu as pltpu
from jax.sharding import PartitionSpec as P

HEADS = 32
KV_HEADS = 4
HEAD_DIM = 64

eps_norm = 1e-05
theta_base = 10000.0
neg_large = -1e30
bf16 = jnp.bfloat16
f32 = jnp.float32
MESH_IDS = pl.DeviceIdType.MESH


def dot(a, b):
    return jnp.dot(a, b, preferred_element_type=f32)


def dot_nt(a, b):
    return lax.dot_general(a, b, (((1,), (1,)), ((), ())), preferred_element_type=f32)


def dot_tn(a, b):
    return lax.dot_general(a, b, (((0,), (0,)), ((), ())), preferred_element_type=f32)


class Place:
    def __init__(self):
        self.f = lax.axis_index("fsdp")
        self.c = lax.axis_index("ctx")
        self.depth = lax.axis_size("fsdp") // 2
        self.z = self.f // 2
        self.core = self.f % 2
        self.other = 1 - self.core
        self.cx = self.c + 1 - 2 * (self.c % 2)
        self.cy = self.c + 2 - 4 * (self.c // 2)
        self.cd = 3 - self.c
        self.sibling = {"fsdp": self.f + 1 - 2 * self.core}
        self.up = {"fsdp": self.f + 2}
        self.down = {"fsdp": self.f - 2}
        self.x = {"ctx": self.cx}
        self.y = {"ctx": self.cy}

    def has_up(self):
        return self.z < self.depth - 1

    def has_down(self):
        return self.z > 0

    def barrier(self):
        sem = pltpu.get_barrier_semaphore()

        def greet(device):
            pl.semaphore_signal(sem, inc=1, device_id=device, device_id_type=MESH_IDS)

        greet(self.sibling)
        greet(self.x)
        greet(self.y)

        @pl.when(self.has_up())
        def _():
            greet(self.up)

        @pl.when(self.has_down())
        def _():
            greet(self.down)

        last = self.depth - 1
        pl.semaphore_wait(sem, 4 - self.z // last + (self.z + last - 1) // last)


def remote(src, dst, send_sem, recv_sem, device):
    return pltpu.make_async_remote_copy(
        src_ref=src,
        dst_ref=dst,
        send_sem=send_sem,
        recv_sem=recv_sem,
        device_id=device,
        device_id_type=MESH_IDS,
    )


class LineGather:
    SEMS = 21

    def __init__(self, place, own, full, sems):
        self.p, self.own, self.full, self.sems = place, own, full, sems
        self.n = place.depth
        self.rows = full.shape[0] // (2 * self.n)

    def view(self, level, core):
        start = pl.multiple_of((2 * level + core) * self.rows, 16)
        return self.full.at[pl.ds(start, self.rows)]

    def to_up(self, hop):
        p = self.p
        level = p.z - (hop - 1)
        src = self.own if hop == 1 and self.own is not None else self.view(level, p.core)
        return remote(
            src, self.view(level, p.core), self.sems.at[hop - 1], self.sems.at[6 + hop - 1], p.up
        )

    def to_down(self, hop):
        p = self.p
        level = p.z + (hop - 1)
        src = self.own if hop == 1 and self.own is not None else self.view(level, p.core)
        return remote(
            src, self.view(level, p.core), self.sems.at[3 + hop - 1], self.sems.at[9 + hop - 1], p.down
        )

    def to_sibling(self, level, own=False):
        p = self.p
        src = self.own if own and self.own is not None else self.view(level, p.core)
        return remote(
            src, self.view(level, p.core), self.sems.at[12 + level], self.sems.at[16 + level], p.sibling
        )

    def local(self):
        p = self.p
        return pltpu.make_async_copy(self.own, self.view(p.z, p.core), self.sems.at[20])

    def start(self):
        p = self.p

        @pl.when(p.has_up())
        def _():
            self.to_up(1).start()

        @pl.when(p.has_down())
        def _():
            self.to_down(1).start()

        self.to_sibling(p.z, True).start()
        if self.own is not None:
            self.local().start()

    def arrived(self, level, sem):
        view = self.view(level, self.p.core)
        remote(view, view, self.sems.at[0], sem, self.p.sibling).wait_recv()

    def hop(self, s):
        p = self.p

        @pl.when(p.z >= s)
        def _():
            self.arrived(p.z - s, self.sems.at[6 + s - 1])
            if s < self.n - 1:

                @pl.when(p.has_up())
                def _():
                    self.to_up(s + 1).start()

            self.to_sibling(p.z - s).start()

        @pl.when(p.z + s < self.n)
        def _():
            self.arrived(p.z + s, self.sems.at[9 + s - 1])
            if s < self.n - 1:

                @pl.when(p.has_down())
                def _():
                    self.to_down(s + 1).start()

            self.to_sibling(p.z + s).start()

    def finish(self):
        p = self.p
        if self.own is not None:
            self.local().wait()
        for level in range(self.n):
            view = self.view(level, p.other)
            remote(view, view, self.sems.at[0], self.sems.at[16 + level], p.sibling).wait_recv()

    def drain(self):
        p = self.p
        for s in range(1, self.n):

            @pl.when(p.has_up() & (p.z >= s - 1))
            def _():
                self.to_up(s).wait_send()

            @pl.when(p.has_down() & (p.z + s - 1 < self.n))
            def _():
                self.to_down(s).wait_send()

        for level in range(self.n):
            self.to_sibling(level).wait_send()


class PlaneGather:
    SEMS = 8

    def __init__(self, place, view, half, sems, own=None):
        self.p, self.view, self.half, self.sems = place, view, half, sems
        self.own = own

    def src(self):
        return self.view(self.p.c) if self.own is None else self.own

    def to_x(self):
        p = self.p
        return remote(self.src(), self.view(p.c), self.sems.at[0], self.sems.at[2], p.x)

    def to_y(self):
        p = self.p
        return remote(self.src(), self.view(p.c), self.sems.at[1], self.sems.at[3], p.y)

    def on_to_y(self):
        p, h = self.p, self.half(self.p.cx, 0)
        return remote(h, h, self.sems.at[4], self.sems.at[6], p.y)

    def on_to_x(self):
        p, h = self.p, self.half(self.p.cy, 1)
        return remote(h, h, self.sems.at[5], self.sems.at[7], p.x)

    def start(self):
        self.to_x().start()
        self.to_y().start()

    def got(self, ref, sem):
        remote(ref, ref, self.sems.at[0], sem, self.p.x).wait_recv()

    def middle(self):
        p = self.p
        self.got(self.view(p.cx), self.sems.at[2])
        self.on_to_y().start()
        self.got(self.view(p.cy), self.sems.at[3])
        self.on_to_x().start()

    def finish(self):
        p = self.p
        self.got(self.half(p.cd, 0), self.sems.at[6])
        self.got(self.half(p.cd, 1), self.sems.at[7])

    def drain(self):
        self.to_x().wait_send()
        self.to_y().wait_send()
        self.on_to_y().wait_send()
        self.on_to_x().wait_send()


def rows_at(index, count):
    return pl.ds(pl.multiple_of(index * count, count), count)


def any_spec(count):
    return [pl.BlockSpec(memory_space=pl.ANY)] * count


def call(kernel, ins, outs, scratch, collective_id, flops, name, vmem=60.0):
    return pl.pallas_call(
        kernel,
        out_shape=[jax.ShapeDtypeStruct(s, d) for s, d in outs],
        in_specs=any_spec(len(ins)),
        out_specs=any_spec(len(outs)),
        scratch_shapes=scratch,
        compiler_params=pltpu.CompilerParams(
            collective_id=collective_id, has_side_effects=True, vmem_limit_bytes=int(vmem * 2**20)
        ),
        cost_estimate=pl.CostEstimate(flops=flops, bytes_accessed=2**26, transcendentals=2**22),
        name=name,
    )(*ins)


def tiles_of(total, most):
    sizes, at = [], 0
    while at < total:
        sizes.append((at, min(most, total - at)))
        at += most
    return sizes


def add_to(ref, other):
    for start, size in tiles_of(ref.shape[0], 96):
        at = pl.ds(start, size)
        ref[at, :] = (ref[at, :].astype(f32) + other[at, :].astype(f32)).astype(bf16)


class PlaneScatter:
    SEMS = 8

    def __init__(self, place, part, half, first, second, sems):
        self.p, self.part, self.half = place, part, half
        self.first, self.second, self.sems = first, second, sems

    def ref(self):
        return self.part(self.p.c)

    def far_to_y(self):
        p = self.p
        return remote(self.half(p.cd, 0), self.first.at[0], self.sems.at[0], self.sems.at[2], p.y)

    def far_to_x(self):
        p = self.p
        return remote(self.half(p.cd, 1), self.first.at[1], self.sems.at[1], self.sems.at[3], p.x)

    def to_x(self):
        p = self.p
        return remote(self.part(p.cx), self.second.at[0], self.sems.at[4], self.sems.at[6], p.x)

    def to_y(self):
        p = self.p
        return remote(self.part(p.cy), self.second.at[1], self.sems.at[5], self.sems.at[7], p.y)

    def start(self):
        self.far_to_y().start()
        self.far_to_x().start()

    def got(self, ref, sem):
        remote(ref, ref, self.sems.at[0], sem, self.p.x).wait_recv()

    def add(self, ref, other):
        add_to(ref, other)

    def middle(self):
        p = self.p
        self.got(self.first.at[0], self.sems.at[2])
        self.add(self.half(p.cx, 0), self.first.at[0])
        self.to_x().start()
        self.got(self.first.at[1], self.sems.at[3])
        self.add(self.half(p.cy, 1), self.first.at[1])
        self.to_y().start()

    def finish(self, at=slice(None), first=True):
        if first:
            self.got(self.second.at[0], self.sems.at[6])
            self.got(self.second.at[1], self.sems.at[7])
        own = self.part(self.p.c)[at].astype(f32)
        return own + self.second[0, at].astype(f32) + self.second[1, at].astype(f32)

    def drain(self):
        self.far_to_y().wait_send()
        self.far_to_x().wait_send()
        self.to_x().wait_send()
        self.to_y().wait_send()


class LineScatter:
    SEMS = 22

    def __init__(self, place, part, acc, slots, sems, stage=None):
        self.p, self.part, self.acc, self.slots, self.sems = place, part, acc, slots, sems
        self.stage = stage
        self.n = place.depth

    def to_sibling(self, level):
        p = self.p
        return remote(
            self.part(level, p.other), self.acc.at[level], self.sems.at[level], self.sems.at[4 + level], p.sibling
        )

    def start(self):
        for level in range(self.n):
            self.to_sibling(level).start()

    def load(self, level):
        return pltpu.make_async_copy(
            self.part(level, self.p.core), self.stage[level % 2], self.sems.at[20 + level % 2]
        )

    def got(self, ref, sem):
        remote(ref, ref, self.sems.at[0], sem, self.p.sibling).wait_recv()

    def add(self, ref, other):
        add_to(ref, other)

    def combine(self):
        if self.stage is not None:
            self.load(0).start()
            self.load(1).start()
        for level in range(self.n):
            self.got(self.acc.at[level], self.sems.at[4 + level])
            if self.stage is None:
                self.add(self.acc.at[level], self.part(level, self.p.core))
            else:
                self.load(level).wait()
                self.add(self.acc.at[level], self.stage[level % 2])
                if level + 2 < self.n:
                    self.load(level + 2).start()

    def slot(self, up, s):
        return self.slots.at[s - 1] if up else self.slots.at[(0, 3, 4)[s - 1]]

    def along(self, up, s):
        p = self.p
        level = p.z if up else self.n - 1 - p.z
        block = self.n - s + level
        block = block if up else self.n - 1 - block
        base = 8 if up else 14
        copy = remote(
            self.acc.at[block],
            self.slot(up, s),
            self.sems.at[base + s - 1],
            self.sems.at[base + 3 + s - 1],
            p.up if up else p.down,
        )
        return copy, (level <= s - 1) & (level < self.n - 1)

    def step(self, s):
        for up in (True, False):
            level = self.p.z if up else self.n - 1 - self.p.z
            if s > 1:
                block = self.n - s + level
                block = block if up else self.n - 1 - block
                base = 11 if up else 17

                @pl.when((level >= 1) & (s - 1 >= level))
                def _():
                    self.got(self.slot(up, s - 1), self.sems.at[base + s - 2])
                    self.add(self.acc.at[block], self.slot(up, s - 1))

            if s < self.n:
                copy, valid = self.along(up, s)

                @pl.when(valid)
                def _():
                    copy.start()

    def result(self):
        return self.acc.at[self.p.z]

    def drain(self):
        for level in range(self.n):
            self.to_sibling(level).wait_send()
        for up in (True, False):
            for s in range(1, self.n):
                copy, valid = self.along(up, s)

                @pl.when(valid)
                def _():
                    copy.wait_send()


def forward_kernel(
    tok, tab, w_query, w_key, w_value, w_out, w_gate, w_up,
    xn_out, r_out, grow_out, gcol_out, qt_out, kt_out, vt_out, lse_out, o_out, m_out,
    wqkv_out, wout_out, wgate, wup, tab_out,
    X, XN, QT, KT, VT, K, LSE, O, M, WQ, WO, TAB, G8, GROW, BIAS, OT, R1,
    WK, WV, GF, UF, GO, UO, GCOL, GOWN,
    line_sems, plane_sems, copy_sems,
):
    p = Place()
    n_ctx = 4
    rows = tok.shape[0]
    half = rows // 2
    qw = QT.shape[0]
    heads = qw // HEAD_DIM
    cw = O.shape[1] // n_ctx
    scale = HEAD_DIM ** (-0.5)

    mine = rows_at(p.f, WK.shape[0])
    loads = []
    for i, (src, dst) in enumerate(
        (
            (w_query.at[:, rows_at(p.c, qw)], WQ.at[mine, pl.ds(0, qw)]),
            (w_key, WK), (w_value, WV), (w_gate, GF), (w_up, UF), (tab, TAB.at[p.c]),
        )
    ):
        loads.append(pltpu.make_async_copy(src, dst, copy_sems.at[15 + i]))
        loads[-1].start()

    p.barrier()

    gain_line = LineGather(p, GOWN, G8, line_sems.at[0])
    qkv_line = LineGather(p, None, WQ, line_sems.at[1])
    out_line = LineGather(p, w_out.at[:, rows_at(p.c, cw)], WO, line_sems.at[2])
    gate_line = LineGather(p, GO, wgate, line_sems.at[3])
    up_line = LineGather(p, UO, wup, line_sems.at[4])

    def row_block(ref):
        return (
            lambda c: ref.at[rows_at(c, rows)],
            lambda c, h: ref.at[pl.ds(pl.multiple_of(c * rows + h * half, half), half)],
        )

    tok_plane = PlaneGather(p, *row_block(X), plane_sems.at[0], own=tok)
    tab_rows = tab.shape[0]
    tab_plane = PlaneGather(
        p,
        lambda c: TAB.at[c],
        lambda c, h: TAB.at[c, pl.ds(h * (tab_rows // 2), tab_rows // 2)],
        plane_sems.at[2],
        own=tab,
    )

    def col_block(ref, b):
        def view(c):
            return ref.at[pl.ds(b * rows, rows), rows_at(c, cw)]

        def halves(c, h):
            return ref.at[pl.ds(b * rows + h * half, half), rows_at(c, cw)]

        return view, halves

    o_plane = [PlaneGather(p, *col_block(O, b), plane_sems.at[3 + b]) for b in range(n_ctx)]
    m_plane = [PlaneGather(p, *col_block(M, b), plane_sems.at[7 + b]) for b in range(n_ctx)]

    tab_plane.start()
    tok_plane.start()
    out_line.start()
    loads[5].wait()
    GOWN[...] = jnp.broadcast_to(TAB[p.c, 72:73, :], GOWN.shape).astype(bf16)
    gain_line.start()
    GCOL[:, 0:8] = TAB[p.c, 72:80, :].T
    for i in range(3):
        loads[i].wait()
    for c in range(n_ctx):

        @pl.when(p.c == c)
        def _():
            WQ[mine, qw : qw + HEAD_DIM] = WK[:, HEAD_DIM * c : HEAD_DIM * (c + 1)]
            WQ[mine, qw + HEAD_DIM :] = WV[:, HEAD_DIM * c : HEAD_DIM * (c + 1)]

    qkv_line.start()
    own_tok = pltpu.make_async_copy(tok, X.at[rows_at(p.c, rows)], copy_sems.at[0])
    own_tok.start()

    for i in range(3, 5):
        loads[i].wait()
    unit = GO.shape[1] // (2 * p.depth)
    for c in range(n_ctx):

        @pl.when(p.c == c)
        def _():
            for f in range(2 * p.depth):
                at = (f * n_ctx + c) * unit
                for src, dst in ((GF, GO), (UF, UO)):
                    part = src[:, at : at + unit].astype(f32) * GCOL[:, 4:5]
                    dst[:, f * unit : (f + 1) * unit] = part.astype(bf16)

    gain_line.hop(1)
    tab_plane.middle()
    gain_line.hop(2)
    qkv_line.hop(1)
    gain_line.hop(3)
    gain_line.finish()
    for f in range(2 * p.depth):
        GROW[:, f * GOWN.shape[1] : (f + 1) * GOWN.shape[1]] = G8[16 * f : 16 * f + 8, :].astype(f32)

    def norm(c):
        at = rows_at(c, rows)
        x = X[at, :].astype(f32)
        r = lax.rsqrt(jnp.mean(x * x, axis=-1, keepdims=True) + eps_norm)
        R1[at, :] = jnp.broadcast_to(r, (rows, 128))
        XN[at, :] = (x * r * GROW[0:1, :]).astype(bf16)

    own_tok.wait()
    norm(p.c)
    out_line.hop(1)
    qkv_line.hop(2)
    tok_plane.middle()
    out_line.hop(2)
    gate_line.start()
    norm(p.cx)
    norm(p.cy)
    qkv_line.hop(3)
    tok_plane.finish()
    out_line.hop(3)
    up_line.start()
    norm(p.cd)
    xn_copy = pltpu.make_async_copy(XN, xn_out, copy_sems.at[3])
    r_copy = pltpu.make_async_copy(R1, r_out, copy_sems.at[4])
    grow_copy = pltpu.make_async_copy(GROW, grow_out, copy_sems.at[14])
    xn_copy.start()
    r_copy.start()
    grow_copy.start()
    tab_plane.finish()
    qkv_line.finish()

    @pl.loop(0, n_ctx)
    def _(b):
        at = rows_at(b, rows)
        pre = dot(XN[at, :], WQ[...]).T
        cosine = TAB[b, 0:32, :]
        sine = TAB[b, 32:64, :]
        for h in range(heads + 1):
            u = pre[64 * h : 64 * h + 32]
            w = pre[64 * h + 32 : 64 * h + 64]
            first = u * cosine - w * sine
            second = w * cosine + u * sine
            if h < heads:
                QT[64 * h : 64 * h + 32, at] = first.astype(bf16)
                QT[64 * h + 32 : 64 * h + 64, at] = second.astype(bf16)
            else:
                KT[0:32, at] = first.astype(bf16)
                KT[32:64, at] = second.astype(bf16)
                K[at, :] = jnp.concatenate([first, second], axis=0).T.astype(bf16)
        VT[:, at] = pre[qw + 64 :].astype(bf16)

    wq_copy = pltpu.make_async_copy(WQ, wqkv_out, copy_sems.at[5])
    wq_copy.start()

    def attend(b):
        n = (b + 1) * rows
        key = lax.broadcasted_iota(jnp.int32, (n, rows), 0)
        query = lax.broadcasted_iota(jnp.int32, (n, rows), 1) + b * rows
        begin = TAB[b, 64:65, :].astype(jnp.int32)
        BIAS[0:n, :] = jnp.where((key <= query) & (key >= begin), 0.0, neg_large)
        cols = slice(b * rows, (b + 1) * rows)

        @pl.loop(0, heads)
        def _(h):
            head = rows_at(h, HEAD_DIM)
            s = dot(K[0:n, :], QT[head, cols]) * scale + BIAS[0:n, :]
            top = jnp.max(s, axis=0, keepdims=True)
            e = jnp.exp(s - top)
            total = jnp.sum(e, axis=0, keepdims=True)
            probs = (e * (1.0 / total)).astype(bf16)
            OT[head, :] = dot(VT[:, 0:n], probs)
            LSE[rows_at(h, 8), cols] = jnp.broadcast_to(top + jnp.log(total), (8, rows))

        O[pl.ds(b * rows, rows), rows_at(p.c, cw)] = OT[...].T.astype(bf16)
        o_plane[b].start()

    def middle(b):
        at = pl.ds(b * rows, rows)
        cols = rows_at(p.c, cw)
        mid = X[at, cols].astype(f32) + dot(O[at, :], WO[...])
        M[at, cols] = mid.astype(bf16)
        m_plane[b].start()

    attend(0)
    attend(1)
    o_plane[0].middle()
    attend(2)
    gate_line.hop(1)
    o_plane[1].middle()
    attend(3)
    o_plane[2].middle()
    out_line.finish()
    o_plane[0].finish()
    middle(0)
    o_plane[1].finish()
    middle(1)
    o_plane[3].middle()
    up_line.hop(1)
    m_plane[0].middle()
    o_plane[2].finish()
    middle(2)
    m_plane[1].middle()
    o_plane[3].finish()
    middle(3)
    m_plane[2].middle()
    gate_line.hop(2)
    m_plane[3].middle()
    up_line.hop(2)
    gcol_copy = pltpu.make_async_copy(GCOL, gcol_out, copy_sems.at[1])
    gcol_copy.start()
    copies = [xn_copy, r_copy, grow_copy, gcol_copy, wq_copy]
    for i, (src, dst) in enumerate(
        ((QT, qt_out), (KT, kt_out), (VT, vt_out), (LSE, lse_out), (O, o_out), (WO, wout_out), (TAB, tab_out))
    ):
        copy = pltpu.make_async_copy(src, dst, copy_sems.at[6 + i])
        copy.start()
        copies.append(copy)
    for b in range(n_ctx):
        m_plane[b].finish()
    m_copy = pltpu.make_async_copy(M, m_out, copy_sems.at[13])
    m_copy.start()
    copies.append(m_copy)
    gate_line.hop(3)
    up_line.hop(3)
    gate_line.finish()
    up_line.finish()
    for copy in copies:
        copy.wait()
    for line in (gain_line, qkv_line, out_line, gate_line, up_line):
        line.drain()
    for plane in [tok_plane, tab_plane] + o_plane + m_plane:
        plane.drain()


def forward_stage(tok, tab, w_query, w_key, w_value, w_out, w_gate, w_up):
    n_fsdp, n_ctx = lax.axis_size("fsdp"), lax.axis_size("ctx")
    rows, width = tok.shape
    seq = rows * n_ctx
    own = w_query.shape[0]
    whole = n_fsdp * own
    qw = HEADS // n_ctx * HEAD_DIM
    nq, nw, nu = qw + 2 * HEAD_DIM, width // n_ctx, w_gate.shape[1] // n_ctx
    heads = qw // HEAD_DIM
    tab_shape = (n_ctx,) + tab.shape
    outs = [
        ((seq, width), bf16), ((seq, 128), f32), ((8, width), f32), ((own, 128), f32), ((qw, seq), bf16), ((64, seq), bf16),
        ((64, seq), bf16), ((8 * heads, seq), f32), ((seq, width), bf16), ((seq, width), bf16), ((whole, nq), bf16),
        ((whole, nw), bf16), ((whole, nu), bf16), ((whole, nu), bf16), (tab_shape, f32),
    ]
    scratch = [
        pltpu.VMEM((seq, width), bf16),
        pltpu.VMEM((seq, width), bf16),
        pltpu.VMEM((qw, seq), bf16),
        pltpu.VMEM((64, seq), bf16),
        pltpu.VMEM((64, seq), bf16),
        pltpu.VMEM((seq, 64), bf16),
        pltpu.VMEM((8 * heads, seq), f32),
        pltpu.VMEM((seq, width), bf16),
        pltpu.VMEM((seq, width), bf16),
        pltpu.VMEM((whole, nq), bf16),
        pltpu.VMEM((whole, nw), bf16),
        pltpu.VMEM(tab_shape, f32),
        pltpu.VMEM((16 * n_fsdp, own), bf16),
        pltpu.VMEM((8, width), f32),
        pltpu.VMEM((seq, rows), f32),
        pltpu.VMEM((qw, rows), f32),
        pltpu.VMEM((seq, 128), f32),
        pltpu.VMEM(w_key.shape, bf16),
        pltpu.VMEM(w_value.shape, bf16),
        pltpu.VMEM(w_gate.shape, bf16),
        pltpu.VMEM(w_up.shape, bf16),
        pltpu.VMEM((own, nu), bf16),
        pltpu.VMEM((own, nu), bf16),
        pltpu.VMEM((own, 128), f32),
        pltpu.VMEM((16, own), bf16),
        pltpu.SemaphoreType.DMA((5, LineGather.SEMS)),
        pltpu.SemaphoreType.DMA((11, PlaneGather.SEMS)),
        pltpu.SemaphoreType.DMA((21,)),
    ]
    ins = (tok, tab, w_query, w_key, w_value, w_out, w_gate, w_up)
    flops = 2 * seq * width * (nq + nw) + 8 * heads * seq * seq * HEAD_DIM
    return call(forward_kernel, ins, outs, scratch, 1, flops, "forward_stage")


def middle_kernel(
    m_in, cot, wgate_in, wup_in, w_down,
    y_out, down_part, down_sum, gate_part, up_part, gm_out,
    M, COT, WG, WU, WD, GATE, UP, HID, R2, PD, PH, D1, D2, H1, H2, DACC, DSLOT,
    line_sems, sum_sems, plane_sems, copy_sems, stage_sems,
):
    p = Place()
    n_ctx = 4
    seq, width = M.shape
    rows = seq // n_ctx
    half = rows // 2
    cw = width // n_ctx
    units = GATE.shape[1]
    loads = []
    for i, (src, dst) in enumerate(((m_in, M), (wgate_in, WG), (wup_in, WU), (cot, COT.at[rows_at(p.c, rows)]))):
        loads.append(pltpu.make_async_copy(src, dst, copy_sems.at[i]))
        loads[-1].start()

    p.barrier()
    unit = w_down.shape[0] // n_ctx
    down_own = w_down.at[pl.ds(pl.multiple_of(p.c * unit, 16), unit)]
    down_line = LineGather(p, down_own, WD, line_sems.at[0])
    down_line.start()
    cot_plane = PlaneGather(
        p,
        lambda c: COT.at[rows_at(c, rows)],
        lambda c, h: COT.at[pl.ds(pl.multiple_of(c * rows + h * half, half), half)],
        plane_sems.at[5],
        own=cot,
    )
    cot_plane.start()

    loads[0].wait()
    loads[1].wait()
    loads[2].wait()

    def activate(b):
        at = rows_at(b, rows)
        mf = M[at, :].astype(f32)
        r = lax.rsqrt(jnp.mean(mf * mf, axis=-1, keepdims=True) + eps_norm)
        R2[at, :] = jnp.broadcast_to(r, (rows, 128))
        for start, size in tiles_of(units, 512):
            cols = slice(start, start + size)
            gate = dot(M[at, :], WG[:, cols]) * r
            up = dot(M[at, :], WU[:, cols]) * r
            GATE[at, cols] = gate.astype(bf16)
            UP[at, cols] = up.astype(bf16)
            HID[at, cols] = (gate * (1.0 / (1.0 + jnp.exp(-gate))) * up).astype(bf16)

    pl.loop(0, 2)(activate)
    down_line.hop(1)
    pl.loop(2, 4)(activate)
    cot_plane.middle()
    down_line.hop(2)
    loads[3].wait()
    cot_plane.finish()
    stage_copies = {}
    for i, (at, size) in enumerate(tiles_of(units, rows)):
        slot = pl.ds(i % 2 * rows, size)
        if i >= 2:
            stage_copies[i - 2].wait()
        for j in range(0, width, cw):
            PH[slot, j : j + cw] = dot_tn(HID[:, at : at + size], COT[:, j : j + cw]).astype(bf16)
        copy = pltpu.make_async_copy(PH.at[slot], down_part.at[pl.ds(at, size)], stage_sems.at[i % 2])
        copy.start()
        stage_copies[i] = copy
    n_down = len(stage_copies)
    stage_copies[n_down - 2].wait()
    stage_copies[n_down - 1].wait()

    def down_block(level, core):
        return down_part.at[pl.ds(pl.multiple_of((2 * level + core) * unit, 16), unit)]

    down_stage = [PH.at[pl.ds(i * rows, unit)] for i in range(2)]
    sum_line = LineScatter(p, down_block, DACC, DSLOT, sum_sems.at[0], down_stage)
    sum_line.start()
    down_line.hop(3)
    down_line.finish()

    y_plane = PlaneScatter(
        p,
        lambda c: PD.at[rows_at(c, rows)],
        lambda c, h: PD.at[pl.ds(pl.multiple_of(c * rows + h * half, half), half)],
        D1,
        D2,
        plane_sems.at[0],
    )

    def col_scatter(b):
        return PlaneScatter(
            p,
            lambda c: PH.at[pl.ds(b * rows, rows), rows_at(c, cw)],
            lambda c, h: PH.at[pl.ds(b * rows + h * half, half), rows_at(c, cw)],
            H1.at[b],
            H2.at[b],
            plane_sems.at[1 + b],
        )

    h_plane = [col_scatter(b) for b in range(n_ctx)]

    def partial_out(c):
        at = rows_at(c, rows)
        for j in range(0, width, cw):
            PD[at, j : j + cw] = dot(HID[at, :], WD[:, j : j + cw]).astype(bf16)

    partial_out(p.cd)
    y_plane.start()
    partial_out(p.cx)
    partial_out(p.cy)
    sum_line.combine()
    sum_line.step(1)
    partial_out(p.c)

    def grads(b):
        at = pl.ds(b * rows, rows)
        r = R2[at, 0:1]
        stat = jnp.zeros((rows, 1), f32)
        for start, size in tiles_of(units, 512):
            cols = slice(start, start + size)
            grad_hidden = dot_nt(COT[at, :], WD[cols, :])
            gate = GATE[at, cols].astype(f32)
            up = UP[at, cols].astype(f32)
            sig = 1.0 / (1.0 + jnp.exp(-gate))
            d_up = grad_hidden * gate * sig
            d_gate = grad_hidden * up * sig * (1.0 + gate * (1.0 - sig))
            stat += jnp.sum(d_gate * gate + d_up * up, axis=-1, keepdims=True)
            GATE[at, cols] = (d_gate * r).astype(bf16)
            UP[at, cols] = (d_up * r).astype(bf16)
        R2[at, :] = jnp.broadcast_to(r * r * stat * (1.0 / width), (rows, 128))

    def push(b):
        at = pl.ds(b * rows, rows)
        coef = R2[at, 0:1]
        for j in range(0, width, cw):
            e = dot_nt(GATE[at, :], WG[j : j + cw, :]) + dot_nt(UP[at, :], WU[j : j + cw, :])
            PH[at, j : j + cw] = (e - M[at, j : j + cw].astype(f32) * coef).astype(bf16)
        h_plane[b].start()

    grads(0)
    y_plane.middle()
    push(0)
    grads(1)
    push(1)
    h_plane[0].middle()
    grads(2)
    sum_line.step(2)
    push(2)
    h_plane[1].middle()
    grads(3)
    push(3)
    h_plane[2].middle()

    stage_copies = {}
    jobs = []
    for src, dst in ((GATE, gate_part), (UP, up_part)):
        for at, size in tiles_of(width, 512):
            jobs.append((src, dst, at, size))

    def weight_tile(i):
        src, dst, at, size = jobs[i]
        slot = pl.ds(i % 2 * size, size)
        if i >= 2:
            stage_copies[i - 2].wait()
        for start, part in tiles_of(units, 512):
            cols = slice(start, start + part)
            HID[slot, cols] = dot_tn(M[:, at : at + size], src[:, cols]).astype(bf16)
        copy = pltpu.make_async_copy(HID.at[slot], dst.at[pl.ds(at, size)], stage_sems.at[2 + i % 2])
        copy.start()
        stage_copies[i] = copy

    def finish_block(b):
        at = pl.ds(b * rows, rows)
        mine = rows_at(p.c, cw)
        COT[at, mine] = (COT[at, mine].astype(f32) + h_plane[b].finish()).astype(bf16)

    weight_tile(0)
    cot_plane.drain()
    sum_line.step(3)
    h_plane[3].middle()
    weight_tile(1)
    weight_tile(2)
    finish_block(0)
    weight_tile(3)
    weight_tile(4)
    finish_block(1)
    weight_tile(5)
    weight_tile(6)
    finish_block(2)
    weight_tile(7)
    sum_line.step(4)
    sum_copy = pltpu.make_async_copy(sum_line.result(), down_sum, copy_sems.at[6])
    sum_copy.start()
    piece = rows // n_ctx
    for i in range(n_ctx):
        own = pl.ds(pl.multiple_of(p.c * rows + i * piece, piece), piece)
        mlp = y_plane.finish(pl.ds(i * piece, piece), i == 0)
        PD[own, :] = (M[own, :].astype(f32) + mlp).astype(bf16)
    y_copy = pltpu.make_async_copy(PD.at[rows_at(p.c, rows)], y_out, copy_sems.at[4])
    y_copy.start()
    finish_block(3)
    gm_copy = pltpu.make_async_copy(COT.at[:, rows_at(p.c, cw)], gm_out, copy_sems.at[5])
    gm_copy.start()
    stage_copies[6].wait()
    stage_copies[7].wait()
    y_copy.wait()
    gm_copy.wait()
    sum_copy.wait()
    sum_line.drain()
    down_line.drain()
    y_plane.drain()
    for b in range(n_ctx):
        h_plane[b].drain()


def middle_stage(m, cot, wgate, wup, w_down):
    n_fsdp, n_ctx = lax.axis_size("fsdp"), lax.axis_size("ctx")
    seq, width = m.shape
    rows = seq // n_ctx
    cw = width // n_ctx
    units = wgate.shape[1]
    unit = units // n_fsdp
    outs = [
        ((rows, width), bf16), ((units, width), bf16), ((unit, width), bf16), ((width, units), bf16),
        ((width, units), bf16), ((seq, cw), bf16),
    ]
    scratch = [
        pltpu.VMEM((seq, width), bf16),
        pltpu.VMEM((seq, width), bf16),
        pltpu.VMEM((width, units), bf16),
        pltpu.VMEM((width, units), bf16),
        pltpu.VMEM((units, width), bf16),
        pltpu.VMEM((seq, units), bf16),
        pltpu.VMEM((seq, units), bf16),
        pltpu.VMEM((seq, units), bf16),
        pltpu.VMEM((seq, 128), f32),
        pltpu.VMEM((seq, width), bf16),
        pltpu.VMEM((seq, width), bf16),
        pltpu.VMEM((2, rows // 2, width), bf16),
        pltpu.VMEM((2, rows, width), bf16),
        pltpu.VMEM((n_ctx, 2, rows // 2, cw), bf16),
        pltpu.VMEM((n_ctx, 2, rows, cw), bf16),
        pltpu.VMEM((n_fsdp // 2, unit, width), bf16),
        pltpu.VMEM((5, unit, width), bf16),
        pltpu.SemaphoreType.DMA((1, LineGather.SEMS)),
        pltpu.SemaphoreType.DMA((1, LineScatter.SEMS)),
        pltpu.SemaphoreType.DMA((6, PlaneScatter.SEMS)),
        pltpu.SemaphoreType.DMA((7,)),
        pltpu.SemaphoreType.DMA((4,)),
    ]
    flops = 18 * seq * width * units
    return call(middle_kernel, (m, cot, wgate, wup, w_down), outs, scratch, 2, flops, "middle_stage")


def backward_kernel(
    xn_in, r_in, grow_in, qt_in, kt_in, vt_in, lse_in, o_in, gm_in, wqkv_in, wout_in, tab_in,
    gate_part, up_part, down_sum,
    tok_out, qkv_all, out_all, gate_all, up_all, down_all,
    XN, R1, GROW, QT, KT, VT, LSE, O, GM, WQ, WO, TAB,
    K, V, DK, DV, DOT, DQT, DPRE, STAT, BIAS, PT, G1, G2, T1, T2, TOK,
    GACC, GSLOT, UACC, USLOT, OACC, OSLOT, QACC, QSLOT,
    line_sems, plane_sems, scatter_sems, copy_sems,
):
    p = Place()
    n_ctx = 4
    seq, width = XN.shape
    rows = seq // n_ctx
    half = rows // 2
    cw = width // n_ctx
    qw = QT.shape[0]
    heads = qw // HEAD_DIM
    nq = WQ.shape[1]
    own_rows = QACC.shape[1]
    scale = HEAD_DIM ** (-0.5)
    loads = []
    for i, (src, dst) in enumerate(
        (
            (gm_in, GM), (wout_in, WO), (o_in, O), (kt_in, KT), (vt_in, VT), (qt_in, QT), (lse_in, LSE),
            (tab_in, TAB), (xn_in, XN), (wqkv_in, WQ), (r_in, R1), (grow_in, GROW),
        )
    ):
        loads.append(pltpu.make_async_copy(src, dst, copy_sems.at[i]))
    loads[0].start()
    loads[1].start()

    p.barrier()

    def block_rows(ref):
        count = ref.shape[0] // (2 * p.depth)
        return lambda level, core: ref.at[pl.ds(pl.multiple_of((2 * level + core) * count, 16), count)]

    nu = GACC.shape[2]
    cols_stage = [XN.at[pl.ds(i * own_rows, own_rows), pl.ds(0, nu)] for i in range(2)]
    gate_line = LineScatter(p, block_rows(gate_part), GACC, GSLOT, line_sems.at[1], cols_stage)
    up_line = LineScatter(p, block_rows(up_part), UACC, USLOT, line_sems.at[2], cols_stage)
    out_line = LineScatter(p, block_rows(WO), OACC, OSLOT, line_sems.at[3])

    def qkv_block(level, core):
        f = 2 * level + core
        at = pl.ds(pl.multiple_of((f % p.depth) * own_rows, own_rows), own_rows)
        return O.at[at, pl.ds(pl.multiple_of((f // p.depth) * nq, 128), nq)]

    qkv_line = LineScatter(p, qkv_block, QACC, QSLOT, line_sems.at[4])
    gate_line.start()
    up_line.start()
    for i in (2, 3, 4, 5, 6, 7, 9, 10, 11):
        loads[i].start()

    def col_scatter(b):
        return PlaneScatter(
            p,
            lambda c: PT.at[pl.ds(b * rows, rows), rows_at(c, cw)],
            lambda c, h: PT.at[pl.ds(b * rows + h * half, half), rows_at(c, cw)],
            G1.at[b],
            G2.at[b],
            scatter_sems.at[b],
        )

    g_plane = [col_scatter(b) for b in range(n_ctx)]
    t_plane = PlaneScatter(
        p,
        lambda c: PT.at[rows_at(c, rows)],
        lambda c, h: PT.at[pl.ds(pl.multiple_of(c * rows + h * half, half), half)],
        T1,
        T2,
        scatter_sems.at[n_ctx],
    )

    def whole(ref, own, index, first):
        count = own.shape[0]

        def halves(c, h):
            return ref(c).at[pl.ds(h * first, count - first if h else first)]

        plane = PlaneGather(p, ref, halves, plane_sems.at[index], own=own)
        return plane, pltpu.make_async_copy(own, ref(p.c), plane_sems.at[index, PlaneGather.SEMS])

    unit = down_sum.shape[0]
    down_plane, down_own = whole(lambda c: down_all.at[c], down_sum, 0, unit // 32 * 16 + unit // 16 % 2 * 16)
    gate_plane, gate_own = whole(lambda c: gate_all.at[c], gate_line.result(), 1, own_rows // 2)
    up_plane, up_own = whole(lambda c: up_all.at[c], up_line.result(), 2, own_rows // 2)
    out_plane, out_own = whole(lambda c: out_all.at[c], out_line.result(), 3, own_rows // 2)
    qkv_plane, qkv_own = whole(lambda c: qkv_all.at[c], qkv_line.result(), 4, own_rows // 2)

    loads[0].wait()
    loads[1].wait()
    for b in range(n_ctx):
        at = pl.ds(b * rows, rows)
        for j in range(0, width, 512):
            PT[at, j : j + 512] = dot_nt(GM[at, :], WO[j : j + 512, :]).astype(bf16)
        g_plane[b].start()
    gate_line.combine()
    gate_line.step(1)
    g_plane[0].middle()
    loads[2].wait()

    @pl.loop(0, width // 512)
    def _(i):
        at = rows_at(i, 512)
        WO[at, :] = dot_tn(O[:, at], GM[...]).astype(bf16)

    out_line.start()
    g_plane[1].middle()
    up_line.combine()
    loads[8].start()
    up_line.step(1)
    g_plane[2].middle()
    for i in (3, 4, 5, 6, 7, 10):
        loads[i].wait()

    @pl.loop(0, n_ctx)
    def _(b):
        at = rows_at(b, rows)
        K[at, :] = KT[:, at].astype(f32).T.astype(bf16)
        V[at, :] = VT[:, at].astype(f32).T.astype(bf16)
        DK[at, :] = jnp.zeros((rows, HEAD_DIM), f32)
        DV[at, :] = jnp.zeros((rows, HEAD_DIM), f32)

    g_plane[3].middle()

    def attend_back(b):
        n = (b + 1) * rows
        cols = slice(b * rows, (b + 1) * rows)
        DOT[...] = g_plane[b].finish().T.astype(bf16)
        at = pl.ds(b * rows, rows)
        DQT[...] = O[at, rows_at(p.c, cw)].astype(f32).T
        key = lax.broadcasted_iota(jnp.int32, (n, rows), 0)
        query = lax.broadcasted_iota(jnp.int32, (n, rows), 1) + b * rows
        begin = TAB[b, 64:65, :].astype(jnp.int32)
        BIAS[0:n, :] = jnp.where((key <= query) & (key >= begin), 0.0, neg_large)
        STAT[...] = jnp.zeros((8, rows), f32)

        @pl.loop(0, heads)
        def _(h):
            head = rows_at(h, HEAD_DIM)
            q = QT[head, cols]
            d_out = DOT[head, :]
            delta = jnp.sum(d_out.astype(f32) * DQT[head, :], axis=0, keepdims=True)
            s = dot(K[0:n, :], q) * scale + BIAS[0:n, :]
            probs = jnp.exp(s - LSE[rows_at(h, 8), cols][0:1])
            d_probs = dot(V[0:n, :], d_out)
            d_s = (probs * (d_probs - delta)).astype(bf16)
            d_q = dot(KT[:, 0:n], d_s) * scale
            DK[0:n, :] += dot_nt(d_s, q) * scale
            DV[0:n, :] += dot_nt(probs.astype(bf16), d_out)
            STAT[...] += jnp.broadcast_to(jnp.sum(d_q * q.astype(f32), axis=0, keepdims=True), (8, rows))
            u, w = d_q[0:32], d_q[32:64]
            cosine, sine = TAB[b, 0:32, :], TAB[b, 32:64, :]
            DQT[head, :] = jnp.concatenate([u * cosine + w * sine, w * cosine - u * sine], axis=0)

        DPRE[at, 0:qw] = DQT[...].T.astype(bf16)
        R1[at, 0:8] = STAT[...].T

    attend_back(0)
    gate_line.step(2)
    attend_back(1)
    attend_back(2)
    down_plane.start()
    down_own.start()
    up_line.step(2)
    attend_back(3)
    loads[8].wait()
    loads[9].wait()
    loads[11].wait()

    @pl.loop(0, n_ctx)
    def _(b):
        at = rows_at(b, rows)
        d_k = DK[at, :].T
        d_v = DV[at, :].T
        stat = jnp.sum(d_k * KT[:, at].astype(f32) + d_v * VT[:, at].astype(f32), axis=0, keepdims=True)
        R1[at, 0:8] += jnp.broadcast_to(stat, (8, rows)).T
        u, w = d_k[0:32], d_k[32:64]
        cosine, sine = TAB[b, 0:32, :], TAB[b, 32:64, :]
        both = jnp.concatenate([u * cosine + w * sine, w * cosine - u * sine, d_v], axis=0)
        DPRE[at, qw:] = both.T.astype(bf16)

    def tokens(c):
        at = rows_at(c, rows)
        r = R1[at, 127:128]
        coef = r * R1[at, 0:1] * (1.0 / width)
        for j in range(0, width, 512):
            cols = slice(j, j + 512)
            gain = GROW[0:1, cols]
            e = dot_nt(DPRE[at, :], WQ[cols, :])
            PT[at, cols] = (e * (gain * r) - XN[at, cols].astype(f32) * ((1.0 / gain) * coef)).astype(bf16)
        mine = rows_at(p.c, cw)
        PT[at, mine] = (PT[at, mine].astype(f32) + GM[at, :].astype(f32)).astype(bf16)

    for b in range(n_ctx):
        g_plane[b].drain()
    tokens(p.cd)
    t_plane.start()
    tokens(p.cx)
    tokens(p.cy)
    t_plane.middle()
    tokens(p.c)

    @pl.loop(0, p.depth)
    def _(i):
        for j in range(2):
            at = rows_at(i + j * p.depth, own_rows)
            O[rows_at(i, own_rows), j * nq : (j + 1) * nq] = dot_tn(XN[:, at], DPRE[...]).astype(bf16)

    qkv_line.start()
    gate_line.step(3)
    down_plane.middle()
    out_line.combine()
    out_line.step(1)
    up_line.step(3)
    qkv_line.combine()
    qkv_line.step(1)
    gate_line.step(4)
    gate_plane.start()
    gate_own.start()
    out_line.step(2)
    tok_copies = []
    for i in range(n_ctx):
        if i >= 2:
            tok_copies[i - 2].wait()
        at = pl.ds(i * (rows // n_ctx), rows // n_ctx)
        TOK[i % 2] = t_plane.finish(at, i == 0)
        tok_copies.append(pltpu.make_async_copy(TOK.at[i % 2], tok_out.at[at], copy_sems.at[12 + i % 2]))
        tok_copies[-1].start()
    qkv_line.step(2)
    up_line.step(4)
    up_plane.start()
    up_own.start()
    gate_plane.middle()
    out_line.step(3)
    qkv_line.step(3)
    out_line.step(4)
    out_plane.start()
    out_own.start()
    up_plane.middle()
    qkv_line.step(4)
    qkv_plane.start()
    qkv_own.start()
    out_plane.middle()
    qkv_plane.middle()
    for plane, own in (
        (down_plane, down_own), (gate_plane, gate_own), (up_plane, up_own), (out_plane, out_own), (qkv_plane, qkv_own),
    ):
        plane.finish()
        own.wait()
        plane.drain()
    tok_copies[2].wait()
    tok_copies[3].wait()
    t_plane.drain()
    for line in (gate_line, up_line, out_line, qkv_line):
        line.drain()


def backward_stage(xn, r, grow, qt, kt, vt, lse, o, gm, wqkv, wout, tabs, gate_part, up_part, down_sum):
    n_fsdp, n_ctx = lax.axis_size("fsdp"), lax.axis_size("ctx")
    seq, width = xn.shape
    rows = seq // n_ctx
    half = rows // 2
    cw = width // n_ctx
    own = width // n_fsdp
    depth = n_fsdp // 2
    nq, nu = wqkv.shape[1], gate_part.shape[1]
    unit = down_sum.shape[0]
    qw = qt.shape[0]
    outs = [
        ((rows, width), f32), ((n_ctx, own, nq), bf16), ((n_ctx, own, cw), bf16), ((n_ctx, own, nu), bf16),
        ((n_ctx, own, nu), bf16), ((n_ctx, unit, width), bf16),
    ]
    ins = (xn, r, grow, qt, kt, vt, lse, o, gm, wqkv, wout, tabs, gate_part, up_part, down_sum)
    scratch = [pltpu.VMEM(a.shape, a.dtype) for a in ins[:12]] + [
        pltpu.VMEM((seq, HEAD_DIM), bf16),
        pltpu.VMEM((seq, HEAD_DIM), bf16),
        pltpu.VMEM((seq, HEAD_DIM), f32),
        pltpu.VMEM((seq, HEAD_DIM), f32),
        pltpu.VMEM((qw, rows), bf16),
        pltpu.VMEM((qw, rows), f32),
        pltpu.VMEM((seq, nq), bf16),
        pltpu.VMEM((8, rows), f32),
        pltpu.VMEM((seq, rows), f32),
        pltpu.VMEM((seq, width), bf16),
        pltpu.VMEM((n_ctx, 2, half, cw), bf16),
        pltpu.VMEM((n_ctx, 2, rows, cw), bf16),
        pltpu.VMEM((2, half, width), bf16),
        pltpu.VMEM((2, rows, width), bf16),
        pltpu.VMEM((2, rows // n_ctx, width), f32),
        pltpu.VMEM((depth, own, nu), bf16),
        pltpu.VMEM((5, own, nu), bf16),
        pltpu.VMEM((depth, own, nu), bf16),
        pltpu.VMEM((5, own, nu), bf16),
        pltpu.VMEM((depth, own, cw), bf16),
        pltpu.VMEM((5, own, cw), bf16),
        pltpu.VMEM((depth, own, nq), bf16),
        pltpu.VMEM((5, own, nq), bf16),
        pltpu.SemaphoreType.DMA((5, LineScatter.SEMS)),
        pltpu.SemaphoreType.DMA((5, PlaneGather.SEMS + 1)),
        pltpu.SemaphoreType.DMA((n_ctx + 1, PlaneScatter.SEMS)),
        pltpu.SemaphoreType.DMA((14,)),
    ]
    flops = 4 * seq * width * (nq + cw) + 20 * qw * seq * seq
    return call(backward_kernel, ins, outs, scratch, 3, flops, "backward_stage")


def finish_kernel(
    unit, qkv, out, gate, up, down, tok, y, w_query, w_key, w_value, w_gate, w_up, gcol,
    o_query, o_key, o_value, o_out, o_gate, o_up, o_down, o_tok, o_y, o_g1, o_g2,
):
    n_ctx = qkv.shape[0]
    qw = o_query.shape[1] // n_ctx
    cw = out.shape[2]
    for c in range(n_ctx):
        o_query[:, c * qw : (c + 1) * qw] = qkv[c, :, 0:qw].astype(f32)
        o_key[:, c * HEAD_DIM : (c + 1) * HEAD_DIM] = qkv[c, :, qw : qw + HEAD_DIM].astype(f32)
        o_value[:, c * HEAD_DIM : (c + 1) * HEAD_DIM] = qkv[c, :, qw + HEAD_DIM :].astype(f32)
        o_out[:, c * cw : (c + 1) * cw] = out[c].astype(f32)

    def total(ref, w):
        return jnp.sum(ref[...] * w[...].astype(f32), axis=-1, keepdims=True)

    first = total(o_query, w_query) + total(o_key, w_key) + total(o_value, w_value)
    o_g1[...] = jnp.broadcast_to(first / gcol[:, 0:1], o_g1.shape)
    gain = gcol[:, 4:5]
    for src, dst in ((gate, o_gate), (up, o_up)):
        for f in range(src.shape[2] // unit):
            for c in range(n_ctx):
                at = (f * n_ctx + c) * unit
                dst[:, at : at + unit] = src[c, :, f * unit : (f + 1) * unit].astype(f32) * gain
    second = total(o_gate, w_gate) + total(o_up, w_up)
    o_g2[...] = jnp.broadcast_to(second / gain, o_g2.shape)
    o_down[...] = down[...].astype(f32)
    o_tok[...] = tok[...]
    o_y[...] = y[...]


def finish_stage(qkv, out, gate, up, down, tok, y, w_query, w_key, w_value, w_gate, w_up, gcol):
    steps = 8
    n_fsdp = lax.axis_size("fsdp")
    own = w_query.shape[0]
    down = down.reshape(-1, down.shape[-1])
    unit = gate.shape[2] // n_fsdp

    def spec(shape):
        if len(shape) == 3:
            return pl.BlockSpec((shape[0], shape[1] // steps, shape[2]), lambda i: (0, i, 0))
        if shape == down.shape:
            return pl.BlockSpec((shape[0] // 2, shape[1] // (steps // 2)), lambda i: (i // (steps // 2), i % (steps // 2)))
        return pl.BlockSpec((shape[0] // steps, shape[1]), lambda i: (i, 0))

    ins = (qkv, out, gate, up, down, tok, y, w_query, w_key, w_value, w_gate, w_up, gcol)
    outs = [
        (w_query.shape, f32), (w_key.shape, f32), (w_value.shape, f32), ((own, out.shape[0] * out.shape[2]), f32),
        (w_gate.shape, f32), (w_up.shape, f32), (down.shape, f32), (tok.shape, f32), (y.shape, bf16),
        ((own, 128), f32), ((own, 128), f32),
    ]
    return pl.pallas_call(
        functools.partial(finish_kernel, unit),
        grid=(steps,),
        out_shape=[jax.ShapeDtypeStruct(s, d) for s, d in outs],
        in_specs=[spec(a.shape) for a in ins],
        out_specs=[spec(s) for s, d in outs],
        compiler_params=pltpu.CompilerParams(vmem_limit_bytes=56 * 2**20),
        name="finish_stage",
    )(*ins)


def rotate(field, cosine, sine_table, direction):
    half_width = field.shape[-1] // 2
    first_half = field[..., :half_width]
    second_half = field[..., half_width:]
    return jnp.concatenate(
        [
            first_half * cosine - direction * second_half * sine_table,
            second_half * cosine + direction * first_half * sine_table,
        ],
        axis=-1,
    )


def gather(x, axis_name, axis=0):
    return lax.all_gather(x, axis_name, axis=axis, tiled=True)


def scatter(x, axis_name, axis=0):
    return lax.psum_scatter(x.astype(bf16), axis_name, scatter_dimension=axis, tiled=True)


def columns(w, start, count):
    return lax.dynamic_slice_in_dim(w, start, count, axis=1)


def visible(begin):
    seq = begin.shape[0]
    index = jnp.arange(seq, dtype=jnp.int32)
    return (index[None, :] <= index[:, None]) & (index[None, :] >= begin[:, None])


def forward_plain(tok, tab, w_query, w_key, w_value, w_out, w_gate, w_up):
    n_ctx, n_fsdp = lax.axis_size("ctx"), lax.axis_size("fsdp")
    c = lax.axis_index("ctx")
    own_rows = w_query.shape[0]
    qw = HEADS // n_ctx * HEAD_DIM
    copies = max(1, n_ctx // KV_HEADS)
    kvw = max(1, KV_HEADS // n_ctx) * HEAD_DIM
    unit = w_gate.shape[1] // (n_fsdp * n_ctx)
    cw = tok.shape[1] // n_ctx
    wqkv_o = jnp.concatenate(
        [
            columns(w_query, c * qw, qw),
            columns(w_key, (c // copies) * kvw, kvw),
            columns(w_value, (c // copies) * kvw, kvw),
        ],
        axis=1,
    )
    wout_o = columns(w_out, c * cw, cw)
    gcol = jnp.concatenate([tab[72:80, :own_rows].T, jnp.zeros((own_rows, 120), f32)], axis=1)

    def units(w):
        parts = w.reshape(own_rows, n_fsdp, n_ctx, unit)
        mine = lax.dynamic_index_in_dim(parts, c, axis=2, keepdims=False)
        return (gcol[:, 4:5] * mine.reshape(own_rows, n_fsdp * unit)).astype(bf16)

    wgate_o, wup_o = units(w_gate), units(w_up)
    x = gather(tok, "ctx")
    tabs = gather(tab[None], "ctx")
    wqkv = gather(wqkv_o, "fsdp")
    wout = gather(wout_o, "fsdp")
    wgate = gather(wgate_o, "fsdp")
    wup = gather(wup_o, "fsdp")
    gain = gather(tab[72:73, :own_rows].astype(bf16), "fsdp", axis=1).astype(f32)
    xf = x.astype(f32)
    r = lax.rsqrt(jnp.mean(xf * xf, axis=-1, keepdims=True) + eps_norm)
    xn = (xf * r * gain).astype(bf16)
    seq, width = x.shape
    heads = HEADS // n_ctx
    qw = heads * HEAD_DIM
    pre = dot(xn, wqkv)
    cosine = tabs[:, 0:32].transpose(0, 2, 1).reshape(seq, 1, 32)
    sine = tabs[:, 32:64].transpose(0, 2, 1).reshape(seq, 1, 32)
    begin = tabs[:, 64].reshape(seq).astype(jnp.int32)
    kvw = (wqkv.shape[1] - qw) // 2
    kv = kvw // HEAD_DIM
    q = rotate(pre[:, :qw].reshape(seq, heads, HEAD_DIM), cosine, sine, 1.0).astype(bf16)
    k = rotate(pre[:, qw : qw + kvw].reshape(seq, kv, HEAD_DIM), cosine, sine, 1.0).astype(bf16)
    v = pre[:, qw + kvw :].astype(bf16).reshape(seq, kv, HEAD_DIM)
    qg = q.reshape(seq, kv, heads // kv, HEAD_DIM)
    scores = jnp.einsum("qkgd,lkd->kgql", qg, k, preferred_element_type=f32) * HEAD_DIM ** (-0.5)
    scores = jnp.where(visible(begin)[None, None], scores, neg_large)
    top = jnp.max(scores, axis=-1, keepdims=True)
    weights = jnp.exp(scores - top)
    total = jnp.sum(weights, axis=-1, keepdims=True)
    probs_low = (weights / total).astype(bf16)
    att = jnp.einsum("kgql,lkd->qkgd", probs_low, v, preferred_element_type=f32)
    o = gather(att.astype(bf16).reshape(seq, qw), "ctx", axis=1)
    lse = (top + jnp.log(total)).reshape(heads, 1, seq)
    lse = jnp.broadcast_to(lse, (heads, 8, seq)).reshape(8 * heads, seq)
    cw = width // n_ctx
    mid = columns(x, c * cw, cw).astype(f32) + dot(o, wout)
    m = gather(mid.astype(bf16), "ctx", axis=1)
    qt = q.reshape(seq, qw).T
    kt = k.reshape(seq, kvw).T
    vt = v.reshape(seq, kvw).T
    r = jnp.broadcast_to(r, (seq, 128))
    grow = jnp.broadcast_to(gain, (8, width))
    return xn, r, grow, gcol, qt, kt, vt, lse, o, m, wqkv, wout, wgate, wup, tabs


def middle_plain(m, cot, wgate, wup, w_down):
    n_ctx = lax.axis_size("ctx")
    c = lax.axis_index("ctx")
    unit = w_down.shape[0] // n_ctx
    wdown_o = lax.dynamic_slice_in_dim(w_down, c * unit, unit, axis=0)
    seq, width = m.shape
    rows = seq // n_ctx
    cw = width // n_ctx
    wdown = gather(wdown_o, "fsdp")
    cot_all = gather(cot, "ctx")
    mf = m.astype(f32)
    r = lax.rsqrt(jnp.mean(mf * mf, axis=-1, keepdims=True) + eps_norm)
    gate = dot(m, wgate) * r
    up = dot(m, wup) * r
    sig = jax.nn.sigmoid(gate)
    hidden = (gate * sig * up).astype(bf16)
    mlp = scatter(dot(hidden, wdown), "ctx").astype(f32)
    mid_rows = lax.dynamic_slice_in_dim(m, c * rows, rows, axis=0).astype(f32)
    output = (mid_rows + mlp).astype(bf16)
    grad_hidden = dot_nt(cot_all, wdown)
    down_sum = scatter(dot_tn(hidden, cot_all), "fsdp")
    d_gate = grad_hidden * up * sig * (1.0 + gate * (1.0 - sig))
    d_up = grad_hidden * gate * sig
    stat = jnp.sum(d_gate * gate + d_up * up, axis=-1, keepdims=True)
    d_gate = (d_gate * r).astype(bf16)
    d_up = (d_up * r).astype(bf16)
    gate_raw = dot_tn(m, d_gate).astype(bf16)
    up_raw = dot_tn(m, d_up).astype(bf16)
    back = dot_nt(d_gate, wgate) + dot_nt(d_up, wup) - mf * (r * r * stat * (1.0 / width))
    back_own = scatter(back, "ctx", axis=1).astype(f32)
    gm = (columns(cot_all, c * cw, cw).astype(f32) + back_own).astype(bf16)
    return output, None, down_sum, gate_raw, up_raw, gm


def backward_plain(xn, r, grow, qt, kt, vt, lse, o, gm, wqkv, wout, tabs, gate_raw, up_raw, down_sum):
    n_ctx = lax.axis_size("ctx")
    c = lax.axis_index("ctx")
    seq, width = xn.shape
    r, gain = r[:, 0:1], grow[0:1]
    heads = HEADS // n_ctx
    qw = heads * HEAD_DIM
    kvw = kt.shape[0]
    kv = kvw // HEAD_DIM
    cw = width // n_ctx
    scale = HEAD_DIM ** (-0.5)
    cosine = tabs[:, 0:32].transpose(0, 2, 1).reshape(seq, 1, 32)
    sine = tabs[:, 32:64].transpose(0, 2, 1).reshape(seq, 1, 32)
    begin = tabs[:, 64].reshape(seq).astype(jnp.int32)
    gate_grad = scatter(gate_raw, "fsdp")
    up_grad = scatter(up_raw, "fsdp")
    out_grad = scatter(dot_tn(o, gm), "fsdp")
    d_att = scatter(dot_nt(gm, wout), "ctx", axis=1).reshape(seq, kv, heads // kv, HEAD_DIM)
    q = qt.T.reshape(seq, kv, heads // kv, HEAD_DIM)
    k = kt.T.reshape(seq, kv, HEAD_DIM)
    v = vt.T.reshape(seq, kv, HEAD_DIM)
    scores = jnp.einsum("qkgd,lkd->kgql", q, k, preferred_element_type=f32) * scale
    scores = jnp.where(visible(begin)[None, None], scores, neg_large)
    lse = lse.reshape(kv, heads // kv, 8, seq)[:, :, 0, :, None]
    probs = jnp.exp(scores - lse)
    d_probs = jnp.einsum("qkgd,lkd->kgql", d_att, v, preferred_element_type=f32)
    delta = jnp.sum(probs * d_probs, axis=-1, keepdims=True)
    d_scores = (probs * (d_probs - delta)).astype(bf16)
    d_q = jnp.einsum("kgql,lkd->qkgd", d_scores, k, preferred_element_type=f32) * scale
    d_k = jnp.einsum("kgql,qkgd->lkd", d_scores, q, preferred_element_type=f32) * scale
    d_v = jnp.einsum("kgql,qkgd->lkd", probs.astype(bf16), d_att, preferred_element_type=f32)
    stat = (
        jnp.sum(d_q * q, axis=(1, 2, 3)) + jnp.sum(d_k * k, axis=(1, 2)) + jnp.sum(d_v * v, axis=(1, 2))
    )[:, None]
    d_q = rotate(d_q.reshape(seq, heads, HEAD_DIM), cosine, sine, -1.0).reshape(seq, qw)
    d_k = rotate(d_k, cosine, sine, -1.0).reshape(seq, kvw)
    d_pre = jnp.concatenate([d_q, d_k, d_v.reshape(seq, kvw)], axis=1).astype(bf16)
    qkv_grad = scatter(dot_tn(xn, d_pre), "fsdp")
    back = dot_nt(d_pre, wqkv) * (gain * r)
    back = back - xn.astype(f32) * ((1.0 / gain) * (r * stat * (1.0 / width)))
    at = (jnp.arange(width, dtype=jnp.int32) // cw == c)[None, :]
    back = back + jnp.where(at, jnp.tile(gm.astype(f32), (1, n_ctx)), 0.0)
    grad_tokens = scatter(back, "ctx").astype(f32)
    qkv_all = gather(qkv_grad[None], "ctx")
    out_all = gather(out_grad[None], "ctx")
    gate_all = gather(gate_grad[None], "ctx")
    up_all = gather(up_grad[None], "ctx")
    down_all = gather(down_sum[None], "ctx")
    return grad_tokens, qkv_all, out_all, gate_all, up_all, down_all


def finish_plain(qkv_all, out_all, gate_all, up_all, down_all, tok, y, w_query, w_key, w_value, w_gate, w_up, gcol):
    n_ctx, n_fsdp = lax.axis_size("ctx"), lax.axis_size("fsdp")
    own_rows = w_query.shape[0]
    qw = HEADS // n_ctx * HEAD_DIM
    copies = max(1, n_ctx // KV_HEADS)
    kvw = max(1, KV_HEADS // n_ctx) * HEAD_DIM
    ff_width = w_gate.shape[1]
    unit = ff_width // (n_fsdp * n_ctx)
    qkv_all = qkv_all.astype(f32)

    def joined(part):
        return jnp.moveaxis(part, 0, 1).reshape(own_rows, -1)

    def kv_part(part):
        return joined(part.reshape(n_ctx // copies, copies, own_rows, kvw).sum(axis=1))

    grad_query = joined(qkv_all[:, :, :qw])
    grad_key = kv_part(qkv_all[:, :, qw : qw + kvw])
    grad_value = kv_part(qkv_all[:, :, qw + kvw :])
    grad_out = joined(out_all.astype(f32))

    def spread(full):
        full = full.reshape(n_ctx, own_rows, n_fsdp, unit)
        return full.transpose(1, 2, 0, 3).reshape(own_rows, ff_width).astype(f32)

    raw_gate, raw_up = spread(gate_all), spread(up_all)
    grad_down = down_all.astype(f32).reshape(-1, down_all.shape[-1])

    def gain_term(grad, w):
        return jnp.sum(grad * w.astype(f32), axis=1, keepdims=True)

    first = gain_term(grad_query, w_query) + gain_term(grad_key, w_key) + gain_term(grad_value, w_value)
    second = gain_term(raw_gate, w_gate) + gain_term(raw_up, w_up)
    g1, g2 = gcol[:, 0:1], gcol[:, 4:5]
    return (
        grad_query, grad_key, grad_value, grad_out, g2 * raw_gate, g2 * raw_up, grad_down, tok, y, first / g1, second,
    )


def per_device(
    tokens,
    positions,
    gain_attn,
    gain_mlp,
    w_query,
    w_key,
    w_value,
    w_out,
    w_gate,
    w_up,
    w_down,
    cotangent,
):
    kernels = lax.axis_size("ctx") == 4 and lax.axis_size("fsdp") == 8
    c = lax.axis_index("ctx")
    rows = tokens.shape[0]
    frequency = theta_base ** (-(jnp.arange(HEAD_DIM // 2, dtype=f32) * 2.0) / HEAD_DIM)
    angles = frequency[:, None] * positions.astype(f32)[None, :]
    begin = c * rows + jnp.arange(rows, dtype=jnp.int32) - positions

    def gain_rows(gain):
        row = jnp.pad(gain.astype(f32), (0, rows - gain.shape[0]))
        return jnp.broadcast_to(row[None, :], (4, rows))

    tab = jnp.concatenate(
        [
            jnp.cos(angles),
            jnp.sin(angles),
            jnp.broadcast_to(begin.astype(f32)[None, :], (8, rows)),
            gain_rows(gain_attn),
            gain_rows(gain_mlp),
        ],
        axis=0,
    )

    forward = forward_stage if kernels else forward_plain
    xn, r, grow, gcol, qt, kt, vt, lse, o, m, wqkv, wout, wgate, wup, tabs = forward(
        tokens, tab, w_query, w_key, w_value, w_out, w_gate, w_up
    )
    middle = middle_stage if kernels else middle_plain
    y, _, down_sum, gate_raw, up_raw, gm = middle(m, cotangent, wgate, wup, w_down)
    backward = backward_stage if kernels else backward_plain
    tok, qkv_all, out_all, gate_all, up_all, down_all = backward(
        xn, r, grow, qt, kt, vt, lse, o, gm, wqkv, wout, tabs, gate_raw, up_raw, down_sum
    )
    finish = finish_stage if kernels else finish_plain
    g_query, g_key, g_value, g_out, g_gate, g_up, g_down, tok, y, g_one, g_two = finish(
        qkv_all, out_all, gate_all, up_all, down_all, tok, y,
        w_query, w_key, w_value, w_gate, w_up, gcol,
    )
    return (y, tok, g_one[:, 0], g_two[:, 0], g_query, g_key, g_value, g_out, g_gate, g_up, g_down)


def solution(mesh):
    both = P(("fsdp", "ctx"), None)
    first = P("fsdp", None)
    return jax.shard_map(
        per_device,
        mesh=mesh,
        in_specs=(both, P(("fsdp", "ctx")), P("fsdp"), P("fsdp")) + (first,) * 7 + (both,),
        out_specs=(both, both, P("fsdp"), P("fsdp")) + (first,) * 7,
        check_vma=False,
    )
```

```python
import functools

import jax
import jax.numpy as jnp
from jax import lax
from jax.experimental import pallas as pl
from jax.experimental.pallas import tpu as pltpu
from jax.sharding import PartitionSpec as P

HEADS = 32
KV_HEADS = 4
HEAD_DIM = 64

eps_norm = 1e-05
theta_base = 10000.0
neg_large = -1e30
bf16 = jnp.bfloat16
f32 = jnp.float32
MESH_IDS = pl.DeviceIdType.MESH


def dot(a, b):
    return jnp.dot(a, b, preferred_element_type=f32)


def dot_nt(a, b):
    return lax.dot_general(a, b, (((1,), (1,)), ((), ())), preferred_element_type=f32)


def dot_tn(a, b):
    return lax.dot_general(a, b, (((0,), (0,)), ((), ())), preferred_element_type=f32)


class Place:
    def __init__(self):
        self.f = lax.axis_index("fsdp")
        self.c = lax.axis_index("ctx")
        self.depth = lax.axis_size("fsdp") // 2
        self.z = self.f // 2
        self.core = self.f % 2
        self.other = 1 - self.core
        self.cx = self.c + 1 - 2 * (self.c % 2)
        self.cy = self.c + 2 - 4 * (self.c // 2)
        self.cd = 3 - self.c
        self.sibling = {"fsdp": self.f + 1 - 2 * self.core}
        self.up = {"fsdp": self.f + 2}
        self.down = {"fsdp": self.f - 2}
        self.x = {"ctx": self.cx}
        self.y = {"ctx": self.cy}

    def has_up(self):
        return self.z < self.depth - 1

    def has_down(self):
        return self.z > 0

    def barrier(self):
        sem = pltpu.get_barrier_semaphore()

        def greet(device):
            pl.semaphore_signal(sem, inc=1, device_id=device, device_id_type=MESH_IDS)

        greet(self.sibling)
        greet(self.x)
        greet(self.y)

        @pl.when(self.has_up())
        def _():
            greet(self.up)

        @pl.when(self.has_down())
        def _():
            greet(self.down)

        last = self.depth - 1
        pl.semaphore_wait(sem, 4 - self.z // last + (self.z + last - 1) // last)


def remote(src, dst, send_sem, recv_sem, device):
    return pltpu.make_async_remote_copy(
        src_ref=src,
        dst_ref=dst,
        send_sem=send_sem,
        recv_sem=recv_sem,
        device_id=device,
        device_id_type=MESH_IDS,
    )


class LineGather:
    SEMS = 21

    def __init__(self, place, own, full, sems):
        self.p, self.own, self.full, self.sems = place, own, full, sems
        self.n = place.depth
        self.rows = full.shape[0] // (2 * self.n)

    def view(self, level, core):
        start = pl.multiple_of((2 * level + core) * self.rows, 16)
        return self.full.at[pl.ds(start, self.rows)]

    def to_up(self, hop):
        p = self.p
        level = p.z - (hop - 1)
        src = self.own if hop == 1 and self.own is not None else self.view(level, p.core)
        return remote(
            src, self.view(level, p.core), self.sems.at[hop - 1], self.sems.at[6 + hop - 1], p.up
        )

    def to_down(self, hop):
        p = self.p
        level = p.z + (hop - 1)
        src = self.own if hop == 1 and self.own is not None else self.view(level, p.core)
        return remote(
            src, self.view(level, p.core), self.sems.at[3 + hop - 1], self.sems.at[9 + hop - 1], p.down
        )

    def to_sibling(self, level, own=False):
        p = self.p
        src = self.own if own and self.own is not None else self.view(level, p.core)
        return remote(
            src, self.view(level, p.core), self.sems.at[12 + level], self.sems.at[16 + level], p.sibling
        )

    def local(self):
        p = self.p
        return pltpu.make_async_copy(self.own, self.view(p.z, p.core), self.sems.at[20])

    def start(self):
        p = self.p

        @pl.when(p.has_up())
        def _():
            self.to_up(1).start()

        @pl.when(p.has_down())
        def _():
            self.to_down(1).start()

        self.to_sibling(p.z, True).start()
        if self.own is not None:
            self.local().start()

    def arrived(self, level, sem):
        view = self.view(level, self.p.core)
        remote(view, view, self.sems.at[0], sem, self.p.sibling).wait_recv()

    def hop(self, s):
        p = self.p

        @pl.when(p.z >= s)
        def _():
            self.arrived(p.z - s, self.sems.at[6 + s - 1])
            if s < self.n - 1:

                @pl.when(p.has_up())
                def _():
                    self.to_up(s + 1).start()

            self.to_sibling(p.z - s).start()

        @pl.when(p.z + s < self.n)
        def _():
            self.arrived(p.z + s, self.sems.at[9 + s - 1])
            if s < self.n - 1:

                @pl.when(p.has_down())
                def _():
                    self.to_down(s + 1).start()

            self.to_sibling(p.z + s).start()

    def finish(self):
        p = self.p
        if self.own is not None:
            self.local().wait()
        for level in range(self.n):
            view = self.view(level, p.other)
            remote(view, view, self.sems.at[0], self.sems.at[16 + level], p.sibling).wait_recv()

    def drain(self):
        p = self.p
        for s in range(1, self.n):

            @pl.when(p.has_up() & (p.z >= s - 1))
            def _():
                self.to_up(s).wait_send()

            @pl.when(p.has_down() & (p.z + s - 1 < self.n))
            def _():
                self.to_down(s).wait_send()

        for level in range(self.n):
            self.to_sibling(level).wait_send()


class PlaneGather:
    SEMS = 8

    def __init__(self, place, view, half, sems, own=None):
        self.p, self.view, self.half, self.sems = place, view, half, sems
        self.own = own

    def src(self):
        return self.view(self.p.c) if self.own is None else self.own

    def to_x(self):
        p = self.p
        return remote(self.src(), self.view(p.c), self.sems.at[0], self.sems.at[2], p.x)

    def to_y(self):
        p = self.p
        return remote(self.src(), self.view(p.c), self.sems.at[1], self.sems.at[3], p.y)

    def on_to_y(self):
        p, h = self.p, self.half(self.p.cx, 0)
        return remote(h, h, self.sems.at[4], self.sems.at[6], p.y)

    def on_to_x(self):
        p, h = self.p, self.half(self.p.cy, 1)
        return remote(h, h, self.sems.at[5], self.sems.at[7], p.x)

    def start(self):
        self.to_x().start()
        self.to_y().start()

    def got(self, ref, sem):
        remote(ref, ref, self.sems.at[0], sem, self.p.x).wait_recv()

    def middle(self):
        p = self.p
        self.got(self.view(p.cx), self.sems.at[2])
        self.on_to_y().start()
        self.got(self.view(p.cy), self.sems.at[3])
        self.on_to_x().start()

    def finish(self):
        p = self.p
        self.got(self.half(p.cd, 0), self.sems.at[6])
        self.got(self.half(p.cd, 1), self.sems.at[7])

    def drain(self):
        self.to_x().wait_send()
        self.to_y().wait_send()
        self.on_to_y().wait_send()
        self.on_to_x().wait_send()


def rows_at(index, count):
    return pl.ds(pl.multiple_of(index * count, count), count)


def any_spec(count):
    return [pl.BlockSpec(memory_space=pl.ANY)] * count


def call(kernel, ins, outs, scratch, collective_id, flops, name, vmem=60.0):
    return pl.pallas_call(
        kernel,
        out_shape=[jax.ShapeDtypeStruct(s, d) for s, d in outs],
        in_specs=any_spec(len(ins)),
        out_specs=any_spec(len(outs)),
        scratch_shapes=scratch,
        compiler_params=pltpu.CompilerParams(
            collective_id=collective_id, has_side_effects=True, vmem_limit_bytes=int(vmem * 2**20)
        ),
        cost_estimate=pl.CostEstimate(flops=flops, bytes_accessed=2**26, transcendentals=2**22),
        name=name,
    )(*ins)


def tiles_of(total, most):
    sizes, at = [], 0
    while at < total:
        sizes.append((at, min(most, total - at)))
        at += most
    return sizes


def add_to(ref, other):
    for start, size in tiles_of(ref.shape[0], 96):
        at = pl.ds(start, size)
        ref[at, :] = (ref[at, :].astype(f32) + other[at, :].astype(f32)).astype(bf16)


class PlaneScatter:
    SEMS = 12

    def __init__(self, place, part, half, first, second, sems):
        self.p, self.part, self.half = place, part, half
        self.first, self.second, self.sems = first, second, sems

    def far(self, h):
        p = self.p
        return remote(
            self.half(p.cd, h), self.first.at[h], self.sems.at[h], self.sems.at[2 + h], p.x if h else p.y
        )

    def direct(self, to_y, h, base):
        p = self.p
        count = self.first.shape[1]
        return remote(
            self.half(p.cy if to_y else p.cx, h),
            self.second.at[to_y, pl.ds(h * count, count)],
            self.sems.at[base + to_y],
            self.sems.at[base + 2 + to_y],
            p.y if to_y else p.x,
        )

    def start(self):
        self.far(0).start()
        self.far(1).start()

    def near(self):
        self.direct(0, 1, 8).start()
        self.direct(1, 0, 8).start()

    def middle(self):
        p = self.p
        for to_y in (0, 1):
            self.far(to_y).wait_recv()
            add_to(self.half(p.cy if to_y else p.cx, to_y), self.first.at[to_y])
            self.direct(to_y, to_y, 4).start()

    def finish(self, at=slice(None), first=True):
        if first:
            for to_y in (0, 1):
                self.direct(to_y, 1 - to_y, 8).wait_recv()
                self.direct(to_y, to_y, 4).wait_recv()
        own = self.part(self.p.c)[at].astype(f32)
        return own + self.second[0, at].astype(f32) + self.second[1, at].astype(f32)

    def drain(self):
        for to_y in (0, 1):
            self.far(to_y).wait_send()
            self.direct(to_y, 1 - to_y, 8).wait_send()
            self.direct(to_y, to_y, 4).wait_send()


class LineScatter:
    SEMS = 22

    def __init__(self, place, part, acc, slots, sems, stage=None):
        self.p, self.part, self.acc, self.slots, self.sems = place, part, acc, slots, sems
        self.stage = stage
        self.n = place.depth

    def to_sibling(self, level):
        p = self.p
        return remote(
            self.part(level, p.other), self.acc.at[level], self.sems.at[level], self.sems.at[4 + level], p.sibling
        )

    def start(self):
        for level in range(self.n):
            self.to_sibling(level).start()

    def load(self, level):
        return pltpu.make_async_copy(
            self.part(level, self.p.core), self.stage[level % 2], self.sems.at[20 + level % 2]
        )

    def got(self, ref, sem):
        remote(ref, ref, self.sems.at[0], sem, self.p.sibling).wait_recv()

    def add(self, ref, other):
        add_to(ref, other)

    def combine(self):
        if self.stage is not None:
            self.load(0).start()
            self.load(1).start()
        for level in range(self.n):
            self.got(self.acc.at[level], self.sems.at[4 + level])
            if self.stage is None:
                self.add(self.acc.at[level], self.part(level, self.p.core))
            else:
                self.load(level).wait()
                self.add(self.acc.at[level], self.stage[level % 2])
                if level + 2 < self.n:
                    self.load(level + 2).start()

    def slot(self, up, s):
        return self.slots.at[s - 1] if up else self.slots.at[(0, 3, 4)[s - 1]]

    def along(self, up, s):
        p = self.p
        level = p.z if up else self.n - 1 - p.z
        block = self.n - s + level
        block = block if up else self.n - 1 - block
        base = 8 if up else 14
        copy = remote(
            self.acc.at[block],
            self.slot(up, s),
            self.sems.at[base + s - 1],
            self.sems.at[base + 3 + s - 1],
            p.up if up else p.down,
        )
        return copy, (level <= s - 1) & (level < self.n - 1)

    def step(self, s):
        for up in (True, False):
            level = self.p.z if up else self.n - 1 - self.p.z
            if s > 1:
                block = self.n - s + level
                block = block if up else self.n - 1 - block
                base = 11 if up else 17

                @pl.when((level >= 1) & (s - 1 >= level))
                def _():
                    self.got(self.slot(up, s - 1), self.sems.at[base + s - 2])
                    self.add(self.acc.at[block], self.slot(up, s - 1))

            if s < self.n:
                copy, valid = self.along(up, s)

                @pl.when(valid)
                def _():
                    copy.start()

    def result(self):
        return self.acc.at[self.p.z]

    def drain(self):
        for level in range(self.n):
            self.to_sibling(level).wait_send()
        for up in (True, False):
            for s in range(1, self.n):
                copy, valid = self.along(up, s)

                @pl.when(valid)
                def _():
                    copy.wait_send()


def forward_kernel(
    tok, tab, gains, gcol, w_query, w_key, w_value, w_out, w_gate, w_up,
    xn_out, r_out, grow_out, qt_out, kt_out, vt_out, lse_out, o_out, m_out,
    wqkv_out, wout_out, wgate, wup, tab_out,
    X, XN, QT, KT, VT, K, LSE, O, M, WQ, WO, TAB, G8, GROW, BIAS, OT, R1,
    WK, WV, GF, UF, GO, UO, GCOL,
    line_sems, plane_sems, copy_sems,
):
    p = Place()
    n_ctx = 4
    rows = tok.shape[0]
    half = rows // 2
    qw = QT.shape[0]
    heads = qw // HEAD_DIM
    cw = O.shape[1] // n_ctx
    scale = HEAD_DIM ** (-0.5)

    mine = rows_at(p.f, WK.shape[0])
    loads = []
    for i, (src, dst) in enumerate(
        (
            (w_query.at[:, rows_at(p.c, qw)], WQ.at[mine, pl.ds(0, qw)]),
            (w_key, WK), (w_value, WV), (w_gate, GF), (w_up, UF), (gcol, GCOL),
        )
    ):
        loads.append(pltpu.make_async_copy(src, dst, copy_sems.at[15 + i]))
        loads[-1].start()

    p.barrier()

    gain_line = LineGather(p, gains, G8, line_sems.at[0])
    qkv_line = LineGather(p, None, WQ, line_sems.at[1])
    out_line = LineGather(p, w_out.at[:, rows_at(p.c, cw)], WO, line_sems.at[2])
    gate_line = LineGather(p, GO, wgate, line_sems.at[3])
    up_line = LineGather(p, UO, wup, line_sems.at[4])

    def row_block(ref):
        return (
            lambda c: ref.at[rows_at(c, rows)],
            lambda c, h: ref.at[pl.ds(pl.multiple_of(c * rows + h * half, half), half)],
        )

    tok_plane = PlaneGather(p, *row_block(X), plane_sems.at[0], own=tok)
    tab_rows = tab.shape[0]
    tab_plane = PlaneGather(
        p,
        lambda c: TAB.at[c],
        lambda c, h: TAB.at[c, pl.ds(h * (tab_rows // 2), tab_rows // 2)],
        plane_sems.at[2],
        own=tab,
    )

    def col_block(ref, b):
        def view(c):
            return ref.at[pl.ds(b * rows, rows), rows_at(c, cw)]

        def halves(c, h):
            return ref.at[pl.ds(b * rows + h * half, half), rows_at(c, cw)]

        return view, halves

    o_plane = [PlaneGather(p, *col_block(O, b), plane_sems.at[3 + b]) for b in range(n_ctx)]
    m_plane = [PlaneGather(p, *col_block(M, b), plane_sems.at[7 + b]) for b in range(n_ctx)]

    gain_line.start()
    tab_plane.start()
    tok_plane.start()
    out_line.start()
    for i in range(3):
        loads[i].wait()
    for c in range(n_ctx):

        @pl.when(p.c == c)
        def _():
            WQ[mine, qw : qw + HEAD_DIM] = WK[:, HEAD_DIM * c : HEAD_DIM * (c + 1)]
            WQ[mine, qw + HEAD_DIM :] = WV[:, HEAD_DIM * c : HEAD_DIM * (c + 1)]

    qkv_line.start()
    own_tok = pltpu.make_async_copy(tok, X.at[rows_at(p.c, rows)], copy_sems.at[0])
    own_tab = pltpu.make_async_copy(tab, TAB.at[p.c], copy_sems.at[1])
    own_tok.start()
    own_tab.start()

    for i in range(3, 6):
        loads[i].wait()
    unit = GO.shape[1] // (2 * p.depth)
    for c in range(n_ctx):

        @pl.when(p.c == c)
        def _():
            for f in range(2 * p.depth):
                at = (f * n_ctx + c) * unit
                for src, dst in ((GF, GO), (UF, UO)):
                    part = src[:, at : at + unit].astype(f32) * GCOL[:, 0:1]
                    dst[:, f * unit : (f + 1) * unit] = part.astype(bf16)

    gain_line.hop(1)
    tab_plane.middle()
    gain_line.hop(2)
    qkv_line.hop(1)
    gain_line.hop(3)
    gain_line.finish()
    for f in range(2 * p.depth):
        GROW[:, f * gains.shape[1] : (f + 1) * gains.shape[1]] = G8[16 * f : 16 * f + 8, :].astype(f32)

    def norm(c):
        at = rows_at(c, rows)
        x = X[at, :].astype(f32)
        r = lax.rsqrt(jnp.mean(x * x, axis=-1, keepdims=True) + eps_norm)
        R1[at, :] = jnp.broadcast_to(r, (rows, 128))
        XN[at, :] = (x * r * GROW[0:1, :]).astype(bf16)

    own_tok.wait()
    norm(p.c)
    out_line.hop(1)
    qkv_line.hop(2)
    tok_plane.middle()
    out_line.hop(2)
    gate_line.start()
    norm(p.cx)
    norm(p.cy)
    qkv_line.hop(3)
    tok_plane.finish()
    out_line.hop(3)
    up_line.start()
    norm(p.cd)
    xn_copy = pltpu.make_async_copy(XN, xn_out, copy_sems.at[3])
    r_copy = pltpu.make_async_copy(R1, r_out, copy_sems.at[4])
    grow_copy = pltpu.make_async_copy(GROW, grow_out, copy_sems.at[14])
    xn_copy.start()
    r_copy.start()
    grow_copy.start()
    own_tab.wait()
    tab_plane.finish()
    qkv_line.finish()

    @pl.loop(0, n_ctx)
    def _(b):
        at = rows_at(b, rows)
        pre = dot(XN[at, :], WQ[...]).T
        cosine = TAB[b, 0:32, :]
        sine = TAB[b, 32:64, :]
        for h in range(heads + 1):
            u = pre[64 * h : 64 * h + 32]
            w = pre[64 * h + 32 : 64 * h + 64]
            first = u * cosine - w * sine
            second = w * cosine + u * sine
            if h < heads:
                QT[64 * h : 64 * h + 32, at] = first.astype(bf16)
                QT[64 * h + 32 : 64 * h + 64, at] = second.astype(bf16)
            else:
                KT[0:32, at] = first.astype(bf16)
                KT[32:64, at] = second.astype(bf16)
                K[at, :] = jnp.concatenate([first, second], axis=0).T.astype(bf16)
        VT[:, at] = pre[qw + 64 :].astype(bf16)

    wq_copy = pltpu.make_async_copy(WQ, wqkv_out, copy_sems.at[5])
    wq_copy.start()

    def attend(b):
        n = (b + 1) * rows
        key = lax.broadcasted_iota(jnp.int32, (n, rows), 0)
        query = lax.broadcasted_iota(jnp.int32, (n, rows), 1) + b * rows
        begin = TAB[b, 64:65, :].astype(jnp.int32)
        BIAS[0:n, :] = jnp.where((key <= query) & (key >= begin), 0.0, neg_large)
        cols = slice(b * rows, (b + 1) * rows)

        @pl.loop(0, heads)
        def _(h):
            head = rows_at(h, HEAD_DIM)
            s = dot(K[0:n, :], QT[head, cols]) * scale + BIAS[0:n, :]
            top = jnp.max(s, axis=0, keepdims=True)
            e = jnp.exp(s - top)
            total = jnp.sum(e, axis=0, keepdims=True)
            probs = (e * (1.0 / total)).astype(bf16)
            OT[head, :] = dot(VT[:, 0:n], probs)
            LSE[rows_at(h, 8), cols] = jnp.broadcast_to(top + jnp.log(total), (8, rows))

        O[pl.ds(b * rows, rows), rows_at(p.c, cw)] = OT[...].T.astype(bf16)
        o_plane[b].start()

    def middle(b):
        at = pl.ds(b * rows, rows)
        cols = rows_at(p.c, cw)
        mid = X[at, cols].astype(f32) + dot(O[at, :], WO[...])
        M[at, cols] = mid.astype(bf16)
        m_plane[b].start()

    attend(0)
    attend(1)
    o_plane[0].middle()
    attend(2)
    gate_line.hop(1)
    o_plane[1].middle()
    attend(3)
    o_plane[2].middle()
    out_line.finish()
    o_plane[0].finish()
    middle(0)
    o_plane[1].finish()
    middle(1)
    o_plane[3].middle()
    up_line.hop(1)
    m_plane[0].middle()
    o_plane[2].finish()
    middle(2)
    m_plane[1].middle()
    o_plane[3].finish()
    middle(3)
    m_plane[2].middle()
    gate_line.hop(2)
    m_plane[3].middle()
    up_line.hop(2)
    copies = [xn_copy, r_copy, grow_copy, wq_copy]
    for i, (src, dst) in enumerate(
        ((QT, qt_out), (KT, kt_out), (VT, vt_out), (LSE, lse_out), (O, o_out), (WO, wout_out), (TAB, tab_out))
    ):
        copy = pltpu.make_async_copy(src, dst, copy_sems.at[6 + i])
        copy.start()
        copies.append(copy)
    for b in range(n_ctx):
        m_plane[b].finish()
    m_copy = pltpu.make_async_copy(M, m_out, copy_sems.at[13])
    m_copy.start()
    copies.append(m_copy)
    gate_line.hop(3)
    up_line.hop(3)
    gate_line.finish()
    up_line.finish()
    for copy in copies:
        copy.wait()
    for line in (gain_line, qkv_line, out_line, gate_line, up_line):
        line.drain()
    for plane in [tok_plane, tab_plane] + o_plane + m_plane:
        plane.drain()


def forward_stage(tok, tab, gains, gcol, w_query, w_key, w_value, w_out, w_gate, w_up):
    n_fsdp, n_ctx = lax.axis_size("fsdp"), lax.axis_size("ctx")
    rows, width = tok.shape
    seq = rows * n_ctx
    own = w_query.shape[0]
    whole = n_fsdp * own
    qw = HEADS // n_ctx * HEAD_DIM
    nq, nw, nu = qw + 2 * HEAD_DIM, width // n_ctx, w_gate.shape[1] // n_ctx
    heads = qw // HEAD_DIM
    tab_shape = (n_ctx,) + tab.shape
    outs = [
        ((seq, width), bf16), ((seq, 128), f32), ((8, width), f32), ((qw, seq), bf16), ((64, seq), bf16),
        ((64, seq), bf16), ((8 * heads, seq), f32), ((seq, width), bf16), ((seq, width), bf16), ((whole, nq), bf16),
        ((whole, nw), bf16), ((whole, nu), bf16), ((whole, nu), bf16), (tab_shape, f32),
    ]
    scratch = [
        pltpu.VMEM((seq, width), bf16),
        pltpu.VMEM((seq, width), bf16),
        pltpu.VMEM((qw, seq), bf16),
        pltpu.VMEM((64, seq), bf16),
        pltpu.VMEM((64, seq), bf16),
        pltpu.VMEM((seq, 64), bf16),
        pltpu.VMEM((8 * heads, seq), f32),
        pltpu.VMEM((seq, width), bf16),
        pltpu.VMEM((seq, width), bf16),
        pltpu.VMEM((whole, nq), bf16),
        pltpu.VMEM((whole, nw), bf16),
        pltpu.VMEM(tab_shape, f32),
        pltpu.VMEM((16 * n_fsdp, gains.shape[1]), bf16),
        pltpu.VMEM((8, width), f32),
        pltpu.VMEM((seq, rows), f32),
        pltpu.VMEM((qw, rows), f32),
        pltpu.VMEM((seq, 128), f32),
        pltpu.VMEM(w_key.shape, bf16),
        pltpu.VMEM(w_value.shape, bf16),
        pltpu.VMEM(w_gate.shape, bf16),
        pltpu.VMEM(w_up.shape, bf16),
        pltpu.VMEM((own, nu), bf16),
        pltpu.VMEM((own, nu), bf16),
        pltpu.VMEM(gcol.shape, f32),
        pltpu.SemaphoreType.DMA((5, LineGather.SEMS)),
        pltpu.SemaphoreType.DMA((11, PlaneGather.SEMS)),
        pltpu.SemaphoreType.DMA((21,)),
    ]
    ins = (tok, tab, gains, gcol, w_query, w_key, w_value, w_out, w_gate, w_up)
    flops = 2 * seq * width * (nq + nw) + 8 * heads * seq * seq * HEAD_DIM
    return call(forward_kernel, ins, outs, scratch, 1, flops, "forward_stage")


def middle_kernel(
    m_in, cot, wgate_in, wup_in, w_down,
    y_out, down_part, down_sum, gate_part, up_part, gm_out,
    M, COT, WG, WU, WD, GATE, UP, HID, R2, PD, PH, D1, D2, H1, H2, DACC, DSLOT,
    line_sems, sum_sems, plane_sems, copy_sems, stage_sems,
):
    p = Place()
    n_ctx = 4
    seq, width = M.shape
    rows = seq // n_ctx
    half = rows // 2
    cw = width // n_ctx
    units = GATE.shape[1]
    loads = []
    for i, (src, dst) in enumerate(((m_in, M), (wgate_in, WG), (wup_in, WU), (cot, COT.at[rows_at(p.c, rows)]))):
        loads.append(pltpu.make_async_copy(src, dst, copy_sems.at[i]))
        loads[-1].start()

    p.barrier()
    unit = w_down.shape[0] // n_ctx
    down_own = w_down.at[pl.ds(pl.multiple_of(p.c * unit, 16), unit)]
    down_line = LineGather(p, down_own, WD, line_sems.at[0])
    down_line.start()
    cot_plane = PlaneGather(
        p,
        lambda c: COT.at[rows_at(c, rows)],
        lambda c, h: COT.at[pl.ds(pl.multiple_of(c * rows + h * half, half), half)],
        plane_sems.at[5],
        own=cot,
    )
    cot_plane.start()

    loads[0].wait()
    loads[1].wait()
    loads[2].wait()

    def activate(b):
        at = rows_at(b, rows)
        mf = M[at, :].astype(f32)
        r = lax.rsqrt(jnp.mean(mf * mf, axis=-1, keepdims=True) + eps_norm)
        R2[at, :] = jnp.broadcast_to(r, (rows, 128))
        for start, size in tiles_of(units, 512):
            cols = slice(start, start + size)
            gate = dot(M[at, :], WG[:, cols]) * r
            up = dot(M[at, :], WU[:, cols]) * r
            GATE[at, cols] = gate.astype(bf16)
            UP[at, cols] = up.astype(bf16)
            HID[at, cols] = (gate * (1.0 / (1.0 + jnp.exp(-gate))) * up).astype(bf16)

    pl.loop(0, 2)(activate)
    down_line.hop(1)
    pl.loop(2, 4)(activate)
    cot_plane.middle()
    down_line.hop(2)
    loads[3].wait()
    cot_plane.finish()
    stage_copies = {}
    for i, (at, size) in enumerate(tiles_of(units, rows)):
        slot = pl.ds(i % 2 * rows, size)
        if i >= 2:
            stage_copies[i - 2].wait()
        for j in range(0, width, cw):
            PH[slot, j : j + cw] = dot_tn(HID[:, at : at + size], COT[:, j : j + cw]).astype(bf16)
        copy = pltpu.make_async_copy(PH.at[slot], down_part.at[pl.ds(at, size)], stage_sems.at[i % 2])
        copy.start()
        stage_copies[i] = copy
    n_down = len(stage_copies)
    stage_copies[n_down - 2].wait()
    stage_copies[n_down - 1].wait()

    def down_block(level, core):
        return down_part.at[pl.ds(pl.multiple_of((2 * level + core) * unit, 16), unit)]

    down_stage = [PH.at[pl.ds(i * rows, unit)] for i in range(2)]
    sum_line = LineScatter(p, down_block, DACC, DSLOT, sum_sems.at[0], down_stage)
    sum_line.start()
    down_line.hop(3)
    down_line.finish()

    y_plane = PlaneScatter(
        p,
        lambda c: PD.at[rows_at(c, rows)],
        lambda c, h: PD.at[pl.ds(pl.multiple_of(c * rows + h * half, half), half)],
        D1,
        D2,
        plane_sems.at[0],
    )

    def col_scatter(b):
        return PlaneScatter(
            p,
            lambda c: PH.at[pl.ds(b * rows, rows), rows_at(c, cw)],
            lambda c, h: PH.at[pl.ds(b * rows + h * half, half), rows_at(c, cw)],
            H1.at[b],
            H2.at[b],
            plane_sems.at[1 + b],
        )

    h_plane = [col_scatter(b) for b in range(n_ctx)]

    def partial_out(c):
        at = rows_at(c, rows)
        for j in range(0, width, cw):
            PD[at, j : j + cw] = dot(HID[at, :], WD[:, j : j + cw]).astype(bf16)

    partial_out(p.cd)
    y_plane.start()
    partial_out(p.cx)
    partial_out(p.cy)
    y_plane.near()
    sum_line.combine()
    sum_line.step(1)
    partial_out(p.c)

    def back(b):
        at = pl.ds(b * rows, rows)
        r = R2[at, 0:1]
        stat = jnp.zeros((rows, 1), f32)
        for start, size in tiles_of(units, 512):
            cols = slice(start, start + size)
            grad_hidden = dot_nt(COT[at, :], WD[cols, :])
            gate = GATE[at, cols].astype(f32)
            up = UP[at, cols].astype(f32)
            sig = 1.0 / (1.0 + jnp.exp(-gate))
            d_up = grad_hidden * gate * sig
            d_gate = grad_hidden * up * sig * (1.0 + gate * (1.0 - sig))
            stat += jnp.sum(d_gate * gate + d_up * up, axis=-1, keepdims=True)
            GATE[at, cols] = (d_gate * r).astype(bf16)
            UP[at, cols] = (d_up * r).astype(bf16)
        coef = r * r * stat * (1.0 / width)
        for j in range(0, width, cw):
            e = dot_nt(GATE[at, :], WG[j : j + cw, :]) + dot_nt(UP[at, :], WU[j : j + cw, :])
            PH[at, j : j + cw] = (e - M[at, j : j + cw].astype(f32) * coef).astype(bf16)
        h_plane[b].start()
        h_plane[b].near()

    back(0)
    y_plane.middle()
    back(1)
    h_plane[0].middle()
    sum_line.step(2)
    back(2)
    h_plane[1].middle()
    back(3)
    h_plane[2].middle()

    stage_copies = {}
    jobs = []
    for src, dst in ((GATE, gate_part), (UP, up_part)):
        for at, size in tiles_of(width, 512):
            jobs.append((src, dst, at, size))

    def weight_tile(i):
        src, dst, at, size = jobs[i]
        slot = pl.ds(i % 2 * size, size)
        if i >= 2:
            stage_copies[i - 2].wait()
        for start, part in tiles_of(units, 512):
            cols = slice(start, start + part)
            HID[slot, cols] = dot_tn(M[:, at : at + size], src[:, cols]).astype(bf16)
        copy = pltpu.make_async_copy(HID.at[slot], dst.at[pl.ds(at, size)], stage_sems.at[2 + i % 2])
        copy.start()
        stage_copies[i] = copy

    def finish_block(b):
        at = pl.ds(b * rows, rows)
        mine = rows_at(p.c, cw)
        COT[at, mine] = (COT[at, mine].astype(f32) + h_plane[b].finish()).astype(bf16)

    weight_tile(0)
    cot_plane.drain()
    sum_line.step(3)
    h_plane[3].middle()
    weight_tile(1)
    weight_tile(2)
    finish_block(0)
    weight_tile(3)
    weight_tile(4)
    finish_block(1)
    weight_tile(5)
    weight_tile(6)
    finish_block(2)
    weight_tile(7)
    sum_line.step(4)
    sum_copy = pltpu.make_async_copy(sum_line.result(), down_sum, copy_sems.at[6])
    sum_copy.start()
    piece = rows // n_ctx
    for i in range(n_ctx):
        own = pl.ds(pl.multiple_of(p.c * rows + i * piece, piece), piece)
        mlp = y_plane.finish(pl.ds(i * piece, piece), i == 0)
        PD[own, :] = (M[own, :].astype(f32) + mlp).astype(bf16)
    y_copy = pltpu.make_async_copy(PD.at[rows_at(p.c, rows)], y_out, copy_sems.at[4])
    y_copy.start()
    finish_block(3)
    gm_copy = pltpu.make_async_copy(COT.at[:, rows_at(p.c, cw)], gm_out, copy_sems.at[5])
    gm_copy.start()
    stage_copies[6].wait()
    stage_copies[7].wait()
    y_copy.wait()
    gm_copy.wait()
    sum_copy.wait()
    sum_line.drain()
    down_line.drain()
    y_plane.drain()
    for b in range(n_ctx):
        h_plane[b].drain()


def middle_stage(m, cot, wgate, wup, w_down):
    n_fsdp, n_ctx = lax.axis_size("fsdp"), lax.axis_size("ctx")
    seq, width = m.shape
    rows = seq // n_ctx
    cw = width // n_ctx
    units = wgate.shape[1]
    unit = units // n_fsdp
    outs = [
        ((rows, width), bf16), ((units, width), bf16), ((unit, width), bf16), ((width, units), bf16),
        ((width, units), bf16), ((seq, cw), bf16),
    ]
    scratch = [
        pltpu.VMEM((seq, width), bf16),
        pltpu.VMEM((seq, width), bf16),
        pltpu.VMEM((width, units), bf16),
        pltpu.VMEM((width, units), bf16),
        pltpu.VMEM((units, width), bf16),
        pltpu.VMEM((seq, units), bf16),
        pltpu.VMEM((seq, units), bf16),
        pltpu.VMEM((seq, units), bf16),
        pltpu.VMEM((seq, 128), f32),
        pltpu.VMEM((seq, width), bf16),
        pltpu.VMEM((seq, width), bf16),
        pltpu.VMEM((2, rows // 2, width), bf16),
        pltpu.VMEM((2, rows, width), bf16),
        pltpu.VMEM((n_ctx, 2, rows // 2, cw), bf16),
        pltpu.VMEM((n_ctx, 2, rows, cw), bf16),
        pltpu.VMEM((n_fsdp // 2, unit, width), bf16),
        pltpu.VMEM((5, unit, width), bf16),
        pltpu.SemaphoreType.DMA((1, LineGather.SEMS)),
        pltpu.SemaphoreType.DMA((1, LineScatter.SEMS)),
        pltpu.SemaphoreType.DMA((6, PlaneScatter.SEMS)),
        pltpu.SemaphoreType.DMA((7,)),
        pltpu.SemaphoreType.DMA((4,)),
    ]
    flops = 18 * seq * width * units
    return call(middle_kernel, (m, cot, wgate, wup, w_down), outs, scratch, 2, flops, "middle_stage")


def backward_kernel(
    xn_in, r_in, grow_in, qt_in, kt_in, vt_in, lse_in, o_in, gm_in, wqkv_in, wout_in, tab_in,
    gate_part, up_part, down_sum,
    tok_out, qkv_all, out_all, gate_all, up_all, down_all,
    XN, R1, GROW, QT, KT, VT, LSE, O, GM, WQ, WO, TAB,
    K, V, DK, DV, DOT, DQT, DPRE, STAT, BIAS, PT, G1, G2, T1, T2, TOK,
    GACC, GSLOT, UACC, USLOT, OACC, OSLOT, QACC, QSLOT,
    line_sems, plane_sems, scatter_sems, copy_sems,
):
    p = Place()
    n_ctx = 4
    seq, width = XN.shape
    rows = seq // n_ctx
    half = rows // 2
    cw = width // n_ctx
    qw = QT.shape[0]
    heads = qw // HEAD_DIM
    nq = WQ.shape[1]
    own_rows = QACC.shape[1]
    scale = HEAD_DIM ** (-0.5)
    loads = []
    for i, (src, dst) in enumerate(
        (
            (gm_in, GM), (wout_in, WO), (o_in, O), (kt_in, KT), (vt_in, VT), (qt_in, QT), (lse_in, LSE),
            (tab_in, TAB), (xn_in, XN), (wqkv_in, WQ), (r_in, R1), (grow_in, GROW),
        )
    ):
        loads.append(pltpu.make_async_copy(src, dst, copy_sems.at[i]))
    loads[0].start()
    loads[1].start()

    p.barrier()

    def block_rows(ref):
        count = ref.shape[0] // (2 * p.depth)
        return lambda level, core: ref.at[pl.ds(pl.multiple_of((2 * level + core) * count, 16), count)]

    nu = GACC.shape[2]
    cols_stage = [XN.at[pl.ds(i * own_rows, own_rows), pl.ds(0, nu)] for i in range(2)]
    gate_line = LineScatter(p, block_rows(gate_part), GACC, GSLOT, line_sems.at[1], cols_stage)
    up_line = LineScatter(p, block_rows(up_part), UACC, USLOT, line_sems.at[2], cols_stage)
    out_line = LineScatter(p, block_rows(WO), OACC, OSLOT, line_sems.at[3])

    def qkv_block(level, core):
        f = 2 * level + core
        at = pl.ds(pl.multiple_of((f % p.depth) * own_rows, own_rows), own_rows)
        return O.at[at, pl.ds(pl.multiple_of((f // p.depth) * nq, 128), nq)]

    qkv_line = LineScatter(p, qkv_block, QACC, QSLOT, line_sems.at[4])
    gate_line.start()
    up_line.start()
    for i in (2, 3, 4, 5, 6, 7, 9, 10, 11):
        loads[i].start()

    def col_scatter(b):
        return PlaneScatter(
            p,
            lambda c: PT.at[pl.ds(b * rows, rows), rows_at(c, cw)],
            lambda c, h: PT.at[pl.ds(b * rows + h * half, half), rows_at(c, cw)],
            G1.at[b],
            G2.at[b],
            scatter_sems.at[b],
        )

    g_plane = [col_scatter(b) for b in range(n_ctx)]
    t_plane = PlaneScatter(
        p,
        lambda c: PT.at[rows_at(c, rows)],
        lambda c, h: PT.at[pl.ds(pl.multiple_of(c * rows + h * half, half), half)],
        T1,
        T2,
        scatter_sems.at[n_ctx],
    )

    def whole(ref, own, index, first):
        count = own.shape[0]

        def halves(c, h):
            return ref(c).at[pl.ds(h * first, count - first if h else first)]

        plane = PlaneGather(p, ref, halves, plane_sems.at[index], own=own)
        return plane, pltpu.make_async_copy(own, ref(p.c), plane_sems.at[index, PlaneGather.SEMS])

    unit = down_sum.shape[0]
    down_plane, down_own = whole(lambda c: down_all.at[c], down_sum, 0, unit // 32 * 16 + unit // 16 % 2 * 16)
    gate_plane, gate_own = whole(lambda c: gate_all.at[c], gate_line.result(), 1, own_rows // 2)
    up_plane, up_own = whole(lambda c: up_all.at[c], up_line.result(), 2, own_rows // 2)
    out_plane, out_own = whole(lambda c: out_all.at[c], out_line.result(), 3, own_rows // 2)
    qkv_plane, qkv_own = whole(lambda c: qkv_all.at[c], qkv_line.result(), 4, own_rows // 2)

    loads[0].wait()
    loads[1].wait()
    for b in range(n_ctx):
        at = pl.ds(b * rows, rows)
        for j in range(0, width, 512):
            PT[at, j : j + 512] = dot_nt(GM[at, :], WO[j : j + 512, :]).astype(bf16)
        g_plane[b].start()
        g_plane[b].near()
    gate_line.combine()
    gate_line.step(1)
    g_plane[0].middle()
    loads[2].wait()

    @pl.loop(0, width // 512)
    def _(i):
        at = rows_at(i, 512)
        WO[at, :] = dot_tn(O[:, at], GM[...]).astype(bf16)

    out_line.start()
    g_plane[1].middle()
    up_line.combine()
    loads[8].start()
    up_line.step(1)
    g_plane[2].middle()
    for i in (3, 4, 5, 6, 7, 10):
        loads[i].wait()

    @pl.loop(0, n_ctx)
    def _(b):
        at = rows_at(b, rows)
        K[at, :] = KT[:, at].astype(f32).T.astype(bf16)
        V[at, :] = VT[:, at].astype(f32).T.astype(bf16)
        DK[at, :] = jnp.zeros((rows, HEAD_DIM), f32)
        DV[at, :] = jnp.zeros((rows, HEAD_DIM), f32)

    g_plane[3].middle()

    def attend_back(b):
        n = (b + 1) * rows
        cols = slice(b * rows, (b + 1) * rows)
        DOT[...] = g_plane[b].finish().T.astype(bf16)
        at = pl.ds(b * rows, rows)
        DQT[...] = O[at, rows_at(p.c, cw)].astype(f32).T
        key = lax.broadcasted_iota(jnp.int32, (n, rows), 0)
        query = lax.broadcasted_iota(jnp.int32, (n, rows), 1) + b * rows
        begin = TAB[b, 64:65, :].astype(jnp.int32)
        BIAS[0:n, :] = jnp.where((key <= query) & (key >= begin), 0.0, neg_large)
        STAT[...] = jnp.zeros((8, rows), f32)

        @pl.loop(0, heads)
        def _(h):
            head = rows_at(h, HEAD_DIM)
            q = QT[head, cols]
            d_out = DOT[head, :]
            delta = jnp.sum(d_out.astype(f32) * DQT[head, :], axis=0, keepdims=True)
            s = dot(K[0:n, :], q) * scale + BIAS[0:n, :]
            probs = jnp.exp(s - LSE[rows_at(h, 8), cols][0:1])
            d_probs = dot(V[0:n, :], d_out)
            d_s = (probs * (d_probs - delta)).astype(bf16)
            d_q = dot(KT[:, 0:n], d_s) * scale
            DK[0:n, :] += dot_nt(d_s, q) * scale
            DV[0:n, :] += dot_nt(probs.astype(bf16), d_out)
            STAT[...] += jnp.broadcast_to(jnp.sum(d_q * q.astype(f32), axis=0, keepdims=True), (8, rows))
            u, w = d_q[0:32], d_q[32:64]
            cosine, sine = TAB[b, 0:32, :], TAB[b, 32:64, :]
            DQT[head, :] = jnp.concatenate([u * cosine + w * sine, w * cosine - u * sine], axis=0)

        DPRE[at, 0:qw] = DQT[...].T.astype(bf16)
        R1[at, 0:8] = STAT[...].T

    attend_back(0)
    gate_line.step(2)
    attend_back(1)
    attend_back(2)
    down_plane.start()
    down_own.start()
    up_line.step(2)
    attend_back(3)
    loads[8].wait()
    loads[9].wait()
    loads[11].wait()

    @pl.loop(0, n_ctx)
    def _(b):
        at = rows_at(b, rows)
        d_k = DK[at, :].T
        d_v = DV[at, :].T
        stat = jnp.sum(d_k * KT[:, at].astype(f32) + d_v * VT[:, at].astype(f32), axis=0, keepdims=True)
        R1[at, 0:8] += jnp.broadcast_to(stat, (8, rows)).T
        u, w = d_k[0:32], d_k[32:64]
        cosine, sine = TAB[b, 0:32, :], TAB[b, 32:64, :]
        both = jnp.concatenate([u * cosine + w * sine, w * cosine - u * sine, d_v], axis=0)
        DPRE[at, qw:] = both.T.astype(bf16)

    def tokens(c):
        at = rows_at(c, rows)
        r = R1[at, 127:128]
        coef = r * R1[at, 0:1] * (1.0 / width)
        for j in range(0, width, 512):
            cols = slice(j, j + 512)
            gain = GROW[0:1, cols]
            e = dot_nt(DPRE[at, :], WQ[cols, :])
            PT[at, cols] = (e * (gain * r) - XN[at, cols].astype(f32) * ((1.0 / gain) * coef)).astype(bf16)
        mine = rows_at(p.c, cw)
        PT[at, mine] = (PT[at, mine].astype(f32) + GM[at, :].astype(f32)).astype(bf16)

    for b in range(n_ctx):
        g_plane[b].drain()
    tokens(p.cd)
    t_plane.start()
    tokens(p.cx)
    tokens(p.cy)
    t_plane.near()
    tokens(p.c)

    @pl.loop(0, p.depth)
    def _(i):
        for j in range(2):
            at = rows_at(i + j * p.depth, own_rows)
            O[rows_at(i, own_rows), j * nq : (j + 1) * nq] = dot_tn(XN[:, at], DPRE[...]).astype(bf16)

    qkv_line.start()
    t_plane.middle()
    gate_line.step(3)
    down_plane.middle()
    out_line.combine()
    out_line.step(1)
    up_line.step(3)
    qkv_line.combine()
    qkv_line.step(1)
    gate_line.step(4)
    gate_plane.start()
    gate_own.start()
    out_line.step(2)
    tok_copies = []
    for i in range(n_ctx):
        if i >= 2:
            tok_copies[i - 2].wait()
        at = pl.ds(i * (rows // n_ctx), rows // n_ctx)
        TOK[i % 2] = t_plane.finish(at, i == 0)
        tok_copies.append(pltpu.make_async_copy(TOK.at[i % 2], tok_out.at[at], copy_sems.at[12 + i % 2]))
        tok_copies[-1].start()
    qkv_line.step(2)
    up_line.step(4)
    up_plane.start()
    up_own.start()
    gate_plane.middle()
    out_line.step(3)
    qkv_line.step(3)
    out_line.step(4)
    out_plane.start()
    out_own.start()
    up_plane.middle()
    qkv_line.step(4)
    qkv_plane.start()
    qkv_own.start()
    out_plane.middle()
    qkv_plane.middle()
    for plane, own in (
        (down_plane, down_own), (gate_plane, gate_own), (up_plane, up_own), (out_plane, out_own), (qkv_plane, qkv_own),
    ):
        plane.finish()
        own.wait()
        plane.drain()
    tok_copies[2].wait()
    tok_copies[3].wait()
    t_plane.drain()
    for line in (gate_line, up_line, out_line, qkv_line):
        line.drain()


def backward_stage(xn, r, grow, qt, kt, vt, lse, o, gm, wqkv, wout, tabs, gate_part, up_part, down_sum):
    n_fsdp, n_ctx = lax.axis_size("fsdp"), lax.axis_size("ctx")
    seq, width = xn.shape
    rows = seq // n_ctx
    half = rows // 2
    cw = width // n_ctx
    own = width // n_fsdp
    depth = n_fsdp // 2
    nq, nu = wqkv.shape[1], gate_part.shape[1]
    unit = down_sum.shape[0]
    qw = qt.shape[0]
    outs = [
        ((rows, width), f32), ((n_ctx, own, nq), bf16), ((n_ctx, own, cw), bf16), ((n_ctx, own, nu), bf16),
        ((n_ctx, own, nu), bf16), ((n_ctx, unit, width), bf16),
    ]
    ins = (xn, r, grow, qt, kt, vt, lse, o, gm, wqkv, wout, tabs, gate_part, up_part, down_sum)
    scratch = [pltpu.VMEM(a.shape, a.dtype) for a in ins[:12]] + [
        pltpu.VMEM((seq, HEAD_DIM), bf16),
        pltpu.VMEM((seq, HEAD_DIM), bf16),
        pltpu.VMEM((seq, HEAD_DIM), f32),
        pltpu.VMEM((seq, HEAD_DIM), f32),
        pltpu.VMEM((qw, rows), bf16),
        pltpu.VMEM((qw, rows), f32),
        pltpu.VMEM((seq, nq), bf16),
        pltpu.VMEM((8, rows), f32),
        pltpu.VMEM((seq, rows), f32),
        pltpu.VMEM((seq, width), bf16),
        pltpu.VMEM((n_ctx, 2, half, cw), bf16),
        pltpu.VMEM((n_ctx, 2, rows, cw), bf16),
        pltpu.VMEM((2, half, width), bf16),
        pltpu.VMEM((2, rows, width), bf16),
        pltpu.VMEM((2, rows // n_ctx, width), f32),
        pltpu.VMEM((depth, own, nu), bf16),
        pltpu.VMEM((5, own, nu), bf16),
        pltpu.VMEM((depth, own, nu), bf16),
        pltpu.VMEM((5, own, nu), bf16),
        pltpu.VMEM((depth, own, cw), bf16),
        pltpu.VMEM((5, own, cw), bf16),
        pltpu.VMEM((depth, own, nq), bf16),
        pltpu.VMEM((5, own, nq), bf16),
        pltpu.SemaphoreType.DMA((5, LineScatter.SEMS)),
        pltpu.SemaphoreType.DMA((5, PlaneGather.SEMS + 1)),
        pltpu.SemaphoreType.DMA((n_ctx + 1, PlaneScatter.SEMS)),
        pltpu.SemaphoreType.DMA((14,)),
    ]
    flops = 4 * seq * width * (nq + cw) + 20 * qw * seq * seq
    return call(backward_kernel, ins, outs, scratch, 3, flops, "backward_stage")


def finish_kernel(
    unit, qkv, out, gate, up, down, tok, y, w_query, w_key, w_value, w_gate, w_up, g1, g2,
    o_query, o_key, o_value, o_out, o_gate, o_up, o_down, o_tok, o_y, o_g1, o_g2,
):
    n_ctx = qkv.shape[0]
    qw = o_query.shape[1] // n_ctx
    cw = out.shape[2]
    for c in range(n_ctx):
        o_query[:, c * qw : (c + 1) * qw] = qkv[c, :, 0:qw].astype(f32)
        o_key[:, c * HEAD_DIM : (c + 1) * HEAD_DIM] = qkv[c, :, qw : qw + HEAD_DIM].astype(f32)
        o_value[:, c * HEAD_DIM : (c + 1) * HEAD_DIM] = qkv[c, :, qw + HEAD_DIM :].astype(f32)
        o_out[:, c * cw : (c + 1) * cw] = out[c].astype(f32)

    def total(ref, w):
        return jnp.sum(ref[...] * w[...].astype(f32), axis=-1, keepdims=True)

    first = total(o_query, w_query) + total(o_key, w_key) + total(o_value, w_value)
    o_g1[...] = jnp.broadcast_to(first / g1[:, 0:1], o_g1.shape)
    gain = g2[:, 0:1]
    for src, dst in ((gate, o_gate), (up, o_up)):
        for f in range(src.shape[2] // unit):
            for c in range(n_ctx):
                at = (f * n_ctx + c) * unit
                dst[:, at : at + unit] = src[c, :, f * unit : (f + 1) * unit].astype(f32) * gain
    second = total(o_gate, w_gate) + total(o_up, w_up)
    o_g2[...] = jnp.broadcast_to(second / gain, o_g2.shape)
    o_down[...] = down[...].astype(f32)
    o_tok[...] = tok[...]
    o_y[...] = y[...]


def finish_stage(qkv, out, gate, up, down, tok, y, w_query, w_key, w_value, w_gate, w_up, g1, g2):
    steps = 4
    n_fsdp = lax.axis_size("fsdp")
    own = w_query.shape[0]
    down = down.reshape(-1, down.shape[-1])
    unit = gate.shape[2] // n_fsdp

    def spec(shape):
        if len(shape) == 3:
            return pl.BlockSpec((shape[0], shape[1] // steps, shape[2]), lambda i: (0, i, 0))
        return pl.BlockSpec((shape[0] // steps, shape[1]), lambda i: (i, 0))

    ins = (qkv, out, gate, up, down, tok, y, w_query, w_key, w_value, w_gate, w_up, g1, g2)
    outs = [
        (w_query.shape, f32), (w_key.shape, f32), (w_value.shape, f32), ((own, out.shape[0] * out.shape[2]), f32),
        (w_gate.shape, f32), (w_up.shape, f32), (down.shape, f32), (tok.shape, f32), (y.shape, bf16),
        ((own, 128), f32), ((own, 128), f32),
    ]
    return pl.pallas_call(
        functools.partial(finish_kernel, unit),
        grid=(steps,),
        out_shape=[jax.ShapeDtypeStruct(s, d) for s, d in outs],
        in_specs=[spec(a.shape) for a in ins],
        out_specs=[spec(s) for s, d in outs],
        compiler_params=pltpu.CompilerParams(vmem_limit_bytes=56 * 2**20),
        name="finish_stage",
    )(*ins)


def rotate(field, cosine, sine_table, direction):
    half_width = field.shape[-1] // 2
    first_half = field[..., :half_width]
    second_half = field[..., half_width:]
    return jnp.concatenate(
        [
            first_half * cosine - direction * second_half * sine_table,
            second_half * cosine + direction * first_half * sine_table,
        ],
        axis=-1,
    )


def gather(x, axis_name, axis=0):
    return lax.all_gather(x, axis_name, axis=axis, tiled=True)


def scatter(x, axis_name, axis=0):
    return lax.psum_scatter(x.astype(bf16), axis_name, scatter_dimension=axis, tiled=True)


def columns(w, start, count):
    return lax.dynamic_slice_in_dim(w, start, count, axis=1)


def visible(begin):
    seq = begin.shape[0]
    index = jnp.arange(seq, dtype=jnp.int32)
    return (index[None, :] <= index[:, None]) & (index[None, :] >= begin[:, None])


def forward_plain(tok, tab, gains, gcol, w_query, w_key, w_value, w_out, w_gate, w_up):
    n_ctx, n_fsdp = lax.axis_size("ctx"), lax.axis_size("fsdp")
    c = lax.axis_index("ctx")
    own_rows = w_query.shape[0]
    qw = HEADS // n_ctx * HEAD_DIM
    copies = max(1, n_ctx // KV_HEADS)
    kvw = max(1, KV_HEADS // n_ctx) * HEAD_DIM
    unit = w_gate.shape[1] // (n_fsdp * n_ctx)
    cw = tok.shape[1] // n_ctx
    wqkv_o = jnp.concatenate(
        [
            columns(w_query, c * qw, qw),
            columns(w_key, (c // copies) * kvw, kvw),
            columns(w_value, (c // copies) * kvw, kvw),
        ],
        axis=1,
    )
    wout_o = columns(w_out, c * cw, cw)

    def units(w):
        parts = w.reshape(own_rows, n_fsdp, n_ctx, unit)
        mine = lax.dynamic_index_in_dim(parts, c, axis=2, keepdims=False)
        return (gcol[:, 0:1] * mine.reshape(own_rows, n_fsdp * unit)).astype(bf16)

    wgate_o, wup_o = units(w_gate), units(w_up)
    x = gather(tok, "ctx")
    tabs = gather(tab[None], "ctx")
    wqkv = gather(wqkv_o, "fsdp")
    wout = gather(wout_o, "fsdp")
    wgate = gather(wgate_o, "fsdp")
    wup = gather(wup_o, "fsdp")
    gain = gather(gains[0:1], "fsdp", axis=1).astype(f32)
    xf = x.astype(f32)
    r = lax.rsqrt(jnp.mean(xf * xf, axis=-1, keepdims=True) + eps_norm)
    xn = (xf * r * gain).astype(bf16)
    seq, width = x.shape
    heads = HEADS // n_ctx
    qw = heads * HEAD_DIM
    pre = dot(xn, wqkv)
    cosine = tabs[:, 0:32].transpose(0, 2, 1).reshape(seq, 1, 32)
    sine = tabs[:, 32:64].transpose(0, 2, 1).reshape(seq, 1, 32)
    begin = tabs[:, 64].reshape(seq).astype(jnp.int32)
    kvw = (wqkv.shape[1] - qw) // 2
    kv = kvw // HEAD_DIM
    q = rotate(pre[:, :qw].reshape(seq, heads, HEAD_DIM), cosine, sine, 1.0).astype(bf16)
    k = rotate(pre[:, qw : qw + kvw].reshape(seq, kv, HEAD_DIM), cosine, sine, 1.0).astype(bf16)
    v = pre[:, qw + kvw :].astype(bf16).reshape(seq, kv, HEAD_DIM)
    qg = q.reshape(seq, kv, heads // kv, HEAD_DIM)
    scores = jnp.einsum("qkgd,lkd->kgql", qg, k, preferred_element_type=f32) * HEAD_DIM ** (-0.5)
    scores = jnp.where(visible(begin)[None, None], scores, neg_large)
    top = jnp.max(scores, axis=-1, keepdims=True)
    weights = jnp.exp(scores - top)
    total = jnp.sum(weights, axis=-1, keepdims=True)
    probs_low = (weights / total).astype(bf16)
    att = jnp.einsum("kgql,lkd->qkgd", probs_low, v, preferred_element_type=f32)
    o = gather(att.astype(bf16).reshape(seq, qw), "ctx", axis=1)
    lse = (top + jnp.log(total)).reshape(heads, 1, seq)
    lse = jnp.broadcast_to(lse, (heads, 8, seq)).reshape(8 * heads, seq)
    cw = width // n_ctx
    mid = columns(x, c * cw, cw).astype(f32) + dot(o, wout)
    m = gather(mid.astype(bf16), "ctx", axis=1)
    qt = q.reshape(seq, qw).T
    kt = k.reshape(seq, kvw).T
    vt = v.reshape(seq, kvw).T
    r = jnp.broadcast_to(r, (seq, 128))
    grow = jnp.broadcast_to(gain, (8, width))
    return xn, r, grow, qt, kt, vt, lse, o, m, wqkv, wout, wgate, wup, tabs


def middle_plain(m, cot, wgate, wup, w_down):
    n_ctx = lax.axis_size("ctx")
    c = lax.axis_index("ctx")
    unit = w_down.shape[0] // n_ctx
    wdown_o = lax.dynamic_slice_in_dim(w_down, c * unit, unit, axis=0)
    seq, width = m.shape
    rows = seq // n_ctx
    cw = width // n_ctx
    wdown = gather(wdown_o, "fsdp")
    cot_all = gather(cot, "ctx")
    mf = m.astype(f32)
    r = lax.rsqrt(jnp.mean(mf * mf, axis=-1, keepdims=True) + eps_norm)
    gate = dot(m, wgate) * r
    up = dot(m, wup) * r
    sig = jax.nn.sigmoid(gate)
    hidden = (gate * sig * up).astype(bf16)
    mlp = scatter(dot(hidden, wdown), "ctx").astype(f32)
    mid_rows = lax.dynamic_slice_in_dim(m, c * rows, rows, axis=0).astype(f32)
    output = (mid_rows + mlp).astype(bf16)
    grad_hidden = dot_nt(cot_all, wdown)
    down_sum = scatter(dot_tn(hidden, cot_all), "fsdp")
    d_gate = grad_hidden * up * sig * (1.0 + gate * (1.0 - sig))
    d_up = grad_hidden * gate * sig
    stat = jnp.sum(d_gate * gate + d_up * up, axis=-1, keepdims=True)
    d_gate = (d_gate * r).astype(bf16)
    d_up = (d_up * r).astype(bf16)
    gate_raw = dot_tn(m, d_gate).astype(bf16)
    up_raw = dot_tn(m, d_up).astype(bf16)
    back = dot_nt(d_gate, wgate) + dot_nt(d_up, wup) - mf * (r * r * stat * (1.0 / width))
    back_own = scatter(back, "ctx", axis=1).astype(f32)
    gm = (columns(cot_all, c * cw, cw).astype(f32) + back_own).astype(bf16)
    return output, None, down_sum, gate_raw, up_raw, gm


def backward_plain(xn, r, grow, qt, kt, vt, lse, o, gm, wqkv, wout, tabs, gate_raw, up_raw, down_sum):
    n_ctx = lax.axis_size("ctx")
    c = lax.axis_index("ctx")
    seq, width = xn.shape
    r, gain = r[:, 0:1], grow[0:1]
    heads = HEADS // n_ctx
    qw = heads * HEAD_DIM
    kvw = kt.shape[0]
    kv = kvw // HEAD_DIM
    cw = width // n_ctx
    scale = HEAD_DIM ** (-0.5)
    cosine = tabs[:, 0:32].transpose(0, 2, 1).reshape(seq, 1, 32)
    sine = tabs[:, 32:64].transpose(0, 2, 1).reshape(seq, 1, 32)
    begin = tabs[:, 64].reshape(seq).astype(jnp.int32)
    gate_grad = scatter(gate_raw, "fsdp")
    up_grad = scatter(up_raw, "fsdp")
    out_grad = scatter(dot_tn(o, gm), "fsdp")
    d_att = scatter(dot_nt(gm, wout), "ctx", axis=1).reshape(seq, kv, heads // kv, HEAD_DIM)
    q = qt.T.reshape(seq, kv, heads // kv, HEAD_DIM)
    k = kt.T.reshape(seq, kv, HEAD_DIM)
    v = vt.T.reshape(seq, kv, HEAD_DIM)
    scores = jnp.einsum("qkgd,lkd->kgql", q, k, preferred_element_type=f32) * scale
    scores = jnp.where(visible(begin)[None, None], scores, neg_large)
    lse = lse.reshape(kv, heads // kv, 8, seq)[:, :, 0, :, None]
    probs = jnp.exp(scores - lse)
    d_probs = jnp.einsum("qkgd,lkd->kgql", d_att, v, preferred_element_type=f32)
    delta = jnp.sum(probs * d_probs, axis=-1, keepdims=True)
    d_scores = (probs * (d_probs - delta)).astype(bf16)
    d_q = jnp.einsum("kgql,lkd->qkgd", d_scores, k, preferred_element_type=f32) * scale
    d_k = jnp.einsum("kgql,qkgd->lkd", d_scores, q, preferred_element_type=f32) * scale
    d_v = jnp.einsum("kgql,qkgd->lkd", probs.astype(bf16), d_att, preferred_element_type=f32)
    stat = (
        jnp.sum(d_q * q, axis=(1, 2, 3)) + jnp.sum(d_k * k, axis=(1, 2)) + jnp.sum(d_v * v, axis=(1, 2))
    )[:, None]
    d_q = rotate(d_q.reshape(seq, heads, HEAD_DIM), cosine, sine, -1.0).reshape(seq, qw)
    d_k = rotate(d_k, cosine, sine, -1.0).reshape(seq, kvw)
    d_pre = jnp.concatenate([d_q, d_k, d_v.reshape(seq, kvw)], axis=1).astype(bf16)
    qkv_grad = scatter(dot_tn(xn, d_pre), "fsdp")
    back = dot_nt(d_pre, wqkv) * (gain * r)
    back = back - xn.astype(f32) * ((1.0 / gain) * (r * stat * (1.0 / width)))
    at = (jnp.arange(width, dtype=jnp.int32) // cw == c)[None, :]
    back = back + jnp.where(at, jnp.tile(gm.astype(f32), (1, n_ctx)), 0.0)
    grad_tokens = scatter(back, "ctx").astype(f32)
    qkv_all = gather(qkv_grad[None], "ctx")
    out_all = gather(out_grad[None], "ctx")
    gate_all = gather(gate_grad[None], "ctx")
    up_all = gather(up_grad[None], "ctx")
    down_all = gather(down_sum[None], "ctx")
    return grad_tokens, qkv_all, out_all, gate_all, up_all, down_all


def finish_plain(qkv_all, out_all, gate_all, up_all, down_all, tok, y, w_query, w_key, w_value, w_gate, w_up, g1, g2):
    n_ctx, n_fsdp = lax.axis_size("ctx"), lax.axis_size("fsdp")
    own_rows = w_query.shape[0]
    qw = HEADS // n_ctx * HEAD_DIM
    copies = max(1, n_ctx // KV_HEADS)
    kvw = max(1, KV_HEADS // n_ctx) * HEAD_DIM
    ff_width = w_gate.shape[1]
    unit = ff_width // (n_fsdp * n_ctx)
    qkv_all = qkv_all.astype(f32)

    def joined(part):
        return jnp.moveaxis(part, 0, 1).reshape(own_rows, -1)

    def kv_part(part):
        return joined(part.reshape(n_ctx // copies, copies, own_rows, kvw).sum(axis=1))

    grad_query = joined(qkv_all[:, :, :qw])
    grad_key = kv_part(qkv_all[:, :, qw : qw + kvw])
    grad_value = kv_part(qkv_all[:, :, qw + kvw :])
    grad_out = joined(out_all.astype(f32))

    def spread(full):
        full = full.reshape(n_ctx, own_rows, n_fsdp, unit)
        return full.transpose(1, 2, 0, 3).reshape(own_rows, ff_width).astype(f32)

    raw_gate, raw_up = spread(gate_all), spread(up_all)
    grad_down = down_all.astype(f32).reshape(-1, down_all.shape[-1])

    def gain_term(grad, w):
        return jnp.sum(grad * w.astype(f32), axis=1, keepdims=True)

    first = gain_term(grad_query, w_query) + gain_term(grad_key, w_key) + gain_term(grad_value, w_value)
    second = gain_term(raw_gate, w_gate) + gain_term(raw_up, w_up)
    g1, g2 = g1[:, 0:1], g2[:, 0:1]
    return (
        grad_query, grad_key, grad_value, grad_out, g2 * raw_gate, g2 * raw_up, grad_down, tok, y, first / g1, second,
    )


def per_device(
    tokens,
    positions,
    gain_attn,
    gain_mlp,
    w_query,
    w_key,
    w_value,
    w_out,
    w_gate,
    w_up,
    w_down,
    cotangent,
):
    kernels = lax.axis_size("ctx") == 4 and lax.axis_size("fsdp") == 8
    c = lax.axis_index("ctx")
    rows = tokens.shape[0]
    own_rows = w_query.shape[0]
    gains = jnp.broadcast_to(gain_attn[None, :], (16, own_rows))
    gain_one = jnp.broadcast_to(gain_attn.astype(f32)[:, None], (own_rows, 128))
    gain_two = jnp.broadcast_to(gain_mlp.astype(f32)[:, None], (own_rows, 128))
    frequency = theta_base ** (-(jnp.arange(HEAD_DIM // 2, dtype=f32) * 2.0) / HEAD_DIM)
    angles = frequency[:, None] * positions.astype(f32)[None, :]
    begin = c * rows + jnp.arange(rows, dtype=jnp.int32) - positions
    tab = jnp.concatenate(
        [jnp.cos(angles), jnp.sin(angles), jnp.broadcast_to(begin.astype(f32)[None, :], (16, rows))],
        axis=0,
    )

    forward = forward_stage if kernels else forward_plain
    xn, r, grow, qt, kt, vt, lse, o, m, wqkv, wout, wgate, wup, tabs = forward(
        tokens, tab, gains, gain_two, w_query, w_key, w_value, w_out, w_gate, w_up
    )
    middle = middle_stage if kernels else middle_plain
    y, _, down_sum, gate_raw, up_raw, gm = middle(m, cotangent, wgate, wup, w_down)
    backward = backward_stage if kernels else backward_plain
    tok, qkv_all, out_all, gate_all, up_all, down_all = backward(
        xn, r, grow, qt, kt, vt, lse, o, gm, wqkv, wout, tabs, gate_raw, up_raw, down_sum
    )
    finish = finish_stage if kernels else finish_plain
    g_query, g_key, g_value, g_out, g_gate, g_up, g_down, tok, y, g_one, g_two = finish(
        qkv_all, out_all, gate_all, up_all, down_all, tok, y,
        w_query, w_key, w_value, w_gate, w_up, gain_one, gain_two,
    )
    return (y, tok, g_one[:, 0], g_two[:, 0], g_query, g_key, g_value, g_out, g_gate, g_up, g_down)


def solution(mesh):
    both = P(("fsdp", "ctx"), None)
    first = P("fsdp", None)
    return jax.shard_map(
        per_device,
        mesh=mesh,
        in_specs=(both, P(("fsdp", "ctx")), P("fsdp"), P("fsdp")) + (first,) * 7 + (both,),
        out_specs=(both, both, P("fsdp"), P("fsdp")) + (first,) * 7,
        check_vma=False,
    )
```

```python
import functools

import jax
import jax.numpy as jnp
from jax import lax
from jax.experimental import pallas as pl
from jax.experimental.pallas import tpu as pltpu
from jax.sharding import PartitionSpec as P

HEADS = 32
KV_HEADS = 4
HEAD_DIM = 64

eps_norm = 1e-05
theta_base = 10000.0
neg_large = -1e30
bf16 = jnp.bfloat16
f32 = jnp.float32
MESH_IDS = pl.DeviceIdType.MESH


def dot(a, b):
    return jnp.dot(a, b, preferred_element_type=f32)


def dot_nt(a, b):
    return lax.dot_general(a, b, (((1,), (1,)), ((), ())), preferred_element_type=f32)


def dot_tn(a, b):
    return lax.dot_general(a, b, (((0,), (0,)), ((), ())), preferred_element_type=f32)


class Place:
    def __init__(self):
        self.f = lax.axis_index("fsdp")
        self.c = lax.axis_index("ctx")
        self.depth = lax.axis_size("fsdp") // 2
        self.z = self.f // 2
        self.core = self.f % 2
        self.other = 1 - self.core
        self.cx = self.c + 1 - 2 * (self.c % 2)
        self.cy = self.c + 2 - 4 * (self.c // 2)
        self.cd = 3 - self.c
        self.sibling = {"fsdp": self.f + 1 - 2 * self.core}
        self.up = {"fsdp": self.f + 2}
        self.down = {"fsdp": self.f - 2}
        self.x = {"ctx": self.cx}
        self.y = {"ctx": self.cy}

    def has_up(self):
        return self.z < self.depth - 1

    def has_down(self):
        return self.z > 0

    def barrier(self):
        sem = pltpu.get_barrier_semaphore()

        def greet(device):
            pl.semaphore_signal(sem, inc=1, device_id=device, device_id_type=MESH_IDS)

        greet(self.sibling)
        greet(self.x)
        greet(self.y)

        @pl.when(self.has_up())
        def _():
            greet(self.up)

        @pl.when(self.has_down())
        def _():
            greet(self.down)

        last = self.depth - 1
        pl.semaphore_wait(sem, 4 - self.z // last + (self.z + last - 1) // last)


def remote(src, dst, send_sem, recv_sem, device):
    return pltpu.make_async_remote_copy(
        src_ref=src,
        dst_ref=dst,
        send_sem=send_sem,
        recv_sem=recv_sem,
        device_id=device,
        device_id_type=MESH_IDS,
    )


class LineGather:
    SEMS = 21

    def __init__(self, place, own, full, sems):
        self.p, self.own, self.full, self.sems = place, own, full, sems
        self.n = place.depth
        self.rows = full.shape[0] // (2 * self.n)

    def view(self, level, core):
        start = pl.multiple_of((2 * level + core) * self.rows, 16)
        return self.full.at[pl.ds(start, self.rows)]

    def to_up(self, hop):
        p = self.p
        level = p.z - (hop - 1)
        src = self.own if hop == 1 and self.own is not None else self.view(level, p.core)
        return remote(
            src, self.view(level, p.core), self.sems.at[hop - 1], self.sems.at[6 + hop - 1], p.up
        )

    def to_down(self, hop):
        p = self.p
        level = p.z + (hop - 1)
        src = self.own if hop == 1 and self.own is not None else self.view(level, p.core)
        return remote(
            src, self.view(level, p.core), self.sems.at[3 + hop - 1], self.sems.at[9 + hop - 1], p.down
        )

    def to_sibling(self, level, own=False):
        p = self.p
        src = self.own if own and self.own is not None else self.view(level, p.core)
        return remote(
            src, self.view(level, p.core), self.sems.at[12 + level], self.sems.at[16 + level], p.sibling
        )

    def local(self):
        p = self.p
        return pltpu.make_async_copy(self.own, self.view(p.z, p.core), self.sems.at[20])

    def start(self):
        p = self.p

        @pl.when(p.has_up())
        def _():
            self.to_up(1).start()

        @pl.when(p.has_down())
        def _():
            self.to_down(1).start()

        self.to_sibling(p.z, True).start()
        if self.own is not None:
            self.local().start()

    def arrived(self, level, sem):
        view = self.view(level, self.p.core)
        remote(view, view, self.sems.at[0], sem, self.p.sibling).wait_recv()

    def hop(self, s):
        p = self.p

        @pl.when(p.z >= s)
        def _():
            self.arrived(p.z - s, self.sems.at[6 + s - 1])
            if s < self.n - 1:

                @pl.when(p.has_up())
                def _():
                    self.to_up(s + 1).start()

            self.to_sibling(p.z - s).start()

        @pl.when(p.z + s < self.n)
        def _():
            self.arrived(p.z + s, self.sems.at[9 + s - 1])
            if s < self.n - 1:

                @pl.when(p.has_down())
                def _():
                    self.to_down(s + 1).start()

            self.to_sibling(p.z + s).start()

    def finish(self):
        p = self.p
        if self.own is not None:
            self.local().wait()
        for level in range(self.n):
            view = self.view(level, p.other)
            remote(view, view, self.sems.at[0], self.sems.at[16 + level], p.sibling).wait_recv()

    def drain(self):
        p = self.p
        for s in range(1, self.n):

            @pl.when(p.has_up() & (p.z >= s - 1))
            def _():
                self.to_up(s).wait_send()

            @pl.when(p.has_down() & (p.z + s - 1 < self.n))
            def _():
                self.to_down(s).wait_send()

        for level in range(self.n):
            self.to_sibling(level).wait_send()


class PlaneGather:
    SEMS = 8

    def __init__(self, place, view, half, sems, own=None):
        self.p, self.view, self.half, self.sems = place, view, half, sems
        self.own = own

    def src(self):
        return self.view(self.p.c) if self.own is None else self.own

    def to_x(self):
        p = self.p
        return remote(self.src(), self.view(p.c), self.sems.at[0], self.sems.at[2], p.x)

    def to_y(self):
        p = self.p
        return remote(self.src(), self.view(p.c), self.sems.at[1], self.sems.at[3], p.y)

    def on_to_y(self):
        p, h = self.p, self.half(self.p.cx, 0)
        return remote(h, h, self.sems.at[4], self.sems.at[6], p.y)

    def on_to_x(self):
        p, h = self.p, self.half(self.p.cy, 1)
        return remote(h, h, self.sems.at[5], self.sems.at[7], p.x)

    def start(self):
        self.to_x().start()
        self.to_y().start()

    def got(self, ref, sem):
        remote(ref, ref, self.sems.at[0], sem, self.p.x).wait_recv()

    def middle(self):
        p = self.p
        self.got(self.view(p.cx), self.sems.at[2])
        self.on_to_y().start()
        self.got(self.view(p.cy), self.sems.at[3])
        self.on_to_x().start()

    def finish(self):
        p = self.p
        self.got(self.half(p.cd, 0), self.sems.at[6])
        self.got(self.half(p.cd, 1), self.sems.at[7])

    def drain(self):
        self.to_x().wait_send()
        self.to_y().wait_send()
        self.on_to_y().wait_send()
        self.on_to_x().wait_send()


def rows_at(index, count):
    return pl.ds(pl.multiple_of(index * count, count), count)


def any_spec(count):
    return [pl.BlockSpec(memory_space=pl.ANY)] * count


def call(kernel, ins, outs, scratch, collective_id, flops, name, vmem=60.0):
    return pl.pallas_call(
        kernel,
        out_shape=[jax.ShapeDtypeStruct(s, d) for s, d in outs],
        in_specs=any_spec(len(ins)),
        out_specs=any_spec(len(outs)),
        scratch_shapes=scratch,
        compiler_params=pltpu.CompilerParams(
            collective_id=collective_id, has_side_effects=True, vmem_limit_bytes=int(vmem * 2**20)
        ),
        cost_estimate=pl.CostEstimate(flops=flops, bytes_accessed=2**26, transcendentals=2**22),
        name=name,
    )(*ins)


def tiles_of(total, most):
    sizes, at = [], 0
    while at < total:
        sizes.append((at, min(most, total - at)))
        at += most
    return sizes


def add_to(ref, other):
    for start, size in tiles_of(ref.shape[0], 96):
        at = pl.ds(start, size)
        ref[at, :] = (ref[at, :].astype(f32) + other[at, :].astype(f32)).astype(bf16)


class PlaneScatter:
    SEMS = 12

    def __init__(self, place, part, half, first, second, sems):
        self.p, self.part, self.half = place, part, half
        self.first, self.second, self.sems = first, second, sems

    def far(self, h):
        p = self.p
        return remote(
            self.half(p.cd, h), self.first.at[h], self.sems.at[h], self.sems.at[2 + h], p.x if h else p.y
        )

    def direct(self, to_y, h, base):
        p = self.p
        count = self.first.shape[1]
        return remote(
            self.half(p.cy if to_y else p.cx, h),
            self.second.at[to_y, pl.ds(h * count, count)],
            self.sems.at[base + to_y],
            self.sems.at[base + 2 + to_y],
            p.y if to_y else p.x,
        )

    def start(self):
        self.far(0).start()
        self.far(1).start()

    def near(self):
        self.direct(0, 1, 8).start()
        self.direct(1, 0, 8).start()

    def middle(self):
        p = self.p
        for to_y in (0, 1):
            self.far(to_y).wait_recv()
            add_to(self.half(p.cy if to_y else p.cx, to_y), self.first.at[to_y])
            self.direct(to_y, to_y, 4).start()

    def finish(self, at=slice(None), first=True):
        if first:
            for to_y in (0, 1):
                self.direct(to_y, 1 - to_y, 8).wait_recv()
                self.direct(to_y, to_y, 4).wait_recv()
        own = self.part(self.p.c)[at].astype(f32)
        return own + self.second[0, at].astype(f32) + self.second[1, at].astype(f32)

    def drain(self):
        for to_y in (0, 1):
            self.far(to_y).wait_send()
            self.direct(to_y, 1 - to_y, 8).wait_send()
            self.direct(to_y, to_y, 4).wait_send()


class LineScatter:
    SEMS = 22

    def __init__(self, place, part, acc, slots, sems, stage=None):
        self.p, self.part, self.acc, self.slots, self.sems = place, part, acc, slots, sems
        self.stage = stage
        self.n = place.depth

    def to_sibling(self, level):
        p = self.p
        return remote(
            self.part(level, p.other), self.acc.at[level], self.sems.at[level], self.sems.at[4 + level], p.sibling
        )

    def start(self):
        for level in range(self.n):
            self.to_sibling(level).start()

    def load(self, level):
        return pltpu.make_async_copy(
            self.part(level, self.p.core), self.stage[level % 2], self.sems.at[20 + level % 2]
        )

    def got(self, ref, sem):
        remote(ref, ref, self.sems.at[0], sem, self.p.sibling).wait_recv()

    def add(self, ref, other):
        add_to(ref, other)

    def combine(self):
        if self.stage is not None:
            self.load(0).start()
            self.load(1).start()
        for level in range(self.n):
            self.got(self.acc.at[level], self.sems.at[4 + level])
            if self.stage is None:
                self.add(self.acc.at[level], self.part(level, self.p.core))
            else:
                self.load(level).wait()
                self.add(self.acc.at[level], self.stage[level % 2])
                if level + 2 < self.n:
                    self.load(level + 2).start()

    def slot(self, up, s):
        return self.slots.at[s - 1] if up else self.slots.at[(0, 3, 4)[s - 1]]

    def along(self, up, s):
        p = self.p
        level = p.z if up else self.n - 1 - p.z
        block = self.n - s + level
        block = block if up else self.n - 1 - block
        base = 8 if up else 14
        copy = remote(
            self.acc.at[block],
            self.slot(up, s),
            self.sems.at[base + s - 1],
            self.sems.at[base + 3 + s - 1],
            p.up if up else p.down,
        )
        return copy, (level <= s - 1) & (level < self.n - 1)

    def step(self, s):
        for up in (True, False):
            level = self.p.z if up else self.n - 1 - self.p.z
            if s > 1:
                block = self.n - s + level
                block = block if up else self.n - 1 - block
                base = 11 if up else 17

                @pl.when((level >= 1) & (s - 1 >= level))
                def _():
                    self.got(self.slot(up, s - 1), self.sems.at[base + s - 2])
                    self.add(self.acc.at[block], self.slot(up, s - 1))

            if s < self.n:
                copy, valid = self.along(up, s)

                @pl.when(valid)
                def _():
                    copy.start()

    def result(self):
        return self.acc.at[self.p.z]

    def drain(self):
        for level in range(self.n):
            self.to_sibling(level).wait_send()
        for up in (True, False):
            for s in range(1, self.n):
                copy, valid = self.along(up, s)

                @pl.when(valid)
                def _():
                    copy.wait_send()


def forward_kernel(
    tok, tab, gains, gcol, w_query, w_key, w_value, w_out, w_gate, w_up,
    xn_out, r_out, grow_out, qt_out, kt_out, vt_out, lse_out, o_out, m_out,
    wqkv_out, wout_out, wgate, wup, tab_out,
    X, XN, QT, KT, VT, K, LSE, O, M, WQ, WO, TAB, G8, GROW, BIAS, OT, R1,
    WK, WV, GF, UF, GO, UO, GCOL,
    line_sems, plane_sems, copy_sems,
):
    p = Place()
    n_ctx = 4
    rows = tok.shape[0]
    half = rows // 2
    qw = QT.shape[0]
    heads = qw // HEAD_DIM
    cw = O.shape[1] // n_ctx
    scale = HEAD_DIM ** (-0.5)

    mine = rows_at(p.f, WK.shape[0])
    loads = []
    for i, (src, dst) in enumerate(
        (
            (w_query.at[:, rows_at(p.c, qw)], WQ.at[mine, pl.ds(0, qw)]),
            (w_key, WK), (w_value, WV), (w_gate, GF), (w_up, UF), (gcol, GCOL),
        )
    ):
        loads.append(pltpu.make_async_copy(src, dst, copy_sems.at[15 + i]))
        loads[-1].start()

    p.barrier()

    gain_line = LineGather(p, gains, G8, line_sems.at[0])
    qkv_line = LineGather(p, None, WQ, line_sems.at[1])
    out_line = LineGather(p, w_out.at[:, rows_at(p.c, cw)], WO, line_sems.at[2])
    gate_line = LineGather(p, GO, wgate, line_sems.at[3])
    up_line = LineGather(p, UO, wup, line_sems.at[4])

    def row_block(ref):
        return (
            lambda c: ref.at[rows_at(c, rows)],
            lambda c, h: ref.at[pl.ds(pl.multiple_of(c * rows + h * half, half), half)],
        )

    tok_plane = PlaneGather(p, *row_block(X), plane_sems.at[0], own=tok)
    tab_rows = tab.shape[0]
    tab_plane = PlaneGather(
        p,
        lambda c: TAB.at[c],
        lambda c, h: TAB.at[c, pl.ds(h * (tab_rows // 2), tab_rows // 2)],
        plane_sems.at[2],
        own=tab,
    )

    def col_block(ref, b):
        def view(c):
            return ref.at[pl.ds(b * rows, rows), rows_at(c, cw)]

        def halves(c, h):
            return ref.at[pl.ds(b * rows + h * half, half), rows_at(c, cw)]

        return view, halves

    o_plane = [PlaneGather(p, *col_block(O, b), plane_sems.at[3 + b]) for b in range(n_ctx)]
    m_plane = [PlaneGather(p, *col_block(M, b), plane_sems.at[7 + b]) for b in range(n_ctx)]

    gain_line.start()
    tab_plane.start()
    tok_plane.start()
    out_line.start()
    for i in range(3):
        loads[i].wait()
    for c in range(n_ctx):

        @pl.when(p.c == c)
        def _():
            WQ[mine, qw : qw + HEAD_DIM] = WK[:, HEAD_DIM * c : HEAD_DIM * (c + 1)]
            WQ[mine, qw + HEAD_DIM :] = WV[:, HEAD_DIM * c : HEAD_DIM * (c + 1)]

    qkv_line.start()
    own_tok = pltpu.make_async_copy(tok, X.at[rows_at(p.c, rows)], copy_sems.at[0])
    own_tab = pltpu.make_async_copy(tab, TAB.at[p.c], copy_sems.at[1])
    own_tok.start()
    own_tab.start()

    for i in range(3, 6):
        loads[i].wait()
    unit = GO.shape[1] // (2 * p.depth)
    for c in range(n_ctx):

        @pl.when(p.c == c)
        def _():
            for f in range(2 * p.depth):
                at = (f * n_ctx + c) * unit
                for src, dst in ((GF, GO), (UF, UO)):
                    part = src[:, at : at + unit].astype(f32) * GCOL[:, 0:1]
                    dst[:, f * unit : (f + 1) * unit] = part.astype(bf16)

    gain_line.hop(1)
    tab_plane.middle()
    gain_line.hop(2)
    qkv_line.hop(1)
    gain_line.hop(3)
    gain_line.finish()
    for f in range(2 * p.depth):
        GROW[:, f * gains.shape[1] : (f + 1) * gains.shape[1]] = G8[16 * f : 16 * f + 8, :].astype(f32)

    def norm(c):
        at = rows_at(c, rows)
        x = X[at, :].astype(f32)
        r = lax.rsqrt(jnp.mean(x * x, axis=-1, keepdims=True) + eps_norm)
        R1[at, :] = jnp.broadcast_to(r, (rows, 128))
        XN[at, :] = (x * r * GROW[0:1, :]).astype(bf16)

    own_tok.wait()
    norm(p.c)
    out_line.hop(1)
    qkv_line.hop(2)
    tok_plane.middle()
    out_line.hop(2)
    gate_line.start()
    norm(p.cx)
    norm(p.cy)
    qkv_line.hop(3)
    tok_plane.finish()
    out_line.hop(3)
    up_line.start()
    norm(p.cd)
    xn_copy = pltpu.make_async_copy(XN, xn_out, copy_sems.at[3])
    r_copy = pltpu.make_async_copy(R1, r_out, copy_sems.at[4])
    grow_copy = pltpu.make_async_copy(GROW, grow_out, copy_sems.at[14])
    xn_copy.start()
    r_copy.start()
    grow_copy.start()
    own_tab.wait()
    tab_plane.finish()
    qkv_line.finish()

    @pl.loop(0, n_ctx)
    def _(b):
        at = rows_at(b, rows)
        pre = dot(XN[at, :], WQ[...]).T
        cosine = TAB[b, 0:32, :]
        sine = TAB[b, 32:64, :]
        for h in range(heads + 1):
            u = pre[64 * h : 64 * h + 32]
            w = pre[64 * h + 32 : 64 * h + 64]
            first = u * cosine - w * sine
            second = w * cosine + u * sine
            if h < heads:
                QT[64 * h : 64 * h + 32, at] = first.astype(bf16)
                QT[64 * h + 32 : 64 * h + 64, at] = second.astype(bf16)
            else:
                KT[0:32, at] = first.astype(bf16)
                KT[32:64, at] = second.astype(bf16)
                K[at, :] = jnp.concatenate([first, second], axis=0).T.astype(bf16)
        VT[:, at] = pre[qw + 64 :].astype(bf16)

    wq_copy = pltpu.make_async_copy(WQ, wqkv_out, copy_sems.at[5])
    wq_copy.start()

    def attend(b):
        n = (b + 1) * rows
        key = lax.broadcasted_iota(jnp.int32, (n, rows), 0)
        query = lax.broadcasted_iota(jnp.int32, (n, rows), 1) + b * rows
        begin = TAB[b, 64:65, :].astype(jnp.int32)
        BIAS[0:n, :] = jnp.where((key <= query) & (key >= begin), 0.0, neg_large)
        cols = slice(b * rows, (b + 1) * rows)

        @pl.loop(0, heads)
        def _(h):
            head = rows_at(h, HEAD_DIM)
            s = dot(K[0:n, :], QT[head, cols]) * scale + BIAS[0:n, :]
            top = jnp.max(s, axis=0, keepdims=True)
            e = jnp.exp(s - top)
            total = jnp.sum(e, axis=0, keepdims=True)
            probs = (e * (1.0 / total)).astype(bf16)
            OT[head, :] = dot(VT[:, 0:n], probs)
            LSE[rows_at(h, 8), cols] = jnp.broadcast_to(top + jnp.log(total), (8, rows))

        O[pl.ds(b * rows, rows), rows_at(p.c, cw)] = OT[...].T.astype(bf16)
        o_plane[b].start()

    def middle(b):
        at = pl.ds(b * rows, rows)
        cols = rows_at(p.c, cw)
        mid = X[at, cols].astype(f32) + dot(O[at, :], WO[...])
        M[at, cols] = mid.astype(bf16)
        m_plane[b].start()

    attend(0)
    attend(1)
    o_plane[0].middle()
    attend(2)
    gate_line.hop(1)
    o_plane[1].middle()
    attend(3)
    o_plane[2].middle()
    out_line.finish()
    o_plane[0].finish()
    middle(0)
    o_plane[1].finish()
    middle(1)
    o_plane[3].middle()
    up_line.hop(1)
    m_plane[0].middle()
    o_plane[2].finish()
    middle(2)
    m_plane[1].middle()
    o_plane[3].finish()
    middle(3)
    m_plane[2].middle()
    gate_line.hop(2)
    m_plane[3].middle()
    up_line.hop(2)
    copies = [xn_copy, r_copy, grow_copy, wq_copy]
    for i, (src, dst) in enumerate(
        ((QT, qt_out), (KT, kt_out), (VT, vt_out), (LSE, lse_out), (O, o_out), (WO, wout_out), (TAB, tab_out))
    ):
        copy = pltpu.make_async_copy(src, dst, copy_sems.at[6 + i])
        copy.start()
        copies.append(copy)
    for b in range(n_ctx):
        m_plane[b].finish()
    m_copy = pltpu.make_async_copy(M, m_out, copy_sems.at[13])
    m_copy.start()
    copies.append(m_copy)
    gate_line.hop(3)
    up_line.hop(3)
    gate_line.finish()
    up_line.finish()
    for copy in copies:
        copy.wait()
    for line in (gain_line, qkv_line, out_line, gate_line, up_line):
        line.drain()
    for plane in [tok_plane, tab_plane] + o_plane + m_plane:
        plane.drain()


def forward_stage(tok, tab, gains, gcol, w_query, w_key, w_value, w_out, w_gate, w_up):
    n_fsdp, n_ctx = lax.axis_size("fsdp"), lax.axis_size("ctx")
    rows, width = tok.shape
    seq = rows * n_ctx
    own = w_query.shape[0]
    whole = n_fsdp * own
    qw = HEADS // n_ctx * HEAD_DIM
    nq, nw, nu = qw + 2 * HEAD_DIM, width // n_ctx, w_gate.shape[1] // n_ctx
    heads = qw // HEAD_DIM
    tab_shape = (n_ctx,) + tab.shape
    outs = [
        ((seq, width), bf16), ((seq, 128), f32), ((8, width), f32), ((qw, seq), bf16), ((64, seq), bf16),
        ((64, seq), bf16), ((8 * heads, seq), f32), ((seq, width), bf16), ((seq, width), bf16), ((whole, nq), bf16),
        ((whole, nw), bf16), ((whole, nu), bf16), ((whole, nu), bf16), (tab_shape, f32),
    ]
    scratch = [
        pltpu.VMEM((seq, width), bf16),
        pltpu.VMEM((seq, width), bf16),
        pltpu.VMEM((qw, seq), bf16),
        pltpu.VMEM((64, seq), bf16),
        pltpu.VMEM((64, seq), bf16),
        pltpu.VMEM((seq, 64), bf16),
        pltpu.VMEM((8 * heads, seq), f32),
        pltpu.VMEM((seq, width), bf16),
        pltpu.VMEM((seq, width), bf16),
        pltpu.VMEM((whole, nq), bf16),
        pltpu.VMEM((whole, nw), bf16),
        pltpu.VMEM(tab_shape, f32),
        pltpu.VMEM((16 * n_fsdp, gains.shape[1]), bf16),
        pltpu.VMEM((8, width), f32),
        pltpu.VMEM((seq, rows), f32),
        pltpu.VMEM((qw, rows), f32),
        pltpu.VMEM((seq, 128), f32),
        pltpu.VMEM(w_key.shape, bf16),
        pltpu.VMEM(w_value.shape, bf16),
        pltpu.VMEM(w_gate.shape, bf16),
        pltpu.VMEM(w_up.shape, bf16),
        pltpu.VMEM((own, nu), bf16),
        pltpu.VMEM((own, nu), bf16),
        pltpu.VMEM(gcol.shape, f32),
        pltpu.SemaphoreType.DMA((5, LineGather.SEMS)),
        pltpu.SemaphoreType.DMA((11, PlaneGather.SEMS)),
        pltpu.SemaphoreType.DMA((21,)),
    ]
    ins = (tok, tab, gains, gcol, w_query, w_key, w_value, w_out, w_gate, w_up)
    flops = 2 * seq * width * (nq + nw) + 8 * heads * seq * seq * HEAD_DIM
    return call(forward_kernel, ins, outs, scratch, 1, flops, "forward_stage")


def middle_kernel(
    m_in, cot, wgate_in, wup_in, w_down,
    y_out, down_part, down_sum, gate_part, up_part, gm_out,
    M, COT, WG, WU, WD, GATE, UP, HID, R2, PD, PH, D1, D2, H1, H2, DACC, DSLOT,
    line_sems, sum_sems, plane_sems, copy_sems, stage_sems,
):
    p = Place()
    n_ctx = 4
    seq, width = M.shape
    rows = seq // n_ctx
    half = rows // 2
    cw = width // n_ctx
    units = GATE.shape[1]
    loads = []
    for i, (src, dst) in enumerate(((m_in, M), (wgate_in, WG), (wup_in, WU), (cot, COT.at[rows_at(p.c, rows)]))):
        loads.append(pltpu.make_async_copy(src, dst, copy_sems.at[i]))
        loads[-1].start()

    p.barrier()
    unit = w_down.shape[0] // n_ctx
    down_own = w_down.at[pl.ds(pl.multiple_of(p.c * unit, 16), unit)]
    down_line = LineGather(p, down_own, WD, line_sems.at[0])
    down_line.start()
    cot_plane = PlaneGather(
        p,
        lambda c: COT.at[rows_at(c, rows)],
        lambda c, h: COT.at[pl.ds(pl.multiple_of(c * rows + h * half, half), half)],
        plane_sems.at[5],
        own=cot,
    )
    cot_plane.start()

    loads[0].wait()
    loads[1].wait()
    loads[2].wait()

    def activate(b):
        at = rows_at(b, rows)
        mf = M[at, :].astype(f32)
        r = lax.rsqrt(jnp.mean(mf * mf, axis=-1, keepdims=True) + eps_norm)
        R2[at, :] = jnp.broadcast_to(r, (rows, 128))
        for start, size in tiles_of(units, 512):
            cols = slice(start, start + size)
            gate = dot(M[at, :], WG[:, cols]) * r
            up = dot(M[at, :], WU[:, cols]) * r
            GATE[at, cols] = gate.astype(bf16)
            UP[at, cols] = up.astype(bf16)
            HID[at, cols] = (gate * (1.0 / (1.0 + jnp.exp(-gate))) * up).astype(bf16)

    pl.loop(0, 2)(activate)
    down_line.hop(1)
    pl.loop(2, 4)(activate)
    cot_plane.middle()
    down_line.hop(2)
    loads[3].wait()
    cot_plane.finish()
    stage_copies = {}
    for i, (at, size) in enumerate(tiles_of(units, rows)):
        slot = pl.ds(i % 2 * rows, size)
        if i >= 2:
            stage_copies[i - 2].wait()
        for j in range(0, width, cw):
            PH[slot, j : j + cw] = dot_tn(HID[:, at : at + size], COT[:, j : j + cw]).astype(bf16)
        copy = pltpu.make_async_copy(PH.at[slot], down_part.at[pl.ds(at, size)], stage_sems.at[i % 2])
        copy.start()
        stage_copies[i] = copy
    n_down = len(stage_copies)
    stage_copies[n_down - 2].wait()
    stage_copies[n_down - 1].wait()

    def down_block(level, core):
        return down_part.at[pl.ds(pl.multiple_of((2 * level + core) * unit, 16), unit)]

    down_stage = [PH.at[pl.ds(i * rows, unit)] for i in range(2)]
    sum_line = LineScatter(p, down_block, DACC, DSLOT, sum_sems.at[0], down_stage)
    sum_line.start()
    sum_line.combine()
    sum_line.step(1)
    down_line.hop(3)
    down_line.finish()

    y_plane = PlaneScatter(
        p,
        lambda c: PD.at[rows_at(c, rows)],
        lambda c, h: PD.at[pl.ds(pl.multiple_of(c * rows + h * half, half), half)],
        D1,
        D2,
        plane_sems.at[0],
    )

    def col_scatter(b):
        return PlaneScatter(
            p,
            lambda c: PH.at[pl.ds(b * rows, rows), rows_at(c, cw)],
            lambda c, h: PH.at[pl.ds(b * rows + h * half, half), rows_at(c, cw)],
            H1.at[b],
            H2.at[b],
            plane_sems.at[1 + b],
        )

    h_plane = [col_scatter(b) for b in range(n_ctx)]

    def partial_out(c):
        at = rows_at(c, rows)
        for j in range(0, width, cw):
            PD[at, j : j + cw] = dot(HID[at, :], WD[:, j : j + cw]).astype(bf16)

    partial_out(p.cd)
    y_plane.start()
    partial_out(p.cx)
    partial_out(p.cy)
    y_plane.near()
    partial_out(p.c)

    def back(b):
        at = pl.ds(b * rows, rows)
        r = R2[at, 0:1]
        stat = jnp.zeros((rows, 1), f32)
        for start, size in tiles_of(units, 512):
            cols = slice(start, start + size)
            grad_hidden = dot_nt(COT[at, :], WD[cols, :])
            gate = GATE[at, cols].astype(f32)
            up = UP[at, cols].astype(f32)
            sig = 1.0 / (1.0 + jnp.exp(-gate))
            d_up = grad_hidden * gate * sig
            d_gate = grad_hidden * up * sig * (1.0 + gate * (1.0 - sig))
            stat += jnp.sum(d_gate * gate + d_up * up, axis=-1, keepdims=True)
            GATE[at, cols] = (d_gate * r).astype(bf16)
            UP[at, cols] = (d_up * r).astype(bf16)
        coef = r * r * stat * (1.0 / width)
        for j in range(0, width, cw):
            e = dot_nt(GATE[at, :], WG[j : j + cw, :]) + dot_nt(UP[at, :], WU[j : j + cw, :])
            PH[at, j : j + cw] = (e - M[at, j : j + cw].astype(f32) * coef).astype(bf16)
        h_plane[b].start()
        h_plane[b].near()

    back(0)
    y_plane.middle()
    back(1)
    sum_line.step(2)
    h_plane[0].middle()
    back(2)
    h_plane[1].middle()
    sum_line.step(3)
    back(3)
    h_plane[2].middle()

    stage_copies = {}
    jobs = []
    for src, dst in ((GATE, gate_part), (UP, up_part)):
        for at, size in tiles_of(width, 512):
            jobs.append((src, dst, at, size))

    def weight_tile(i):
        src, dst, at, size = jobs[i]
        slot = pl.ds(i % 2 * size, size)
        if i >= 2:
            stage_copies[i - 2].wait()
        for start, part in tiles_of(units, 512):
            cols = slice(start, start + part)
            HID[slot, cols] = dot_tn(M[:, at : at + size], src[:, cols]).astype(bf16)
        copy = pltpu.make_async_copy(HID.at[slot], dst.at[pl.ds(at, size)], stage_sems.at[2 + i % 2])
        copy.start()
        stage_copies[i] = copy

    def finish_block(b):
        at = pl.ds(b * rows, rows)
        mine = rows_at(p.c, cw)
        COT[at, mine] = (COT[at, mine].astype(f32) + h_plane[b].finish()).astype(bf16)

    weight_tile(0)
    cot_plane.drain()
    h_plane[3].middle()
    weight_tile(1)
    weight_tile(2)
    finish_block(0)
    weight_tile(3)
    weight_tile(4)
    finish_block(1)
    sum_line.step(4)
    sum_copy = pltpu.make_async_copy(sum_line.result(), down_sum, copy_sems.at[6])
    sum_copy.start()
    weight_tile(5)
    weight_tile(6)
    finish_block(2)
    weight_tile(7)
    piece = rows // n_ctx
    for i in range(n_ctx):
        own = pl.ds(pl.multiple_of(p.c * rows + i * piece, piece), piece)
        mlp = y_plane.finish(pl.ds(i * piece, piece), i == 0)
        PD[own, :] = (M[own, :].astype(f32) + mlp).astype(bf16)
    y_copy = pltpu.make_async_copy(PD.at[rows_at(p.c, rows)], y_out, copy_sems.at[4])
    y_copy.start()
    finish_block(3)
    gm_copy = pltpu.make_async_copy(COT.at[:, rows_at(p.c, cw)], gm_out, copy_sems.at[5])
    gm_copy.start()
    stage_copies[6].wait()
    stage_copies[7].wait()
    y_copy.wait()
    gm_copy.wait()
    sum_copy.wait()
    sum_line.drain()
    down_line.drain()
    y_plane.drain()
    for b in range(n_ctx):
        h_plane[b].drain()


def middle_stage(m, cot, wgate, wup, w_down):
    n_fsdp, n_ctx = lax.axis_size("fsdp"), lax.axis_size("ctx")
    seq, width = m.shape
    rows = seq // n_ctx
    cw = width // n_ctx
    units = wgate.shape[1]
    unit = units // n_fsdp
    outs = [
        ((rows, width), bf16), ((units, width), bf16), ((unit, width), bf16), ((width, units), bf16),
        ((width, units), bf16), ((seq, cw), bf16),
    ]
    scratch = [
        pltpu.VMEM((seq, width), bf16),
        pltpu.VMEM((seq, width), bf16),
        pltpu.VMEM((width, units), bf16),
        pltpu.VMEM((width, units), bf16),
        pltpu.VMEM((units, width), bf16),
        pltpu.VMEM((seq, units), bf16),
        pltpu.VMEM((seq, units), bf16),
        pltpu.VMEM((seq, units), bf16),
        pltpu.VMEM((seq, 128), f32),
        pltpu.VMEM((seq, width), bf16),
        pltpu.VMEM((seq, width), bf16),
        pltpu.VMEM((2, rows // 2, width), bf16),
        pltpu.VMEM((2, rows, width), bf16),
        pltpu.VMEM((n_ctx, 2, rows // 2, cw), bf16),
        pltpu.VMEM((n_ctx, 2, rows, cw), bf16),
        pltpu.VMEM((n_fsdp // 2, unit, width), bf16),
        pltpu.VMEM((5, unit, width), bf16),
        pltpu.SemaphoreType.DMA((1, LineGather.SEMS)),
        pltpu.SemaphoreType.DMA((1, LineScatter.SEMS)),
        pltpu.SemaphoreType.DMA((6, PlaneScatter.SEMS)),
        pltpu.SemaphoreType.DMA((7,)),
        pltpu.SemaphoreType.DMA((4,)),
    ]
    flops = 18 * seq * width * units
    return call(middle_kernel, (m, cot, wgate, wup, w_down), outs, scratch, 2, flops, "middle_stage")


def backward_kernel(
    xn_in, r_in, grow_in, qt_in, kt_in, vt_in, lse_in, o_in, gm_in, wqkv_in, wout_in, tab_in,
    gate_part, up_part, down_sum,
    tok_out, qkv_all, out_all, gate_all, up_all, down_all,
    XN, R1, GROW, QT, KT, VT, LSE, O, GM, WQ, WO, TAB,
    K, V, DK, DV, DOT, DQT, DPRE, STAT, BIAS, PT, G1, G2, T1, T2, TOK,
    GACC, GSLOT, UACC, USLOT, OACC, OSLOT, QACC, QSLOT,
    line_sems, plane_sems, scatter_sems, copy_sems,
):
    p = Place()
    n_ctx = 4
    seq, width = XN.shape
    rows = seq // n_ctx
    half = rows // 2
    cw = width // n_ctx
    qw = QT.shape[0]
    heads = qw // HEAD_DIM
    nq = WQ.shape[1]
    own_rows = QACC.shape[1]
    scale = HEAD_DIM ** (-0.5)
    loads = []
    for i, (src, dst) in enumerate(
        (
            (gm_in, GM), (wout_in, WO), (o_in, O), (kt_in, KT), (vt_in, VT), (qt_in, QT), (lse_in, LSE),
            (tab_in, TAB), (xn_in, XN), (wqkv_in, WQ), (r_in, R1), (grow_in, GROW),
        )
    ):
        loads.append(pltpu.make_async_copy(src, dst, copy_sems.at[i]))
    loads[0].start()
    loads[1].start()

    p.barrier()

    def block_rows(ref):
        count = ref.shape[0] // (2 * p.depth)
        return lambda level, core: ref.at[pl.ds(pl.multiple_of((2 * level + core) * count, 16), count)]

    nu = GACC.shape[2]
    cols_stage = [XN.at[pl.ds(i * own_rows, own_rows), pl.ds(0, nu)] for i in range(2)]
    gate_line = LineScatter(p, block_rows(gate_part), GACC, GSLOT, line_sems.at[1], cols_stage)
    up_line = LineScatter(p, block_rows(up_part), UACC, USLOT, line_sems.at[2], cols_stage)
    out_line = LineScatter(p, block_rows(WO), OACC, OSLOT, line_sems.at[3])

    def qkv_block(level, core):
        f = 2 * level + core
        at = pl.ds(pl.multiple_of((f % p.depth) * own_rows, own_rows), own_rows)
        return O.at[at, pl.ds(pl.multiple_of((f // p.depth) * nq, 128), nq)]

    qkv_line = LineScatter(p, qkv_block, QACC, QSLOT, line_sems.at[4])
    gate_line.start()
    up_line.start()
    for i in (2, 3, 4, 5, 6, 7, 9, 10, 11):
        loads[i].start()

    def col_scatter(b):
        return PlaneScatter(
            p,
            lambda c: PT.at[pl.ds(b * rows, rows), rows_at(c, cw)],
            lambda c, h: PT.at[pl.ds(b * rows + h * half, half), rows_at(c, cw)],
            G1.at[b],
            G2.at[b],
            scatter_sems.at[b],
        )

    g_plane = [col_scatter(b) for b in range(n_ctx)]
    t_plane = PlaneScatter(
        p,
        lambda c: PT.at[rows_at(c, rows)],
        lambda c, h: PT.at[pl.ds(pl.multiple_of(c * rows + h * half, half), half)],
        T1,
        T2,
        scatter_sems.at[n_ctx],
    )

    def whole(ref, own, index, first):
        count = own.shape[0]

        def halves(c, h):
            return ref(c).at[pl.ds(h * first, count - first if h else first)]

        plane = PlaneGather(p, ref, halves, plane_sems.at[index], own=own)
        return plane, pltpu.make_async_copy(own, ref(p.c), plane_sems.at[index, PlaneGather.SEMS])

    unit = down_sum.shape[0]
    down_plane, down_own = whole(lambda c: down_all.at[c], down_sum, 0, unit // 32 * 16 + unit // 16 % 2 * 16)
    gate_plane, gate_own = whole(lambda c: gate_all.at[c], gate_line.result(), 1, own_rows // 2)
    up_plane, up_own = whole(lambda c: up_all.at[c], up_line.result(), 2, own_rows // 2)
    out_plane, out_own = whole(lambda c: out_all.at[c], out_line.result(), 3, own_rows // 2)
    qkv_plane, qkv_own = whole(lambda c: qkv_all.at[c], qkv_line.result(), 4, own_rows // 2)

    loads[0].wait()
    loads[1].wait()
    for b in range(n_ctx):
        at = pl.ds(b * rows, rows)
        for j in range(0, width, 512):
            PT[at, j : j + 512] = dot_nt(GM[at, :], WO[j : j + 512, :]).astype(bf16)
        g_plane[b].start()
        g_plane[b].near()
    gate_line.combine()
    gate_line.step(1)
    g_plane[0].middle()
    loads[2].wait()

    @pl.loop(0, width // 512)
    def _(i):
        at = rows_at(i, 512)
        WO[at, :] = dot_tn(O[:, at], GM[...]).astype(bf16)

    out_line.start()
    g_plane[1].middle()
    up_line.combine()
    loads[8].start()
    up_line.step(1)
    g_plane[2].middle()
    out_line.combine()
    out_line.step(1)
    for i in (3, 4, 5, 6, 7, 10):
        loads[i].wait()

    @pl.loop(0, n_ctx)
    def _(b):
        at = rows_at(b, rows)
        K[at, :] = KT[:, at].astype(f32).T.astype(bf16)
        V[at, :] = VT[:, at].astype(f32).T.astype(bf16)
        DK[at, :] = jnp.zeros((rows, HEAD_DIM), f32)
        DV[at, :] = jnp.zeros((rows, HEAD_DIM), f32)

    g_plane[3].middle()

    def attend_back(b):
        n = (b + 1) * rows
        cols = slice(b * rows, (b + 1) * rows)
        DOT[...] = g_plane[b].finish().T.astype(bf16)
        at = pl.ds(b * rows, rows)
        DQT[...] = O[at, rows_at(p.c, cw)].astype(f32).T
        key = lax.broadcasted_iota(jnp.int32, (n, rows), 0)
        query = lax.broadcasted_iota(jnp.int32, (n, rows), 1) + b * rows
        begin = TAB[b, 64:65, :].astype(jnp.int32)
        BIAS[0:n, :] = jnp.where((key <= query) & (key >= begin), 0.0, neg_large)
        STAT[...] = jnp.zeros((8, rows), f32)

        @pl.loop(0, heads)
        def _(h):
            head = rows_at(h, HEAD_DIM)
            q = QT[head, cols]
            d_out = DOT[head, :]
            delta = jnp.sum(d_out.astype(f32) * DQT[head, :], axis=0, keepdims=True)
            s = dot(K[0:n, :], q) * scale + BIAS[0:n, :]
            probs = jnp.exp(s - LSE[rows_at(h, 8), cols][0:1])
            d_probs = dot(V[0:n, :], d_out)
            d_s = (probs * (d_probs - delta)).astype(bf16)
            d_q = dot(KT[:, 0:n], d_s) * scale
            DK[0:n, :] += dot_nt(d_s, q) * scale
            DV[0:n, :] += dot_nt(probs.astype(bf16), d_out)
            STAT[...] += jnp.broadcast_to(jnp.sum(d_q * q.astype(f32), axis=0, keepdims=True), (8, rows))
            u, w = d_q[0:32], d_q[32:64]
            cosine, sine = TAB[b, 0:32, :], TAB[b, 32:64, :]
            DQT[head, :] = jnp.concatenate([u * cosine + w * sine, w * cosine - u * sine], axis=0)

        DPRE[at, 0:qw] = DQT[...].T.astype(bf16)
        R1[at, 0:8] = STAT[...].T

    attend_back(0)
    gate_line.step(2)
    attend_back(1)
    attend_back(2)
    down_plane.start()
    down_own.start()
    up_line.step(2)
    attend_back(3)
    loads[8].wait()
    loads[9].wait()
    loads[11].wait()

    @pl.loop(0, n_ctx)
    def _(b):
        at = rows_at(b, rows)
        d_k = DK[at, :].T
        d_v = DV[at, :].T
        stat = jnp.sum(d_k * KT[:, at].astype(f32) + d_v * VT[:, at].astype(f32), axis=0, keepdims=True)
        R1[at, 0:8] += jnp.broadcast_to(stat, (8, rows)).T
        u, w = d_k[0:32], d_k[32:64]
        cosine, sine = TAB[b, 0:32, :], TAB[b, 32:64, :]
        both = jnp.concatenate([u * cosine + w * sine, w * cosine - u * sine, d_v], axis=0)
        DPRE[at, qw:] = both.T.astype(bf16)

    def tokens(c):
        at = rows_at(c, rows)
        r = R1[at, 127:128]
        coef = r * R1[at, 0:1] * (1.0 / width)
        for j in range(0, width, 512):
            cols = slice(j, j + 512)
            gain = GROW[0:1, cols]
            e = dot_nt(DPRE[at, :], WQ[cols, :])
            PT[at, cols] = (e * (gain * r) - XN[at, cols].astype(f32) * ((1.0 / gain) * coef)).astype(bf16)
        mine = rows_at(p.c, cw)
        PT[at, mine] = (PT[at, mine].astype(f32) + GM[at, :].astype(f32)).astype(bf16)

    for b in range(n_ctx):
        g_plane[b].drain()
    tokens(p.cd)
    t_plane.start()
    tokens(p.cx)
    tokens(p.cy)
    t_plane.near()
    tokens(p.c)
    gate_line.step(3)

    @pl.loop(0, p.depth)
    def _(i):
        for j in range(2):
            at = rows_at(i + j * p.depth, own_rows)
            O[rows_at(i, own_rows), j * nq : (j + 1) * nq] = dot_tn(XN[:, at], DPRE[...]).astype(bf16)

    qkv_line.start()
    t_plane.middle()
    down_plane.middle()
    out_line.step(2)
    qkv_line.combine()
    qkv_line.step(1)
    up_line.step(3)
    gate_line.step(4)
    gate_plane.start()
    gate_own.start()
    out_line.step(3)
    tok_copies = []
    for i in range(n_ctx):
        if i >= 2:
            tok_copies[i - 2].wait()
        at = pl.ds(i * (rows // n_ctx), rows // n_ctx)
        TOK[i % 2] = t_plane.finish(at, i == 0)
        tok_copies.append(pltpu.make_async_copy(TOK.at[i % 2], tok_out.at[at], copy_sems.at[12 + i % 2]))
        tok_copies[-1].start()
    qkv_line.step(2)
    up_line.step(4)
    up_plane.start()
    up_own.start()
    gate_plane.middle()
    out_line.step(4)
    out_plane.start()
    out_own.start()
    qkv_line.step(3)
    up_plane.middle()
    qkv_line.step(4)
    qkv_plane.start()
    qkv_own.start()
    out_plane.middle()
    qkv_plane.middle()
    for plane, own in (
        (down_plane, down_own), (gate_plane, gate_own), (up_plane, up_own), (out_plane, out_own), (qkv_plane, qkv_own),
    ):
        plane.finish()
        own.wait()
        plane.drain()
    tok_copies[2].wait()
    tok_copies[3].wait()
    t_plane.drain()
    for line in (gate_line, up_line, out_line, qkv_line):
        line.drain()


def backward_stage(xn, r, grow, qt, kt, vt, lse, o, gm, wqkv, wout, tabs, gate_part, up_part, down_sum):
    n_fsdp, n_ctx = lax.axis_size("fsdp"), lax.axis_size("ctx")
    seq, width = xn.shape
    rows = seq // n_ctx
    half = rows // 2
    cw = width // n_ctx
    own = width // n_fsdp
    depth = n_fsdp // 2
    nq, nu = wqkv.shape[1], gate_part.shape[1]
    unit = down_sum.shape[0]
    qw = qt.shape[0]
    outs = [
        ((rows, width), f32), ((n_ctx, own, nq), bf16), ((n_ctx, own, cw), bf16), ((n_ctx, own, nu), bf16),
        ((n_ctx, own, nu), bf16), ((n_ctx, unit, width), bf16),
    ]
    ins = (xn, r, grow, qt, kt, vt, lse, o, gm, wqkv, wout, tabs, gate_part, up_part, down_sum)
    scratch = [pltpu.VMEM(a.shape, a.dtype) for a in ins[:12]] + [
        pltpu.VMEM((seq, HEAD_DIM), bf16),
        pltpu.VMEM((seq, HEAD_DIM), bf16),
        pltpu.VMEM((seq, HEAD_DIM), f32),
        pltpu.VMEM((seq, HEAD_DIM), f32),
        pltpu.VMEM((qw, rows), bf16),
        pltpu.VMEM((qw, rows), f32),
        pltpu.VMEM((seq, nq), bf16),
        pltpu.VMEM((8, rows), f32),
        pltpu.VMEM((seq, rows), f32),
        pltpu.VMEM((seq, width), bf16),
        pltpu.VMEM((n_ctx, 2, half, cw), bf16),
        pltpu.VMEM((n_ctx, 2, rows, cw), bf16),
        pltpu.VMEM((2, half, width), bf16),
        pltpu.VMEM((2, rows, width), bf16),
        pltpu.VMEM((2, rows // n_ctx, width), f32),
        pltpu.VMEM((depth, own, nu), bf16),
        pltpu.VMEM((5, own, nu), bf16),
        pltpu.VMEM((depth, own, nu), bf16),
        pltpu.VMEM((5, own, nu), bf16),
        pltpu.VMEM((depth, own, cw), bf16),
        pltpu.VMEM((5, own, cw), bf16),
        pltpu.VMEM((depth, own, nq), bf16),
        pltpu.VMEM((5, own, nq), bf16),
        pltpu.SemaphoreType.DMA((5, LineScatter.SEMS)),
        pltpu.SemaphoreType.DMA((5, PlaneGather.SEMS + 1)),
        pltpu.SemaphoreType.DMA((n_ctx + 1, PlaneScatter.SEMS)),
        pltpu.SemaphoreType.DMA((14,)),
    ]
    flops = 4 * seq * width * (nq + cw) + 20 * qw * seq * seq
    return call(backward_kernel, ins, outs, scratch, 3, flops, "backward_stage")


def finish_kernel(
    unit, qkv, out, gate, up, down, tok, y, w_query, w_key, w_value, w_gate, w_up, g1, g2,
    o_query, o_key, o_value, o_out, o_gate, o_up, o_down, o_tok, o_y, o_g1, o_g2,
):
    n_ctx = qkv.shape[0]
    qw = o_query.shape[1] // n_ctx
    cw = out.shape[2]
    for c in range(n_ctx):
        o_query[:, c * qw : (c + 1) * qw] = qkv[c, :, 0:qw].astype(f32)
        o_key[:, c * HEAD_DIM : (c + 1) * HEAD_DIM] = qkv[c, :, qw : qw + HEAD_DIM].astype(f32)
        o_value[:, c * HEAD_DIM : (c + 1) * HEAD_DIM] = qkv[c, :, qw + HEAD_DIM :].astype(f32)
        o_out[:, c * cw : (c + 1) * cw] = out[c].astype(f32)

    def total(ref, w):
        return jnp.sum(ref[...] * w[...].astype(f32), axis=-1, keepdims=True)

    first = total(o_query, w_query) + total(o_key, w_key) + total(o_value, w_value)
    o_g1[...] = jnp.broadcast_to(first / g1[:, 0:1], o_g1.shape)
    gain = g2[:, 0:1]
    for src, dst in ((gate, o_gate), (up, o_up)):
        for f in range(src.shape[2] // unit):
            for c in range(n_ctx):
                at = (f * n_ctx + c) * unit
                dst[:, at : at + unit] = src[c, :, f * unit : (f + 1) * unit].astype(f32) * gain
    second = total(o_gate, w_gate) + total(o_up, w_up)
    o_g2[...] = jnp.broadcast_to(second / gain, o_g2.shape)
    o_down[...] = down[...].astype(f32)
    o_tok[...] = tok[...]
    o_y[...] = y[...]


def finish_stage(qkv, out, gate, up, down, tok, y, w_query, w_key, w_value, w_gate, w_up, g1, g2):
    steps = 4
    n_fsdp = lax.axis_size("fsdp")
    own = w_query.shape[0]
    down = down.reshape(-1, down.shape[-1])
    unit = gate.shape[2] // n_fsdp

    def spec(shape):
        if len(shape) == 3:
            return pl.BlockSpec((shape[0], shape[1] // steps, shape[2]), lambda i: (0, i, 0))
        return pl.BlockSpec((shape[0] // steps, shape[1]), lambda i: (i, 0))

    ins = (qkv, out, gate, up, down, tok, y, w_query, w_key, w_value, w_gate, w_up, g1, g2)
    outs = [
        (w_query.shape, f32), (w_key.shape, f32), (w_value.shape, f32), ((own, out.shape[0] * out.shape[2]), f32),
        (w_gate.shape, f32), (w_up.shape, f32), (down.shape, f32), (tok.shape, f32), (y.shape, bf16),
        ((own, 128), f32), ((own, 128), f32),
    ]
    return pl.pallas_call(
        functools.partial(finish_kernel, unit),
        grid=(steps,),
        out_shape=[jax.ShapeDtypeStruct(s, d) for s, d in outs],
        in_specs=[spec(a.shape) for a in ins],
        out_specs=[spec(s) for s, d in outs],
        compiler_params=pltpu.CompilerParams(vmem_limit_bytes=56 * 2**20),
        name="finish_stage",
    )(*ins)


def rotate(field, cosine, sine_table, direction):
    half_width = field.shape[-1] // 2
    first_half = field[..., :half_width]
    second_half = field[..., half_width:]
    return jnp.concatenate(
        [
            first_half * cosine - direction * second_half * sine_table,
            second_half * cosine + direction * first_half * sine_table,
        ],
        axis=-1,
    )


def gather(x, axis_name, axis=0):
    return lax.all_gather(x, axis_name, axis=axis, tiled=True)


def scatter(x, axis_name, axis=0):
    return lax.psum_scatter(x.astype(bf16), axis_name, scatter_dimension=axis, tiled=True)


def columns(w, start, count):
    return lax.dynamic_slice_in_dim(w, start, count, axis=1)


def visible(begin):
    seq = begin.shape[0]
    index = jnp.arange(seq, dtype=jnp.int32)
    return (index[None, :] <= index[:, None]) & (index[None, :] >= begin[:, None])


def forward_plain(tok, tab, gains, gcol, w_query, w_key, w_value, w_out, w_gate, w_up):
    n_ctx, n_fsdp = lax.axis_size("ctx"), lax.axis_size("fsdp")
    c = lax.axis_index("ctx")
    own_rows = w_query.shape[0]
    qw = HEADS // n_ctx * HEAD_DIM
    copies = max(1, n_ctx // KV_HEADS)
    kvw = max(1, KV_HEADS // n_ctx) * HEAD_DIM
    unit = w_gate.shape[1] // (n_fsdp * n_ctx)
    cw = tok.shape[1] // n_ctx
    wqkv_o = jnp.concatenate(
        [
            columns(w_query, c * qw, qw),
            columns(w_key, (c // copies) * kvw, kvw),
            columns(w_value, (c // copies) * kvw, kvw),
        ],
        axis=1,
    )
    wout_o = columns(w_out, c * cw, cw)

    def units(w):
        parts = w.reshape(own_rows, n_fsdp, n_ctx, unit)
        mine = lax.dynamic_index_in_dim(parts, c, axis=2, keepdims=False)
        return (gcol[:, 0:1] * mine.reshape(own_rows, n_fsdp * unit)).astype(bf16)

    wgate_o, wup_o = units(w_gate), units(w_up)
    x = gather(tok, "ctx")
    tabs = gather(tab[None], "ctx")
    wqkv = gather(wqkv_o, "fsdp")
    wout = gather(wout_o, "fsdp")
    wgate = gather(wgate_o, "fsdp")
    wup = gather(wup_o, "fsdp")
    gain = gather(gains[0:1], "fsdp", axis=1).astype(f32)
    xf = x.astype(f32)
    r = lax.rsqrt(jnp.mean(xf * xf, axis=-1, keepdims=True) + eps_norm)
    xn = (xf * r * gain).astype(bf16)
    seq, width = x.shape
    heads = HEADS // n_ctx
    qw = heads * HEAD_DIM
    pre = dot(xn, wqkv)
    cosine = tabs[:, 0:32].transpose(0, 2, 1).reshape(seq, 1, 32)
    sine = tabs[:, 32:64].transpose(0, 2, 1).reshape(seq, 1, 32)
    begin = tabs[:, 64].reshape(seq).astype(jnp.int32)
    kvw = (wqkv.shape[1] - qw) // 2
    kv = kvw // HEAD_DIM
    q = rotate(pre[:, :qw].reshape(seq, heads, HEAD_DIM), cosine, sine, 1.0).astype(bf16)
    k = rotate(pre[:, qw : qw + kvw].reshape(seq, kv, HEAD_DIM), cosine, sine, 1.0).astype(bf16)
    v = pre[:, qw + kvw :].astype(bf16).reshape(seq, kv, HEAD_DIM)
    qg = q.reshape(seq, kv, heads // kv, HEAD_DIM)
    scores = jnp.einsum("qkgd,lkd->kgql", qg, k, preferred_element_type=f32) * HEAD_DIM ** (-0.5)
    scores = jnp.where(visible(begin)[None, None], scores, neg_large)
    top = jnp.max(scores, axis=-1, keepdims=True)
    weights = jnp.exp(scores - top)
    total = jnp.sum(weights, axis=-1, keepdims=True)
    probs_low = (weights / total).astype(bf16)
    att = jnp.einsum("kgql,lkd->qkgd", probs_low, v, preferred_element_type=f32)
    o = gather(att.astype(bf16).reshape(seq, qw), "ctx", axis=1)
    lse = (top + jnp.log(total)).reshape(heads, 1, seq)
    lse = jnp.broadcast_to(lse, (heads, 8, seq)).reshape(8 * heads, seq)
    cw = width // n_ctx
    mid = columns(x, c * cw, cw).astype(f32) + dot(o, wout)
    m = gather(mid.astype(bf16), "ctx", axis=1)
    qt = q.reshape(seq, qw).T
    kt = k.reshape(seq, kvw).T
    vt = v.reshape(seq, kvw).T
    r = jnp.broadcast_to(r, (seq, 128))
    grow = jnp.broadcast_to(gain, (8, width))
    return xn, r, grow, qt, kt, vt, lse, o, m, wqkv, wout, wgate, wup, tabs


def middle_plain(m, cot, wgate, wup, w_down):
    n_ctx = lax.axis_size("ctx")
    c = lax.axis_index("ctx")
    unit = w_down.shape[0] // n_ctx
    wdown_o = lax.dynamic_slice_in_dim(w_down, c * unit, unit, axis=0)
    seq, width = m.shape
    rows = seq // n_ctx
    cw = width // n_ctx
    wdown = gather(wdown_o, "fsdp")
    cot_all = gather(cot, "ctx")
    mf = m.astype(f32)
    r = lax.rsqrt(jnp.mean(mf * mf, axis=-1, keepdims=True) + eps_norm)
    gate = dot(m, wgate) * r
    up = dot(m, wup) * r
    sig = jax.nn.sigmoid(gate)
    hidden = (gate * sig * up).astype(bf16)
    mlp = scatter(dot(hidden, wdown), "ctx").astype(f32)
    mid_rows = lax.dynamic_slice_in_dim(m, c * rows, rows, axis=0).astype(f32)
    output = (mid_rows + mlp).astype(bf16)
    grad_hidden = dot_nt(cot_all, wdown)
    down_sum = scatter(dot_tn(hidden, cot_all), "fsdp")
    d_gate = grad_hidden * up * sig * (1.0 + gate * (1.0 - sig))
    d_up = grad_hidden * gate * sig
    stat = jnp.sum(d_gate * gate + d_up * up, axis=-1, keepdims=True)
    d_gate = (d_gate * r).astype(bf16)
    d_up = (d_up * r).astype(bf16)
    gate_raw = dot_tn(m, d_gate).astype(bf16)
    up_raw = dot_tn(m, d_up).astype(bf16)
    back = dot_nt(d_gate, wgate) + dot_nt(d_up, wup) - mf * (r * r * stat * (1.0 / width))
    back_own = scatter(back, "ctx", axis=1).astype(f32)
    gm = (columns(cot_all, c * cw, cw).astype(f32) + back_own).astype(bf16)
    return output, None, down_sum, gate_raw, up_raw, gm


def backward_plain(xn, r, grow, qt, kt, vt, lse, o, gm, wqkv, wout, tabs, gate_raw, up_raw, down_sum):
    n_ctx = lax.axis_size("ctx")
    c = lax.axis_index("ctx")
    seq, width = xn.shape
    r, gain = r[:, 0:1], grow[0:1]
    heads = HEADS // n_ctx
    qw = heads * HEAD_DIM
    kvw = kt.shape[0]
    kv = kvw // HEAD_DIM
    cw = width // n_ctx
    scale = HEAD_DIM ** (-0.5)
    cosine = tabs[:, 0:32].transpose(0, 2, 1).reshape(seq, 1, 32)
    sine = tabs[:, 32:64].transpose(0, 2, 1).reshape(seq, 1, 32)
    begin = tabs[:, 64].reshape(seq).astype(jnp.int32)
    gate_grad = scatter(gate_raw, "fsdp")
    up_grad = scatter(up_raw, "fsdp")
    out_grad = scatter(dot_tn(o, gm), "fsdp")
    d_att = scatter(dot_nt(gm, wout), "ctx", axis=1).reshape(seq, kv, heads // kv, HEAD_DIM)
    q = qt.T.reshape(seq, kv, heads // kv, HEAD_DIM)
    k = kt.T.reshape(seq, kv, HEAD_DIM)
    v = vt.T.reshape(seq, kv, HEAD_DIM)
    scores = jnp.einsum("qkgd,lkd->kgql", q, k, preferred_element_type=f32) * scale
    scores = jnp.where(visible(begin)[None, None], scores, neg_large)
    lse = lse.reshape(kv, heads // kv, 8, seq)[:, :, 0, :, None]
    probs = jnp.exp(scores - lse)
    d_probs = jnp.einsum("qkgd,lkd->kgql", d_att, v, preferred_element_type=f32)
    delta = jnp.sum(probs * d_probs, axis=-1, keepdims=True)
    d_scores = (probs * (d_probs - delta)).astype(bf16)
    d_q = jnp.einsum("kgql,lkd->qkgd", d_scores, k, preferred_element_type=f32) * scale
    d_k = jnp.einsum("kgql,qkgd->lkd", d_scores, q, preferred_element_type=f32) * scale
    d_v = jnp.einsum("kgql,qkgd->lkd", probs.astype(bf16), d_att, preferred_element_type=f32)
    stat = (
        jnp.sum(d_q * q, axis=(1, 2, 3)) + jnp.sum(d_k * k, axis=(1, 2)) + jnp.sum(d_v * v, axis=(1, 2))
    )[:, None]
    d_q = rotate(d_q.reshape(seq, heads, HEAD_DIM), cosine, sine, -1.0).reshape(seq, qw)
    d_k = rotate(d_k, cosine, sine, -1.0).reshape(seq, kvw)
    d_pre = jnp.concatenate([d_q, d_k, d_v.reshape(seq, kvw)], axis=1).astype(bf16)
    qkv_grad = scatter(dot_tn(xn, d_pre), "fsdp")
    back = dot_nt(d_pre, wqkv) * (gain * r)
    back = back - xn.astype(f32) * ((1.0 / gain) * (r * stat * (1.0 / width)))
    at = (jnp.arange(width, dtype=jnp.int32) // cw == c)[None, :]
    back = back + jnp.where(at, jnp.tile(gm.astype(f32), (1, n_ctx)), 0.0)
    grad_tokens = scatter(back, "ctx").astype(f32)
    qkv_all = gather(qkv_grad[None], "ctx")
    out_all = gather(out_grad[None], "ctx")
    gate_all = gather(gate_grad[None], "ctx")
    up_all = gather(up_grad[None], "ctx")
    down_all = gather(down_sum[None], "ctx")
    return grad_tokens, qkv_all, out_all, gate_all, up_all, down_all


def finish_plain(qkv_all, out_all, gate_all, up_all, down_all, tok, y, w_query, w_key, w_value, w_gate, w_up, g1, g2):
    n_ctx, n_fsdp = lax.axis_size("ctx"), lax.axis_size("fsdp")
    own_rows = w_query.shape[0]
    qw = HEADS // n_ctx * HEAD_DIM
    copies = max(1, n_ctx // KV_HEADS)
    kvw = max(1, KV_HEADS // n_ctx) * HEAD_DIM
    ff_width = w_gate.shape[1]
    unit = ff_width // (n_fsdp * n_ctx)
    qkv_all = qkv_all.astype(f32)

    def joined(part):
        return jnp.moveaxis(part, 0, 1).reshape(own_rows, -1)

    def kv_part(part):
        return joined(part.reshape(n_ctx // copies, copies, own_rows, kvw).sum(axis=1))

    grad_query = joined(qkv_all[:, :, :qw])
    grad_key = kv_part(qkv_all[:, :, qw : qw + kvw])
    grad_value = kv_part(qkv_all[:, :, qw + kvw :])
    grad_out = joined(out_all.astype(f32))

    def spread(full):
        full = full.reshape(n_ctx, own_rows, n_fsdp, unit)
        return full.transpose(1, 2, 0, 3).reshape(own_rows, ff_width).astype(f32)

    raw_gate, raw_up = spread(gate_all), spread(up_all)
    grad_down = down_all.astype(f32).reshape(-1, down_all.shape[-1])

    def gain_term(grad, w):
        return jnp.sum(grad * w.astype(f32), axis=1, keepdims=True)

    first = gain_term(grad_query, w_query) + gain_term(grad_key, w_key) + gain_term(grad_value, w_value)
    second = gain_term(raw_gate, w_gate) + gain_term(raw_up, w_up)
    g1, g2 = g1[:, 0:1], g2[:, 0:1]
    return (
        grad_query, grad_key, grad_value, grad_out, g2 * raw_gate, g2 * raw_up, grad_down, tok, y, first / g1, second,
    )


def per_device(
    tokens,
    positions,
    gain_attn,
    gain_mlp,
    w_query,
    w_key,
    w_value,
    w_out,
    w_gate,
    w_up,
    w_down,
    cotangent,
):
    kernels = lax.axis_size("ctx") == 4 and lax.axis_size("fsdp") == 8
    c = lax.axis_index("ctx")
    rows = tokens.shape[0]
    own_rows = w_query.shape[0]
    gains = jnp.broadcast_to(gain_attn[None, :], (16, own_rows))
    gain_one = jnp.broadcast_to(gain_attn.astype(f32)[:, None], (own_rows, 128))
    gain_two = jnp.broadcast_to(gain_mlp.astype(f32)[:, None], (own_rows, 128))
    frequency = theta_base ** (-(jnp.arange(HEAD_DIM // 2, dtype=f32) * 2.0) / HEAD_DIM)
    angles = frequency[:, None] * positions.astype(f32)[None, :]
    begin = c * rows + jnp.arange(rows, dtype=jnp.int32) - positions
    tab = jnp.concatenate(
        [jnp.cos(angles), jnp.sin(angles), jnp.broadcast_to(begin.astype(f32)[None, :], (16, rows))],
        axis=0,
    )

    forward = forward_stage if kernels else forward_plain
    xn, r, grow, qt, kt, vt, lse, o, m, wqkv, wout, wgate, wup, tabs = forward(
        tokens, tab, gains, gain_two, w_query, w_key, w_value, w_out, w_gate, w_up
    )
    middle = middle_stage if kernels else middle_plain
    y, _, down_sum, gate_raw, up_raw, gm = middle(m, cotangent, wgate, wup, w_down)
    backward = backward_stage if kernels else backward_plain
    tok, qkv_all, out_all, gate_all, up_all, down_all = backward(
        xn, r, grow, qt, kt, vt, lse, o, gm, wqkv, wout, tabs, gate_raw, up_raw, down_sum
    )
    finish = finish_stage if kernels else finish_plain
    g_query, g_key, g_value, g_out, g_gate, g_up, g_down, tok, y, g_one, g_two = finish(
        qkv_all, out_all, gate_all, up_all, down_all, tok, y,
        w_query, w_key, w_value, w_gate, w_up, gain_one, gain_two,
    )
    return (y, tok, g_one[:, 0], g_two[:, 0], g_query, g_key, g_value, g_out, g_gate, g_up, g_down)


def solution(mesh):
    both = P(("fsdp", "ctx"), None)
    first = P("fsdp", None)
    return jax.shard_map(
        per_device,
        mesh=mesh,
        in_specs=(both, P(("fsdp", "ctx")), P("fsdp"), P("fsdp")) + (first,) * 7 + (both,),
        out_specs=(both, both, P("fsdp"), P("fsdp")) + (first,) * 7,
        check_vma=False,
    )
```

```python
import functools

import jax
import jax.numpy as jnp
from jax import lax
from jax.experimental import pallas as pl
from jax.experimental.pallas import tpu as pltpu
from jax.sharding import PartitionSpec as P

HEADS = 32
KV_HEADS = 4
HEAD_DIM = 64

eps_norm = 1e-05
theta_base = 10000.0
neg_large = -1e30
bf16 = jnp.bfloat16
f32 = jnp.float32
MESH_IDS = pl.DeviceIdType.MESH


def dot(a, b):
    return jnp.dot(a, b, preferred_element_type=f32)


def dot_nt(a, b):
    return lax.dot_general(a, b, (((1,), (1,)), ((), ())), preferred_element_type=f32)


def dot_tn(a, b):
    return lax.dot_general(a, b, (((0,), (0,)), ((), ())), preferred_element_type=f32)


class Place:
    def __init__(self):
        self.f = lax.axis_index("fsdp")
        self.c = lax.axis_index("ctx")
        self.depth = lax.axis_size("fsdp") // 2
        self.z = self.f // 2
        self.core = self.f % 2
        self.other = 1 - self.core
        self.cx = self.c + 1 - 2 * (self.c % 2)
        self.cy = self.c + 2 - 4 * (self.c // 2)
        self.cd = 3 - self.c
        self.sibling = {"fsdp": self.f + 1 - 2 * self.core}
        self.up = {"fsdp": self.f + 2}
        self.down = {"fsdp": self.f - 2}
        self.x = {"ctx": self.cx}
        self.y = {"ctx": self.cy}

    def has_up(self):
        return self.z < self.depth - 1

    def has_down(self):
        return self.z > 0

    def barrier(self):
        sem = pltpu.get_barrier_semaphore()

        def greet(device):
            pl.semaphore_signal(sem, inc=1, device_id=device, device_id_type=MESH_IDS)

        greet(self.sibling)
        greet(self.x)
        greet(self.y)

        @pl.when(self.has_up())
        def _():
            greet(self.up)

        @pl.when(self.has_down())
        def _():
            greet(self.down)

        last = self.depth - 1
        pl.semaphore_wait(sem, 4 - self.z // last + (self.z + last - 1) // last)


def remote(src, dst, send_sem, recv_sem, device):
    return pltpu.make_async_remote_copy(
        src_ref=src,
        dst_ref=dst,
        send_sem=send_sem,
        recv_sem=recv_sem,
        device_id=device,
        device_id_type=MESH_IDS,
    )


class LineGather:
    SEMS = 21

    def __init__(self, place, own, full, sems):
        self.p, self.own, self.full, self.sems = place, own, full, sems
        self.n = place.depth
        self.rows = full.shape[0] // (2 * self.n)

    def view(self, level, core):
        start = pl.multiple_of((2 * level + core) * self.rows, 16)
        return self.full.at[pl.ds(start, self.rows)]

    def to_up(self, hop):
        p = self.p
        level = p.z - (hop - 1)
        src = self.own if hop == 1 and self.own is not None else self.view(level, p.core)
        return remote(
            src, self.view(level, p.core), self.sems.at[hop - 1], self.sems.at[6 + hop - 1], p.up
        )

    def to_down(self, hop):
        p = self.p
        level = p.z + (hop - 1)
        src = self.own if hop == 1 and self.own is not None else self.view(level, p.core)
        return remote(
            src, self.view(level, p.core), self.sems.at[3 + hop - 1], self.sems.at[9 + hop - 1], p.down
        )

    def to_sibling(self, level, own=False):
        p = self.p
        src = self.own if own and self.own is not None else self.view(level, p.core)
        return remote(
            src, self.view(level, p.core), self.sems.at[12 + level], self.sems.at[16 + level], p.sibling
        )

    def local(self):
        p = self.p
        return pltpu.make_async_copy(self.own, self.view(p.z, p.core), self.sems.at[20])

    def start(self):
        p = self.p

        @pl.when(p.has_up())
        def _():
            self.to_up(1).start()

        @pl.when(p.has_down())
        def _():
            self.to_down(1).start()

        self.to_sibling(p.z, True).start()
        if self.own is not None:
            self.local().start()

    def arrived(self, level, sem):
        view = self.view(level, self.p.core)
        remote(view, view, self.sems.at[0], sem, self.p.sibling).wait_recv()

    def hop(self, s):
        p = self.p

        @pl.when(p.z >= s)
        def _():
            self.arrived(p.z - s, self.sems.at[6 + s - 1])
            if s < self.n - 1:

                @pl.when(p.has_up())
                def _():
                    self.to_up(s + 1).start()

            self.to_sibling(p.z - s).start()

        @pl.when(p.z + s < self.n)
        def _():
            self.arrived(p.z + s, self.sems.at[9 + s - 1])
            if s < self.n - 1:

                @pl.when(p.has_down())
                def _():
                    self.to_down(s + 1).start()

            self.to_sibling(p.z + s).start()

    def finish(self):
        p = self.p
        if self.own is not None:
            self.local().wait()
        for level in range(self.n):
            view = self.view(level, p.other)
            remote(view, view, self.sems.at[0], self.sems.at[16 + level], p.sibling).wait_recv()

    def drain(self):
        p = self.p
        for s in range(1, self.n):

            @pl.when(p.has_up() & (p.z >= s - 1))
            def _():
                self.to_up(s).wait_send()

            @pl.when(p.has_down() & (p.z + s - 1 < self.n))
            def _():
                self.to_down(s).wait_send()

        for level in range(self.n):
            self.to_sibling(level).wait_send()


class PlaneGather:
    SEMS = 8

    def __init__(self, place, view, half, sems, own=None):
        self.p, self.view, self.half, self.sems = place, view, half, sems
        self.own = own

    def src(self):
        return self.view(self.p.c) if self.own is None else self.own

    def to_x(self):
        p = self.p
        return remote(self.src(), self.view(p.c), self.sems.at[0], self.sems.at[2], p.x)

    def to_y(self):
        p = self.p
        return remote(self.src(), self.view(p.c), self.sems.at[1], self.sems.at[3], p.y)

    def on_to_y(self):
        p, h = self.p, self.half(self.p.cx, 0)
        return remote(h, h, self.sems.at[4], self.sems.at[6], p.y)

    def on_to_x(self):
        p, h = self.p, self.half(self.p.cy, 1)
        return remote(h, h, self.sems.at[5], self.sems.at[7], p.x)

    def start(self):
        self.to_x().start()
        self.to_y().start()

    def got(self, ref, sem):
        remote(ref, ref, self.sems.at[0], sem, self.p.x).wait_recv()

    def middle(self):
        p = self.p
        self.got(self.view(p.cx), self.sems.at[2])
        self.on_to_y().start()
        self.got(self.view(p.cy), self.sems.at[3])
        self.on_to_x().start()

    def finish(self):
        p = self.p
        self.got(self.half(p.cd, 0), self.sems.at[6])
        self.got(self.half(p.cd, 1), self.sems.at[7])

    def drain(self):
        self.to_x().wait_send()
        self.to_y().wait_send()
        self.on_to_y().wait_send()
        self.on_to_x().wait_send()


def rows_at(index, count):
    return pl.ds(pl.multiple_of(index * count, count), count)


def any_spec(count):
    return [pl.BlockSpec(memory_space=pl.ANY)] * count


def call(kernel, ins, outs, scratch, collective_id, flops, name, vmem=60.0):
    return pl.pallas_call(
        kernel,
        out_shape=[jax.ShapeDtypeStruct(s, d) for s, d in outs],
        in_specs=any_spec(len(ins)),
        out_specs=any_spec(len(outs)),
        scratch_shapes=scratch,
        compiler_params=pltpu.CompilerParams(
            collective_id=collective_id, has_side_effects=True, vmem_limit_bytes=int(vmem * 2**20)
        ),
        cost_estimate=pl.CostEstimate(flops=flops, bytes_accessed=2**26, transcendentals=2**22),
        name=name,
    )(*ins)


def tiles_of(total, most):
    sizes, at = [], 0
    while at < total:
        sizes.append((at, min(most, total - at)))
        at += most
    return sizes


def add_to(ref, other):
    for start, size in tiles_of(ref.shape[0], 96):
        at = pl.ds(start, size)
        ref[at, :] = (ref[at, :].astype(f32) + other[at, :].astype(f32)).astype(bf16)


class PlaneScatter:
    SEMS = 8

    def __init__(self, place, part, half, first, second, sems):
        self.p, self.part, self.half = place, part, half
        self.first, self.second, self.sems = first, second, sems

    def ref(self):
        return self.part(self.p.c)

    def far_to_y(self):
        p = self.p
        return remote(self.half(p.cd, 0), self.first.at[0], self.sems.at[0], self.sems.at[2], p.y)

    def far_to_x(self):
        p = self.p
        return remote(self.half(p.cd, 1), self.first.at[1], self.sems.at[1], self.sems.at[3], p.x)

    def to_x(self):
        p = self.p
        return remote(self.part(p.cx), self.second.at[0], self.sems.at[4], self.sems.at[6], p.x)

    def to_y(self):
        p = self.p
        return remote(self.part(p.cy), self.second.at[1], self.sems.at[5], self.sems.at[7], p.y)

    def start(self):
        self.far_to_y().start()
        self.far_to_x().start()

    def got(self, ref, sem):
        remote(ref, ref, self.sems.at[0], sem, self.p.x).wait_recv()

    def add(self, ref, other):
        add_to(ref, other)

    def middle(self):
        p = self.p
        self.got(self.first.at[0], self.sems.at[2])
        self.add(self.half(p.cx, 0), self.first.at[0])
        self.to_x().start()
        self.got(self.first.at[1], self.sems.at[3])
        self.add(self.half(p.cy, 1), self.first.at[1])
        self.to_y().start()

    def finish(self, at=slice(None), first=True):
        if first:
            self.got(self.second.at[0], self.sems.at[6])
            self.got(self.second.at[1], self.sems.at[7])
        own = self.part(self.p.c)[at].astype(f32)
        return own + self.second[0, at].astype(f32) + self.second[1, at].astype(f32)

    def drain(self):
        self.far_to_y().wait_send()
        self.far_to_x().wait_send()
        self.to_x().wait_send()
        self.to_y().wait_send()


class LineScatter:
    SEMS = 22

    def __init__(self, place, part, acc, slots, sems, stage=None):
        self.p, self.part, self.acc, self.slots, self.sems = place, part, acc, slots, sems
        self.stage = stage
        self.n = place.depth

    def to_sibling(self, level):
        p = self.p
        return remote(
            self.part(level, p.other), self.acc.at[level], self.sems.at[level], self.sems.at[4 + level], p.sibling
        )

    def start(self):
        for level in range(self.n):
            self.to_sibling(level).start()

    def load(self, level):
        return pltpu.make_async_copy(
            self.part(level, self.p.core), self.stage[level % 2], self.sems.at[20 + level % 2]
        )

    def got(self, ref, sem):
        remote(ref, ref, self.sems.at[0], sem, self.p.sibling).wait_recv()

    def add(self, ref, other):
        add_to(ref, other)

    def combine(self):
        if self.stage is not None:
            self.load(0).start()
            self.load(1).start()
        for level in range(self.n):
            self.got(self.acc.at[level], self.sems.at[4 + level])
            if self.stage is None:
                self.add(self.acc.at[level], self.part(level, self.p.core))
            else:
                self.load(level).wait()
                self.add(self.acc.at[level], self.stage[level % 2])
                if level + 2 < self.n:
                    self.load(level + 2).start()

    def slot(self, up, s):
        return self.slots.at[s - 1] if up else self.slots.at[(0, 3, 4)[s - 1]]

    def along(self, up, s):
        p = self.p
        level = p.z if up else self.n - 1 - p.z
        block = self.n - s + level
        block = block if up else self.n - 1 - block
        base = 8 if up else 14
        copy = remote(
            self.acc.at[block],
            self.slot(up, s),
            self.sems.at[base + s - 1],
            self.sems.at[base + 3 + s - 1],
            p.up if up else p.down,
        )
        return copy, (level <= s - 1) & (level < self.n - 1)

    def step(self, s):
        for up in (True, False):
            level = self.p.z if up else self.n - 1 - self.p.z
            if s > 1:
                block = self.n - s + level
                block = block if up else self.n - 1 - block
                base = 11 if up else 17

                @pl.when((level >= 1) & (s - 1 >= level))
                def _():
                    self.got(self.slot(up, s - 1), self.sems.at[base + s - 2])
                    self.add(self.acc.at[block], self.slot(up, s - 1))

            if s < self.n:
                copy, valid = self.along(up, s)

                @pl.when(valid)
                def _():
                    copy.start()

    def result(self):
        return self.acc.at[self.p.z]

    def drain(self):
        for level in range(self.n):
            self.to_sibling(level).wait_send()
        for up in (True, False):
            for s in range(1, self.n):
                copy, valid = self.along(up, s)

                @pl.when(valid)
                def _():
                    copy.wait_send()


def forward_kernel(
    tok, tab, gains, gcol, w_query, w_key, w_value, w_out, w_gate, w_up,
    xn_out, r_out, grow_out, qt_out, kt_out, vt_out, lse_out, o_out, m_out,
    wqkv_out, wout_out, wgate, wup, tab_out,
    X, XN, QT, KT, VT, K, LSE, O, M, WQ, WO, TAB, G8, GROW, BIAS, OT, R1,
    WK, WV, GF, UF, GO, UO, GCOL,
    line_sems, plane_sems, copy_sems,
):
    p = Place()
    n_ctx = 4
    rows = tok.shape[0]
    half = rows // 2
    qw = QT.shape[0]
    heads = qw // HEAD_DIM
    cw = O.shape[1] // n_ctx
    scale = HEAD_DIM ** (-0.5)

    mine = rows_at(p.f, WK.shape[0])
    loads = []
    for i, (src, dst) in enumerate(
        (
            (w_query.at[:, rows_at(p.c, qw)], WQ.at[mine, pl.ds(0, qw)]),
            (w_key, WK), (w_value, WV), (w_gate, GF), (w_up, UF), (gcol, GCOL),
        )
    ):
        loads.append(pltpu.make_async_copy(src, dst, copy_sems.at[15 + i]))
        loads[-1].start()

    p.barrier()

    gain_line = LineGather(p, gains, G8, line_sems.at[0])
    qkv_line = LineGather(p, None, WQ, line_sems.at[1])
    out_line = LineGather(p, w_out.at[:, rows_at(p.c, cw)], WO, line_sems.at[2])
    gate_line = LineGather(p, GO, wgate, line_sems.at[3])
    up_line = LineGather(p, UO, wup, line_sems.at[4])

    def row_block(ref):
        return (
            lambda c: ref.at[rows_at(c, rows)],
            lambda c, h: ref.at[pl.ds(pl.multiple_of(c * rows + h * half, half), half)],
        )

    tok_plane = PlaneGather(p, *row_block(X), plane_sems.at[0], own=tok)
    tab_rows = tab.shape[0]
    tab_plane = PlaneGather(
        p,
        lambda c: TAB.at[c],
        lambda c, h: TAB.at[c, pl.ds(h * (tab_rows // 2), tab_rows // 2)],
        plane_sems.at[2],
        own=tab,
    )

    def col_block(ref, b):
        def view(c):
            return ref.at[pl.ds(b * rows, rows), rows_at(c, cw)]

        def halves(c, h):
            return ref.at[pl.ds(b * rows + h * half, half), rows_at(c, cw)]

        return view, halves

    o_plane = [PlaneGather(p, *col_block(O, b), plane_sems.at[3 + b]) for b in range(n_ctx)]
    m_plane = [PlaneGather(p, *col_block(M, b), plane_sems.at[7 + b]) for b in range(n_ctx)]

    gain_line.start()
    tab_plane.start()
    tok_plane.start()
    out_line.start()
    for i in range(3):
        loads[i].wait()
    for c in range(n_ctx):

        @pl.when(p.c == c)
        def _():
            WQ[mine, qw : qw + HEAD_DIM] = WK[:, HEAD_DIM * c : HEAD_DIM * (c + 1)]
            WQ[mine, qw + HEAD_DIM :] = WV[:, HEAD_DIM * c : HEAD_DIM * (c + 1)]

    qkv_line.start()
    own_tok = pltpu.make_async_copy(tok, X.at[rows_at(p.c, rows)], copy_sems.at[0])
    own_tab = pltpu.make_async_copy(tab, TAB.at[p.c], copy_sems.at[1])
    own_tok.start()
    own_tab.start()

    for i in range(3, 6):
        loads[i].wait()
    unit = GO.shape[1] // (2 * p.depth)
    for c in range(n_ctx):

        @pl.when(p.c == c)
        def _():
            for f in range(2 * p.depth):
                at = (f * n_ctx + c) * unit
                for src, dst in ((GF, GO), (UF, UO)):
                    part = src[:, at : at + unit].astype(f32) * GCOL[:, 0:1]
                    dst[:, f * unit : (f + 1) * unit] = part.astype(bf16)

    gain_line.hop(1)
    tab_plane.middle()
    gain_line.hop(2)
    qkv_line.hop(1)
    gain_line.hop(3)
    gain_line.finish()
    for f in range(2 * p.depth):
        GROW[:, f * gains.shape[1] : (f + 1) * gains.shape[1]] = G8[16 * f : 16 * f + 8, :].astype(f32)

    def norm(c):
        at = rows_at(c, rows)
        x = X[at, :].astype(f32)
        r = lax.rsqrt(jnp.mean(x * x, axis=-1, keepdims=True) + eps_norm)
        R1[at, :] = jnp.broadcast_to(r, (rows, 128))
        XN[at, :] = (x * r * GROW[0:1, :]).astype(bf16)

    own_tok.wait()
    norm(p.c)
    out_line.hop(1)
    qkv_line.hop(2)
    tok_plane.middle()
    out_line.hop(2)
    gate_line.start()
    norm(p.cx)
    norm(p.cy)
    qkv_line.hop(3)
    tok_plane.finish()
    out_line.hop(3)
    up_line.start()
    norm(p.cd)
    xn_copy = pltpu.make_async_copy(XN, xn_out, copy_sems.at[3])
    r_copy = pltpu.make_async_copy(R1, r_out, copy_sems.at[4])
    grow_copy = pltpu.make_async_copy(GROW, grow_out, copy_sems.at[14])
    xn_copy.start()
    r_copy.start()
    grow_copy.start()
    own_tab.wait()
    tab_plane.finish()
    qkv_line.finish()

    @pl.loop(0, n_ctx)
    def _(b):
        at = rows_at(b, rows)
        pre = dot(XN[at, :], WQ[...]).T
        cosine = TAB[b, 0:32, :]
        sine = TAB[b, 32:64, :]
        for h in range(heads + 1):
            u = pre[64 * h : 64 * h + 32]
            w = pre[64 * h + 32 : 64 * h + 64]
            first = u * cosine - w * sine
            second = w * cosine + u * sine
            if h < heads:
                QT[64 * h : 64 * h + 32, at] = first.astype(bf16)
                QT[64 * h + 32 : 64 * h + 64, at] = second.astype(bf16)
            else:
                KT[0:32, at] = first.astype(bf16)
                KT[32:64, at] = second.astype(bf16)
                K[at, :] = jnp.concatenate([first, second], axis=0).T.astype(bf16)
        VT[:, at] = pre[qw + 64 :].astype(bf16)

    wq_copy = pltpu.make_async_copy(WQ, wqkv_out, copy_sems.at[5])
    wq_copy.start()

    def attend(b):
        n = (b + 1) * rows
        key = lax.broadcasted_iota(jnp.int32, (n, rows), 0)
        query = lax.broadcasted_iota(jnp.int32, (n, rows), 1) + b * rows
        begin = TAB[b, 64:65, :].astype(jnp.int32)
        BIAS[0:n, :] = jnp.where((key <= query) & (key >= begin), 0.0, neg_large)
        cols = slice(b * rows, (b + 1) * rows)

        @pl.loop(0, heads)
        def _(h):
            head = rows_at(h, HEAD_DIM)
            s = dot(K[0:n, :], QT[head, cols]) * scale + BIAS[0:n, :]
            top = jnp.max(s, axis=0, keepdims=True)
            e = jnp.exp(s - top)
            total = jnp.sum(e, axis=0, keepdims=True)
            probs = (e * (1.0 / total)).astype(bf16)
            OT[head, :] = dot(VT[:, 0:n], probs)
            LSE[rows_at(h, 8), cols] = jnp.broadcast_to(top + jnp.log(total), (8, rows))

        O[pl.ds(b * rows, rows), rows_at(p.c, cw)] = OT[...].T.astype(bf16)
        o_plane[b].start()

    def middle(b):
        at = pl.ds(b * rows, rows)
        cols = rows_at(p.c, cw)
        mid = X[at, cols].astype(f32) + dot(O[at, :], WO[...])
        M[at, cols] = mid.astype(bf16)
        m_plane[b].start()

    attend(0)
    attend(1)
    o_plane[0].middle()
    attend(2)
    gate_line.hop(1)
    o_plane[1].middle()
    attend(3)
    o_plane[2].middle()
    out_line.finish()
    o_plane[0].finish()
    middle(0)
    o_plane[1].finish()
    middle(1)
    o_plane[3].middle()
    up_line.hop(1)
    m_plane[0].middle()
    o_plane[2].finish()
    middle(2)
    m_plane[1].middle()
    o_plane[3].finish()
    middle(3)
    m_plane[2].middle()
    gate_line.hop(2)
    m_plane[3].middle()
    up_line.hop(2)
    copies = [xn_copy, r_copy, grow_copy, wq_copy]
    for i, (src, dst) in enumerate(
        ((QT, qt_out), (KT, kt_out), (VT, vt_out), (LSE, lse_out), (O, o_out), (WO, wout_out), (TAB, tab_out))
    ):
        copy = pltpu.make_async_copy(src, dst, copy_sems.at[6 + i])
        copy.start()
        copies.append(copy)
    for b in range(n_ctx):
        m_plane[b].finish()
    m_copy = pltpu.make_async_copy(M, m_out, copy_sems.at[13])
    m_copy.start()
    copies.append(m_copy)
    gate_line.hop(3)
    up_line.hop(3)
    gate_line.finish()
    up_line.finish()
    for copy in copies:
        copy.wait()
    for line in (gain_line, qkv_line, out_line, gate_line, up_line):
        line.drain()
    for plane in [tok_plane, tab_plane] + o_plane + m_plane:
        plane.drain()


def forward_stage(tok, tab, gains, gcol, w_query, w_key, w_value, w_out, w_gate, w_up):
    n_fsdp, n_ctx = lax.axis_size("fsdp"), lax.axis_size("ctx")
    rows, width = tok.shape
    seq = rows * n_ctx
    own = w_query.shape[0]
    whole = n_fsdp * own
    qw = HEADS // n_ctx * HEAD_DIM
    nq, nw, nu = qw + 2 * HEAD_DIM, width // n_ctx, w_gate.shape[1] // n_ctx
    heads = qw // HEAD_DIM
    tab_shape = (n_ctx,) + tab.shape
    outs = [
        ((seq, width), bf16), ((seq, 128), f32), ((8, width), f32), ((qw, seq), bf16), ((64, seq), bf16),
        ((64, seq), bf16), ((8 * heads, seq), f32), ((seq, width), bf16), ((seq, width), bf16), ((whole, nq), bf16),
        ((whole, nw), bf16), ((whole, nu), bf16), ((whole, nu), bf16), (tab_shape, f32),
    ]
    scratch = [
        pltpu.VMEM((seq, width), bf16),
        pltpu.VMEM((seq, width), bf16),
        pltpu.VMEM((qw, seq), bf16),
        pltpu.VMEM((64, seq), bf16),
        pltpu.VMEM((64, seq), bf16),
        pltpu.VMEM((seq, 64), bf16),
        pltpu.VMEM((8 * heads, seq), f32),
        pltpu.VMEM((seq, width), bf16),
        pltpu.VMEM((seq, width), bf16),
        pltpu.VMEM((whole, nq), bf16),
        pltpu.VMEM((whole, nw), bf16),
        pltpu.VMEM(tab_shape, f32),
        pltpu.VMEM((16 * n_fsdp, gains.shape[1]), bf16),
        pltpu.VMEM((8, width), f32),
        pltpu.VMEM((seq, rows), f32),
        pltpu.VMEM((qw, rows), f32),
        pltpu.VMEM((seq, 128), f32),
        pltpu.VMEM(w_key.shape, bf16),
        pltpu.VMEM(w_value.shape, bf16),
        pltpu.VMEM(w_gate.shape, bf16),
        pltpu.VMEM(w_up.shape, bf16),
        pltpu.VMEM((own, nu), bf16),
        pltpu.VMEM((own, nu), bf16),
        pltpu.VMEM(gcol.shape, f32),
        pltpu.SemaphoreType.DMA((5, LineGather.SEMS)),
        pltpu.SemaphoreType.DMA((11, PlaneGather.SEMS)),
        pltpu.SemaphoreType.DMA((21,)),
    ]
    ins = (tok, tab, gains, gcol, w_query, w_key, w_value, w_out, w_gate, w_up)
    flops = 2 * seq * width * (nq + nw) + 8 * heads * seq * seq * HEAD_DIM
    return call(forward_kernel, ins, outs, scratch, 1, flops, "forward_stage")


def middle_kernel(
    m_in, cot, wgate_in, wup_in, w_down,
    y_out, down_part, down_sum, gate_part, up_part, gm_out,
    M, COT, WG, WU, WD, GATE, UP, HID, R2, PD, PH, D1, D2, H1, H2, DACC, DSLOT,
    line_sems, sum_sems, plane_sems, copy_sems, stage_sems,
):
    p = Place()
    n_ctx = 4
    seq, width = M.shape
    rows = seq // n_ctx
    half = rows // 2
    cw = width // n_ctx
    units = GATE.shape[1]
    loads = []
    for i, (src, dst) in enumerate(((m_in, M), (wgate_in, WG), (wup_in, WU), (cot, COT.at[rows_at(p.c, rows)]))):
        loads.append(pltpu.make_async_copy(src, dst, copy_sems.at[i]))
        loads[-1].start()

    p.barrier()
    unit = w_down.shape[0] // n_ctx
    down_own = w_down.at[pl.ds(pl.multiple_of(p.c * unit, 16), unit)]
    down_line = LineGather(p, down_own, WD, line_sems.at[0])
    down_line.start()
    cot_plane = PlaneGather(
        p,
        lambda c: COT.at[rows_at(c, rows)],
        lambda c, h: COT.at[pl.ds(pl.multiple_of(c * rows + h * half, half), half)],
        plane_sems.at[5],
        own=cot,
    )
    cot_plane.start()

    loads[0].wait()
    loads[1].wait()
    loads[2].wait()

    def activate(b):
        at = rows_at(b, rows)
        mf = M[at, :].astype(f32)
        r = lax.rsqrt(jnp.mean(mf * mf, axis=-1, keepdims=True) + eps_norm)
        R2[at, :] = jnp.broadcast_to(r, (rows, 128))
        for start, size in tiles_of(units, 512):
            cols = slice(start, start + size)
            gate = dot(M[at, :], WG[:, cols]) * r
            up = dot(M[at, :], WU[:, cols]) * r
            GATE[at, cols] = gate.astype(bf16)
            UP[at, cols] = up.astype(bf16)
            HID[at, cols] = (gate * (0.5 + 0.5 * jnp.tanh(0.5 * gate)) * up).astype(bf16)

    pl.loop(0, 2)(activate)
    down_line.hop(1)
    pl.loop(2, 4)(activate)
    cot_plane.middle()
    down_line.hop(2)
    loads[3].wait()
    cot_plane.finish()
    stage_copies = {}
    for i, (at, size) in enumerate(tiles_of(units, rows)):
        slot = pl.ds(i % 2 * rows, size)
        if i >= 2:
            stage_copies[i - 2].wait()
        for j in range(0, width, cw):
            PH[slot, j : j + cw] = dot_tn(HID[:, at : at + size], COT[:, j : j + cw]).astype(bf16)
        copy = pltpu.make_async_copy(PH.at[slot], down_part.at[pl.ds(at, size)], stage_sems.at[i % 2])
        copy.start()
        stage_copies[i] = copy
    n_down = len(stage_copies)
    stage_copies[n_down - 2].wait()
    stage_copies[n_down - 1].wait()

    def down_block(level, core):
        return down_part.at[pl.ds(pl.multiple_of((2 * level + core) * unit, 16), unit)]

    down_stage = [PH.at[pl.ds(i * rows, unit)] for i in range(2)]
    sum_line = LineScatter(p, down_block, DACC, DSLOT, sum_sems.at[0], down_stage)
    sum_line.start()
    down_line.hop(3)
    down_line.finish()

    y_plane = PlaneScatter(
        p,
        lambda c: PD.at[rows_at(c, rows)],
        lambda c, h: PD.at[pl.ds(pl.multiple_of(c * rows + h * half, half), half)],
        D1,
        D2,
        plane_sems.at[0],
    )

    def col_scatter(b):
        return PlaneScatter(
            p,
            lambda c: PH.at[pl.ds(b * rows, rows), rows_at(c, cw)],
            lambda c, h: PH.at[pl.ds(b * rows + h * half, half), rows_at(c, cw)],
            H1.at[b],
            H2.at[b],
            plane_sems.at[1 + b],
        )

    h_plane = [col_scatter(b) for b in range(n_ctx)]

    def partial_out(c):
        at = rows_at(c, rows)
        for j in range(0, width, cw):
            PD[at, j : j + cw] = dot(HID[at, :], WD[:, j : j + cw]).astype(bf16)

    partial_out(p.cd)
    y_plane.start()
    partial_out(p.cx)
    partial_out(p.cy)
    sum_line.combine()
    sum_line.step(1)
    partial_out(p.c)

    def back(b):
        at = pl.ds(b * rows, rows)
        r = R2[at, 0:1]
        stat = jnp.zeros((rows, 1), f32)
        for start, size in tiles_of(units, 512):
            cols = slice(start, start + size)
            grad_hidden = dot_nt(COT[at, :], WD[cols, :])
            gate = GATE[at, cols].astype(f32)
            up = UP[at, cols].astype(f32)
            sig = 0.5 + 0.5 * jnp.tanh(0.5 * gate)
            d_up = grad_hidden * gate * sig
            d_gate = grad_hidden * up * sig * (1.0 + gate * (1.0 - sig))
            stat += jnp.sum(d_gate * gate + d_up * up, axis=-1, keepdims=True)
            GATE[at, cols] = (d_gate * r).astype(bf16)
            UP[at, cols] = (d_up * r).astype(bf16)
        coef = r * r * stat * (1.0 / width)
        for j in range(0, width, cw):
            e = dot_nt(GATE[at, :], WG[j : j + cw, :]) + dot_nt(UP[at, :], WU[j : j + cw, :])
            PH[at, j : j + cw] = (e - M[at, j : j + cw].astype(f32) * coef).astype(bf16)
        h_plane[b].start()

    back(0)
    y_plane.middle()
    back(1)
    h_plane[0].middle()
    sum_line.step(2)
    back(2)
    h_plane[1].middle()
    back(3)
    h_plane[2].middle()

    stage_copies = {}
    jobs = []
    for src, dst in ((GATE, gate_part), (UP, up_part)):
        for at, size in tiles_of(width, 512):
            jobs.append((src, dst, at, size))

    def weight_tile(i):
        src, dst, at, size = jobs[i]
        slot = pl.ds(i % 2 * size, size)
        if i >= 2:
            stage_copies[i - 2].wait()
        for start, part in tiles_of(units, 512):
            cols = slice(start, start + part)
            HID[slot, cols] = dot_tn(M[:, at : at + size], src[:, cols]).astype(bf16)
        copy = pltpu.make_async_copy(HID.at[slot], dst.at[pl.ds(at, size)], stage_sems.at[2 + i % 2])
        copy.start()
        stage_copies[i] = copy

    def finish_block(b):
        at = pl.ds(b * rows, rows)
        mine = rows_at(p.c, cw)
        COT[at, mine] = (COT[at, mine].astype(f32) + h_plane[b].finish()).astype(bf16)

    weight_tile(0)
    cot_plane.drain()
    sum_line.step(3)
    h_plane[3].middle()
    weight_tile(1)
    weight_tile(2)
    finish_block(0)
    weight_tile(3)
    weight_tile(4)
    finish_block(1)
    weight_tile(5)
    weight_tile(6)
    finish_block(2)
    weight_tile(7)
    sum_line.step(4)
    sum_copy = pltpu.make_async_copy(sum_line.result(), down_sum, copy_sems.at[6])
    sum_copy.start()
    piece = rows // n_ctx
    for i in range(n_ctx):
        own = pl.ds(pl.multiple_of(p.c * rows + i * piece, piece), piece)
        mlp = y_plane.finish(pl.ds(i * piece, piece), i == 0)
        PD[own, :] = (M[own, :].astype(f32) + mlp).astype(bf16)
    y_copy = pltpu.make_async_copy(PD.at[rows_at(p.c, rows)], y_out, copy_sems.at[4])
    y_copy.start()
    finish_block(3)
    gm_copy = pltpu.make_async_copy(COT.at[:, rows_at(p.c, cw)], gm_out, copy_sems.at[5])
    gm_copy.start()
    stage_copies[6].wait()
    stage_copies[7].wait()
    y_copy.wait()
    gm_copy.wait()
    sum_copy.wait()
    sum_line.drain()
    down_line.drain()
    y_plane.drain()
    for b in range(n_ctx):
        h_plane[b].drain()


def middle_stage(m, cot, wgate, wup, w_down):
    n_fsdp, n_ctx = lax.axis_size("fsdp"), lax.axis_size("ctx")
    seq, width = m.shape
    rows = seq // n_ctx
    cw = width // n_ctx
    units = wgate.shape[1]
    unit = units // n_fsdp
    outs = [
        ((rows, width), bf16), ((units, width), bf16), ((unit, width), bf16), ((width, units), bf16),
        ((width, units), bf16), ((seq, cw), bf16),
    ]
    scratch = [
        pltpu.VMEM((seq, width), bf16),
        pltpu.VMEM((seq, width), bf16),
        pltpu.VMEM((width, units), bf16),
        pltpu.VMEM((width, units), bf16),
        pltpu.VMEM((units, width), bf16),
        pltpu.VMEM((seq, units), bf16),
        pltpu.VMEM((seq, units), bf16),
        pltpu.VMEM((seq, units), bf16),
        pltpu.VMEM((seq, 128), f32),
        pltpu.VMEM((seq, width), bf16),
        pltpu.VMEM((seq, width), bf16),
        pltpu.VMEM((2, rows // 2, width), bf16),
        pltpu.VMEM((2, rows, width), bf16),
        pltpu.VMEM((n_ctx, 2, rows // 2, cw), bf16),
        pltpu.VMEM((n_ctx, 2, rows, cw), bf16),
        pltpu.VMEM((n_fsdp // 2, unit, width), bf16),
        pltpu.VMEM((5, unit, width), bf16),
        pltpu.SemaphoreType.DMA((1, LineGather.SEMS)),
        pltpu.SemaphoreType.DMA((1, LineScatter.SEMS)),
        pltpu.SemaphoreType.DMA((6, PlaneScatter.SEMS)),
        pltpu.SemaphoreType.DMA((7,)),
        pltpu.SemaphoreType.DMA((4,)),
    ]
    flops = 18 * seq * width * units
    return call(middle_kernel, (m, cot, wgate, wup, w_down), outs, scratch, 2, flops, "middle_stage")


def backward_kernel(
    xn_in, r_in, grow_in, qt_in, kt_in, vt_in, lse_in, o_in, gm_in, wqkv_in, wout_in, tab_in,
    gate_part, up_part, down_sum,
    tok_out, qkv_all, out_all, gate_all, up_all, down_all,
    XN, R1, GROW, QT, KT, VT, LSE, O, GM, WQ, WO, TAB,
    K, V, DK, DV, DOT, DQT, DPRE, STAT, BIAS, PT, G1, G2, T1, T2, TOK,
    GACC, GSLOT, UACC, USLOT, OACC, OSLOT, QACC, QSLOT,
    line_sems, plane_sems, scatter_sems, copy_sems,
):
    p = Place()
    n_ctx = 4
    seq, width = XN.shape
    rows = seq // n_ctx
    half = rows // 2
    cw = width // n_ctx
    qw = QT.shape[0]
    heads = qw // HEAD_DIM
    nq = WQ.shape[1]
    own_rows = QACC.shape[1]
    scale = HEAD_DIM ** (-0.5)
    loads = []
    for i, (src, dst) in enumerate(
        (
            (gm_in, GM), (wout_in, WO), (o_in, O), (kt_in, KT), (vt_in, VT), (qt_in, QT), (lse_in, LSE),
            (tab_in, TAB), (xn_in, XN), (wqkv_in, WQ), (r_in, R1), (grow_in, GROW),
        )
    ):
        loads.append(pltpu.make_async_copy(src, dst, copy_sems.at[i]))
    loads[0].start()
    loads[1].start()

    p.barrier()

    def block_rows(ref):
        count = ref.shape[0] // (2 * p.depth)
        return lambda level, core: ref.at[pl.ds(pl.multiple_of((2 * level + core) * count, 16), count)]

    nu = GACC.shape[2]
    cols_stage = [XN.at[pl.ds(i * own_rows, own_rows), pl.ds(0, nu)] for i in range(2)]
    gate_line = LineScatter(p, block_rows(gate_part), GACC, GSLOT, line_sems.at[1], cols_stage)
    up_line = LineScatter(p, block_rows(up_part), UACC, USLOT, line_sems.at[2], cols_stage)
    out_line = LineScatter(p, block_rows(WO), OACC, OSLOT, line_sems.at[3])

    def qkv_block(level, core):
        f = 2 * level + core
        at = pl.ds(pl.multiple_of((f % p.depth) * own_rows, own_rows), own_rows)
        return O.at[at, pl.ds(pl.multiple_of((f // p.depth) * nq, 128), nq)]

    qkv_line = LineScatter(p, qkv_block, QACC, QSLOT, line_sems.at[4])
    gate_line.start()
    up_line.start()
    for i in (2, 3, 4, 5, 6, 7, 9, 10, 11):
        loads[i].start()

    def col_scatter(b):
        return PlaneScatter(
            p,
            lambda c: PT.at[pl.ds(b * rows, rows), rows_at(c, cw)],
            lambda c, h: PT.at[pl.ds(b * rows + h * half, half), rows_at(c, cw)],
            G1.at[b],
            G2.at[b],
            scatter_sems.at[b],
        )

    g_plane = [col_scatter(b) for b in range(n_ctx)]
    t_plane = PlaneScatter(
        p,
        lambda c: PT.at[rows_at(c, rows)],
        lambda c, h: PT.at[pl.ds(pl.multiple_of(c * rows + h * half, half), half)],
        T1,
        T2,
        scatter_sems.at[n_ctx],
    )

    def whole(ref, own, index, first):
        count = own.shape[0]

        def halves(c, h):
            return ref(c).at[pl.ds(h * first, count - first if h else first)]

        plane = PlaneGather(p, ref, halves, plane_sems.at[index], own=own)
        return plane, pltpu.make_async_copy(own, ref(p.c), plane_sems.at[index, PlaneGather.SEMS])

    unit = down_sum.shape[0]
    down_plane, down_own = whole(lambda c: down_all.at[c], down_sum, 0, unit // 32 * 16 + unit // 16 % 2 * 16)
    gate_plane, gate_own = whole(lambda c: gate_all.at[c], gate_line.result(), 1, own_rows // 2)
    up_plane, up_own = whole(lambda c: up_all.at[c], up_line.result(), 2, own_rows // 2)
    out_plane, out_own = whole(lambda c: out_all.at[c], out_line.result(), 3, own_rows // 2)
    qkv_plane, qkv_own = whole(lambda c: qkv_all.at[c], qkv_line.result(), 4, own_rows // 2)

    loads[0].wait()
    loads[1].wait()
    for b in range(n_ctx):
        at = pl.ds(b * rows, rows)
        for j in range(0, width, 512):
            PT[at, j : j + 512] = dot_nt(GM[at, :], WO[j : j + 512, :]).astype(bf16)
        g_plane[b].start()
    gate_line.combine()
    gate_line.step(1)
    g_plane[0].middle()
    loads[2].wait()

    @pl.loop(0, width // 512)
    def _(i):
        at = rows_at(i, 512)
        WO[at, :] = dot_tn(O[:, at], GM[...]).astype(bf16)

    out_line.start()
    g_plane[1].middle()
    up_line.combine()
    loads[8].start()
    up_line.step(1)
    g_plane[2].middle()
    for i in (3, 4, 5, 6, 7, 10):
        loads[i].wait()

    @pl.loop(0, n_ctx)
    def _(b):
        at = rows_at(b, rows)
        K[at, :] = KT[:, at].astype(f32).T.astype(bf16)
        V[at, :] = VT[:, at].astype(f32).T.astype(bf16)
        DK[at, :] = jnp.zeros((rows, HEAD_DIM), f32)
        DV[at, :] = jnp.zeros((rows, HEAD_DIM), f32)

    g_plane[3].middle()

    def attend_back(b):
        n = (b + 1) * rows
        cols = slice(b * rows, (b + 1) * rows)
        DOT[...] = g_plane[b].finish().T.astype(bf16)
        at = pl.ds(b * rows, rows)
        DQT[...] = O[at, rows_at(p.c, cw)].astype(f32).T
        key = lax.broadcasted_iota(jnp.int32, (n, rows), 0)
        query = lax.broadcasted_iota(jnp.int32, (n, rows), 1) + b * rows
        begin = TAB[b, 64:65, :].astype(jnp.int32)
        BIAS[0:n, :] = jnp.where((key <= query) & (key >= begin), 0.0, neg_large)
        STAT[...] = jnp.zeros((8, rows), f32)

        @pl.loop(0, heads)
        def _(h):
            head = rows_at(h, HEAD_DIM)
            q = QT[head, cols]
            d_out = DOT[head, :]
            delta = jnp.sum(d_out.astype(f32) * DQT[head, :], axis=0, keepdims=True)
            s = dot(K[0:n, :], q) * scale + BIAS[0:n, :]
            probs = jnp.exp(s - LSE[rows_at(h, 8), cols][0:1])
            d_probs = dot(V[0:n, :], d_out)
            d_s = (probs * (d_probs - delta)).astype(bf16)
            d_q = dot(KT[:, 0:n], d_s) * scale
            DK[0:n, :] += dot_nt(d_s, q) * scale
            DV[0:n, :] += dot_nt(probs.astype(bf16), d_out)
            STAT[...] += jnp.broadcast_to(jnp.sum(d_q * q.astype(f32), axis=0, keepdims=True), (8, rows))
            u, w = d_q[0:32], d_q[32:64]
            cosine, sine = TAB[b, 0:32, :], TAB[b, 32:64, :]
            DQT[head, :] = jnp.concatenate([u * cosine + w * sine, w * cosine - u * sine], axis=0)

        DPRE[at, 0:qw] = DQT[...].T.astype(bf16)
        R1[at, 0:8] = STAT[...].T

    attend_back(0)
    gate_line.step(2)
    attend_back(1)
    attend_back(2)
    down_plane.start()
    down_own.start()
    up_line.step(2)
    attend_back(3)
    loads[8].wait()
    loads[9].wait()
    loads[11].wait()

    @pl.loop(0, n_ctx)
    def _(b):
        at = rows_at(b, rows)
        d_k = DK[at, :].T
        d_v = DV[at, :].T
        stat = jnp.sum(d_k * KT[:, at].astype(f32) + d_v * VT[:, at].astype(f32), axis=0, keepdims=True)
        R1[at, 0:8] += jnp.broadcast_to(stat, (8, rows)).T
        u, w = d_k[0:32], d_k[32:64]
        cosine, sine = TAB[b, 0:32, :], TAB[b, 32:64, :]
        both = jnp.concatenate([u * cosine + w * sine, w * cosine - u * sine, d_v], axis=0)
        DPRE[at, qw:] = both.T.astype(bf16)

    def tokens(c):
        at = rows_at(c, rows)
        r = R1[at, 127:128]
        coef = r * R1[at, 0:1] * (1.0 / width)
        for j in range(0, width, 512):
            cols = slice(j, j + 512)
            gain = GROW[0:1, cols]
            e = dot_nt(DPRE[at, :], WQ[cols, :])
            PT[at, cols] = (e * (gain * r) - XN[at, cols].astype(f32) * ((1.0 / gain) * coef)).astype(bf16)
        mine = rows_at(p.c, cw)
        PT[at, mine] = (PT[at, mine].astype(f32) + GM[at, :].astype(f32)).astype(bf16)

    for b in range(n_ctx):
        g_plane[b].drain()
    tokens(p.cd)
    t_plane.start()
    tokens(p.cx)
    tokens(p.cy)
    t_plane.middle()
    tokens(p.c)

    @pl.loop(0, p.depth)
    def _(i):
        for j in range(2):
            at = rows_at(i + j * p.depth, own_rows)
            O[rows_at(i, own_rows), j * nq : (j + 1) * nq] = dot_tn(XN[:, at], DPRE[...]).astype(bf16)

    qkv_line.start()
    gate_line.step(3)
    down_plane.middle()
    out_line.combine()
    out_line.step(1)
    up_line.step(3)
    qkv_line.combine()
    qkv_line.step(1)
    gate_line.step(4)
    gate_plane.start()
    gate_own.start()
    out_line.step(2)
    tok_copies = []
    for i in range(n_ctx):
        if i >= 2:
            tok_copies[i - 2].wait()
        at = pl.ds(i * (rows // n_ctx), rows // n_ctx)
        TOK[i % 2] = t_plane.finish(at, i == 0)
        tok_copies.append(pltpu.make_async_copy(TOK.at[i % 2], tok_out.at[at], copy_sems.at[12 + i % 2]))
        tok_copies[-1].start()
    qkv_line.step(2)
    up_line.step(4)
    up_plane.start()
    up_own.start()
    gate_plane.middle()
    out_line.step(3)
    qkv_line.step(3)
    out_line.step(4)
    out_plane.start()
    out_own.start()
    up_plane.middle()
    qkv_line.step(4)
    qkv_plane.start()
    qkv_own.start()
    out_plane.middle()
    qkv_plane.middle()
    for plane, own in (
        (down_plane, down_own), (gate_plane, gate_own), (up_plane, up_own), (out_plane, out_own), (qkv_plane, qkv_own),
    ):
        plane.finish()
        own.wait()
        plane.drain()
    tok_copies[2].wait()
    tok_copies[3].wait()
    t_plane.drain()
    for line in (gate_line, up_line, out_line, qkv_line):
        line.drain()


def backward_stage(xn, r, grow, qt, kt, vt, lse, o, gm, wqkv, wout, tabs, gate_part, up_part, down_sum):
    n_fsdp, n_ctx = lax.axis_size("fsdp"), lax.axis_size("ctx")
    seq, width = xn.shape
    rows = seq // n_ctx
    half = rows // 2
    cw = width // n_ctx
    own = width // n_fsdp
    depth = n_fsdp // 2
    nq, nu = wqkv.shape[1], gate_part.shape[1]
    unit = down_sum.shape[0]
    qw = qt.shape[0]
    outs = [
        ((rows, width), f32), ((n_ctx, own, nq), bf16), ((n_ctx, own, cw), bf16), ((n_ctx, own, nu), bf16),
        ((n_ctx, own, nu), bf16), ((n_ctx, unit, width), bf16),
    ]
    ins = (xn, r, grow, qt, kt, vt, lse, o, gm, wqkv, wout, tabs, gate_part, up_part, down_sum)
    scratch = [pltpu.VMEM(a.shape, a.dtype) for a in ins[:12]] + [
        pltpu.VMEM((seq, HEAD_DIM), bf16),
        pltpu.VMEM((seq, HEAD_DIM), bf16),
        pltpu.VMEM((seq, HEAD_DIM), f32),
        pltpu.VMEM((seq, HEAD_DIM), f32),
        pltpu.VMEM((qw, rows), bf16),
        pltpu.VMEM((qw, rows), f32),
        pltpu.VMEM((seq, nq), bf16),
        pltpu.VMEM((8, rows), f32),
        pltpu.VMEM((seq, rows), f32),
        pltpu.VMEM((seq, width), bf16),
        pltpu.VMEM((n_ctx, 2, half, cw), bf16),
        pltpu.VMEM((n_ctx, 2, rows, cw), bf16),
        pltpu.VMEM((2, half, width), bf16),
        pltpu.VMEM((2, rows, width), bf16),
        pltpu.VMEM((2, rows // n_ctx, width), f32),
        pltpu.VMEM((depth, own, nu), bf16),
        pltpu.VMEM((5, own, nu), bf16),
        pltpu.VMEM((depth, own, nu), bf16),
        pltpu.VMEM((5, own, nu), bf16),
        pltpu.VMEM((depth, own, cw), bf16),
        pltpu.VMEM((5, own, cw), bf16),
        pltpu.VMEM((depth, own, nq), bf16),
        pltpu.VMEM((5, own, nq), bf16),
        pltpu.SemaphoreType.DMA((5, LineScatter.SEMS)),
        pltpu.SemaphoreType.DMA((5, PlaneGather.SEMS + 1)),
        pltpu.SemaphoreType.DMA((n_ctx + 1, PlaneScatter.SEMS)),
        pltpu.SemaphoreType.DMA((14,)),
    ]
    flops = 4 * seq * width * (nq + cw) + 20 * qw * seq * seq
    return call(backward_kernel, ins, outs, scratch, 3, flops, "backward_stage")


def finish_kernel(
    unit, qkv, out, gate, up, down, tok, y, w_query, w_key, w_value, w_gate, w_up, g1, g2,
    o_query, o_key, o_value, o_out, o_gate, o_up, o_down, o_tok, o_y, o_g1, o_g2,
):
    n_ctx = qkv.shape[0]
    qw = o_query.shape[1] // n_ctx
    cw = out.shape[2]
    for c in range(n_ctx):
        o_query[:, c * qw : (c + 1) * qw] = qkv[c, :, 0:qw].astype(f32)
        o_key[:, c * HEAD_DIM : (c + 1) * HEAD_DIM] = qkv[c, :, qw : qw + HEAD_DIM].astype(f32)
        o_value[:, c * HEAD_DIM : (c + 1) * HEAD_DIM] = qkv[c, :, qw + HEAD_DIM :].astype(f32)
        o_out[:, c * cw : (c + 1) * cw] = out[c].astype(f32)

    def total(ref, w):
        return jnp.sum(ref[...] * w[...].astype(f32), axis=-1, keepdims=True)

    first = total(o_query, w_query) + total(o_key, w_key) + total(o_value, w_value)
    o_g1[...] = jnp.broadcast_to(first / g1[:, 0:1], o_g1.shape)
    gain = g2[:, 0:1]
    for src, dst in ((gate, o_gate), (up, o_up)):
        for f in range(src.shape[2] // unit):
            for c in range(n_ctx):
                at = (f * n_ctx + c) * unit
                dst[:, at : at + unit] = src[c, :, f * unit : (f + 1) * unit].astype(f32) * gain
    second = total(o_gate, w_gate) + total(o_up, w_up)
    o_g2[...] = jnp.broadcast_to(second / gain, o_g2.shape)
    o_down[...] = down[...].astype(f32)
    o_tok[...] = tok[...]
    o_y[...] = y[...]


def finish_stage(qkv, out, gate, up, down, tok, y, w_query, w_key, w_value, w_gate, w_up, g1, g2):
    steps = 4
    n_fsdp = lax.axis_size("fsdp")
    own = w_query.shape[0]
    down = down.reshape(-1, down.shape[-1])
    unit = gate.shape[2] // n_fsdp

    def spec(shape):
        if len(shape) == 3:
            return pl.BlockSpec((shape[0], shape[1] // steps, shape[2]), lambda i: (0, i, 0))
        return pl.BlockSpec((shape[0] // steps, shape[1]), lambda i: (i, 0))

    ins = (qkv, out, gate, up, down, tok, y, w_query, w_key, w_value, w_gate, w_up, g1, g2)
    outs = [
        (w_query.shape, f32), (w_key.shape, f32), (w_value.shape, f32), ((own, out.shape[0] * out.shape[2]), f32),
        (w_gate.shape, f32), (w_up.shape, f32), (down.shape, f32), (tok.shape, f32), (y.shape, bf16),
        ((own, 128), f32), ((own, 128), f32),
    ]
    return pl.pallas_call(
        functools.partial(finish_kernel, unit),
        grid=(steps,),
        out_shape=[jax.ShapeDtypeStruct(s, d) for s, d in outs],
        in_specs=[spec(a.shape) for a in ins],
        out_specs=[spec(s) for s, d in outs],
        compiler_params=pltpu.CompilerParams(vmem_limit_bytes=56 * 2**20),
        name="finish_stage",
    )(*ins)


def rotate(field, cosine, sine_table, direction):
    half_width = field.shape[-1] // 2
    first_half = field[..., :half_width]
    second_half = field[..., half_width:]
    return jnp.concatenate(
        [
            first_half * cosine - direction * second_half * sine_table,
            second_half * cosine + direction * first_half * sine_table,
        ],
        axis=-1,
    )


def gather(x, axis_name, axis=0):
    return lax.all_gather(x, axis_name, axis=axis, tiled=True)


def scatter(x, axis_name, axis=0):
    return lax.psum_scatter(x.astype(bf16), axis_name, scatter_dimension=axis, tiled=True)


def columns(w, start, count):
    return lax.dynamic_slice_in_dim(w, start, count, axis=1)


def visible(begin):
    seq = begin.shape[0]
    index = jnp.arange(seq, dtype=jnp.int32)
    return (index[None, :] <= index[:, None]) & (index[None, :] >= begin[:, None])


def forward_plain(tok, tab, gains, gcol, w_query, w_key, w_value, w_out, w_gate, w_up):
    n_ctx, n_fsdp = lax.axis_size("ctx"), lax.axis_size("fsdp")
    c = lax.axis_index("ctx")
    own_rows = w_query.shape[0]
    qw = HEADS // n_ctx * HEAD_DIM
    copies = max(1, n_ctx // KV_HEADS)
    kvw = max(1, KV_HEADS // n_ctx) * HEAD_DIM
    unit = w_gate.shape[1] // (n_fsdp * n_ctx)
    cw = tok.shape[1] // n_ctx
    wqkv_o = jnp.concatenate(
        [
            columns(w_query, c * qw, qw),
            columns(w_key, (c // copies) * kvw, kvw),
            columns(w_value, (c // copies) * kvw, kvw),
        ],
        axis=1,
    )
    wout_o = columns(w_out, c * cw, cw)

    def units(w):
        parts = w.reshape(own_rows, n_fsdp, n_ctx, unit)
        mine = lax.dynamic_index_in_dim(parts, c, axis=2, keepdims=False)
        return (gcol[:, 0:1] * mine.reshape(own_rows, n_fsdp * unit)).astype(bf16)

    wgate_o, wup_o = units(w_gate), units(w_up)
    x = gather(tok, "ctx")
    tabs = gather(tab[None], "ctx")
    wqkv = gather(wqkv_o, "fsdp")
    wout = gather(wout_o, "fsdp")
    wgate = gather(wgate_o, "fsdp")
    wup = gather(wup_o, "fsdp")
    gain = gather(gains[0:1], "fsdp", axis=1).astype(f32)
    xf = x.astype(f32)
    r = lax.rsqrt(jnp.mean(xf * xf, axis=-1, keepdims=True) + eps_norm)
    xn = (xf * r * gain).astype(bf16)
    seq, width = x.shape
    heads = HEADS // n_ctx
    qw = heads * HEAD_DIM
    pre = dot(xn, wqkv)
    cosine = tabs[:, 0:32].transpose(0, 2, 1).reshape(seq, 1, 32)
    sine = tabs[:, 32:64].transpose(0, 2, 1).reshape(seq, 1, 32)
    begin = tabs[:, 64].reshape(seq).astype(jnp.int32)
    kvw = (wqkv.shape[1] - qw) // 2
    kv = kvw // HEAD_DIM
    q = rotate(pre[:, :qw].reshape(seq, heads, HEAD_DIM), cosine, sine, 1.0).astype(bf16)
    k = rotate(pre[:, qw : qw + kvw].reshape(seq, kv, HEAD_DIM), cosine, sine, 1.0).astype(bf16)
    v = pre[:, qw + kvw :].astype(bf16).reshape(seq, kv, HEAD_DIM)
    qg = q.reshape(seq, kv, heads // kv, HEAD_DIM)
    scores = jnp.einsum("qkgd,lkd->kgql", qg, k, preferred_element_type=f32) * HEAD_DIM ** (-0.5)
    scores = jnp.where(visible(begin)[None, None], scores, neg_large)
    top = jnp.max(scores, axis=-1, keepdims=True)
    weights = jnp.exp(scores - top)
    total = jnp.sum(weights, axis=-1, keepdims=True)
    probs_low = (weights / total).astype(bf16)
    att = jnp.einsum("kgql,lkd->qkgd", probs_low, v, preferred_element_type=f32)
    o = gather(att.astype(bf16).reshape(seq, qw), "ctx", axis=1)
    lse = (top + jnp.log(total)).reshape(heads, 1, seq)
    lse = jnp.broadcast_to(lse, (heads, 8, seq)).reshape(8 * heads, seq)
    cw = width // n_ctx
    mid = columns(x, c * cw, cw).astype(f32) + dot(o, wout)
    m = gather(mid.astype(bf16), "ctx", axis=1)
    qt = q.reshape(seq, qw).T
    kt = k.reshape(seq, kvw).T
    vt = v.reshape(seq, kvw).T
    r = jnp.broadcast_to(r, (seq, 128))
    grow = jnp.broadcast_to(gain, (8, width))
    return xn, r, grow, qt, kt, vt, lse, o, m, wqkv, wout, wgate, wup, tabs


def middle_plain(m, cot, wgate, wup, w_down):
    n_ctx = lax.axis_size("ctx")
    c = lax.axis_index("ctx")
    unit = w_down.shape[0] // n_ctx
    wdown_o = lax.dynamic_slice_in_dim(w_down, c * unit, unit, axis=0)
    seq, width = m.shape
    rows = seq // n_ctx
    cw = width // n_ctx
    wdown = gather(wdown_o, "fsdp")
    cot_all = gather(cot, "ctx")
    mf = m.astype(f32)
    r = lax.rsqrt(jnp.mean(mf * mf, axis=-1, keepdims=True) + eps_norm)
    gate = dot(m, wgate) * r
    up = dot(m, wup) * r
    sig = jax.nn.sigmoid(gate)
    hidden = (gate * sig * up).astype(bf16)
    mlp = scatter(dot(hidden, wdown), "ctx").astype(f32)
    mid_rows = lax.dynamic_slice_in_dim(m, c * rows, rows, axis=0).astype(f32)
    output = (mid_rows + mlp).astype(bf16)
    grad_hidden = dot_nt(cot_all, wdown)
    down_sum = scatter(dot_tn(hidden, cot_all), "fsdp")
    d_gate = grad_hidden * up * sig * (1.0 + gate * (1.0 - sig))
    d_up = grad_hidden * gate * sig
    stat = jnp.sum(d_gate * gate + d_up * up, axis=-1, keepdims=True)
    d_gate = (d_gate * r).astype(bf16)
    d_up = (d_up * r).astype(bf16)
    gate_raw = dot_tn(m, d_gate).astype(bf16)
    up_raw = dot_tn(m, d_up).astype(bf16)
    back = dot_nt(d_gate, wgate) + dot_nt(d_up, wup) - mf * (r * r * stat * (1.0 / width))
    back_own = scatter(back, "ctx", axis=1).astype(f32)
    gm = (columns(cot_all, c * cw, cw).astype(f32) + back_own).astype(bf16)
    return output, None, down_sum, gate_raw, up_raw, gm


def backward_plain(xn, r, grow, qt, kt, vt, lse, o, gm, wqkv, wout, tabs, gate_raw, up_raw, down_sum):
    n_ctx = lax.axis_size("ctx")
    c = lax.axis_index("ctx")
    seq, width = xn.shape
    r, gain = r[:, 0:1], grow[0:1]
    heads = HEADS // n_ctx
    qw = heads * HEAD_DIM
    kvw = kt.shape[0]
    kv = kvw // HEAD_DIM
    cw = width // n_ctx
    scale = HEAD_DIM ** (-0.5)
    cosine = tabs[:, 0:32].transpose(0, 2, 1).reshape(seq, 1, 32)
    sine = tabs[:, 32:64].transpose(0, 2, 1).reshape(seq, 1, 32)
    begin = tabs[:, 64].reshape(seq).astype(jnp.int32)
    gate_grad = scatter(gate_raw, "fsdp")
    up_grad = scatter(up_raw, "fsdp")
    out_grad = scatter(dot_tn(o, gm), "fsdp")
    d_att = scatter(dot_nt(gm, wout), "ctx", axis=1).reshape(seq, kv, heads // kv, HEAD_DIM)
    q = qt.T.reshape(seq, kv, heads // kv, HEAD_DIM)
    k = kt.T.reshape(seq, kv, HEAD_DIM)
    v = vt.T.reshape(seq, kv, HEAD_DIM)
    scores = jnp.einsum("qkgd,lkd->kgql", q, k, preferred_element_type=f32) * scale
    scores = jnp.where(visible(begin)[None, None], scores, neg_large)
    lse = lse.reshape(kv, heads // kv, 8, seq)[:, :, 0, :, None]
    probs = jnp.exp(scores - lse)
    d_probs = jnp.einsum("qkgd,lkd->kgql", d_att, v, preferred_element_type=f32)
    delta = jnp.sum(probs * d_probs, axis=-1, keepdims=True)
    d_scores = (probs * (d_probs - delta)).astype(bf16)
    d_q = jnp.einsum("kgql,lkd->qkgd", d_scores, k, preferred_element_type=f32) * scale
    d_k = jnp.einsum("kgql,qkgd->lkd", d_scores, q, preferred_element_type=f32) * scale
    d_v = jnp.einsum("kgql,qkgd->lkd", probs.astype(bf16), d_att, preferred_element_type=f32)
    stat = (
        jnp.sum(d_q * q, axis=(1, 2, 3)) + jnp.sum(d_k * k, axis=(1, 2)) + jnp.sum(d_v * v, axis=(1, 2))
    )[:, None]
    d_q = rotate(d_q.reshape(seq, heads, HEAD_DIM), cosine, sine, -1.0).reshape(seq, qw)
    d_k = rotate(d_k, cosine, sine, -1.0).reshape(seq, kvw)
    d_pre = jnp.concatenate([d_q, d_k, d_v.reshape(seq, kvw)], axis=1).astype(bf16)
    qkv_grad = scatter(dot_tn(xn, d_pre), "fsdp")
    back = dot_nt(d_pre, wqkv) * (gain * r)
    back = back - xn.astype(f32) * ((1.0 / gain) * (r * stat * (1.0 / width)))
    at = (jnp.arange(width, dtype=jnp.int32) // cw == c)[None, :]
    back = back + jnp.where(at, jnp.tile(gm.astype(f32), (1, n_ctx)), 0.0)
    grad_tokens = scatter(back, "ctx").astype(f32)
    qkv_all = gather(qkv_grad[None], "ctx")
    out_all = gather(out_grad[None], "ctx")
    gate_all = gather(gate_grad[None], "ctx")
    up_all = gather(up_grad[None], "ctx")
    down_all = gather(down_sum[None], "ctx")
    return grad_tokens, qkv_all, out_all, gate_all, up_all, down_all


def finish_plain(qkv_all, out_all, gate_all, up_all, down_all, tok, y, w_query, w_key, w_value, w_gate, w_up, g1, g2):
    n_ctx, n_fsdp = lax.axis_size("ctx"), lax.axis_size("fsdp")
    own_rows = w_query.shape[0]
    qw = HEADS // n_ctx * HEAD_DIM
    copies = max(1, n_ctx // KV_HEADS)
    kvw = max(1, KV_HEADS // n_ctx) * HEAD_DIM
    ff_width = w_gate.shape[1]
    unit = ff_width // (n_fsdp * n_ctx)
    qkv_all = qkv_all.astype(f32)

    def joined(part):
        return jnp.moveaxis(part, 0, 1).reshape(own_rows, -1)

    def kv_part(part):
        return joined(part.reshape(n_ctx // copies, copies, own_rows, kvw).sum(axis=1))

    grad_query = joined(qkv_all[:, :, :qw])
    grad_key = kv_part(qkv_all[:, :, qw : qw + kvw])
    grad_value = kv_part(qkv_all[:, :, qw + kvw :])
    grad_out = joined(out_all.astype(f32))

    def spread(full):
        full = full.reshape(n_ctx, own_rows, n_fsdp, unit)
        return full.transpose(1, 2, 0, 3).reshape(own_rows, ff_width).astype(f32)

    raw_gate, raw_up = spread(gate_all), spread(up_all)
    grad_down = down_all.astype(f32).reshape(-1, down_all.shape[-1])

    def gain_term(grad, w):
        return jnp.sum(grad * w.astype(f32), axis=1, keepdims=True)

    first = gain_term(grad_query, w_query) + gain_term(grad_key, w_key) + gain_term(grad_value, w_value)
    second = gain_term(raw_gate, w_gate) + gain_term(raw_up, w_up)
    g1, g2 = g1[:, 0:1], g2[:, 0:1]
    return (
        grad_query, grad_key, grad_value, grad_out, g2 * raw_gate, g2 * raw_up, grad_down, tok, y, first / g1, second,
    )


def per_device(
    tokens,
    positions,
    gain_attn,
    gain_mlp,
    w_query,
    w_key,
    w_value,
    w_out,
    w_gate,
    w_up,
    w_down,
    cotangent,
):
    kernels = lax.axis_size("ctx") == 4 and lax.axis_size("fsdp") == 8
    c = lax.axis_index("ctx")
    rows = tokens.shape[0]
    own_rows = w_query.shape[0]
    gains = jnp.broadcast_to(gain_attn[None, :], (16, own_rows))
    gain_one = jnp.broadcast_to(gain_attn.astype(f32)[:, None], (own_rows, 128))
    gain_two = jnp.broadcast_to(gain_mlp.astype(f32)[:, None], (own_rows, 128))
    frequency = theta_base ** (-(jnp.arange(HEAD_DIM // 2, dtype=f32) * 2.0) / HEAD_DIM)
    angles = frequency[:, None] * positions.astype(f32)[None, :]
    begin = c * rows + jnp.arange(rows, dtype=jnp.int32) - positions
    tab = jnp.concatenate(
        [jnp.cos(angles), jnp.sin(angles), jnp.broadcast_to(begin.astype(f32)[None, :], (16, rows))],
        axis=0,
    )

    forward = forward_stage if kernels else forward_plain
    xn, r, grow, qt, kt, vt, lse, o, m, wqkv, wout, wgate, wup, tabs = forward(
        tokens, tab, gains, gain_two, w_query, w_key, w_value, w_out, w_gate, w_up
    )
    middle = middle_stage if kernels else middle_plain
    y, _, down_sum, gate_raw, up_raw, gm = middle(m, cotangent, wgate, wup, w_down)
    backward = backward_stage if kernels else backward_plain
    tok, qkv_all, out_all, gate_all, up_all, down_all = backward(
        xn, r, grow, qt, kt, vt, lse, o, gm, wqkv, wout, tabs, gate_raw, up_raw, down_sum
    )
    finish = finish_stage if kernels else finish_plain
    g_query, g_key, g_value, g_out, g_gate, g_up, g_down, tok, y, g_one, g_two = finish(
        qkv_all, out_all, gate_all, up_all, down_all, tok, y,
        w_query, w_key, w_value, w_gate, w_up, gain_one, gain_two,
    )
    return (y, tok, g_one[:, 0], g_two[:, 0], g_query, g_key, g_value, g_out, g_gate, g_up, g_down)


def solution(mesh):
    both = P(("fsdp", "ctx"), None)
    first = P("fsdp", None)
    return jax.shard_map(
        per_device,
        mesh=mesh,
        in_specs=(both, P(("fsdp", "ctx")), P("fsdp"), P("fsdp")) + (first,) * 7 + (both,),
        out_specs=(both, both, P("fsdp"), P("fsdp")) + (first,) * 7,
        check_vma=False,
    )
```
